32 devices in a mesh: runs: 2 (over y), gx: 16 (over z, x, core).
Axes of the slice: x: 2, y: 2, z: 4, core: 2. Of those that a mesh axis runs over, the one named last changes fastest.
Arguments:
- blocks: float32 [2048, 5, 512], P(('runs', 'gx')), parts along dimension 0, as said below
- owner_list: int32 [2048], P('runs'), parts along dimension 0, may hold values from 0 to 15, as said below
- slot_list: int32 [2048], P('runs'), parts along dimension 0, may hold values from 0 to 63, as said below
Outputs:
- advanced: float32 [5, 256, 32, 128], P(None, ('runs', 'gx')), parts along dimension 1
The draws below stay inside these ranges and needn't reach their ends.
There are 2 independent parts, one for each index of `runs`. The reference program is written for one: setup_inputs(seed, part) draws one part's arguments, and reference() takes and returns one part's arrays. A program takes and returns all parts, laid end to end along the dimension named above; each array names one. Nothing has to cross between parts.
Inputs may be any that keep to these rules, and one draw needn't show every extreme that they name: `owner_list`: entry i names block i's new owner; the 64 blocks listed for one device (entries in aligned groups of 64) go to 8 distinct devices, exactly 8 to each, and every device receives 64 blocks. The pairs (owner_list[i], slot_list[i]) are all distinct. `blocks`: density and pressure are positive in every cell.
All inputs are finite; a program needn't handle non-finite values.
Results may differ from the reference program's by a relative error of at most 0.00002.
Values sent between devices are 32-bit elements; how exact they have to be, the bound alone decides.
No kernel may reach another device: no remote copies, remote signals or barrier semaphores. Data moves between devices by JAX's collectives and lax.ppermute only.
A program may use at most 64 MiB of HBM per device.

```python
import jax
import jax.numpy as jnp
from jax import lax

BLOCK = 8
BY = 4
BZ = 16
BPD = 64
CAP = 8
NBLK = 1024
NX = 128
NY = 32
NZ = 128
N_GX = 16


def routing(key):
    key_tau, key_pi, key_offset, key_rho, key_phi = jax.random.split(key, 5)
    groups = BPD // CAP
    tau_perm = jax.random.permutation(key_tau, N_GX)
    pi_perm = jax.random.permutation(key_pi, N_GX)
    offsets = jax.random.permutation(key_offset, N_GX)[:groups]
    rho_perm = jax.vmap(lambda sub_key: jax.random.permutation(sub_key, BPD))(jax.random.split(key_rho, N_GX))
    group_of = rho_perm // CAP
    within = rho_perm % CAP
    destination = pi_perm[(tau_perm[:, None] + offsets[group_of]) % N_GX]
    phi_perm = jax.vmap(lambda sub_key: jax.random.permutation(sub_key, BPD))(jax.random.split(key_phi, N_GX))
    new_slot = phi_perm[destination, group_of * CAP + within]
    return (destination.reshape(-1).astype(jnp.int32), new_slot.reshape(-1).astype(jnp.int32))


def draw_owner_list(key, part):
    return routing(key)[0]


def draw_slot_list(key, part):
    return routing(key)[1]


def heated_rows(key, owners, slots):
    key_owner, key_slot = jax.random.split(key, 2)
    hot_owner = jax.random.randint(key_owner, (), N_GX // 2, N_GX)
    hot_slot = jax.random.randint(key_slot, (), 0, BPD)
    hot_block = jnp.argmax(((owners == hot_owner) & (slots == hot_slot)).astype(jnp.int32))
    return (jnp.arange(NBLK) == hot_block)[:, None]


def draw_blocks(key, part):
    owners, slots = routing(key)
    key = jax.random.fold_in(key, 7)
    key_density, key_pressure, key_velocity, key_hot, key_strength = jax.random.split(key, 5)
    trend = (owners.astype(jnp.float32) / (N_GX - 1))[:, None]
    hot_row = heated_rows(key_hot, owners, slots)
    cells = BLOCK ** 3
    density = jax.random.uniform(key_density, (NBLK, cells), jnp.float32, 0.8, 1.6)
    pressure = (1.0 + 2.0 * trend) * jax.random.uniform(key_pressure, (NBLK, cells), jnp.float32, 0.8, 1.6)
    velocity = 0.2 * jax.random.truncated_normal(key_velocity, -3.0, 3.0, (3, NBLK, cells), jnp.float32)
    strength = jnp.exp(jax.random.uniform(key_strength, (), jnp.float32, jnp.log(2.0), jnp.log(10.0)))
    pressure = jnp.where(hot_row, strength * pressure, pressure)
    momentum = density[None] * velocity
    energy = pressure / 0.4 + 0.5 * density * jnp.sum(velocity * velocity, axis=0)
    return jnp.stack([density, momentum[0], momentum[1], momentum[2], energy], axis=1).astype(jnp.float32)


def setup_inputs(seed: int = 0, part: int = 0) -> dict:
    streams_of = jax.random.split(jax.random.key(seed), 4)
    part_splits = jax.random.split(jax.random.fold_in(streams_of[3], part), 4)
    return {
        "blocks": draw_blocks(jax.random.fold_in(jax.random.fold_in(streams_of[3], part), 71), part),
        "owner_list": draw_owner_list(jax.random.fold_in(jax.random.fold_in(streams_of[3], part), 71), part),
        "slot_list": draw_slot_list(jax.random.fold_in(jax.random.fold_in(streams_of[3], part), 71), part),
    }


gamma_gas = 1.4
courant = 0.25
smooth_epsilon = 1e-06

def primitive(fields):
    density = fields[0]
    velocity = (fields[1] / density, fields[2] / density, fields[3] / density)
    kinetic = 0.5 * (fields[1] * velocity[0] + fields[2] * velocity[1] + fields[3] * velocity[2])
    pressure = (gamma_gas - 1.0) * (fields[4] - kinetic)
    return (density, velocity, pressure)

def wave_speed(fields):
    density, velocity, pressure = primitive(fields)
    sound_speed = jnp.sqrt(gamma_gas * pressure / density)
    fastest = jnp.maximum(jnp.maximum(jnp.abs(velocity[0]), jnp.abs(velocity[1])), jnp.abs(velocity[2]))
    return fastest + sound_speed

def euler_flux(conserved, direction):
    density, velocity, pressure = primitive(conserved)
    normal_speed = velocity[direction]
    components = [conserved[1 + direction], conserved[1] * normal_speed, conserved[2] * normal_speed, conserved[3] * normal_speed, (conserved[4] + pressure) * normal_speed]
    components[1 + direction] = components[1 + direction] + pressure
    return jnp.stack(components, axis=0)

def split_flux(conserved, direction, speed_max):
    flux_total = euler_flux(conserved, direction)
    return (0.5 * (flux_total + speed_max * conserved), 0.5 * (flux_total - speed_max * conserved))

def reconstruct(outer_left, inner_left, centre, inner_right, outer_right):
    smooth_zero = 13.0 / 12.0 * (outer_left - 2.0 * inner_left + centre) ** 2 + 0.25 * (outer_left - 4.0 * inner_left + 3.0 * centre) ** 2
    smooth_one = 13.0 / 12.0 * (inner_left - 2.0 * centre + inner_right) ** 2 + 0.25 * (inner_left - inner_right) ** 2
    smooth_two = 13.0 / 12.0 * (centre - 2.0 * inner_right + outer_right) ** 2 + 0.25 * (3.0 * centre - 4.0 * inner_right + outer_right) ** 2
    guess_zero = (2.0 * outer_left - 7.0 * inner_left + 11.0 * centre) / 6.0
    guess_one = (-inner_left + 5.0 * centre + 2.0 * inner_right) / 6.0
    guess_two = (2.0 * centre + 5.0 * inner_right - outer_right) / 6.0
    weight_zero = 0.1 / (smooth_epsilon + smooth_zero) ** 2
    weight_one = 0.6 / (smooth_epsilon + smooth_one) ** 2
    weight_two = 0.3 / (smooth_epsilon + smooth_two) ** 2
    return (weight_zero * guess_zero + weight_one * guess_one + weight_two * guess_two) / (weight_zero + weight_one + weight_two)

def rolled_divergence(conserved, direction, speed_max):
    flux_plus, flux_minus = split_flux(conserved, direction, speed_max)

    def one_field(pair):
        upwind, downwind = pair

        def rolled(values, amount):
            return jnp.roll(values, amount, axis=direction)
        face_flux = reconstruct(rolled(upwind, 3), rolled(upwind, 2), rolled(upwind, 1), upwind, rolled(upwind, -1)) + reconstruct(rolled(downwind, -2), rolled(downwind, -1), downwind, rolled(downwind, 1), rolled(downwind, 2))
        return jnp.roll(face_flux, -1, axis=direction) - face_flux
    return lax.map(one_field, (flux_plus, flux_minus))

def tendency(conserved, speed_max):
    return -(rolled_divergence(conserved, 0, speed_max) + rolled_divergence(conserved, 1, speed_max) + rolled_divergence(conserved, 2, speed_max))

def reference(blocks, owner_list, slot_list):
    placed = jnp.zeros_like(blocks).at[owner_list * BPD + slot_list].set(blocks)
    start = placed.reshape(N_GX, BY, BZ, 5, BLOCK, BLOCK, BLOCK).transpose(3, 0, 4, 1, 5, 2, 6).reshape(5, NX, NY, NZ)
    first_max = jnp.max(wave_speed(start))
    step_size = courant / first_max
    middle = start + step_size * tendency(start, first_max)
    second_max = jnp.max(wave_speed(middle))
    return 0.5 * start + 0.5 * (middle + step_size * tendency(middle, second_max))
```

```python
import functools
import math

import jax
import jax.numpy as jnp
from jax import lax
from jax.experimental import pallas as pl
from jax.experimental.pallas import tpu as pltpu
from jax.sharding import PartitionSpec as P

BLOCK = 8
BY = 4
BZ = 16
FIELDS = 5
LANES = 128
ROWS = BY * BLOCK
CHUNKS = ((0, 3), (1, 2))

gamma_gas = 1.4
courant = 0.25
smooth_epsilon = 1e-06

VMEM = pl.BlockSpec(memory_space=pltpu.VMEM)
SMEM = pl.BlockSpec(memory_space=pltpu.SMEM)


def params():
    return pltpu.CompilerParams(vmem_limit_bytes=40 * 1024 * 1024)


def cost(flops, size):
    return pl.CostEstimate(flops=flops, bytes_accessed=size, transcendentals=0)


def wave_speed(fields):
    density, mom_x, mom_y, mom_z, energy = fields
    inverse = 1.0 / density
    vel = (mom_x * inverse, mom_y * inverse, mom_z * inverse)
    kinetic = 0.5 * (mom_x * vel[0] + mom_y * vel[1] + mom_z * vel[2])
    pressure = (gamma_gas - 1.0) * (energy - kinetic)
    sound = jnp.sqrt(gamma_gas * pressure * inverse)
    fastest = jnp.maximum(jnp.maximum(jnp.abs(vel[0]), jnp.abs(vel[1])), jnp.abs(vel[2]))
    return fastest + sound


def pack_kernel(dev_count, cap, per_dev, owner_ref, blocks_ref, out_a, out_b, count, best):
    own = lax.axis_index("gx")
    tiles = (2 * FIELDS + 1, 2 * FIELDS)
    outs = (out_a, out_b)

    def clear(dest, carry):
        count[dest] = 0
        return carry

    lax.fori_loop(0, dev_count, clear, 0)

    def place(block, carry):
        dest = owner_ref[own * per_dev + block]
        rank = count[dest]
        count[dest] = rank + 1
        for chunk in range(2):
            base = dest * (tiles[chunk] * cap) + rank
            for half in range(2):
                pair = CHUNKS[chunk][half]
                value = blocks_ref[block, :, pair * LANES : (pair + 1) * LANES]
                outs[chunk][pl.ds(base + half * FIELDS * cap, FIELDS, stride=cap), :] = value
        return carry

    lax.fori_loop(0, per_dev, place, 0, unroll=4)
    best[...] = jnp.zeros_like(best)

    def speeds(dest, carry):
        @pl.when(count[dest] > 0)
        def _():
            for chunk in range(2):
                for half in range(2):
                    base = dest * (tiles[chunk] * cap) + half * FIELDS * cap
                    fields = [
                        outs[chunk][pl.ds(pl.multiple_of(base + f * cap, cap), cap), :]
                        for f in range(FIELDS)
                    ]
                    best[...] = jnp.maximum(best[...], wave_speed(fields))

        return carry

    lax.fori_loop(0, dev_count, speeds, 0)
    top = jnp.full((cap, LANES), jnp.max(best[...]), jnp.float32)

    def publish(dest, carry):
        base = dest * (tiles[0] * cap) + 2 * FIELDS * cap
        out_a[pl.ds(pl.multiple_of(base, cap), cap), :] = top
        return carry

    lax.fori_loop(0, dev_count, publish, 0)


def pack(blocks, owner_list, dev_count, cap):
    per_dev = blocks.shape[0]
    rows_a = dev_count * cap * (2 * FIELDS + 1)
    rows_b = dev_count * cap * 2 * FIELDS
    return pl.pallas_call(
        functools.partial(pack_kernel, dev_count, cap, per_dev),
        out_shape=(
            jax.ShapeDtypeStruct((rows_a, LANES), jnp.float32),
            jax.ShapeDtypeStruct((rows_b, LANES), jnp.float32),
        ),
        in_specs=[SMEM, VMEM],
        out_specs=(VMEM, VMEM),
        scratch_shapes=[
            pltpu.SMEM((dev_count,), jnp.int32),
            pltpu.VMEM((cap, LANES), jnp.float32),
        ],
        compiler_params=params(),
        cost_estimate=cost(10_000_000, 3_000_000),
        name="pack",
    )(owner_list, blocks)


def arrival_rows(owner_list, slot_list, own, per_dev, dev_count, cap):
    owners = owner_list.reshape(dev_count, per_dev)
    slots = slot_list.reshape(dev_count, per_dev)
    mine = owners == own
    spot = jnp.arange(per_dev, dtype=jnp.int32)
    earlier = spot[None, :] < spot[:, None]
    rank = jnp.sum((mine[:, None, :] & earlier[None]).astype(jnp.int32), axis=2)
    row = jnp.arange(dev_count, dtype=jnp.int32)[:, None] * cap + rank
    key = jnp.where(mine, slots, -1)
    hit = key.reshape(1, -1) == spot[:, None]
    return jnp.max(jnp.where(hit, row.reshape(1, -1), 0), axis=1)


def transposed(rows, group):
    rows = list(rows)
    for bit in range(4):
        step = 1 << bit
        low = (group & step) == 0
        for index in range(16):
            if index & step:
                continue
            first, second = rows[index], rows[index | step]
            rows[index] = jnp.where(low, first, pltpu.roll(second, 8 * step, 1))
            rows[index | step] = jnp.where(low, pltpu.roll(first, LANES - 8 * step, 1), second)
    return rows


def unpack_kernel(dev_count, cap, chunk, table, in_ref, *refs):
    tiles = 2 * FIELDS + (1 if chunk == 0 else 0)
    if chunk == 0:
        state, low_halo, high_halo, speed, scratch = refs
    else:
        state, low_halo, high_halo, scratch = refs
    for slot in range(BY * BZ):
        p, q = divmod(slot, BZ)
        where = table[slot]
        base = (where // cap) * (tiles * cap) + where % cap
        for half in range(2):
            value = in_ref[pl.ds(base + half * FIELDS * cap, FIELDS, stride=cap), :]
            scratch[pl.ds(q * 8 + half * 4 + p, FIELDS, stride=BZ * 8), :] = value
    group = lax.broadcasted_iota(jnp.int32, (8, LANES), 1) // 8

    def one_field(f, carry):
        rows = [
            scratch[pl.ds(pl.multiple_of((f * BZ + q) * 8, 8), 8), :] for q in range(BZ)
        ]
        moved = transposed(rows, group)
        for g in range(BZ):
            second, b = divmod(g, BLOCK)
            spot = pl.ds((b % 4) * 8 + b // 4, 4, stride=2)
            for half in range(2):
                value = moved[g][half * 4 : half * 4 + 4]
                plane = 2 * half + second
                state[f, plane, spot, :] = value
                if chunk == 0:
                    if half == 0:
                        low_halo[f, second, spot, :] = value
                    else:
                        high_halo[f, second, spot, :] = value
                else:
                    if plane == 0:
                        low_halo[f, 0, spot, :] = value
                    if plane == 3:
                        high_halo[f, 0, spot, :] = value
        return carry

    lax.fori_loop(0, FIELDS, one_field, 0)
    if chunk == 0:
        best = in_ref[pl.ds(2 * FIELDS * cap, cap), :]
        for source in range(1, dev_count):
            start = source * tiles * cap + 2 * FIELDS * cap
            best = jnp.maximum(best, in_ref[pl.ds(start, cap), :])
        speed[...] = jnp.full((8, LANES), jnp.max(best), jnp.float32)


def unpack(table, arrived, chunk, dev_count, cap):
    planes = 2 if chunk == 0 else 1
    halo = jax.ShapeDtypeStruct((FIELDS, planes, ROWS, LANES), jnp.float32)
    shapes = [jax.ShapeDtypeStruct((FIELDS, 4, ROWS, LANES), jnp.float32), halo, halo]
    if chunk == 0:
        shapes.append(jax.ShapeDtypeStruct((8, LANES), jnp.float32))
    return pl.pallas_call(
        functools.partial(unpack_kernel, dev_count, cap, chunk),
        out_shape=shapes,
        in_specs=[SMEM, VMEM],
        out_specs=[VMEM] * len(shapes),
        scratch_shapes=[pltpu.VMEM((FIELDS * BZ * 8, LANES), jnp.float32)],
        compiler_params=params(),
        cost_estimate=cost(5_000_000, 2_000_000),
        name="unpack",
    )(table, arrived)


def y_up(x):
    return jnp.concatenate([x[8:], pltpu.roll(x[:8], 7, 0)], axis=0)


def y_down(x):
    return jnp.concatenate([pltpu.roll(x[24:], 1, 0), x[:24]], axis=0)


def z_up(x):
    return pltpu.roll(x, LANES - 1, 1)


def z_down(x):
    return pltpu.roll(x, 1, 1)


def inverse(x):
    return 1.0 / x


def smoothness(before, after):
    curve = after - before
    middle = 0.5 * (after + before)
    base = curve * curve * (13.0 / 12.0) + smooth_epsilon
    plus = middle + curve
    minus = middle - curve
    left = inverse(base + plus * plus)
    centre = inverse(base + middle * middle)
    right = inverse(base + minus * minus)
    return curve, left * left, centre * centre, right * right


def upwind_term(left, centre, right, jump_before, jump_after):
    right = 3.0 * right
    top = left * (jump_before + jump_before) + right * jump_after
    return top * inverse(left + 6.0 * centre + right)


def periodic_divergence(half_flux, scaled, up, down):
    plus = half_flux + scaled
    minus = half_flux - scaled

    def side(values):
        after = up(values) - values
        curve, left, centre, right = smoothness(down(after), after)
        jump = up(curve) - curve
        return curve, down(left), centre, up(right), down(jump), jump

    curve, left, centre, right, jump_before, jump_after = side(plus)
    face = 6.0 * (half_flux + up(half_flux)) - curve
    face = face - upwind_term(left, centre, right, jump_before, jump_after)
    curve, left, centre, right, jump_before, jump_after = side(minus)
    face = face + up(upwind_term(right, centre, left, jump_after, jump_before) - curve)
    return face - down(face)


def open_divergence(half_flux, scaled):
    count = len(half_flux)
    plus = [a + b for a, b in zip(half_flux, scaled)]
    minus = [a - b for a, b in zip(half_flux, scaled)]
    faces = [None] * count

    def side(values):
        steps = [values[i + 1] - values[i] for i in range(count - 1)]
        parts = [None] + [smoothness(steps[i - 1], steps[i]) for i in range(1, count - 1)]
        return parts

    parts = side(plus)
    for i in range(2, count - 3):
        jump_before = parts[i][0] - parts[i - 1][0]
        jump_after = parts[i + 1][0] - parts[i][0]
        faces[i] = 6.0 * (half_flux[i] + half_flux[i + 1]) - parts[i][0] - upwind_term(
            parts[i - 1][1], parts[i][2], parts[i + 1][3], jump_before, jump_after
        )
    parts = side(minus)
    for i in range(3, count - 2):
        jump_before = parts[i][0] - parts[i - 1][0]
        jump_after = parts[i + 1][0] - parts[i][0]
        faces[i - 1] = faces[i - 1] + (
            upwind_term(parts[i + 1][3], parts[i][2], parts[i - 1][1], jump_after, jump_before)
            - parts[i][0]
        )
    return [faces[i] - faces[i - 1] for i in range(3, count - 3)]


def half_velocities(fields):
    density, mom_x, mom_y, mom_z, energy = fields
    over = 0.5 / density
    vel = (mom_x * over, mom_y * over, mom_z * over)
    kinetic = mom_x * vel[0] + mom_y * vel[1] + mom_z * vel[2]
    pressure = (gamma_gas - 1.0) * (energy - kinetic)
    return vel, pressure


def half_flux(fields, field, direction, speed, pressure):
    if field == 0:
        return 0.5 * fields[1 + direction]
    if field == 4:
        return (fields[4] + pressure) * speed
    flux = fields[field] * speed
    return flux + 0.5 * pressure if field == 1 + direction else flux


def side_planes(fields, half_speed):
    vel, pressure = half_velocities(fields)
    for field in range(FIELDS):
        scaled = half_speed * fields[field]
        along_z = periodic_divergence(
            half_flux(fields, field, 2, vel[2], pressure), scaled, z_up, z_down
        )
        along_y = periodic_divergence(
            half_flux(fields, field, 1, vel[1], pressure), scaled, y_up, y_down
        )
        yield field, along_y + along_z


def plane_kernel(state, speed, out):
    half_speed = 0.5 * speed[0:1, :]

    def one_plane(plane, carry):
        fields = [state[f, plane] for f in range(FIELDS)]
        for field, total in side_planes(fields, half_speed):
            out[field, plane] = total
        return carry

    lax.fori_loop(0, state.shape[1], one_plane, 0)


def along_planes(state, speed):
    return pl.pallas_call(
        plane_kernel,
        out_shape=jax.ShapeDtypeStruct(state.shape, jnp.float32),
        in_specs=[VMEM, VMEM],
        out_specs=VMEM,
        compiler_params=params(),
        cost_estimate=cost(20_000_000, 1_000_000),
        name="planes",
    )(state, speed)


def across(get, half_speed):
    span = range(-3, BLOCK + 3)
    speeds, pressures = [], []
    for plane in span:
        vel, pressure = half_velocities([get(f, plane) for f in range(FIELDS)])
        speeds.append(vel[0])
        pressures.append(pressure)
    for field in range(FIELDS):
        fluxes, scaled = [], []
        for i, plane in enumerate(span):
            if field == 0:
                flux = 0.5 * get(1, plane)
            elif field == 4:
                flux = (get(4, plane) + pressures[i]) * speeds[i]
            else:
                flux = get(field, plane) * speeds[i]
                if field == 1:
                    flux = flux + 0.5 * pressures[i]
            fluxes.append(flux)
            scaled.append(half_speed * get(field, plane))
        yield field, open_divergence(fluxes, scaled)


def first_kernel(
    state_a, state_b, sides_a, sides_b, below_a, below_b, above_a, above_b, speed,
    middle, low, high, top,
):
    half_speed = 0.5 * speed[0:1, :]
    factor = (courant / 6.0) / speed[0:1, :]
    where = {0: 0, 1: 1, 6: 2, 7: 3}

    def group(j, best):
        rows = pl.ds(pl.multiple_of(j * 8, 8), 8)

        def pick(of_a, of_b, f, plane):
            if plane in where:
                return of_a[f, where[plane], rows, :]
            return of_b[f, plane - 2, rows, :]

        def get(f, plane):
            if plane < 0:
                return below_b[f, 0, rows, :] if plane == -3 else below_a[f, plane + 2, rows, :]
            if plane >= BLOCK:
                return above_b[f, 0, rows, :] if plane == 10 else above_a[f, plane - 8, rows, :]
            return pick(state_a, state_b, f, plane)

        for field, along_x in across(get, half_speed):
            for plane in range(BLOCK):
                total = along_x[plane] + pick(sides_a, sides_b, field, plane)
                value = get(field, plane) - factor * total
                middle[field, plane, rows, :] = value
                if plane < 3:
                    low[field, plane, rows, :] = value
                if plane >= 5:
                    high[field, plane - 5, rows, :] = value
        for plane in range(BLOCK):
            best = jnp.maximum(
                best, wave_speed([middle[f, plane, rows, :] for f in range(FIELDS)])
            )
        return best

    best = lax.fori_loop(0, 4, group, jnp.zeros((8, LANES), jnp.float32))
    top[...] = jnp.full((8, LANES), jnp.max(best), jnp.float32)


def first_stage(*operands):
    whole = jax.ShapeDtypeStruct((FIELDS, BLOCK, ROWS, LANES), jnp.float32)
    halo = jax.ShapeDtypeStruct((FIELDS, 3, ROWS, LANES), jnp.float32)
    return pl.pallas_call(
        first_kernel,
        out_shape=(whole, halo, halo, jax.ShapeDtypeStruct((8, LANES), jnp.float32)),
        in_specs=[VMEM] * len(operands),
        out_specs=(VMEM,) * 4,
        compiler_params=params(),
        cost_estimate=cost(30_000_000, 3_000_000),
        name="first_stage",
    )(*operands)


def second_kernel(
    state_a, state_b, middle, below, above, first_speed, speeds, out, sides
):
    first = first_speed[0:1, :]
    second = speeds[0:1, :]
    half_speed = 0.5 * second
    factor = (courant / 12.0) / first
    where = {0: 0, 1: 1, 6: 2, 7: 3}

    def one_plane(plane, carry):
        fields = [middle[f, plane] for f in range(FIELDS)]
        for field, total in side_planes(fields, half_speed):
            sides[field, plane] = total
        return carry

    lax.fori_loop(0, BLOCK, one_plane, 0)

    def group(j, carry):
        rows = pl.ds(pl.multiple_of(j * 8, 8), 8)
        spread = pl.ds(j, 8, stride=4)

        def get(f, plane):
            if plane < 0:
                return below[f, plane + 3, rows, :]
            if plane >= BLOCK:
                return above[f, plane - BLOCK, rows, :]
            return middle[f, plane, rows, :]

        for field, along_x in across(get, half_speed):
            for plane in range(BLOCK):
                total = along_x[plane] + sides[field, plane, rows, :]
                if plane in where:
                    start = state_a[field, where[plane], rows, :]
                else:
                    start = state_b[field, plane - 2, rows, :]
                value = 0.5 * start + (0.5 * get(field, plane) - factor * total)
                out[field, plane, spread, :] = value
        return carry

    lax.fori_loop(0, 4, group, 0)


def second_stage(*operands):
    whole = (FIELDS, BLOCK, ROWS, LANES)
    return pl.pallas_call(
        second_kernel,
        out_shape=jax.ShapeDtypeStruct(whole, jnp.float32),
        in_specs=[VMEM] * len(operands),
        out_specs=VMEM,
        scratch_shapes=[pltpu.VMEM(whole, jnp.float32)],
        compiler_params=params(),
        cost_estimate=cost(60_000_000, 3_000_000),
        name="second_stage",
    )(*operands)


def everyone_max(value, axis, size):
    reach = 1
    while reach < size:
        copies = [value]
        for times in range(1, 4):
            shift = reach * times
            if shift < size:
                pairs = [(i, (i + shift) % size) for i in range(size)]
                copies.append(lax.ppermute(value, axis, pairs))
        value = functools.reduce(jnp.maximum, copies)
        reach *= 4
    return value


def per_device(blocks, owner_list, slot_list):
    size = lax.axis_size("gx")
    own = lax.axis_index("gx")
    per_dev = blocks.shape[0]
    cap = max(2, 2 * per_dev // size)
    up = [(i, (i + 1) % size) for i in range(size)]
    down = [(j, i) for i, j in up]

    out_a, out_b = pack(blocks, owner_list, size, cap)
    come_a = lax.all_to_all(out_a, "gx", split_axis=0, concat_axis=0, tiled=True)
    come_b = lax.all_to_all(out_b, "gx", split_axis=0, concat_axis=0, tiled=True)
    table = arrival_rows(owner_list, slot_list, own, per_dev, size, cap)
    state_a, low_a, high_a, speed = unpack(table, come_a, 0, size, cap)
    below_a = lax.ppermute(high_a, "gx", up)
    above_a = lax.ppermute(low_a, "gx", down)
    sides_a = along_planes(state_a, speed)
    state_b, low_b, high_b = unpack(table, come_b, 1, size, cap)
    below_b = lax.ppermute(high_b, "gx", up)
    above_b = lax.ppermute(low_b, "gx", down)
    sides_b = along_planes(state_b, speed)
    middle, low, high, top = first_stage(
        state_a, state_b, sides_a, sides_b, below_a, below_b, above_a, above_b, speed
    )
    below = lax.ppermute(high, "gx", up)
    above = lax.ppermute(low, "gx", down)
    second = everyone_max(top, "gx", size)
    return second_stage(state_a, state_b, middle, below, above, speed, second)


def solution(mesh):
    return jax.shard_map(
        per_device,
        mesh=mesh,
        in_specs=(P(("runs", "gx"), None, None), P("runs"), P("runs")),
        out_specs=P(None, ("runs", "gx"), None, None),
        check_vma=False,
    )
```

```python
import functools
import math

import jax
import jax.numpy as jnp
from jax import lax
from jax.experimental import pallas as pl
from jax.experimental.pallas import tpu as pltpu
from jax.sharding import PartitionSpec as P

BLOCK = 8
BY = 4
BZ = 16
FIELDS = 5
LANES = 128
ROWS = BY * BLOCK
CHUNKS = ((0, 3), (1, 2))

gamma_gas = 1.4
courant = 0.25
smooth_epsilon = 1e-06

VMEM = pl.BlockSpec(memory_space=pltpu.VMEM)
SMEM = pl.BlockSpec(memory_space=pltpu.SMEM)


def params():
    return pltpu.CompilerParams(vmem_limit_bytes=40 * 1024 * 1024)


def cost(flops, size):
    return pl.CostEstimate(flops=flops, bytes_accessed=size, transcendentals=0)


def wave_speed(fields):
    density, mom_x, mom_y, mom_z, energy = fields
    inverse = 1.0 / density
    vel = (mom_x * inverse, mom_y * inverse, mom_z * inverse)
    kinetic = 0.5 * (mom_x * vel[0] + mom_y * vel[1] + mom_z * vel[2])
    pressure = (gamma_gas - 1.0) * (energy - kinetic)
    sound = jnp.sqrt(gamma_gas * pressure * inverse)
    fastest = jnp.maximum(jnp.maximum(jnp.abs(vel[0]), jnp.abs(vel[1])), jnp.abs(vel[2]))
    return fastest + sound


def turns(size):
    half = size // 2
    order = []
    for i in range(half - 1, -1, -1):
        order += [half + i, i]
    return order


def pack_kernel(size, cap, per_dev, owner_ref, blocks_ref, *refs):
    outs = (refs[:size], refs[size : 2 * size])
    count, member, best = refs[2 * size :]
    own = lax.axis_index("gx")

    def clear(dest, carry):
        count[dest] = 0
        return carry

    lax.fori_loop(0, size, clear, 0)

    def note(block, carry):
        dest = owner_ref[own * per_dev + block]
        rank = count[dest]
        count[dest] = rank + 1
        member[dest * cap + rank] = block
        return carry

    lax.fori_loop(0, per_dev, note, 0, unroll=8)
    best[...] = jnp.zeros_like(best)
    for turn in range(size):
        dest = own ^ turn

        @pl.when(count[dest] > 0)
        def _():
            for rank in range(cap):
                block = member[dest * cap + rank]
                for chunk in range(2):
                    for half in range(2):
                        pair = CHUNKS[chunk][half]
                        spot = pl.ds(half * FIELDS * cap + rank, FIELDS, stride=cap)
                        outs[chunk][turn][spot, :] = blocks_ref[
                            block, :, pair * LANES : (pair + 1) * LANES
                        ]
            for chunk in range(2):
                for half in range(2):
                    first = half * FIELDS * cap
                    fields = [
                        outs[chunk][turn][first + f * cap : first + (f + 1) * cap, :]
                        for f in range(FIELDS)
                    ]
                    best[...] = jnp.maximum(best[...], wave_speed(fields))

    top = jnp.full((cap, LANES), jnp.max(best[...]), jnp.float32)
    for turn in range(size):
        outs[0][turn][2 * FIELDS * cap :, :] = top


def pack(blocks, owner_list, size, cap):
    per_dev = blocks.shape[0]
    shape_a = jax.ShapeDtypeStruct((cap * (2 * FIELDS + 1), LANES), jnp.float32)
    shape_b = jax.ShapeDtypeStruct((cap * 2 * FIELDS, LANES), jnp.float32)
    out = pl.pallas_call(
        functools.partial(pack_kernel, size, cap, per_dev),
        out_shape=[shape_a] * size + [shape_b] * size,
        in_specs=[SMEM, VMEM],
        out_specs=[VMEM] * (2 * size),
        scratch_shapes=[
            pltpu.SMEM((size,), jnp.int32),
            pltpu.SMEM((size * cap,), jnp.int32),
            pltpu.VMEM((cap, LANES), jnp.float32),
        ],
        compiler_params=params(),
        cost_estimate=cost(10_000_000, 3_000_000),
        name="pack",
    )(owner_list, blocks)
    return out[:size], out[size:]


def exchanged(parts, axis, size):
    come = list(parts)
    for turn in turns(size):
        if turn:
            pairs = [(i, i ^ turn) for i in range(size)]
            come[turn] = lax.ppermute(parts[turn], axis, pairs)
    return come


def arrivals(owner_list, slot_list, own, per_dev, size, cap):
    owners = owner_list.reshape(size, per_dev)
    slots = slot_list.reshape(size, per_dev)
    mine = owners == own
    spot = jnp.arange(per_dev, dtype=jnp.int32)
    earlier = spot[None, :] < spot[:, None]
    rank = jnp.sum((mine[:, None, :] & earlier[None]).astype(jnp.int32), axis=2)
    row = (slots % BZ) * 8 + slots // BZ
    order = jnp.arange(cap, dtype=jnp.int32)
    hit = mine[:, None, :] & (rank[:, None, :] == order[None, :, None])
    return jnp.max(jnp.where(hit, row[:, None, :], -1), axis=2).reshape(-1)


def transposed(rows, group):
    rows = list(rows)
    for bit in range(4):
        step = 1 << bit
        low = (group & step) == 0
        for index in range(16):
            if index & step:
                continue
            first, second = rows[index], rows[index | step]
            rows[index] = jnp.where(low, first, pltpu.roll(second, 8 * step, 1))
            rows[index | step] = jnp.where(low, pltpu.roll(first, LANES - 8 * step, 1), second)
    return rows


def unpack_kernel(size, cap, chunk, table, *refs):
    come, refs = refs[:size], refs[size:]
    if chunk == 0:
        state, low_halo, high_halo, speed, scratch = refs
    else:
        state, low_halo, high_halo, scratch = refs
    own = lax.axis_index("gx")
    for turn in range(size):
        source = own ^ turn

        @pl.when(table[source * cap] >= 0)
        def _():
            for rank in range(cap):
                row = table[source * cap + rank]
                for half in range(2):
                    value = come[turn][pl.ds(half * FIELDS * cap + rank, FIELDS, stride=cap), :]
                    scratch[pl.ds(row + half * 4, FIELDS, stride=BZ * 8), :] = value

    group = lax.broadcasted_iota(jnp.int32, (8, LANES), 1) // 8

    def one_field(f, carry):
        rows = [
            scratch[pl.ds(pl.multiple_of((f * BZ + q) * 8, 8), 8), :] for q in range(BZ)
        ]
        moved = transposed(rows, group)
        for g in range(BZ):
            second, b = divmod(g, BLOCK)
            spot = pl.ds((b % 4) * 8 + b // 4, 4, stride=2)
            for half in range(2):
                value = moved[g][half * 4 : half * 4 + 4]
                plane = 2 * half + second
                state[f, plane, spot, :] = value
                if chunk == 0:
                    if half == 0:
                        low_halo[f, second, spot, :] = value
                    else:
                        high_halo[f, second, spot, :] = value
                else:
                    if plane == 0:
                        low_halo[f, 0, spot, :] = value
                    if plane == 3:
                        high_halo[f, 0, spot, :] = value
        return carry

    lax.fori_loop(0, FIELDS, one_field, 0)
    if chunk == 0:
        best = come[0][2 * FIELDS * cap :, :]
        for other in come[1:]:
            best = jnp.maximum(best, other[2 * FIELDS * cap :, :])
        speed[...] = jnp.full((8, LANES), jnp.max(best), jnp.float32)


def unpack(table, come, chunk, size, cap):
    planes = 2 if chunk == 0 else 1
    halo = jax.ShapeDtypeStruct((FIELDS, planes, ROWS, LANES), jnp.float32)
    shapes = [jax.ShapeDtypeStruct((FIELDS, 4, ROWS, LANES), jnp.float32), halo, halo]
    if chunk == 0:
        shapes.append(jax.ShapeDtypeStruct((8, LANES), jnp.float32))
    return pl.pallas_call(
        functools.partial(unpack_kernel, size, cap, chunk),
        out_shape=shapes,
        in_specs=[SMEM] + [VMEM] * size,
        out_specs=[VMEM] * len(shapes),
        scratch_shapes=[pltpu.VMEM((FIELDS * BZ * 8, LANES), jnp.float32)],
        compiler_params=params(),
        cost_estimate=cost(5_000_000, 2_000_000),
        name="unpack",
    )(table, *come)


def y_up(x):
    return jnp.concatenate([x[8:], pltpu.roll(x[:8], 7, 0)], axis=0)


def y_down(x):
    return jnp.concatenate([pltpu.roll(x[24:], 1, 0), x[:24]], axis=0)


def z_up(x):
    return pltpu.roll(x, LANES - 1, 1)


def z_down(x):
    return pltpu.roll(x, 1, 1)


def inverse(x):
    return 1.0 / x


def smoothness(before, after):
    curve = after - before
    middle = 0.5 * (after + before)
    base = curve * curve * (13.0 / 12.0) + smooth_epsilon
    plus = middle + curve
    minus = middle - curve
    left = inverse(base + plus * plus)
    centre = inverse(base + middle * middle)
    right = inverse(base + minus * minus)
    return curve, left * left, centre * centre, right * right


def upwind_term(left, centre, right, jump_before, jump_after):
    right = 3.0 * right
    top = left * (jump_before + jump_before) + right * jump_after
    return top * inverse(left + 6.0 * centre + right)


def periodic_divergence(half_flux, scaled, up, down):
    plus = half_flux + scaled
    minus = half_flux - scaled

    def side(values):
        after = up(values) - values
        curve, left, centre, right = smoothness(down(after), after)
        jump = up(curve) - curve
        return curve, down(left), centre, up(right), down(jump), jump

    curve, left, centre, right, jump_before, jump_after = side(plus)
    face = 6.0 * (half_flux + up(half_flux)) - curve
    face = face - upwind_term(left, centre, right, jump_before, jump_after)
    curve, left, centre, right, jump_before, jump_after = side(minus)
    face = face + up(upwind_term(right, centre, left, jump_after, jump_before) - curve)
    return face - down(face)


def open_divergence(half_flux, scaled):
    count = len(half_flux)
    plus = [a + b for a, b in zip(half_flux, scaled)]
    minus = [a - b for a, b in zip(half_flux, scaled)]
    faces = [None] * count

    def side(values):
        steps = [values[i + 1] - values[i] for i in range(count - 1)]
        parts = [None] + [smoothness(steps[i - 1], steps[i]) for i in range(1, count - 1)]
        return parts

    parts = side(plus)
    for i in range(2, count - 3):
        jump_before = parts[i][0] - parts[i - 1][0]
        jump_after = parts[i + 1][0] - parts[i][0]
        faces[i] = 6.0 * (half_flux[i] + half_flux[i + 1]) - parts[i][0] - upwind_term(
            parts[i - 1][1], parts[i][2], parts[i + 1][3], jump_before, jump_after
        )
    parts = side(minus)
    for i in range(3, count - 2):
        jump_before = parts[i][0] - parts[i - 1][0]
        jump_after = parts[i + 1][0] - parts[i][0]
        faces[i - 1] = faces[i - 1] + (
            upwind_term(parts[i + 1][3], parts[i][2], parts[i - 1][1], jump_after, jump_before)
            - parts[i][0]
        )
    return [faces[i] - faces[i - 1] for i in range(3, count - 3)]


def half_velocities(fields):
    density, mom_x, mom_y, mom_z, energy = fields
    over = 0.5 / density
    vel = (mom_x * over, mom_y * over, mom_z * over)
    kinetic = mom_x * vel[0] + mom_y * vel[1] + mom_z * vel[2]
    pressure = (gamma_gas - 1.0) * (energy - kinetic)
    return vel, pressure


def half_flux(fields, field, direction, speed, pressure):
    if field == 0:
        return 0.5 * fields[1 + direction]
    if field == 4:
        return (fields[4] + pressure) * speed
    flux = fields[field] * speed
    return flux + 0.5 * pressure if field == 1 + direction else flux


def side_planes(fields, half_speed):
    vel, pressure = half_velocities(fields)
    for field in range(FIELDS):
        scaled = half_speed * fields[field]
        along_z = periodic_divergence(
            half_flux(fields, field, 2, vel[2], pressure), scaled, z_up, z_down
        )
        along_y = periodic_divergence(
            half_flux(fields, field, 1, vel[1], pressure), scaled, y_up, y_down
        )
        yield field, along_y + along_z


def plane_kernel(state, speed, out):
    half_speed = 0.5 * speed[0:1, :]

    def one_plane(plane, carry):
        fields = [state[f, plane] for f in range(FIELDS)]
        for field, total in side_planes(fields, half_speed):
            out[field, plane] = total
        return carry

    lax.fori_loop(0, state.shape[1], one_plane, 0)


def along_planes(state, speed):
    return pl.pallas_call(
        plane_kernel,
        out_shape=jax.ShapeDtypeStruct(state.shape, jnp.float32),
        in_specs=[VMEM, VMEM],
        out_specs=VMEM,
        compiler_params=params(),
        cost_estimate=cost(20_000_000, 1_000_000),
        name="planes",
    )(state, speed)


def across(get, half_speed):
    span = range(-3, BLOCK + 3)
    speeds, pressures = [], []
    for plane in span:
        vel, pressure = half_velocities([get(f, plane) for f in range(FIELDS)])
        speeds.append(vel[0])
        pressures.append(pressure)
    for field in range(FIELDS):
        fluxes, scaled = [], []
        for i, plane in enumerate(span):
            if field == 0:
                flux = 0.5 * get(1, plane)
            elif field == 4:
                flux = (get(4, plane) + pressures[i]) * speeds[i]
            else:
                flux = get(field, plane) * speeds[i]
                if field == 1:
                    flux = flux + 0.5 * pressures[i]
            fluxes.append(flux)
            scaled.append(half_speed * get(field, plane))
        yield field, open_divergence(fluxes, scaled)


def first_kernel(
    state_a, state_b, sides_a, sides_b, below_a, below_b, above_a, above_b, speed,
    middle, low, high, top,
):
    half_speed = 0.5 * speed[0:1, :]
    factor = (courant / 6.0) / speed[0:1, :]
    where = {0: 0, 1: 1, 6: 2, 7: 3}

    def group(j, best):
        rows = pl.ds(pl.multiple_of(j * 8, 8), 8)

        def pick(of_a, of_b, f, plane):
            if plane in where:
                return of_a[f, where[plane], rows, :]
            return of_b[f, plane - 2, rows, :]

        def get(f, plane):
            if plane < 0:
                return below_b[f, 0, rows, :] if plane == -3 else below_a[f, plane + 2, rows, :]
            if plane >= BLOCK:
                return above_b[f, 0, rows, :] if plane == 10 else above_a[f, plane - 8, rows, :]
            return pick(state_a, state_b, f, plane)

        for field, along_x in across(get, half_speed):
            for plane in range(BLOCK):
                total = along_x[plane] + pick(sides_a, sides_b, field, plane)
                value = get(field, plane) - factor * total
                middle[field, plane, rows, :] = value
                if plane < 3:
                    low[field, plane, rows, :] = value
                if plane >= 5:
                    high[field, plane - 5, rows, :] = value
        for plane in range(BLOCK):
            best = jnp.maximum(
                best, wave_speed([middle[f, plane, rows, :] for f in range(FIELDS)])
            )
        return best

    best = lax.fori_loop(0, 4, group, jnp.zeros((8, LANES), jnp.float32))
    top[...] = jnp.full((8, LANES), jnp.max(best), jnp.float32)


def first_stage(*operands):
    whole = jax.ShapeDtypeStruct((FIELDS, BLOCK, ROWS, LANES), jnp.float32)
    halo = jax.ShapeDtypeStruct((FIELDS, 3, ROWS, LANES), jnp.float32)
    return pl.pallas_call(
        first_kernel,
        out_shape=(whole, halo, halo, jax.ShapeDtypeStruct((8, LANES), jnp.float32)),
        in_specs=[VMEM] * len(operands),
        out_specs=(VMEM,) * 4,
        compiler_params=params(),
        cost_estimate=cost(30_000_000, 3_000_000),
        name="first_stage",
    )(*operands)


def second_kernel(
    state_a, state_b, middle, below, above, first_speed, speeds, out, sides
):
    first = first_speed[0:1, :]
    second = speeds[0:1, :]
    half_speed = 0.5 * second
    factor = (courant / 12.0) / first
    where = {0: 0, 1: 1, 6: 2, 7: 3}

    def one_plane(plane, carry):
        fields = [middle[f, plane] for f in range(FIELDS)]
        for field, total in side_planes(fields, half_speed):
            sides[field, plane] = total
        return carry

    lax.fori_loop(0, BLOCK, one_plane, 0)

    def group(j, carry):
        rows = pl.ds(pl.multiple_of(j * 8, 8), 8)
        spread = pl.ds(j, 8, stride=4)

        def get(f, plane):
            if plane < 0:
                return below[f, plane + 3, rows, :]
            if plane >= BLOCK:
                return above[f, plane - BLOCK, rows, :]
            return middle[f, plane, rows, :]

        for field, along_x in across(get, half_speed):
            for plane in range(BLOCK):
                total = along_x[plane] + sides[field, plane, rows, :]
                if plane in where:
                    start = state_a[field, where[plane], rows, :]
                else:
                    start = state_b[field, plane - 2, rows, :]
                value = 0.5 * start + (0.5 * get(field, plane) - factor * total)
                out[field, plane, spread, :] = value
        return carry

    lax.fori_loop(0, 4, group, 0)


def second_stage(*operands):
    whole = (FIELDS, BLOCK, ROWS, LANES)
    return pl.pallas_call(
        second_kernel,
        out_shape=jax.ShapeDtypeStruct(whole, jnp.float32),
        in_specs=[VMEM] * len(operands),
        out_specs=VMEM,
        scratch_shapes=[pltpu.VMEM(whole, jnp.float32)],
        compiler_params=params(),
        cost_estimate=cost(60_000_000, 3_000_000),
        name="second_stage",
    )(*operands)


def everyone_max(value, axis, size):
    reach = 1
    while reach < size:
        copies = [value]
        for times in range(1, 4):
            turn = reach * times
            if turn < size:
                pairs = [(i, i ^ turn) for i in range(size)]
                copies.append(lax.ppermute(value, axis, pairs))
        value = functools.reduce(jnp.maximum, copies)
        reach *= 4
    return value


def per_device(blocks, owner_list, slot_list):
    size = lax.axis_size("gx")
    own = lax.axis_index("gx")
    per_dev = blocks.shape[0]
    cap = max(2, 2 * per_dev // size)
    up = [(i, (i + 1) % size) for i in range(size)]
    down = [(j, i) for i, j in up]

    parts_a, parts_b = pack(blocks, owner_list, size, cap)
    come_a = exchanged(parts_a, "gx", size)
    come_b = exchanged(parts_b, "gx", size)
    table = arrivals(owner_list, slot_list, own, per_dev, size, cap)
    state_a, low_a, high_a, speed = unpack(table, come_a, 0, size, cap)
    below_a = lax.ppermute(high_a, "gx", up)
    above_a = lax.ppermute(low_a, "gx", down)
    sides_a = along_planes(state_a, speed)
    state_b, low_b, high_b = unpack(table, come_b, 1, size, cap)
    below_b = lax.ppermute(high_b, "gx", up)
    above_b = lax.ppermute(low_b, "gx", down)
    sides_b = along_planes(state_b, speed)
    middle, low, high, top = first_stage(
        state_a, state_b, sides_a, sides_b, below_a, below_b, above_a, above_b, speed
    )
    below = lax.ppermute(high, "gx", up)
    above = lax.ppermute(low, "gx", down)
    second = everyone_max(top, "gx", size)
    return second_stage(state_a, state_b, middle, below, above, speed, second)


def solution(mesh):
    return jax.shard_map(
        per_device,
        mesh=mesh,
        in_specs=(P(("runs", "gx"), None, None), P("runs"), P("runs")),
        out_specs=P(None, ("runs", "gx"), None, None),
        check_vma=False,
    )
```

```python
import functools

import jax
import jax.numpy as jnp
from jax import lax
from jax.experimental import pallas as pl
from jax.experimental.pallas import tpu as pltpu
from jax.sharding import PartitionSpec as P

BLOCK = 8
BY = 4
BZ = 16
FIELDS = 5
LANES = 128
ROWS = BY * BLOCK
PAIRS = BLOCK // 2
TILES = PAIRS * FIELDS

gamma_gas = 1.4
courant = 0.25
smooth_epsilon = 1e-06

VMEM = pl.BlockSpec(memory_space=pltpu.VMEM)
SMEM = pl.BlockSpec(memory_space=pltpu.SMEM)


def params():
    return pltpu.CompilerParams(vmem_limit_bytes=40 * 1024 * 1024)


def cost(flops, size):
    return pl.CostEstimate(flops=flops, bytes_accessed=size, transcendentals=0)


def wave_speed(fields):
    density, mom_x, mom_y, mom_z, energy = fields
    inverse = 1.0 / density
    vel = (mom_x * inverse, mom_y * inverse, mom_z * inverse)
    kinetic = 0.5 * (mom_x * vel[0] + mom_y * vel[1] + mom_z * vel[2])
    pressure = (gamma_gas - 1.0) * (energy - kinetic)
    sound = jnp.sqrt(gamma_gas * pressure * inverse)
    fastest = jnp.maximum(jnp.maximum(jnp.abs(vel[0]), jnp.abs(vel[1])), jnp.abs(vel[2]))
    return fastest + sound


def tiled_rows(blocks):
    count = blocks.shape[0] // 8
    groups = blocks.reshape(count, 8, FIELDS, PAIRS, LANES).transpose(2, 0, 3, 1, 4)
    return groups.reshape(FIELDS * count * PAIRS * 8, LANES)


def pack_kernel(size, cap, per_dev, owner_ref, rows_ref, out, count):
    own = lax.axis_index("gx")

    def clear(dest, carry):
        count[dest] = 0
        return carry

    lax.fori_loop(0, size, clear, 0)

    def place(group, carry):
        for member in range(8):
            dest = owner_ref[own * per_dev + group * 8 + member]
            rank = count[dest]
            count[dest] = rank + 1
            to = dest * (TILES * cap) + rank
            for pair in range(PAIRS):
                source = pl.ds((group * PAIRS + pair) * 8 + member, FIELDS, stride=per_dev * PAIRS)
                target = pl.ds(to + pair * (FIELDS * cap), FIELDS, stride=cap)
                out[target, :] = rows_ref[source, :]
        return carry

    lax.fori_loop(0, per_dev // 8, place, 0, unroll=2)


def pack(rows, owner_list, size, cap, per_dev):
    return pl.pallas_call(
        functools.partial(pack_kernel, size, cap, per_dev),
        out_shape=jax.ShapeDtypeStruct((size * TILES * cap, LANES), jnp.float32),
        in_specs=[SMEM, VMEM],
        out_specs=VMEM,
        scratch_shapes=[pltpu.SMEM((size,), jnp.int32)],
        compiler_params=params(),
        cost_estimate=cost(1_000_000, 3_000_000),
        name="pack",
    )(owner_list, rows)


def fastest_kernel(rows_ref, out):
    best = jnp.zeros((8, LANES), jnp.float32)
    step = rows_ref.shape[0] // FIELDS
    for first in range(0, step, 8):
        fields = [rows_ref[f * step + first : f * step + first + 8, :] for f in range(FIELDS)]
        best = jnp.maximum(best, wave_speed(fields))
    out[...] = jnp.full((8, LANES), jnp.max(best), jnp.float32)


def fastest(rows):
    return pl.pallas_call(
        fastest_kernel,
        out_shape=jax.ShapeDtypeStruct((8, LANES), jnp.float32),
        in_specs=[VMEM],
        out_specs=VMEM,
        compiler_params=params(),
        cost_estimate=cost(2_000_000, 700_000),
        name="fastest",
    )(rows)


def arrival_spots(owner_list, slot_list, own, per_dev, size, cap):
    owners = owner_list.reshape(size, per_dev)
    slots = slot_list.reshape(size, per_dev)
    mine = owners == own
    spot = jnp.arange(per_dev, dtype=jnp.int32)
    earlier = spot[None, :] < spot[:, None]
    rank = jnp.sum((mine[:, None, :] & earlier[None]).astype(jnp.int32), axis=2)
    row = jnp.arange(size, dtype=jnp.int32)[:, None] * cap + rank
    key = jnp.where(mine, slots, -1)
    hit = key.reshape(1, -1) == spot[:, None]
    return jnp.max(jnp.where(hit, row.reshape(1, -1), 0), axis=1)


def exchanged_bits(rows, group):
    rows = list(rows)
    for bit in range(4):
        step = 1 << bit
        low = (group & step) == 0
        for index in range(16):
            if index & step:
                continue
            first, second = rows[index], rows[index | step]
            rows[index] = jnp.where(low, first, pltpu.roll(second, 8 * step, 1))
            rows[index | step] = jnp.where(low, pltpu.roll(first, LANES - 8 * step, 1), second)
    return rows


def unpack_kernel(cap, table, come, state, low_halo, high_halo, scratch):
    for slot in range(BY * BZ):
        p, q = divmod(slot, BZ)
        where = table[slot]
        source = lax.div(where, cap)
        rank = lax.rem(where, cap)
        for pair in range(PAIRS):
            couple, h = divmod(pair, 2)
            base = source * (TILES * cap) + rank + pair * (FIELDS * cap)
            value = come[pl.ds(base, FIELDS, stride=cap), :]
            row = (couple * BZ + q) * 8 + 2 * p + h
            scratch[pl.ds(row, FIELDS, stride=PAIRS // 2 * BZ * 8), :] = value
    group = lax.broadcasted_iota(jnp.int32, (8, LANES), 1) // BLOCK
    even = lax.broadcasted_iota(jnp.int32, (8, LANES), 0) % 2 == 0

    for f in range(FIELDS):
        for couple in range(PAIRS // 2):
            first = (f * (PAIRS // 2) + couple) * BZ * 8
            rows = [scratch[first + q * 8 : first + q * 8 + 8, :] for q in range(BZ)]
            moved = exchanged_bits(rows, group)
            for second in range(2):
                for j in range(4):
                    lower = moved[second * BLOCK + j]
                    upper = moved[second * BLOCK + j + 4]
                    planes = (
                        jnp.where(even, lower, pltpu.roll(upper, 1, 0)),
                        jnp.where(even, pltpu.roll(lower, 7, 0), upper),
                    )
                    rows = slice(j * 8, j * 8 + 8)
                    for h in range(2):
                        plane = 4 * couple + 2 * h + second
                        state[f, plane, rows, :] = planes[h]
                        if plane < 3:
                            low_halo[f, plane, rows, :] = planes[h]
                        if plane >= 5:
                            high_halo[f, plane - 5, rows, :] = planes[h]


def unpack(table, come, cap):
    halo = jax.ShapeDtypeStruct((FIELDS, 3, ROWS, LANES), jnp.float32)
    return pl.pallas_call(
        functools.partial(unpack_kernel, cap),
        out_shape=(jax.ShapeDtypeStruct((FIELDS, BLOCK, ROWS, LANES), jnp.float32), halo, halo),
        in_specs=[SMEM, VMEM],
        out_specs=(VMEM,) * 3,
        scratch_shapes=[pltpu.VMEM((FIELDS * (PAIRS // 2) * BZ * 8, LANES), jnp.float32)],
        compiler_params=params(),
        cost_estimate=cost(5_000_000, 2_000_000),
        name="unpack",
    )(table, come)


def y_up(x):
    return jnp.concatenate([x[8:], pltpu.roll(x[:8], 7, 0)], axis=0)


def y_down(x):
    return jnp.concatenate([pltpu.roll(x[24:], 1, 0), x[:24]], axis=0)


def z_up(x):
    return pltpu.roll(x, LANES - 1, 1)


def z_down(x):
    return pltpu.roll(x, 1, 1)


def inverse(x):
    return 1.0 / x


def smoothness(before, after):
    curve = after - before
    middle = 0.5 * (after + before)
    base = curve * curve * (13.0 / 12.0) + smooth_epsilon
    plus = middle + curve
    minus = middle - curve
    left = inverse(base + plus * plus)
    centre = inverse(base + middle * middle)
    right = inverse(base + minus * minus)
    return curve, left * left, centre * centre, right * right


def upwind_term(left, centre, right, jump_before, jump_after):
    right = 3.0 * right
    top = left * (jump_before + jump_before) + right * jump_after
    return top * inverse(left + 6.0 * centre + right)


def periodic_divergence(half_flux, scaled, up, down):
    plus = half_flux + scaled
    minus = half_flux - scaled

    def side(values):
        after = up(values) - values
        curve, left, centre, right = smoothness(down(after), after)
        jump = up(curve) - curve
        return curve, down(left), centre, up(right), down(jump), jump

    curve, left, centre, right, jump_before, jump_after = side(plus)
    face = 6.0 * (half_flux + up(half_flux)) - curve
    face = face - upwind_term(left, centre, right, jump_before, jump_after)
    curve, left, centre, right, jump_before, jump_after = side(minus)
    face = face + up(upwind_term(right, centre, left, jump_after, jump_before) - curve)
    return face - down(face)


def open_divergence(half_flux, scaled):
    count = len(half_flux)
    plus = [a + b for a, b in zip(half_flux, scaled)]
    minus = [a - b for a, b in zip(half_flux, scaled)]
    faces = [None] * count

    def side(values):
        steps = [values[i + 1] - values[i] for i in range(count - 1)]
        parts = [None] + [smoothness(steps[i - 1], steps[i]) for i in range(1, count - 1)]
        return parts

    parts = side(plus)
    for i in range(2, count - 3):
        jump_before = parts[i][0] - parts[i - 1][0]
        jump_after = parts[i + 1][0] - parts[i][0]
        faces[i] = 6.0 * (half_flux[i] + half_flux[i + 1]) - parts[i][0] - upwind_term(
            parts[i - 1][1], parts[i][2], parts[i + 1][3], jump_before, jump_after
        )
    parts = side(minus)
    for i in range(3, count - 2):
        jump_before = parts[i][0] - parts[i - 1][0]
        jump_after = parts[i + 1][0] - parts[i][0]
        faces[i - 1] = faces[i - 1] + (
            upwind_term(parts[i + 1][3], parts[i][2], parts[i - 1][1], jump_after, jump_before)
            - parts[i][0]
        )
    return [faces[i] - faces[i - 1] for i in range(3, count - 3)]


def half_velocities(fields):
    density, mom_x, mom_y, mom_z, energy = fields
    over = 0.5 / density
    vel = (mom_x * over, mom_y * over, mom_z * over)
    kinetic = mom_x * vel[0] + mom_y * vel[1] + mom_z * vel[2]
    pressure = (gamma_gas - 1.0) * (energy - kinetic)
    return vel, pressure


def half_flux(fields, field, direction, speed, pressure):
    if field == 0:
        return 0.5 * fields[1 + direction]
    if field == 4:
        return (fields[4] + pressure) * speed
    flux = fields[field] * speed
    return flux + 0.5 * pressure if field == 1 + direction else flux


def side_planes(fields, half_speed):
    vel, pressure = half_velocities(fields)
    for field in range(FIELDS):
        scaled = half_speed * fields[field]
        along_z = periodic_divergence(
            half_flux(fields, field, 2, vel[2], pressure), scaled, z_up, z_down
        )
        along_y = periodic_divergence(
            half_flux(fields, field, 1, vel[1], pressure), scaled, y_up, y_down
        )
        yield field, along_y + along_z


def plane_kernel(state, speed, out):
    half_speed = 0.5 * speed[0:1, :]

    def one_plane(plane, carry):
        fields = [state[f, plane] for f in range(FIELDS)]
        for field, total in side_planes(fields, half_speed):
            out[field, plane] = total
        return carry

    lax.fori_loop(0, state.shape[1], one_plane, 0)


def along_planes(state, speed):
    return pl.pallas_call(
        plane_kernel,
        out_shape=jax.ShapeDtypeStruct(state.shape, jnp.float32),
        in_specs=[VMEM, VMEM],
        out_specs=VMEM,
        compiler_params=params(),
        cost_estimate=cost(20_000_000, 1_000_000),
        name="planes",
    )(state, speed)


def across(get, half_speed):
    span = range(-3, BLOCK + 3)
    speeds, pressures = [], []
    for plane in span:
        vel, pressure = half_velocities([get(f, plane) for f in range(FIELDS)])
        speeds.append(vel[0])
        pressures.append(pressure)
    for field in range(FIELDS):
        fluxes, scaled = [], []
        for i, plane in enumerate(span):
            if field == 0:
                flux = 0.5 * get(1, plane)
            elif field == 4:
                flux = (get(4, plane) + pressures[i]) * speeds[i]
            else:
                flux = get(field, plane) * speeds[i]
                if field == 1:
                    flux = flux + 0.5 * pressures[i]
            fluxes.append(flux)
            scaled.append(half_speed * get(field, plane))
        yield field, open_divergence(fluxes, scaled)


def first_kernel(state, sides, below, above, speed, middle, low, high, top):
    half_speed = 0.5 * speed[0:1, :]
    factor = (courant / 6.0) / speed[0:1, :]

    def group(j, best):
        rows = pl.ds(pl.multiple_of(j * 8, 8), 8)

        def get(f, plane):
            if plane < 0:
                return below[f, plane + 3, rows, :]
            if plane >= BLOCK:
                return above[f, plane - BLOCK, rows, :]
            return state[f, plane, rows, :]

        for field, along_x in across(get, half_speed):
            for plane in range(BLOCK):
                total = along_x[plane] + sides[field, plane, rows, :]
                value = get(field, plane) - factor * total
                middle[field, plane, rows, :] = value
                if plane < 3:
                    low[field, plane, rows, :] = value
                if plane >= 5:
                    high[field, plane - 5, rows, :] = value
        for plane in range(BLOCK):
            best = jnp.maximum(
                best, wave_speed([middle[f, plane, rows, :] for f in range(FIELDS)])
            )
        return best

    best = lax.fori_loop(0, 4, group, jnp.zeros((8, LANES), jnp.float32))
    size = top.shape[0] // 8
    most = jnp.full((8, LANES), jnp.max(best), jnp.float32)
    for dest in range(size):
        top[dest * 8 : dest * 8 + 8, :] = most


def first_stage(size, *operands):
    whole = jax.ShapeDtypeStruct((FIELDS, BLOCK, ROWS, LANES), jnp.float32)
    halo = jax.ShapeDtypeStruct((FIELDS, 3, ROWS, LANES), jnp.float32)
    return pl.pallas_call(
        first_kernel,
        out_shape=(whole, halo, halo, jax.ShapeDtypeStruct((size * 8, LANES), jnp.float32)),
        in_specs=[VMEM] * len(operands),
        out_specs=(VMEM,) * 4,
        compiler_params=params(),
        cost_estimate=cost(30_000_000, 3_000_000),
        name="first_stage",
    )(*operands)


def second_kernel(start, middle, below, above, first_speed, speeds, out, sides):
    first = first_speed[0:1, :]
    second = jnp.full((1, LANES), jnp.max(speeds[...]), jnp.float32)
    half_speed = 0.5 * second
    factor = (courant / 12.0) / first

    def one_plane(plane, carry):
        fields = [middle[f, plane] for f in range(FIELDS)]
        for field, total in side_planes(fields, half_speed):
            sides[field, plane] = total
        return carry

    lax.fori_loop(0, BLOCK, one_plane, 0)

    def group(j, carry):
        rows = pl.ds(pl.multiple_of(j * 8, 8), 8)
        spread = pl.ds(j, 8, stride=4)

        def get(f, plane):
            if plane < 0:
                return below[f, plane + 3, rows, :]
            if plane >= BLOCK:
                return above[f, plane - BLOCK, rows, :]
            return middle[f, plane, rows, :]

        for field, along_x in across(get, half_speed):
            for plane in range(BLOCK):
                total = along_x[plane] + sides[field, plane, rows, :]
                value = 0.5 * start[field, plane, rows, :] + (
                    0.5 * get(field, plane) - factor * total
                )
                out[field, plane, spread, :] = value
        return carry

    lax.fori_loop(0, 4, group, 0)


def second_stage(*operands):
    whole = (FIELDS, BLOCK, ROWS, LANES)
    return pl.pallas_call(
        second_kernel,
        out_shape=jax.ShapeDtypeStruct(whole, jnp.float32),
        in_specs=[VMEM] * len(operands),
        out_specs=VMEM,
        scratch_shapes=[pltpu.VMEM(whole, jnp.float32)],
        compiler_params=params(),
        cost_estimate=cost(60_000_000, 3_000_000),
        name="second_stage",
    )(*operands)


def everyone_max(value, axis, size):
    reach = 1
    while reach < size:
        copies = [value]
        for times in range(1, 4):
            turn = reach * times
            if turn < size:
                pairs = [(i, i ^ turn) for i in range(size)]
                copies.append(lax.ppermute(value, axis, pairs))
        value = functools.reduce(jnp.maximum, copies)
        reach *= 4
    return value


def per_device(blocks, owner_list, slot_list):
    size = lax.axis_size("gx")
    own = lax.axis_index("gx")
    per_dev = blocks.shape[0]
    cap = max(2, 2 * per_dev // size)
    up = [(i, (i + 1) % size) for i in range(size)]
    down = [(j, i) for i, j in up]

    rows = tiled_rows(blocks)
    parts = pack(rows, owner_list, size, cap, per_dev)
    parts, rows, owner_list, slot_list = lax.optimization_barrier(
        (parts, rows, owner_list, slot_list)
    )
    come = lax.all_to_all(parts, "gx", split_axis=0, concat_axis=0, tiled=True)
    table = arrival_spots(owner_list, slot_list, own, per_dev, size, cap)
    speed = everyone_max(fastest(rows), "gx", size)
    state, low, high = unpack(table, come, cap)
    below = lax.ppermute(high, "gx", up)
    above = lax.ppermute(low, "gx", down)
    sides = along_planes(state, speed)
    middle, low, high, top = first_stage(size, state, sides, below, above, speed)
    speeds = lax.all_to_all(top, "gx", split_axis=0, concat_axis=0, tiled=True)
    below = lax.ppermute(high, "gx", up)
    above = lax.ppermute(low, "gx", down)
    return second_stage(state, middle, below, above, speed, speeds)


def solution(mesh):
    return jax.shard_map(
        per_device,
        mesh=mesh,
        in_specs=(P(("runs", "gx"), None, None), P("runs"), P("runs")),
        out_specs=P(None, ("runs", "gx"), None, None),
        check_vma=False,
    )
```

```python
import functools

import jax
import jax.numpy as jnp
from jax import lax
from jax.experimental import pallas as pl
from jax.experimental.pallas import tpu as pltpu
from jax.sharding import PartitionSpec as P

BLOCK = 8
BY = 4
BZ = 16
FIELDS = 5
LANES = 128
ROWS = BY * BLOCK
PAIRS = BLOCK // 2
TILES = PAIRS * FIELDS

gamma_gas = 1.4
courant = 0.25
smooth_epsilon = 1e-06

VMEM = pl.BlockSpec(memory_space=pltpu.VMEM)
SMEM = pl.BlockSpec(memory_space=pltpu.SMEM)


def params():
    return pltpu.CompilerParams(vmem_limit_bytes=40 * 1024 * 1024)


def cost(flops, size):
    return pl.CostEstimate(flops=flops, bytes_accessed=size, transcendentals=0)


def wave_speed(fields):
    density, mom_x, mom_y, mom_z, energy = fields
    inverse = 1.0 / density
    vel = (mom_x * inverse, mom_y * inverse, mom_z * inverse)
    kinetic = 0.5 * (mom_x * vel[0] + mom_y * vel[1] + mom_z * vel[2])
    pressure = (gamma_gas - 1.0) * (energy - kinetic)
    sound = jnp.sqrt(gamma_gas * pressure * inverse)
    fastest = jnp.maximum(jnp.maximum(jnp.abs(vel[0]), jnp.abs(vel[1])), jnp.abs(vel[2]))
    return fastest + sound


def tiled_rows(blocks):
    count = blocks.shape[0] // 8
    return blocks.reshape(count, 8, FIELDS, PAIRS, LANES).transpose(2, 0, 3, 1, 4)


def pack_kernel(size, per_dev, owner_hbm, rows_hbm, out, owner, count, sems):
    own = lax.axis_index("gx")
    fetch = pltpu.make_async_copy(owner_hbm, owner, sems.at[0])
    fetch.start()

    def clear(dest, carry):
        count[dest] = 0
        return carry

    lax.fori_loop(0, size, clear, 0)
    fetch.wait()

    def place(block, carry):
        dest = owner[own * per_dev + block]
        rank = count[dest]
        count[dest] = rank + 1
        pltpu.make_async_copy(
            rows_hbm.at[:, lax.div(block, 8), :, lax.rem(block, 8)],
            out.at[dest, :, :, rank],
            sems.at[1],
        ).start()
        return carry

    lax.fori_loop(0, per_dev, place, 0, unroll=8)
    half = out.at[pl.ds(0, size // 2)]
    pltpu.make_async_copy(half, half, sems.at[1]).wait()


def pack(rows, owner_list, size, cap, per_dev):
    return pl.pallas_call(
        functools.partial(pack_kernel, size, per_dev),
        out_shape=jax.ShapeDtypeStruct((size, FIELDS, PAIRS, cap, 1, LANES), jnp.float32),
        in_specs=[pl.BlockSpec(memory_space=pltpu.HBM)] * 2,
        out_specs=VMEM,
        scratch_shapes=[
            pltpu.SMEM(owner_list.shape, jnp.int32),
            pltpu.SMEM((size,), jnp.int32),
            pltpu.SemaphoreType.DMA((2,)),
        ],
        compiler_params=params(),
        cost_estimate=cost(1_000_000, 3_000_000),
        name="pack",
    )(owner_list, rows[:, :, :, :, None, :])


def fastest_kernel(rows_ref, out):
    best = jnp.zeros((8, LANES), jnp.float32)
    for group in range(rows_ref.shape[1]):
        for pair in range(PAIRS):
            fields = [rows_ref[f, group, pair] for f in range(FIELDS)]
            best = jnp.maximum(best, wave_speed(fields))
    out[...] = jnp.full((8, LANES), jnp.max(best), jnp.float32)


def fastest(rows):
    return pl.pallas_call(
        fastest_kernel,
        out_shape=jax.ShapeDtypeStruct((8, LANES), jnp.float32),
        in_specs=[VMEM],
        out_specs=VMEM,
        compiler_params=params(),
        cost_estimate=cost(2_000_000, 700_000),
        name="fastest",
    )(rows)


def arrival_spots(owner_list, slot_list, own, per_dev, size, cap):
    owners = owner_list.reshape(size, per_dev)
    slots = slot_list.reshape(size, per_dev)
    mine = owners == own
    spot = jnp.arange(per_dev, dtype=jnp.int32)
    earlier = spot[None, :] < spot[:, None]
    rank = jnp.sum((mine[:, None, :] & earlier[None]).astype(jnp.int32), axis=2)
    row = jnp.arange(size, dtype=jnp.int32)[:, None] * cap + rank
    key = jnp.where(mine, slots, -1)
    hit = key.reshape(1, -1) == spot[:, None]
    return jnp.max(jnp.where(hit, row.reshape(1, -1), 0), axis=1)


def exchanged_bits(rows, group):
    rows = list(rows)
    for bit in range(4):
        step = 1 << bit
        low = (group & step) == 0
        for index in range(16):
            if index & step:
                continue
            first, second = rows[index], rows[index | step]
            rows[index] = jnp.where(low, first, pltpu.roll(second, 8 * step, 1))
            rows[index | step] = jnp.where(low, pltpu.roll(first, LANES - 8 * step, 1), second)
    return rows


def unpack_kernel(cap, table, come, state, low_halo, high_halo, scratch):
    for slot in range(BY * BZ):
        p, q = divmod(slot, BZ)
        where = table[slot]
        source = lax.div(where, cap)
        rank = lax.rem(where, cap)
        for pair in range(PAIRS):
            couple, h = divmod(pair, 2)
            base = source * (TILES * cap) + rank + pair * cap
            value = come[pl.ds(base, FIELDS, stride=PAIRS * cap), :]
            row = (couple * BZ + q) * 8 + 2 * p + h
            scratch[pl.ds(row, FIELDS, stride=PAIRS // 2 * BZ * 8), :] = value
    group = lax.broadcasted_iota(jnp.int32, (8, LANES), 1) // BLOCK
    even = lax.broadcasted_iota(jnp.int32, (8, LANES), 0) % 2 == 0

    for f in range(FIELDS):
        for couple in range(PAIRS // 2):
            first = (f * (PAIRS // 2) + couple) * BZ * 8
            rows = [scratch[first + q * 8 : first + q * 8 + 8, :] for q in range(BZ)]
            moved = exchanged_bits(rows, group)
            for second in range(2):
                for j in range(4):
                    lower = moved[second * BLOCK + j]
                    upper = moved[second * BLOCK + j + 4]
                    planes = (
                        jnp.where(even, lower, pltpu.roll(upper, 1, 0)),
                        jnp.where(even, pltpu.roll(lower, 7, 0), upper),
                    )
                    rows = slice(j * 8, j * 8 + 8)
                    for h in range(2):
                        plane = 4 * couple + 2 * h + second
                        state[f, plane, rows, :] = planes[h]
                        if plane < 3:
                            low_halo[f, plane, rows, :] = planes[h]
                        if plane >= 5:
                            high_halo[f, plane - 5, rows, :] = planes[h]


def unpack(table, come, cap):
    halo = jax.ShapeDtypeStruct((FIELDS, 3, ROWS, LANES), jnp.float32)
    return pl.pallas_call(
        functools.partial(unpack_kernel, cap),
        out_shape=(jax.ShapeDtypeStruct((FIELDS, BLOCK, ROWS, LANES), jnp.float32), halo, halo),
        in_specs=[SMEM, VMEM],
        out_specs=(VMEM,) * 3,
        scratch_shapes=[pltpu.VMEM((FIELDS * (PAIRS // 2) * BZ * 8, LANES), jnp.float32)],
        compiler_params=params(),
        cost_estimate=cost(5_000_000, 2_000_000),
        name="unpack",
    )(table, come)


def y_up(x):
    return jnp.concatenate([x[8:], pltpu.roll(x[:8], 7, 0)], axis=0)


def y_down(x):
    return jnp.concatenate([pltpu.roll(x[24:], 1, 0), x[:24]], axis=0)


def z_up(x):
    return pltpu.roll(x, LANES - 1, 1)


def z_down(x):
    return pltpu.roll(x, 1, 1)


def inverse(x):
    return 1.0 / x


def smoothness(before, after):
    curve = after - before
    middle = 0.5 * (after + before)
    base = curve * curve * (13.0 / 12.0) + smooth_epsilon
    plus = middle + curve
    minus = middle - curve
    left = inverse(base + plus * plus)
    centre = inverse(base + middle * middle)
    right = inverse(base + minus * minus)
    return curve, left * left, centre * centre, right * right


def upwind_term(left, centre, right, jump_before, jump_after):
    right = 3.0 * right
    top = left * (jump_before + jump_before) + right * jump_after
    return top * inverse(left + 6.0 * centre + right)


def periodic_divergence(half_flux, scaled, up, down):
    plus = half_flux + scaled
    minus = half_flux - scaled

    def side(values):
        after = up(values) - values
        curve, left, centre, right = smoothness(down(after), after)
        jump = up(curve) - curve
        return curve, down(left), centre, up(right), down(jump), jump

    curve, left, centre, right, jump_before, jump_after = side(plus)
    face = 6.0 * (half_flux + up(half_flux)) - curve
    face = face - upwind_term(left, centre, right, jump_before, jump_after)
    curve, left, centre, right, jump_before, jump_after = side(minus)
    face = face + up(upwind_term(right, centre, left, jump_after, jump_before) - curve)
    return face - down(face)


def open_divergence(half_flux, scaled):
    count = len(half_flux)
    plus = [a + b for a, b in zip(half_flux, scaled)]
    minus = [a - b for a, b in zip(half_flux, scaled)]
    faces = [None] * count

    def side(values):
        steps = [values[i + 1] - values[i] for i in range(count - 1)]
        parts = [None] + [smoothness(steps[i - 1], steps[i]) for i in range(1, count - 1)]
        return parts

    parts = side(plus)
    for i in range(2, count - 3):
        jump_before = parts[i][0] - parts[i - 1][0]
        jump_after = parts[i + 1][0] - parts[i][0]
        faces[i] = 6.0 * (half_flux[i] + half_flux[i + 1]) - parts[i][0] - upwind_term(
            parts[i - 1][1], parts[i][2], parts[i + 1][3], jump_before, jump_after
        )
    parts = side(minus)
    for i in range(3, count - 2):
        jump_before = parts[i][0] - parts[i - 1][0]
        jump_after = parts[i + 1][0] - parts[i][0]
        faces[i - 1] = faces[i - 1] + (
            upwind_term(parts[i + 1][3], parts[i][2], parts[i - 1][1], jump_after, jump_before)
            - parts[i][0]
        )
    return [faces[i] - faces[i - 1] for i in range(3, count - 3)]


def half_velocities(fields):
    density, mom_x, mom_y, mom_z, energy = fields
    over = 0.5 / density
    vel = (mom_x * over, mom_y * over, mom_z * over)
    kinetic = mom_x * vel[0] + mom_y * vel[1] + mom_z * vel[2]
    pressure = (gamma_gas - 1.0) * (energy - kinetic)
    return vel, pressure


def half_flux(fields, field, direction, speed, pressure):
    if field == 0:
        return 0.5 * fields[1 + direction]
    if field == 4:
        return (fields[4] + pressure) * speed
    flux = fields[field] * speed
    return flux + 0.5 * pressure if field == 1 + direction else flux


def side_planes(fields, half_speed):
    vel, pressure = half_velocities(fields)
    for field in range(FIELDS):
        scaled = half_speed * fields[field]
        along_z = periodic_divergence(
            half_flux(fields, field, 2, vel[2], pressure), scaled, z_up, z_down
        )
        along_y = periodic_divergence(
            half_flux(fields, field, 1, vel[1], pressure), scaled, y_up, y_down
        )
        yield field, along_y + along_z


def plane_kernel(state, speed, out):
    half_speed = 0.5 * speed[0:1, :]

    def one_plane(plane, carry):
        fields = [state[f, plane] for f in range(FIELDS)]
        for field, total in side_planes(fields, half_speed):
            out[field, plane] = total
        return carry

    lax.fori_loop(0, state.shape[1], one_plane, 0)


def along_planes(state, speed):
    return pl.pallas_call(
        plane_kernel,
        out_shape=jax.ShapeDtypeStruct(state.shape, jnp.float32),
        in_specs=[VMEM, VMEM],
        out_specs=VMEM,
        compiler_params=params(),
        cost_estimate=cost(20_000_000, 1_000_000),
        name="planes",
    )(state, speed)


def across(get, half_speed):
    span = range(-3, BLOCK + 3)
    speeds, pressures = [], []
    for plane in span:
        vel, pressure = half_velocities([get(f, plane) for f in range(FIELDS)])
        speeds.append(vel[0])
        pressures.append(pressure)
    for field in range(FIELDS):
        fluxes, scaled = [], []
        for i, plane in enumerate(span):
            if field == 0:
                flux = 0.5 * get(1, plane)
            elif field == 4:
                flux = (get(4, plane) + pressures[i]) * speeds[i]
            else:
                flux = get(field, plane) * speeds[i]
                if field == 1:
                    flux = flux + 0.5 * pressures[i]
            fluxes.append(flux)
            scaled.append(half_speed * get(field, plane))
        yield field, open_divergence(fluxes, scaled)


def first_kernel(state, sides, below, above, speed, middle, low, high, top):
    half_speed = 0.5 * speed[0:1, :]
    factor = (courant / 6.0) / speed[0:1, :]

    def group(j, best):
        rows = pl.ds(pl.multiple_of(j * 8, 8), 8)

        def get(f, plane):
            if plane < 0:
                return below[f, plane + 3, rows, :]
            if plane >= BLOCK:
                return above[f, plane - BLOCK, rows, :]
            return state[f, plane, rows, :]

        for field, along_x in across(get, half_speed):
            for plane in range(BLOCK):
                total = along_x[plane] + sides[field, plane, rows, :]
                value = get(field, plane) - factor * total
                middle[field, plane, rows, :] = value
                if plane < 3:
                    low[field, plane, rows, :] = value
                if plane >= 5:
                    high[field, plane - 5, rows, :] = value
        for plane in range(BLOCK):
            best = jnp.maximum(
                best, wave_speed([middle[f, plane, rows, :] for f in range(FIELDS)])
            )
        return best

    best = lax.fori_loop(0, 4, group, jnp.zeros((8, LANES), jnp.float32))
    top[...] = jnp.full((8, LANES), jnp.max(best), jnp.float32)


def first_stage(*operands):
    whole = jax.ShapeDtypeStruct((FIELDS, BLOCK, ROWS, LANES), jnp.float32)
    halo = jax.ShapeDtypeStruct((FIELDS, 3, ROWS, LANES), jnp.float32)
    return pl.pallas_call(
        first_kernel,
        out_shape=(whole, halo, halo, jax.ShapeDtypeStruct((8, LANES), jnp.float32)),
        in_specs=[VMEM] * len(operands),
        out_specs=(VMEM,) * 4,
        compiler_params=params(),
        cost_estimate=cost(30_000_000, 3_000_000),
        name="first_stage",
    )(*operands)


def second_kernel(start, middle, sides, below, above, first_speed, speed, out):
    half_speed = 0.5 * speed[0:1, :]
    factor = (courant / 12.0) / first_speed[0:1, :]

    def group(j, carry):
        rows = pl.ds(pl.multiple_of(j * 8, 8), 8)
        spread = pl.ds(j, 8, stride=4)

        def get(f, plane):
            if plane < 0:
                return below[f, plane + 3, rows, :]
            if plane >= BLOCK:
                return above[f, plane - BLOCK, rows, :]
            return middle[f, plane, rows, :]

        for field, along_x in across(get, half_speed):
            for plane in range(BLOCK):
                total = along_x[plane] + sides[field, plane, rows, :]
                value = 0.5 * start[field, plane, rows, :] + (
                    0.5 * get(field, plane) - factor * total
                )
                out[field, plane, spread, :] = value
        return carry

    lax.fori_loop(0, 4, group, 0)


def second_stage(*operands):
    return pl.pallas_call(
        second_kernel,
        out_shape=jax.ShapeDtypeStruct((FIELDS, BLOCK, ROWS, LANES), jnp.float32),
        in_specs=[VMEM] * len(operands),
        out_specs=VMEM,
        compiler_params=params(),
        cost_estimate=cost(30_000_000, 3_000_000),
        name="second_stage",
    )(*operands)


def everyone_max(value, axis, size):
    reach = 1
    while reach < size:
        copies = [value]
        for times in range(1, 4):
            turn = reach * times
            if turn < size:
                pairs = [(i, i ^ turn) for i in range(size)]
                copies.append(lax.ppermute(value, axis, pairs))
        value = functools.reduce(jnp.maximum, copies)
        reach *= 4
    return value


def per_device(blocks, owner_list, slot_list):
    size = lax.axis_size("gx")
    own = lax.axis_index("gx")
    per_dev = blocks.shape[0]
    cap = max(2, 2 * per_dev // size)
    up = [(i, (i + 1) % size) for i in range(size)]
    down = [(j, i) for i, j in up]

    rows = tiled_rows(blocks)
    parts = pack(rows, owner_list, size, cap, per_dev)
    parts, rows, owner_list, slot_list = lax.optimization_barrier(
        (parts, rows, owner_list, slot_list)
    )
    parts = parts.reshape(size * TILES * cap, LANES)
    come = lax.all_to_all(parts, "gx", split_axis=0, concat_axis=0, tiled=True)
    table = arrival_spots(owner_list, slot_list, own, per_dev, size, cap)
    speed = jnp.max(lax.all_gather(fastest(rows), "gx"), axis=0)
    come, table, speed = lax.optimization_barrier((come, table, speed))
    state, low, high = unpack(table, come, cap)
    below = lax.ppermute(high, "gx", up)
    above = lax.ppermute(low, "gx", down)
    sides = along_planes(state, speed)
    middle, low, high, top = first_stage(state, sides, below, above, speed)
    second = everyone_max(top, "gx", size)
    low, high, second = lax.optimization_barrier((low, high, second))
    below = lax.ppermute(high, "gx", up)
    above = lax.ppermute(low, "gx", down)
    sides = along_planes(middle, second)
    return second_stage(state, middle, sides, below, above, speed, second)


def solution(mesh):
    return jax.shard_map(
        per_device,
        mesh=mesh,
        in_specs=(P(("runs", "gx"), None, None), P("runs"), P("runs")),
        out_specs=P(None, ("runs", "gx"), None, None),
        check_vma=False,
    )
```

```python
import functools

import jax
import jax.numpy as jnp
from jax import lax
from jax.experimental import pallas as pl
from jax.experimental.pallas import tpu as pltpu
from jax.sharding import PartitionSpec as P

BLOCK = 8
BY = 4
BZ = 16
FIELDS = 5
LANES = 128
ROWS = BY * BLOCK
PAIRS = BLOCK // 2
TILES = PAIRS * FIELDS

gamma_gas = 1.4
courant = 0.25
smooth_epsilon = 1e-06

VMEM = pl.BlockSpec(memory_space=pltpu.VMEM)
SMEM = pl.BlockSpec(memory_space=pltpu.SMEM)


def params(mebibytes=40):
    return pltpu.CompilerParams(vmem_limit_bytes=mebibytes * 1024 * 1024)


def cost(flops, size):
    return pl.CostEstimate(flops=flops, bytes_accessed=size, transcendentals=0)


def wave_speed(fields):
    density, mom_x, mom_y, mom_z, energy = fields
    inverse = 1.0 / density
    vel = (mom_x * inverse, mom_y * inverse, mom_z * inverse)
    kinetic = 0.5 * (mom_x * vel[0] + mom_y * vel[1] + mom_z * vel[2])
    pressure = (gamma_gas - 1.0) * (energy - kinetic)
    sound = jnp.sqrt(gamma_gas * pressure * inverse)
    fastest = jnp.maximum(jnp.maximum(jnp.abs(vel[0]), jnp.abs(vel[1])), jnp.abs(vel[2]))
    return fastest + sound


def tiled_rows(blocks):
    count = blocks.shape[0] // 8
    return blocks.reshape(count, 8, FIELDS, PAIRS, LANES).transpose(2, 0, 3, 1, 4)


def pack_kernel(size, per_dev, owner_hbm, rows_hbm, out, owner, count, sems):
    own = lax.axis_index("gx")
    fetch = pltpu.make_async_copy(owner_hbm, owner, sems.at[0])
    fetch.start()

    def clear(dest, carry):
        count[dest] = 0
        return carry

    lax.fori_loop(0, size, clear, 0)
    fetch.wait()

    def place(block, carry):
        dest = owner[own * per_dev + block]
        rank = count[dest]
        count[dest] = rank + 1
        pltpu.make_async_copy(
            rows_hbm.at[:, lax.div(block, 8), :, lax.rem(block, 8)],
            out.at[dest, :, :, rank],
            sems.at[1],
        ).start()
        return carry

    lax.fori_loop(0, per_dev, place, 0, unroll=8)
    half = out.at[pl.ds(0, size // 2)]
    pltpu.make_async_copy(half, half, sems.at[1]).wait()


def pack(rows, owner_list, size, cap, per_dev):
    return pl.pallas_call(
        functools.partial(pack_kernel, size, per_dev),
        out_shape=jax.ShapeDtypeStruct((size, FIELDS, PAIRS, cap, 1, LANES), jnp.float32),
        in_specs=[pl.BlockSpec(memory_space=pltpu.HBM)] * 2,
        out_specs=pl.BlockSpec(memory_space=pltpu.HBM),
        scratch_shapes=[
            pltpu.SMEM(owner_list.shape, jnp.int32),
            pltpu.SMEM((size,), jnp.int32),
            pltpu.SemaphoreType.DMA((2,)),
        ],
        compiler_params=params(62),
        cost_estimate=cost(1_000_000, 3_000_000),
        name="pack",
    )(owner_list, rows[:, :, :, :, None, :])


def fastest_kernel(rows_ref, out):
    best = jnp.zeros((8, LANES), jnp.float32)
    for group in range(rows_ref.shape[1]):
        for pair in range(PAIRS):
            fields = [rows_ref[f, group, pair] for f in range(FIELDS)]
            best = jnp.maximum(best, wave_speed(fields))
    out[...] = jnp.full((8, LANES), jnp.max(best), jnp.float32)


def fastest(rows):
    return pl.pallas_call(
        fastest_kernel,
        out_shape=jax.ShapeDtypeStruct((8, LANES), jnp.float32),
        in_specs=[VMEM],
        out_specs=VMEM,
        compiler_params=params(),
        cost_estimate=cost(2_000_000, 700_000),
        name="fastest",
    )(rows)


def arrival_spots(owner_list, slot_list, own, per_dev, size, cap):
    owners = owner_list.reshape(size, per_dev)
    slots = slot_list.reshape(size, per_dev)
    mine = owners == own
    spot = jnp.arange(per_dev, dtype=jnp.int32)
    earlier = spot[None, :] < spot[:, None]
    rank = jnp.sum((mine[:, None, :] & earlier[None]).astype(jnp.int32), axis=2)
    row = jnp.arange(size, dtype=jnp.int32)[:, None] * cap + rank
    key = jnp.where(mine, slots, -1)
    hit = key.reshape(1, -1) == spot[:, None]
    return jnp.max(jnp.where(hit, row.reshape(1, -1), 0), axis=1)


def exchanged_bits(rows, group):
    rows = list(rows)
    for bit in range(4):
        step = 1 << bit
        low = (group & step) == 0
        for index in range(16):
            if index & step:
                continue
            first, second = rows[index], rows[index | step]
            rows[index] = jnp.where(low, first, pltpu.roll(second, 8 * step, 1))
            rows[index | step] = jnp.where(low, pltpu.roll(first, LANES - 8 * step, 1), second)
    return rows


def unpack_kernel(cap, table, come, state, low_halo, high_halo, scratch):
    for slot in range(BY * BZ):
        p, q = divmod(slot, BZ)
        where = table[slot]
        source = lax.div(where, cap)
        rank = lax.rem(where, cap)
        for pair in range(PAIRS):
            couple, h = divmod(pair, 2)
            base = source * (TILES * cap) + rank + pair * cap
            value = come[pl.ds(base, FIELDS, stride=PAIRS * cap), :]
            row = (couple * BZ + q) * 8 + 2 * p + h
            scratch[pl.ds(row, FIELDS, stride=PAIRS // 2 * BZ * 8), :] = value
    group = lax.broadcasted_iota(jnp.int32, (8, LANES), 1) // BLOCK
    even = lax.broadcasted_iota(jnp.int32, (8, LANES), 0) % 2 == 0

    for f in range(FIELDS):
        for couple in range(PAIRS // 2):
            first = (f * (PAIRS // 2) + couple) * BZ * 8
            rows = [scratch[first + q * 8 : first + q * 8 + 8, :] for q in range(BZ)]
            moved = exchanged_bits(rows, group)
            for second in range(2):
                for j in range(4):
                    lower = moved[second * BLOCK + j]
                    upper = moved[second * BLOCK + j + 4]
                    planes = (
                        jnp.where(even, lower, pltpu.roll(upper, 1, 0)),
                        jnp.where(even, pltpu.roll(lower, 7, 0), upper),
                    )
                    rows = slice(j * 8, j * 8 + 8)
                    for h in range(2):
                        plane = 4 * couple + 2 * h + second
                        state[f, plane, rows, :] = planes[h]
                        if plane < 3:
                            low_halo[f, plane, rows, :] = planes[h]
                        if plane >= 5:
                            high_halo[f, plane - 5, rows, :] = planes[h]


def unpack(table, come, cap):
    halo = jax.ShapeDtypeStruct((FIELDS, 3, ROWS, LANES), jnp.float32)
    return pl.pallas_call(
        functools.partial(unpack_kernel, cap),
        out_shape=(jax.ShapeDtypeStruct((FIELDS, BLOCK, ROWS, LANES), jnp.float32), halo, halo),
        in_specs=[SMEM, VMEM],
        out_specs=(VMEM,) * 3,
        scratch_shapes=[pltpu.VMEM((FIELDS * (PAIRS // 2) * BZ * 8, LANES), jnp.float32)],
        compiler_params=params(),
        cost_estimate=cost(5_000_000, 2_000_000),
        name="unpack",
    )(table, come)


def y_up(x):
    return jnp.concatenate([x[8:], pltpu.roll(x[:8], 7, 0)], axis=0)


def y_down(x):
    return jnp.concatenate([pltpu.roll(x[24:], 1, 0), x[:24]], axis=0)


def z_up(x):
    return pltpu.roll(x, LANES - 1, 1)


def z_down(x):
    return pltpu.roll(x, 1, 1)


def inverse(x):
    return 1.0 / x


def smoothness(before, after):
    curve = after - before
    middle = 0.5 * (after + before)
    base = curve * curve * (13.0 / 12.0) + smooth_epsilon
    plus = middle + curve
    minus = middle - curve
    left = inverse(base + plus * plus)
    centre = inverse(base + middle * middle)
    right = inverse(base + minus * minus)
    return curve, left * left, centre * centre, right * right


def upwind_term(left, centre, right, jump_before, jump_after):
    right = 3.0 * right
    top = left * (jump_before + jump_before) + right * jump_after
    return top * inverse(left + 6.0 * centre + right)


def periodic_divergence(half_flux, scaled, up, down):
    plus = half_flux + scaled
    minus = half_flux - scaled

    def side(values):
        after = up(values) - values
        curve, left, centre, right = smoothness(down(after), after)
        jump = up(curve) - curve
        return curve, down(left), centre, up(right), down(jump), jump

    curve, left, centre, right, jump_before, jump_after = side(plus)
    face = 6.0 * (half_flux + up(half_flux)) - curve
    face = face - upwind_term(left, centre, right, jump_before, jump_after)
    curve, left, centre, right, jump_before, jump_after = side(minus)
    face = face + up(upwind_term(right, centre, left, jump_after, jump_before) - curve)
    return face - down(face)


def open_divergence(half_flux, scaled):
    count = len(half_flux)
    plus = [a + b for a, b in zip(half_flux, scaled)]
    minus = [a - b for a, b in zip(half_flux, scaled)]
    faces = [None] * count

    def side(values):
        steps = [values[i + 1] - values[i] for i in range(count - 1)]
        parts = [None] + [smoothness(steps[i - 1], steps[i]) for i in range(1, count - 1)]
        return parts

    parts = side(plus)
    for i in range(2, count - 3):
        jump_before = parts[i][0] - parts[i - 1][0]
        jump_after = parts[i + 1][0] - parts[i][0]
        faces[i] = 6.0 * (half_flux[i] + half_flux[i + 1]) - parts[i][0] - upwind_term(
            parts[i - 1][1], parts[i][2], parts[i + 1][3], jump_before, jump_after
        )
    parts = side(minus)
    for i in range(3, count - 2):
        jump_before = parts[i][0] - parts[i - 1][0]
        jump_after = parts[i + 1][0] - parts[i][0]
        faces[i - 1] = faces[i - 1] + (
            upwind_term(parts[i + 1][3], parts[i][2], parts[i - 1][1], jump_after, jump_before)
            - parts[i][0]
        )
    return [faces[i] - faces[i - 1] for i in range(3, count - 3)]


def half_velocities(fields):
    density, mom_x, mom_y, mom_z, energy = fields
    over = 0.5 / density
    vel = (mom_x * over, mom_y * over, mom_z * over)
    kinetic = mom_x * vel[0] + mom_y * vel[1] + mom_z * vel[2]
    pressure = (gamma_gas - 1.0) * (energy - kinetic)
    return vel, pressure


def half_flux(fields, field, direction, speed, pressure):
    if field == 0:
        return 0.5 * fields[1 + direction]
    if field == 4:
        return (fields[4] + pressure) * speed
    flux = fields[field] * speed
    return flux + 0.5 * pressure if field == 1 + direction else flux


def side_planes(fields, half_speed):
    vel, pressure = half_velocities(fields)
    for field in range(FIELDS):
        scaled = half_speed * fields[field]
        along_z = periodic_divergence(
            half_flux(fields, field, 2, vel[2], pressure), scaled, z_up, z_down
        )
        along_y = periodic_divergence(
            half_flux(fields, field, 1, vel[1], pressure), scaled, y_up, y_down
        )
        yield field, along_y + along_z


def plane_kernel(state, speed, out):
    half_speed = 0.5 * speed[0:1, :]

    def one_plane(plane, carry):
        fields = [state[f, plane] for f in range(FIELDS)]
        for field, total in side_planes(fields, half_speed):
            out[field, plane] = total
        return carry

    lax.fori_loop(0, state.shape[1], one_plane, 0)


def along_planes(state, speed):
    return pl.pallas_call(
        plane_kernel,
        out_shape=jax.ShapeDtypeStruct(state.shape, jnp.float32),
        in_specs=[VMEM, VMEM],
        out_specs=VMEM,
        compiler_params=params(),
        cost_estimate=cost(20_000_000, 1_000_000),
        name="planes",
    )(state, speed)


def across(get, half_speed):
    span = range(-3, BLOCK + 3)
    speeds, pressures = [], []
    for plane in span:
        vel, pressure = half_velocities([get(f, plane) for f in range(FIELDS)])
        speeds.append(vel[0])
        pressures.append(pressure)
    for field in range(FIELDS):
        fluxes, scaled = [], []
        for i, plane in enumerate(span):
            if field == 0:
                flux = 0.5 * get(1, plane)
            elif field == 4:
                flux = (get(4, plane) + pressures[i]) * speeds[i]
            else:
                flux = get(field, plane) * speeds[i]
                if field == 1:
                    flux = flux + 0.5 * pressures[i]
            fluxes.append(flux)
            scaled.append(half_speed * get(field, plane))
        yield field, open_divergence(fluxes, scaled)


def first_kernel(state, sides, below, above, speed, middle, low, high, top):
    half_speed = 0.5 * speed[0:1, :]
    factor = (courant / 6.0) / speed[0:1, :]

    def group(j, best):
        rows = pl.ds(pl.multiple_of(j * 8, 8), 8)

        def get(f, plane):
            if plane < 0:
                return below[f, plane + 3, rows, :]
            if plane >= BLOCK:
                return above[f, plane - BLOCK, rows, :]
            return state[f, plane, rows, :]

        for field, along_x in across(get, half_speed):
            for plane in range(BLOCK):
                total = along_x[plane] + sides[field, plane, rows, :]
                value = get(field, plane) - factor * total
                middle[field, plane, rows, :] = value
                if plane < 3:
                    low[field, plane, rows, :] = value
                if plane >= 5:
                    high[field, plane - 5, rows, :] = value
        for plane in range(BLOCK):
            best = jnp.maximum(
                best, wave_speed([middle[f, plane, rows, :] for f in range(FIELDS)])
            )
        return best

    best = lax.fori_loop(0, 4, group, jnp.zeros((8, LANES), jnp.float32))
    top[...] = jnp.full((8, LANES), jnp.max(best), jnp.float32)


def first_stage(*operands):
    whole = jax.ShapeDtypeStruct((FIELDS, BLOCK, ROWS, LANES), jnp.float32)
    halo = jax.ShapeDtypeStruct((FIELDS, 3, ROWS, LANES), jnp.float32)
    return pl.pallas_call(
        first_kernel,
        out_shape=(whole, halo, halo, jax.ShapeDtypeStruct((8, LANES), jnp.float32)),
        in_specs=[VMEM] * len(operands),
        out_specs=(VMEM,) * 4,
        compiler_params=params(),
        cost_estimate=cost(30_000_000, 3_000_000),
        name="first_stage",
    )(*operands)


def second_kernel(start, middle, sides, below, above, first_speed, speed, out):
    half_speed = 0.5 * speed[0:1, :]
    factor = (courant / 12.0) / first_speed[0:1, :]

    def group(j, carry):
        rows = pl.ds(pl.multiple_of(j * 8, 8), 8)
        spread = pl.ds(j, 8, stride=4)

        def get(f, plane):
            if plane < 0:
                return below[f, plane + 3, rows, :]
            if plane >= BLOCK:
                return above[f, plane - BLOCK, rows, :]
            return middle[f, plane, rows, :]

        for field, along_x in across(get, half_speed):
            for plane in range(BLOCK):
                total = along_x[plane] + sides[field, plane, rows, :]
                value = 0.5 * start[field, plane, rows, :] + (
                    0.5 * get(field, plane) - factor * total
                )
                out[field, plane, spread, :] = value
        return carry

    lax.fori_loop(0, 4, group, 0)


def second_stage(*operands):
    return pl.pallas_call(
        second_kernel,
        out_shape=jax.ShapeDtypeStruct((FIELDS, BLOCK, ROWS, LANES), jnp.float32),
        in_specs=[VMEM] * len(operands),
        out_specs=VMEM,
        compiler_params=params(),
        cost_estimate=cost(30_000_000, 3_000_000),
        name="second_stage",
    )(*operands)


def everyone_max(value, axis, size):
    reach = 1
    while reach < size:
        copies = [value]
        for times in range(1, 4):
            turn = reach * times
            if turn < size:
                pairs = [(i, i ^ turn) for i in range(size)]
                copies.append(lax.ppermute(value, axis, pairs))
        value = functools.reduce(jnp.maximum, copies)
        reach *= 4
    return value


def swapped_max(value, axis, size):
    reach = 1
    while reach < size:
        width = min(4, size // reach)
        groups = [
            [first + reach * times for times in range(width)]
            for first in range(size)
            if first // reach % width == 0
        ]
        copies = jnp.broadcast_to(value[None], (width,) + value.shape)
        copies = lax.all_to_all(
            copies, axis, split_axis=0, concat_axis=0, tiled=True, axis_index_groups=groups
        )
        value = jnp.max(copies, axis=0)
        reach *= width
    return value


def per_device(blocks, owner_list, slot_list):
    size = lax.axis_size("gx")
    own = lax.axis_index("gx")
    per_dev = blocks.shape[0]
    cap = max(2, 2 * per_dev // size)
    up = [(i, (i + 1) % size) for i in range(size)]
    down = [(j, i) for i, j in up]

    rows = tiled_rows(blocks)
    parts = pack(rows, owner_list, size, cap, per_dev)
    parts, rows, owner_list, slot_list = lax.optimization_barrier(
        (parts, rows, owner_list, slot_list)
    )
    parts = parts.reshape(size * TILES * cap, LANES)
    come = lax.all_to_all(parts, "gx", split_axis=0, concat_axis=0, tiled=True)
    table = arrival_spots(owner_list, slot_list, own, per_dev, size, cap)
    speed = everyone_max(fastest(rows), "gx", size)
    come, table, speed = lax.optimization_barrier((come, table, speed))
    state, low, high = unpack(table, come, cap)
    below = lax.ppermute(high, "gx", up)
    above = lax.ppermute(low, "gx", down)
    sides = along_planes(state, speed)
    middle, low, high, top = first_stage(state, sides, below, above, speed)
    second = swapped_max(top, "gx", size)
    below = lax.ppermute(high, "gx", up)
    above = lax.ppermute(low, "gx", down)
    sides = along_planes(middle, second)
    return second_stage(state, middle, sides, below, above, speed, second)


def solution(mesh):
    return jax.shard_map(
        per_device,
        mesh=mesh,
        in_specs=(P(("runs", "gx"), None, None), P("runs"), P("runs")),
        out_specs=P(None, ("runs", "gx"), None, None),
        check_vma=False,
    )
```

```python
import functools

import jax
import jax.numpy as jnp
from jax import lax
from jax.experimental import pallas as pl
from jax.experimental.pallas import tpu as pltpu
from jax.sharding import PartitionSpec as P

BLOCK = 8
BY = 4
BZ = 16
FIELDS = 5
LANES = 128
ROWS = BY * BLOCK
PAIRS = BLOCK // 2
TILES = PAIRS * FIELDS

gamma_gas = 1.4
courant = 0.25
smooth_epsilon = 1e-06

VMEM = pl.BlockSpec(memory_space=pltpu.VMEM)
SMEM = pl.BlockSpec(memory_space=pltpu.SMEM)


def params(mebibytes=40):
    return pltpu.CompilerParams(vmem_limit_bytes=mebibytes * 1024 * 1024)


def cost(flops, size):
    return pl.CostEstimate(flops=flops, bytes_accessed=size, transcendentals=0)


def wave_speed(fields):
    density, mom_x, mom_y, mom_z, energy = fields
    inverse = 1.0 / density
    vel = (mom_x * inverse, mom_y * inverse, mom_z * inverse)
    kinetic = 0.5 * (mom_x * vel[0] + mom_y * vel[1] + mom_z * vel[2])
    pressure = (gamma_gas - 1.0) * (energy - kinetic)
    sound = jnp.sqrt(gamma_gas * pressure * inverse)
    fastest = jnp.maximum(jnp.maximum(jnp.abs(vel[0]), jnp.abs(vel[1])), jnp.abs(vel[2]))
    return fastest + sound


def tiled_rows(blocks):
    count = blocks.shape[0] // 8
    groups = blocks.reshape(count, 8, FIELDS, PAIRS, LANES).transpose(2, 0, 3, 1, 4)
    return groups.reshape(FIELDS * count * PAIRS * 8, LANES)


def pack_kernel(
    size, cap, per_dev, owner_hbm, rows_hbm, out_hbm, owner, rows, out, count, member, sems
):
    own = lax.axis_index("gx")
    fetch_owner = pltpu.make_async_copy(owner_hbm, owner, sems.at[0])
    fetch_rows = pltpu.make_async_copy(rows_hbm, rows, sems.at[1])
    fetch_owner.start()
    fetch_rows.start()

    def clear(dest, carry):
        count[dest] = 0
        return carry

    lax.fori_loop(0, size, clear, 0, unroll=8)
    fetch_owner.wait()

    def note(block, carry):
        dest = owner[own * per_dev + block]
        rank = count[dest]
        count[dest] = rank + 1
        member[dest * cap + rank] = lax.div(block, 8) * (PAIRS * 8) + lax.rem(block, 8)
        return carry

    lax.fori_loop(0, per_dev, note, 0, unroll=8)
    fetch_rows.wait()
    tiles = TILES * cap

    def message(dest, carry):
        @pl.when(count[dest] > 0)
        def _():
            for rank in range(cap):
                first = member[dest * cap + rank]
                for pair in range(PAIRS):
                    source = pl.ds(first + pair * 8, FIELDS, stride=per_dev * PAIRS)
                    to = dest * tiles + pair * (FIELDS * cap) + rank
                    out[pl.ds(to, FIELDS, stride=cap), :] = rows[source, :]
            part = pl.ds(pl.multiple_of(dest * tiles, tiles), tiles)
            pltpu.make_async_copy(out.at[part], out_hbm.at[part], sems.at[2]).start()

        return carry

    lax.fori_loop(0, size, message, 0)
    half = out.at[pl.ds(0, per_dev * TILES)]
    pltpu.make_async_copy(half, half, sems.at[2]).wait()


def pack(rows, owner_list, size, cap, per_dev):
    send = (size * TILES * cap, LANES)
    return pl.pallas_call(
        functools.partial(pack_kernel, size, cap, per_dev),
        out_shape=jax.ShapeDtypeStruct(send, jnp.float32),
        in_specs=[pl.BlockSpec(memory_space=pltpu.HBM)] * 2,
        out_specs=pl.BlockSpec(memory_space=pltpu.HBM),
        scratch_shapes=[
            pltpu.SMEM(owner_list.shape, jnp.int32),
            pltpu.VMEM(rows.shape, jnp.float32),
            pltpu.VMEM(send, jnp.float32),
            pltpu.SMEM((size,), jnp.int32),
            pltpu.SMEM((size * cap,), jnp.int32),
            pltpu.SemaphoreType.DMA((3,)),
        ],
        compiler_params=params(62),
        cost_estimate=cost(1_000_000, 3_000_000),
        name="pack",
    )(owner_list, rows)


def fastest_kernel(rows_ref, out):
    best = jnp.zeros((8, LANES), jnp.float32)
    step = rows_ref.shape[0] // FIELDS
    for first in range(0, step, 8):
        fields = [rows_ref[f * step + first : f * step + first + 8, :] for f in range(FIELDS)]
        best = jnp.maximum(best, wave_speed(fields))
    out[...] = jnp.full((8, LANES), jnp.max(best), jnp.float32)


def fastest(rows):
    return pl.pallas_call(
        fastest_kernel,
        out_shape=jax.ShapeDtypeStruct((8, LANES), jnp.float32),
        in_specs=[VMEM],
        out_specs=VMEM,
        compiler_params=params(),
        cost_estimate=cost(2_000_000, 700_000),
        name="fastest",
    )(rows)


def arrival_spots(owner_list, slot_list, own, per_dev, size, cap):
    owners = owner_list.reshape(size, per_dev)
    slots = slot_list.reshape(size, per_dev)
    mine = owners == own
    spot = jnp.arange(per_dev, dtype=jnp.int32)
    earlier = spot[None, :] < spot[:, None]
    rank = jnp.sum((mine[:, None, :] & earlier[None]).astype(jnp.int32), axis=2)
    row = jnp.arange(size, dtype=jnp.int32)[:, None] * cap + rank
    key = jnp.where(mine, slots, -1)
    hit = key.reshape(1, -1) == spot[:, None]
    return jnp.max(jnp.where(hit, row.reshape(1, -1), 0), axis=1)


def exchanged_bits(rows, group):
    rows = list(rows)
    for bit in range(4):
        step = 1 << bit
        low = (group & step) == 0
        for index in range(16):
            if index & step:
                continue
            first, second = rows[index], rows[index | step]
            rows[index] = jnp.where(low, first, pltpu.roll(second, 8 * step, 1))
            rows[index | step] = jnp.where(low, pltpu.roll(first, LANES - 8 * step, 1), second)
    return rows


def unpack_kernel(cap, table, come, state, low_halo, high_halo, scratch):
    for slot in range(BY * BZ):
        p, q = divmod(slot, BZ)
        where = table[slot]
        source = lax.div(where, cap)
        rank = lax.rem(where, cap)
        for pair in range(PAIRS):
            couple, h = divmod(pair, 2)
            base = source * (TILES * cap) + rank + pair * (FIELDS * cap)
            value = come[pl.ds(base, FIELDS, stride=cap), :]
            row = (couple * BZ + q) * 8 + 2 * p + h
            scratch[pl.ds(row, FIELDS, stride=PAIRS // 2 * BZ * 8), :] = value
    group = lax.broadcasted_iota(jnp.int32, (8, LANES), 1) // BLOCK
    even = lax.broadcasted_iota(jnp.int32, (8, LANES), 0) % 2 == 0

    for f in range(FIELDS):
        for couple in range(PAIRS // 2):
            first = (f * (PAIRS // 2) + couple) * BZ * 8
            rows = [scratch[first + q * 8 : first + q * 8 + 8, :] for q in range(BZ)]
            moved = exchanged_bits(rows, group)
            for second in range(2):
                for j in range(4):
                    lower = moved[second * BLOCK + j]
                    upper = moved[second * BLOCK + j + 4]
                    planes = (
                        jnp.where(even, lower, pltpu.roll(upper, 1, 0)),
                        jnp.where(even, pltpu.roll(lower, 7, 0), upper),
                    )
                    rows = slice(j * 8, j * 8 + 8)
                    for h in range(2):
                        plane = 4 * couple + 2 * h + second
                        state[f, plane, rows, :] = planes[h]
                        if plane < 3:
                            low_halo[f, plane, rows, :] = planes[h]
                        if plane >= 5:
                            high_halo[f, plane - 5, rows, :] = planes[h]


def unpack(table, come, cap):
    halo = jax.ShapeDtypeStruct((FIELDS, 3, ROWS, LANES), jnp.float32)
    return pl.pallas_call(
        functools.partial(unpack_kernel, cap),
        out_shape=(jax.ShapeDtypeStruct((FIELDS, BLOCK, ROWS, LANES), jnp.float32), halo, halo),
        in_specs=[SMEM, VMEM],
        out_specs=(VMEM,) * 3,
        scratch_shapes=[pltpu.VMEM((FIELDS * (PAIRS // 2) * BZ * 8, LANES), jnp.float32)],
        compiler_params=params(),
        cost_estimate=cost(5_000_000, 2_000_000),
        name="unpack",
    )(table, come)


def y_up(x):
    return jnp.concatenate([x[8:], pltpu.roll(x[:8], 7, 0)], axis=0)


def y_down(x):
    return jnp.concatenate([pltpu.roll(x[24:], 1, 0), x[:24]], axis=0)


def z_up(x):
    return pltpu.roll(x, LANES - 1, 1)


def z_down(x):
    return pltpu.roll(x, 1, 1)


def inverse(x):
    return 1.0 / x


def smoothness(before, after):
    curve = after - before
    middle = 0.5 * (after + before)
    base = curve * curve * (13.0 / 12.0) + smooth_epsilon
    plus = middle + curve
    minus = middle - curve
    left = inverse(base + plus * plus)
    centre = inverse(base + middle * middle)
    right = inverse(base + minus * minus)
    return curve, left * left, centre * centre, right * right


def upwind_term(left, centre, right, jump_before, jump_after):
    right = 3.0 * right
    top = left * (jump_before + jump_before) + right * jump_after
    return top * inverse(left + 6.0 * centre + right)


def periodic_divergence(half_flux, scaled, up, down):
    plus = half_flux + scaled
    minus = half_flux - scaled

    def side(values):
        after = up(values) - values
        curve, left, centre, right = smoothness(down(after), after)
        jump = up(curve) - curve
        return curve, down(left), centre, up(right), down(jump), jump

    curve, left, centre, right, jump_before, jump_after = side(plus)
    face = 6.0 * (half_flux + up(half_flux)) - curve
    face = face - upwind_term(left, centre, right, jump_before, jump_after)
    curve, left, centre, right, jump_before, jump_after = side(minus)
    face = face + up(upwind_term(right, centre, left, jump_after, jump_before) - curve)
    return face - down(face)


def open_divergence(half_flux, scaled):
    count = len(half_flux)
    plus = [a + b for a, b in zip(half_flux, scaled)]
    minus = [a - b for a, b in zip(half_flux, scaled)]
    faces = [None] * count

    def side(values):
        steps = [values[i + 1] - values[i] for i in range(count - 1)]
        parts = [None] + [smoothness(steps[i - 1], steps[i]) for i in range(1, count - 1)]
        return parts

    parts = side(plus)
    for i in range(2, count - 3):
        jump_before = parts[i][0] - parts[i - 1][0]
        jump_after = parts[i + 1][0] - parts[i][0]
        faces[i] = 6.0 * (half_flux[i] + half_flux[i + 1]) - parts[i][0] - upwind_term(
            parts[i - 1][1], parts[i][2], parts[i + 1][3], jump_before, jump_after
        )
    parts = side(minus)
    for i in range(3, count - 2):
        jump_before = parts[i][0] - parts[i - 1][0]
        jump_after = parts[i + 1][0] - parts[i][0]
        faces[i - 1] = faces[i - 1] + (
            upwind_term(parts[i + 1][3], parts[i][2], parts[i - 1][1], jump_after, jump_before)
            - parts[i][0]
        )
    return [faces[i] - faces[i - 1] for i in range(3, count - 3)]


def half_velocities(fields):
    density, mom_x, mom_y, mom_z, energy = fields
    over = 0.5 / density
    vel = (mom_x * over, mom_y * over, mom_z * over)
    kinetic = mom_x * vel[0] + mom_y * vel[1] + mom_z * vel[2]
    pressure = (gamma_gas - 1.0) * (energy - kinetic)
    return vel, pressure


def half_flux(fields, field, direction, speed, pressure):
    if field == 0:
        return 0.5 * fields[1 + direction]
    if field == 4:
        return (fields[4] + pressure) * speed
    flux = fields[field] * speed
    return flux + 0.5 * pressure if field == 1 + direction else flux


def side_planes(fields, half_speed):
    vel, pressure = half_velocities(fields)
    for field in range(FIELDS):
        scaled = half_speed * fields[field]
        along_z = periodic_divergence(
            half_flux(fields, field, 2, vel[2], pressure), scaled, z_up, z_down
        )
        along_y = periodic_divergence(
            half_flux(fields, field, 1, vel[1], pressure), scaled, y_up, y_down
        )
        yield field, along_y + along_z


def plane_kernel(state, speed, out):
    half_speed = 0.5 * speed[0:1, :]

    def one_plane(plane, carry):
        fields = [state[f, plane] for f in range(FIELDS)]
        for field, total in side_planes(fields, half_speed):
            out[field, plane] = total
        return carry

    lax.fori_loop(0, state.shape[1], one_plane, 0)


def along_planes(state, speed):
    return pl.pallas_call(
        plane_kernel,
        out_shape=jax.ShapeDtypeStruct(state.shape, jnp.float32),
        in_specs=[VMEM, VMEM],
        out_specs=VMEM,
        compiler_params=params(),
        cost_estimate=cost(20_000_000, 1_000_000),
        name="planes",
    )(state, speed)


def across(get, half_speed):
    span = range(-3, BLOCK + 3)
    speeds, pressures = [], []
    for plane in span:
        vel, pressure = half_velocities([get(f, plane) for f in range(FIELDS)])
        speeds.append(vel[0])
        pressures.append(pressure)
    for field in range(FIELDS):
        fluxes, scaled = [], []
        for i, plane in enumerate(span):
            if field == 0:
                flux = 0.5 * get(1, plane)
            elif field == 4:
                flux = (get(4, plane) + pressures[i]) * speeds[i]
            else:
                flux = get(field, plane) * speeds[i]
                if field == 1:
                    flux = flux + 0.5 * pressures[i]
            fluxes.append(flux)
            scaled.append(half_speed * get(field, plane))
        yield field, open_divergence(fluxes, scaled)


def first_kernel(state, sides, below, above, speed, middle, low, high, top):
    half_speed = 0.5 * speed[0:1, :]
    factor = (courant / 6.0) / speed[0:1, :]

    def group(j, best):
        rows = pl.ds(pl.multiple_of(j * 8, 8), 8)

        def get(f, plane):
            if plane < 0:
                return below[f, plane + 3, rows, :]
            if plane >= BLOCK:
                return above[f, plane - BLOCK, rows, :]
            return state[f, plane, rows, :]

        for field, along_x in across(get, half_speed):
            for plane in range(BLOCK):
                total = along_x[plane] + sides[field, plane, rows, :]
                value = get(field, plane) - factor * total
                middle[field, plane, rows, :] = value
                if plane < 3:
                    low[field, plane, rows, :] = value
                if plane >= 5:
                    high[field, plane - 5, rows, :] = value
        for plane in range(BLOCK):
            best = jnp.maximum(
                best, wave_speed([middle[f, plane, rows, :] for f in range(FIELDS)])
            )
        return best

    best = lax.fori_loop(0, 4, group, jnp.zeros((8, LANES), jnp.float32))
    top[...] = jnp.full((8, LANES), jnp.max(best), jnp.float32)


def first_stage(*operands):
    whole = jax.ShapeDtypeStruct((FIELDS, BLOCK, ROWS, LANES), jnp.float32)
    halo = jax.ShapeDtypeStruct((FIELDS, 3, ROWS, LANES), jnp.float32)
    return pl.pallas_call(
        first_kernel,
        out_shape=(whole, halo, halo, jax.ShapeDtypeStruct((8, LANES), jnp.float32)),
        in_specs=[VMEM] * len(operands),
        out_specs=(VMEM,) * 4,
        compiler_params=params(),
        cost_estimate=cost(30_000_000, 3_000_000),
        name="first_stage",
    )(*operands)


def second_kernel(start, middle, sides, below, above, first_speed, speed, out):
    half_speed = 0.5 * speed[0:1, :]
    factor = (courant / 12.0) / first_speed[0:1, :]

    def group(j, carry):
        rows = pl.ds(pl.multiple_of(j * 8, 8), 8)
        spread = pl.ds(j, 8, stride=4)

        def get(f, plane):
            if plane < 0:
                return below[f, plane + 3, rows, :]
            if plane >= BLOCK:
                return above[f, plane - BLOCK, rows, :]
            return middle[f, plane, rows, :]

        for field, along_x in across(get, half_speed):
            for plane in range(BLOCK):
                total = along_x[plane] + sides[field, plane, rows, :]
                value = 0.5 * start[field, plane, rows, :] + (
                    0.5 * get(field, plane) - factor * total
                )
                out[field, plane, spread, :] = value
        return carry

    lax.fori_loop(0, 4, group, 0)


def second_stage(*operands):
    return pl.pallas_call(
        second_kernel,
        out_shape=jax.ShapeDtypeStruct((FIELDS, BLOCK, ROWS, LANES), jnp.float32),
        in_specs=[VMEM] * len(operands),
        out_specs=VMEM,
        compiler_params=params(),
        cost_estimate=cost(30_000_000, 3_000_000),
        name="second_stage",
    )(*operands)


def everyone_max(value, axis, size):
    reach = 1
    while reach < size:
        copies = [value]
        for times in range(1, 4):
            turn = reach * times
            if turn < size:
                pairs = [(i, i ^ turn) for i in range(size)]
                copies.append(lax.ppermute(value, axis, pairs))
        value = functools.reduce(jnp.maximum, copies)
        reach *= 4
    return value


def per_device(blocks, owner_list, slot_list):
    size = lax.axis_size("gx")
    own = lax.axis_index("gx")
    per_dev = blocks.shape[0]
    cap = max(2, 2 * per_dev // size)
    up = [(i, (i + 1) % size) for i in range(size)]
    down = [(j, i) for i, j in up]

    rows = tiled_rows(blocks)
    parts = pack(rows, owner_list, size, cap, per_dev)
    parts, rows, owner_list, slot_list = lax.optimization_barrier(
        (parts, rows, owner_list, slot_list)
    )
    come = lax.all_to_all(parts, "gx", split_axis=0, concat_axis=0, tiled=True)
    table = arrival_spots(owner_list, slot_list, own, per_dev, size, cap)
    speed = everyone_max(fastest(rows), "gx", size)
    come, table, speed = lax.optimization_barrier((come, table, speed))
    state, low, high = unpack(table, come, cap)
    below = lax.ppermute(high, "gx", up)
    above = lax.ppermute(low, "gx", down)
    sides = along_planes(state, speed)
    middle, low, high, top = first_stage(state, sides, below, above, speed)
    second = everyone_max(top, "gx", size)
    below = lax.ppermute(high, "gx", up)
    above = lax.ppermute(low, "gx", down)
    sides = along_planes(middle, second)
    return second_stage(state, middle, sides, below, above, speed, second)


def solution(mesh):
    return jax.shard_map(
        per_device,
        mesh=mesh,
        in_specs=(P(("runs", "gx"), None, None), P("runs"), P("runs")),
        out_specs=P(None, ("runs", "gx"), None, None),
        check_vma=False,
    )
```

```python
import functools

import jax
import jax.numpy as jnp
from jax import lax
from jax.experimental import pallas as pl
from jax.experimental.pallas import tpu as pltpu
from jax.sharding import PartitionSpec as P

BLOCK = 8
BY = 4
BZ = 16
FIELDS = 5
LANES = 128
ROWS = BY * BLOCK
PAIRS = BLOCK // 2
TILES = PAIRS * FIELDS

gamma_gas = 1.4
courant = 0.25
smooth_epsilon = 1e-06

VMEM = pl.BlockSpec(memory_space=pltpu.VMEM)
SMEM = pl.BlockSpec(memory_space=pltpu.SMEM)


def params(mebibytes=40):
    return pltpu.CompilerParams(vmem_limit_bytes=mebibytes * 1024 * 1024)


def cost(flops, size):
    return pl.CostEstimate(flops=flops, bytes_accessed=size, transcendentals=0)


def wave_speed(fields):
    density, mom_x, mom_y, mom_z, energy = fields
    inverse = 1.0 / density
    vel = (mom_x * inverse, mom_y * inverse, mom_z * inverse)
    kinetic = 0.5 * (mom_x * vel[0] + mom_y * vel[1] + mom_z * vel[2])
    pressure = (gamma_gas - 1.0) * (energy - kinetic)
    sound = jnp.sqrt(gamma_gas * pressure * inverse)
    fastest = jnp.maximum(jnp.maximum(jnp.abs(vel[0]), jnp.abs(vel[1])), jnp.abs(vel[2]))
    return fastest + sound


def tiled_rows(blocks):
    count = blocks.shape[0] // 8
    groups = blocks.reshape(count, 8, FIELDS, PAIRS, LANES).transpose(2, 0, 3, 1, 4)
    return groups.reshape(FIELDS * count * PAIRS * 8, LANES)


def pack_kernel(
    size, cap, per_dev, owner_hbm, rows_hbm, out_hbm, owner, rows, out, top, count, member, sems
):
    own = lax.axis_index("gx")
    fetch_owner = pltpu.make_async_copy(owner_hbm, owner, sems.at[0])
    fetch_rows = pltpu.make_async_copy(rows_hbm, rows, sems.at[1])
    fetch_owner.start()
    fetch_rows.start()

    def clear(dest, carry):
        count[dest] = 0
        return carry

    lax.fori_loop(0, size, clear, 0, unroll=8)
    fetch_owner.wait()

    def note(block, carry):
        dest = owner[own * per_dev + block]
        rank = count[dest]
        count[dest] = rank + 1
        member[dest * cap + rank] = lax.div(block, 8) * (PAIRS * 8) + lax.rem(block, 8)
        return carry

    lax.fori_loop(0, per_dev, note, 0, unroll=8)
    fetch_rows.wait()
    tiles = TILES * cap

    def message(dest, carry):
        @pl.when(count[dest] > 0)
        def _():
            for rank in range(cap):
                first = member[dest * cap + rank]
                for pair in range(PAIRS):
                    source = pl.ds(first + pair * 8, FIELDS, stride=per_dev * PAIRS)
                    to = dest * tiles + pair * (FIELDS * cap) + rank
                    out[pl.ds(to, FIELDS, stride=cap), :] = rows[source, :]
            part = out.at[pl.ds(pl.multiple_of(dest * tiles, tiles), tiles)]
            pltpu.make_async_copy(part, out_hbm.at[dest, pl.ds(0, tiles), 0], sems.at[2]).start()

        return carry

    lax.fori_loop(0, size, message, 0)
    best = jnp.zeros((8, LANES), jnp.float32)
    step = per_dev * PAIRS
    for first in range(0, step, 8):
        fields = [rows[f * step + first : f * step + first + 8, :] for f in range(FIELDS)]
        best = jnp.maximum(best, wave_speed(fields))
    top[...] = jnp.full(top.shape, jnp.max(best), jnp.float32)
    for dest in range(size):
        pltpu.make_async_copy(
            top.at[pl.ds(dest, 1)], out_hbm.at[dest, tiles], sems.at[3]
        ).start()
    half = out.at[pl.ds(0, per_dev * TILES)]
    pltpu.make_async_copy(half, half, sems.at[2]).wait()
    pltpu.make_async_copy(top, top, sems.at[3]).wait()


def pack(rows, owner_list, size, cap, per_dev):
    return pl.pallas_call(
        functools.partial(pack_kernel, size, cap, per_dev),
        out_shape=jax.ShapeDtypeStruct((size, TILES * cap + 1, 1, LANES), jnp.float32),
        in_specs=[pl.BlockSpec(memory_space=pltpu.HBM)] * 2,
        out_specs=pl.BlockSpec(memory_space=pltpu.HBM),
        scratch_shapes=[
            pltpu.SMEM(owner_list.shape, jnp.int32),
            pltpu.VMEM(rows.shape, jnp.float32),
            pltpu.VMEM((size * TILES * cap, LANES), jnp.float32),
            pltpu.VMEM((size, LANES), jnp.float32),
            pltpu.SMEM((size,), jnp.int32),
            pltpu.SMEM((size * cap,), jnp.int32),
            pltpu.SemaphoreType.DMA((4,)),
        ],
        compiler_params=params(62),
        cost_estimate=cost(1_000_000, 3_000_000),
        name="pack",
    )(owner_list, rows)


def arrival_spots(owner_list, slot_list, own, per_dev, size, cap):
    owners = owner_list.reshape(size, per_dev)
    slots = slot_list.reshape(size, per_dev)
    mine = owners == own
    spot = jnp.arange(per_dev, dtype=jnp.int32)
    earlier = spot[None, :] < spot[:, None]
    rank = jnp.sum((mine[:, None, :] & earlier[None]).astype(jnp.int32), axis=2)
    row = jnp.arange(size, dtype=jnp.int32)[:, None] * cap + rank
    key = jnp.where(mine, slots, -1)
    hit = key.reshape(1, -1) == spot[:, None]
    return jnp.max(jnp.where(hit, row.reshape(1, -1), 0), axis=1)


def exchanged_bits(rows, group):
    rows = list(rows)
    for bit in range(4):
        step = 1 << bit
        low = (group & step) == 0
        for index in range(16):
            if index & step:
                continue
            first, second = rows[index], rows[index | step]
            rows[index] = jnp.where(low, first, pltpu.roll(second, 8 * step, 1))
            rows[index | step] = jnp.where(low, pltpu.roll(first, LANES - 8 * step, 1), second)
    return rows


def unpack_kernel(size, cap, table, come, state, low_halo, high_halo, speed, scratch):
    message = TILES * cap + 1
    best = come[message - 1 : message, :]
    for source in range(1, size):
        best = jnp.maximum(best, come[(source + 1) * message - 1 : (source + 1) * message, :])
    speed[...] = jnp.broadcast_to(best, speed.shape)
    for slot in range(BY * BZ):
        p, q = divmod(slot, BZ)
        where = table[slot]
        source = lax.div(where, cap)
        rank = lax.rem(where, cap)
        for pair in range(PAIRS):
            couple, h = divmod(pair, 2)
            base = source * message + rank + pair * (FIELDS * cap)
            value = come[pl.ds(base, FIELDS, stride=cap), :]
            row = (couple * BZ + q) * 8 + 2 * p + h
            scratch[pl.ds(row, FIELDS, stride=PAIRS // 2 * BZ * 8), :] = value
    group = lax.broadcasted_iota(jnp.int32, (8, LANES), 1) // BLOCK
    even = lax.broadcasted_iota(jnp.int32, (8, LANES), 0) % 2 == 0

    for f in range(FIELDS):
        for couple in range(PAIRS // 2):
            first = (f * (PAIRS // 2) + couple) * BZ * 8
            rows = [scratch[first + q * 8 : first + q * 8 + 8, :] for q in range(BZ)]
            moved = exchanged_bits(rows, group)
            for second in range(2):
                for j in range(4):
                    lower = moved[second * BLOCK + j]
                    upper = moved[second * BLOCK + j + 4]
                    planes = (
                        jnp.where(even, lower, pltpu.roll(upper, 1, 0)),
                        jnp.where(even, pltpu.roll(lower, 7, 0), upper),
                    )
                    rows = slice(j * 8, j * 8 + 8)
                    for h in range(2):
                        plane = 4 * couple + 2 * h + second
                        state[f, plane, rows, :] = planes[h]
                        if plane < 3:
                            low_halo[f, plane, rows, :] = planes[h]
                        if plane >= 5:
                            high_halo[f, plane - 5, rows, :] = planes[h]


def unpack(table, come, size, cap):
    halo = jax.ShapeDtypeStruct((FIELDS, 3, ROWS, LANES), jnp.float32)
    return pl.pallas_call(
        functools.partial(unpack_kernel, size, cap),
        out_shape=(
            jax.ShapeDtypeStruct((FIELDS, BLOCK, ROWS, LANES), jnp.float32),
            halo,
            halo,
            jax.ShapeDtypeStruct((8, LANES), jnp.float32),
        ),
        in_specs=[SMEM, VMEM],
        out_specs=(VMEM,) * 4,
        scratch_shapes=[pltpu.VMEM((FIELDS * (PAIRS // 2) * BZ * 8, LANES), jnp.float32)],
        compiler_params=params(),
        cost_estimate=cost(5_000_000, 2_000_000),
        name="unpack",
    )(table, come)


def y_up(x):
    return jnp.concatenate([x[8:], pltpu.roll(x[:8], 7, 0)], axis=0)


def y_down(x):
    return jnp.concatenate([pltpu.roll(x[24:], 1, 0), x[:24]], axis=0)


def y_up_two(x):
    return jnp.concatenate([x[16:], pltpu.roll(x[:8], 7, 0), pltpu.roll(x[8:16], 7, 0)], axis=0)


def z_up(x):
    return pltpu.roll(x, LANES - 1, 1)


def z_up_two(x):
    return pltpu.roll(x, LANES - 2, 1)


def z_down(x):
    return pltpu.roll(x, 1, 1)


def inverse(x):
    return 1.0 / x


def smoothness(before, after):
    curve = after - before
    middle = 0.5 * (after + before)
    base = curve * curve * (13.0 / 12.0) + smooth_epsilon
    plus = middle + curve
    minus = middle - curve
    left = inverse(base + plus * plus)
    centre = inverse(base + middle * middle)
    right = inverse(base + minus * minus)
    return curve, left * left, centre * centre, right * right


def upwind_term(left, centre, right, jump_before, jump_after):
    right = 3.0 * right
    top = left * (jump_before + jump_before) + right * jump_after
    return top * inverse(left + 6.0 * centre + right)


def periodic_divergence(half_flux, scaled, up, up_two, down):
    plus = half_flux + scaled
    minus = half_flux - scaled

    def side(values):
        after = up(values) - values
        curve, left, centre, right = smoothness(down(after), after)
        above = up(curve)
        return curve, above, left, centre, right, above - curve

    curve, _, left, centre, right, jump = side(plus)
    face = 6.0 * (half_flux + up(half_flux)) - curve
    face = face - upwind_term(down(left), centre, up(right), down(jump), jump)
    _, curve, left, centre, right, jump = side(minus)
    face = face + (upwind_term(up_two(right), up(centre), left, up(jump), jump) - curve)
    return face - down(face)


def open_divergence(half_flux, scaled):
    count = len(half_flux)
    plus = [a + b for a, b in zip(half_flux, scaled)]
    minus = [a - b for a, b in zip(half_flux, scaled)]
    faces = [None] * count

    def side(values):
        steps = [values[i + 1] - values[i] for i in range(count - 1)]
        parts = [None] + [smoothness(steps[i - 1], steps[i]) for i in range(1, count - 1)]
        return parts

    parts = side(plus)
    for i in range(2, count - 3):
        jump_before = parts[i][0] - parts[i - 1][0]
        jump_after = parts[i + 1][0] - parts[i][0]
        faces[i] = 6.0 * (half_flux[i] + half_flux[i + 1]) - parts[i][0] - upwind_term(
            parts[i - 1][1], parts[i][2], parts[i + 1][3], jump_before, jump_after
        )
    parts = side(minus)
    for i in range(3, count - 2):
        jump_before = parts[i][0] - parts[i - 1][0]
        jump_after = parts[i + 1][0] - parts[i][0]
        faces[i - 1] = faces[i - 1] + (
            upwind_term(parts[i + 1][3], parts[i][2], parts[i - 1][1], jump_after, jump_before)
            - parts[i][0]
        )
    return [faces[i] - faces[i - 1] for i in range(3, count - 3)]


def half_velocities(fields):
    density, mom_x, mom_y, mom_z, energy = fields
    over = 0.5 / density
    vel = (mom_x * over, mom_y * over, mom_z * over)
    kinetic = mom_x * vel[0] + mom_y * vel[1] + mom_z * vel[2]
    pressure = (gamma_gas - 1.0) * (energy - kinetic)
    return vel, pressure


def half_flux(fields, field, direction, speed, pressure):
    if field == 0:
        return 0.5 * fields[1 + direction]
    if field == 4:
        return (fields[4] + pressure) * speed
    flux = fields[field] * speed
    return flux + 0.5 * pressure if field == 1 + direction else flux


def side_planes(fields, half_speed):
    vel, pressure = half_velocities(fields)
    for field in range(FIELDS):
        scaled = half_speed * fields[field]
        along_y = periodic_divergence(
            half_flux(fields, field, 1, vel[1], pressure), scaled, y_up, y_up_two, y_down
        )
        flux = half_flux(fields, field, 2, vel[2], pressure)
        for first in range(0, ROWS, 8):
            rows = slice(first, first + 8)
            along_z = periodic_divergence(flux[rows], scaled[rows], z_up, z_up_two, z_down)
            yield field, rows, along_y[rows] + along_z


def plane_kernel(state, speed, out):
    half_speed = 0.5 * speed[0:1, :]

    def one_plane(plane, carry):
        fields = [state[f, plane] for f in range(FIELDS)]
        for field, rows, total in side_planes(fields, half_speed):
            out[field, plane, rows, :] = total
        return carry

    lax.fori_loop(0, state.shape[1], one_plane, 0)


def along_planes(state, speed):
    return pl.pallas_call(
        plane_kernel,
        out_shape=jax.ShapeDtypeStruct(state.shape, jnp.float32),
        in_specs=[VMEM, VMEM],
        out_specs=VMEM,
        compiler_params=params(),
        cost_estimate=cost(20_000_000, 1_000_000),
        name="planes",
    )(state, speed)


def across(get, half_speed):
    span = range(-3, BLOCK + 3)
    speeds, pressures = [], []
    for plane in span:
        vel, pressure = half_velocities([get(f, plane) for f in range(FIELDS)])
        speeds.append(vel[0])
        pressures.append(pressure)
    for field in range(FIELDS):
        fluxes, scaled = [], []
        for i, plane in enumerate(span):
            if field == 0:
                flux = 0.5 * get(1, plane)
            elif field == 4:
                flux = (get(4, plane) + pressures[i]) * speeds[i]
            else:
                flux = get(field, plane) * speeds[i]
                if field == 1:
                    flux = flux + 0.5 * pressures[i]
            fluxes.append(flux)
            scaled.append(half_speed * get(field, plane))
        yield field, open_divergence(fluxes, scaled)


def first_kernel(state, sides, below, above, speed, middle, low, high, top):
    half_speed = 0.5 * speed[0:1, :]
    factor = (courant / 6.0) / speed[0:1, :]

    def group(j, best):
        rows = pl.ds(pl.multiple_of(j * 8, 8), 8)

        def get(f, plane):
            if plane < 0:
                return below[f, plane + 3, rows, :]
            if plane >= BLOCK:
                return above[f, plane - BLOCK, rows, :]
            return state[f, plane, rows, :]

        for field, along_x in across(get, half_speed):
            for plane in range(BLOCK):
                total = along_x[plane] + sides[field, plane, rows, :]
                value = get(field, plane) - factor * total
                middle[field, plane, rows, :] = value
                if plane < 3:
                    low[field, plane, rows, :] = value
                if plane >= 5:
                    high[field, plane - 5, rows, :] = value
        for plane in range(BLOCK):
            best = jnp.maximum(
                best, wave_speed([middle[f, plane, rows, :] for f in range(FIELDS)])
            )
        return best

    best = lax.fori_loop(0, 4, group, jnp.zeros((8, LANES), jnp.float32))
    top[...] = jnp.full((8, LANES), jnp.max(best), jnp.float32)


def first_stage(*operands):
    whole = jax.ShapeDtypeStruct((FIELDS, BLOCK, ROWS, LANES), jnp.float32)
    halo = jax.ShapeDtypeStruct((FIELDS, 3, ROWS, LANES), jnp.float32)
    return pl.pallas_call(
        first_kernel,
        out_shape=(whole, halo, halo, jax.ShapeDtypeStruct((8, LANES), jnp.float32)),
        in_specs=[VMEM] * len(operands),
        out_specs=(VMEM,) * 4,
        compiler_params=params(),
        cost_estimate=cost(30_000_000, 3_000_000),
        name="first_stage",
    )(*operands)


def second_kernel(start, middle, sides, below, above, first_speed, speed, out):
    half_speed = 0.5 * speed[0:1, :]
    factor = (courant / 12.0) / first_speed[0:1, :]

    def group(j, carry):
        rows = pl.ds(pl.multiple_of(j * 8, 8), 8)
        spread = pl.ds(j, 8, stride=4)

        def get(f, plane):
            if plane < 0:
                return below[f, plane + 3, rows, :]
            if plane >= BLOCK:
                return above[f, plane - BLOCK, rows, :]
            return middle[f, plane, rows, :]

        for field, along_x in across(get, half_speed):
            for plane in range(BLOCK):
                total = along_x[plane] + sides[field, plane, rows, :]
                value = 0.5 * start[field, plane, rows, :] + (
                    0.5 * get(field, plane) - factor * total
                )
                out[field, plane, spread, :] = value
        return carry

    lax.fori_loop(0, 4, group, 0)


def second_stage(*operands):
    return pl.pallas_call(
        second_kernel,
        out_shape=jax.ShapeDtypeStruct((FIELDS, BLOCK, ROWS, LANES), jnp.float32),
        in_specs=[VMEM] * len(operands),
        out_specs=VMEM,
        compiler_params=params(),
        cost_estimate=cost(30_000_000, 3_000_000),
        name="second_stage",
    )(*operands)


def everyone_max(value, axis, size):
    reach = 1
    while reach < size:
        copies = [value]
        for times in range(1, 4):
            turn = reach * times
            if turn < size:
                pairs = [(i, i ^ turn) for i in range(size)]
                copies.append(lax.ppermute(value, axis, pairs))
        value = functools.reduce(jnp.maximum, copies)
        reach *= 4
    return value


def per_device(blocks, owner_list, slot_list):
    size = lax.axis_size("gx")
    own = lax.axis_index("gx")
    per_dev = blocks.shape[0]
    cap = max(2, 2 * per_dev // size)
    up = [(i, (i + 1) % size) for i in range(size)]
    down = [(j, i) for i, j in up]

    parts = pack(tiled_rows(blocks), owner_list, size, cap, per_dev)
    parts, owner_list, slot_list = lax.optimization_barrier((parts, owner_list, slot_list))
    come = lax.all_to_all(parts, "gx", split_axis=0, concat_axis=0, tiled=True)
    table = arrival_spots(owner_list, slot_list, own, per_dev, size, cap)
    state, low, high, speed = unpack(table, come.reshape(-1, LANES), size, cap)
    below = lax.ppermute(high, "gx", up)
    above = lax.ppermute(low, "gx", down)
    sides = along_planes(state, speed)
    middle, low, high, top = first_stage(state, sides, below, above, speed)
    second = everyone_max(top, "gx", size)
    below = lax.ppermute(high, "gx", up)
    above = lax.ppermute(low, "gx", down)
    sides = along_planes(middle, second)
    return second_stage(state, middle, sides, below, above, speed, second)


def solution(mesh):
    return jax.shard_map(
        per_device,
        mesh=mesh,
        in_specs=(P(("runs", "gx"), None, None), P("runs"), P("runs")),
        out_specs=P(None, ("runs", "gx"), None, None),
        check_vma=False,
    )
```

```python
import functools

import jax
import jax.numpy as jnp
from jax import lax
from jax.experimental import pallas as pl
from jax.experimental.pallas import tpu as pltpu
from jax.sharding import PartitionSpec as P

BLOCK = 8
BY = 4
BZ = 16
FIELDS = 5
LANES = 128
ROWS = BY * BLOCK
PAIRS = BLOCK // 2
TILES = PAIRS * FIELDS

gamma_gas = 1.4
courant = 0.25
smooth_epsilon = 1e-06

VMEM = pl.BlockSpec(memory_space=pltpu.VMEM)
SMEM = pl.BlockSpec(memory_space=pltpu.SMEM)


def params(mebibytes=40):
    return pltpu.CompilerParams(vmem_limit_bytes=mebibytes * 1024 * 1024)


def cost(flops, size):
    return pl.CostEstimate(flops=flops, bytes_accessed=size, transcendentals=0)


def wave_speed(fields):
    density, mom_x, mom_y, mom_z, energy = fields
    inverse = 1.0 / density
    vel = (mom_x * inverse, mom_y * inverse, mom_z * inverse)
    kinetic = 0.5 * (mom_x * vel[0] + mom_y * vel[1] + mom_z * vel[2])
    pressure = (gamma_gas - 1.0) * (energy - kinetic)
    sound = jnp.sqrt(gamma_gas * pressure * inverse)
    fastest = jnp.maximum(jnp.maximum(jnp.abs(vel[0]), jnp.abs(vel[1])), jnp.abs(vel[2]))
    return fastest + sound


def tiled_rows(blocks):
    count = blocks.shape[0] // 8
    groups = blocks.reshape(count, 8, FIELDS, PAIRS, LANES).transpose(2, 0, 3, 1, 4)
    return groups.reshape(FIELDS * count * PAIRS * 8, LANES)


def pack_kernel(
    size, cap, per_dev, owner_hbm, rows_hbm, out_hbm, owner, rows, out, top, count, member, sems
):
    own = lax.axis_index("gx")
    fetch_owner = pltpu.make_async_copy(owner_hbm, owner, sems.at[0])
    fetch_rows = pltpu.make_async_copy(rows_hbm, rows, sems.at[1])
    fetch_owner.start()
    fetch_rows.start()

    def clear(dest, carry):
        count[dest] = 0
        return carry

    lax.fori_loop(0, size, clear, 0, unroll=8)
    fetch_owner.wait()

    def note(block, carry):
        dest = owner[own * per_dev + block]
        rank = count[dest]
        count[dest] = rank + 1
        member[dest * cap + rank] = lax.div(block, 8) * (PAIRS * 8) + lax.rem(block, 8)
        return carry

    lax.fori_loop(0, per_dev, note, 0, unroll=8)
    fetch_rows.wait()
    tiles = TILES * cap

    def message(dest, carry):
        @pl.when(count[dest] > 0)
        def _():
            for rank in range(cap):
                first = member[dest * cap + rank]
                for pair in range(PAIRS):
                    source = pl.ds(first + pair * 8, FIELDS, stride=per_dev * PAIRS)
                    to = dest * tiles + pair * (FIELDS * cap) + rank
                    out[pl.ds(to, FIELDS, stride=cap), :] = rows[source, :]
            part = out.at[pl.ds(pl.multiple_of(dest * tiles, tiles), tiles)]
            pltpu.make_async_copy(part, out_hbm.at[dest, pl.ds(0, tiles), 0], sems.at[2]).start()

        return carry

    lax.fori_loop(0, size, message, 0)
    best = jnp.zeros((8, LANES), jnp.float32)
    step = per_dev * PAIRS
    for first in range(0, step, 8):
        fields = [rows[f * step + first : f * step + first + 8, :] for f in range(FIELDS)]
        best = jnp.maximum(best, wave_speed(fields))
    top[...] = jnp.full(top.shape, jnp.max(best), jnp.float32)
    for dest in range(size):
        pltpu.make_async_copy(
            top.at[pl.ds(dest, 1)], out_hbm.at[dest, tiles], sems.at[3]
        ).start()
    half = out.at[pl.ds(0, per_dev * TILES)]
    pltpu.make_async_copy(half, half, sems.at[2]).wait()
    pltpu.make_async_copy(top, top, sems.at[3]).wait()


def pack(rows, owner_list, size, cap, per_dev):
    return pl.pallas_call(
        functools.partial(pack_kernel, size, cap, per_dev),
        out_shape=jax.ShapeDtypeStruct((size, TILES * cap + 1, 1, LANES), jnp.float32),
        in_specs=[pl.BlockSpec(memory_space=pltpu.HBM)] * 2,
        out_specs=pl.BlockSpec(memory_space=pltpu.HBM),
        scratch_shapes=[
            pltpu.SMEM(owner_list.shape, jnp.int32),
            pltpu.VMEM(rows.shape, jnp.float32),
            pltpu.VMEM((size * TILES * cap, LANES), jnp.float32),
            pltpu.VMEM((size, LANES), jnp.float32),
            pltpu.SMEM((size,), jnp.int32),
            pltpu.SMEM((size * cap,), jnp.int32),
            pltpu.SemaphoreType.DMA((4,)),
        ],
        compiler_params=params(62),
        cost_estimate=cost(1_000_000, 3_000_000),
        name="pack",
    )(owner_list, rows)


def arrival_spots(owner_list, slot_list, own, per_dev, size, cap):
    owners = owner_list.reshape(size, per_dev)
    slots = slot_list.reshape(size, per_dev)
    mine = owners == own
    spot = jnp.arange(per_dev, dtype=jnp.int32)
    earlier = spot[None, :] < spot[:, None]
    rank = jnp.sum((mine[:, None, :] & earlier[None]).astype(jnp.int32), axis=2)
    row = jnp.arange(size, dtype=jnp.int32)[:, None] * cap + rank
    key = jnp.where(mine, slots, -1)
    hit = key.reshape(1, -1) == spot[:, None]
    return jnp.max(jnp.where(hit, row.reshape(1, -1), 0), axis=1)


def exchanged_bits(rows, group):
    rows = list(rows)
    for bit in range(4):
        step = 1 << bit
        low = (group & step) == 0
        for index in range(16):
            if index & step:
                continue
            first, second = rows[index], rows[index | step]
            rows[index] = jnp.where(low, first, pltpu.roll(second, 8 * step, 1))
            rows[index | step] = jnp.where(low, pltpu.roll(first, LANES - 8 * step, 1), second)
    return rows


def unpack_kernel(size, cap, table, come, state, low_halo, high_halo, speed, scratch):
    message = TILES * cap + 1
    best = come[message - 1 : message, :]
    for source in range(1, size):
        best = jnp.maximum(best, come[(source + 1) * message - 1 : (source + 1) * message, :])
    speed[...] = jnp.broadcast_to(best, speed.shape)
    for slot in range(BY * BZ):
        p, q = divmod(slot, BZ)
        where = table[slot]
        source = lax.div(where, cap)
        rank = lax.rem(where, cap)
        for pair in range(PAIRS):
            couple, h = divmod(pair, 2)
            base = source * message + rank + pair * (FIELDS * cap)
            value = come[pl.ds(base, FIELDS, stride=cap), :]
            row = (couple * BZ + q) * 8 + 2 * p + h
            scratch[pl.ds(row, FIELDS, stride=PAIRS // 2 * BZ * 8), :] = value
    group = lax.broadcasted_iota(jnp.int32, (8, LANES), 1) // BLOCK
    even = lax.broadcasted_iota(jnp.int32, (8, LANES), 0) % 2 == 0

    for f in range(FIELDS):
        for couple in range(PAIRS // 2):
            first = (f * (PAIRS // 2) + couple) * BZ * 8
            rows = [scratch[first + q * 8 : first + q * 8 + 8, :] for q in range(BZ)]
            moved = exchanged_bits(rows, group)
            for second in range(2):
                for j in range(4):
                    lower = moved[second * BLOCK + j]
                    upper = moved[second * BLOCK + j + 4]
                    planes = (
                        jnp.where(even, lower, pltpu.roll(upper, 1, 0)),
                        jnp.where(even, pltpu.roll(lower, 7, 0), upper),
                    )
                    rows = slice(j * 8, j * 8 + 8)
                    for h in range(2):
                        plane = 4 * couple + 2 * h + second
                        state[f, plane, rows, :] = planes[h]
                        if plane < 3:
                            low_halo[f, plane, rows, :] = planes[h]
                        if plane >= 5:
                            high_halo[f, plane - 5, rows, :] = planes[h]


def unpack(table, come, size, cap):
    halo = jax.ShapeDtypeStruct((FIELDS, 3, ROWS, LANES), jnp.float32)
    return pl.pallas_call(
        functools.partial(unpack_kernel, size, cap),
        out_shape=(
            jax.ShapeDtypeStruct((FIELDS, BLOCK, ROWS, LANES), jnp.float32),
            halo,
            halo,
            jax.ShapeDtypeStruct((8, LANES), jnp.float32),
        ),
        in_specs=[SMEM, VMEM],
        out_specs=(VMEM,) * 4,
        scratch_shapes=[pltpu.VMEM((FIELDS * (PAIRS // 2) * BZ * 8, LANES), jnp.float32)],
        compiler_params=params(),
        cost_estimate=cost(5_000_000, 2_000_000),
        name="unpack",
    )(table, come)


def y_up(x):
    return jnp.concatenate([x[8:], pltpu.roll(x[:8], 7, 0)], axis=0)


def y_down(x):
    return jnp.concatenate([pltpu.roll(x[24:], 1, 0), x[:24]], axis=0)


def y_up_two(x):
    return jnp.concatenate([x[16:], pltpu.roll(x[:8], 7, 0), pltpu.roll(x[8:16], 7, 0)], axis=0)


def z_up(x):
    return pltpu.roll(x, LANES - 1, 1)


def z_up_two(x):
    return pltpu.roll(x, LANES - 2, 1)


def z_down(x):
    return pltpu.roll(x, 1, 1)


def inverse(x):
    return 1.0 / x


def smoothness(before, after):
    curve = after - before
    middle = 0.5 * (after + before)
    base = curve * curve * (13.0 / 12.0) + smooth_epsilon
    plus = middle + curve
    minus = middle - curve
    left = inverse(base + plus * plus)
    centre = inverse(base + middle * middle)
    right = inverse(base + minus * minus)
    return curve, left * left, centre * centre, right * right


def upwind_term(left, centre, right, jump_before, jump_after):
    right = 3.0 * right
    top = left * (jump_before + jump_before) + right * jump_after
    return top * inverse(left + 6.0 * centre + right)


def periodic_divergence(half_flux, scaled, up, up_two, down):
    plus = half_flux + scaled
    minus = half_flux - scaled

    def side(values):
        after = up(values) - values
        curve, left, centre, right = smoothness(down(after), after)
        above = up(curve)
        return curve, above, left, centre, right, above - curve

    curve, _, left, centre, right, jump = side(plus)
    face = 6.0 * (half_flux + up(half_flux)) - curve
    face = face - upwind_term(down(left), centre, up(right), down(jump), jump)
    _, curve, left, centre, right, jump = side(minus)
    face = face + (upwind_term(up_two(right), up(centre), left, up(jump), jump) - curve)
    return face - down(face)


def open_divergence(half_flux, scaled):
    count = len(half_flux)
    plus = [a + b for a, b in zip(half_flux, scaled)]
    minus = [a - b for a, b in zip(half_flux, scaled)]
    faces = [None] * count

    def side(values):
        steps = [values[i + 1] - values[i] for i in range(count - 1)]
        parts = [None] + [smoothness(steps[i - 1], steps[i]) for i in range(1, count - 1)]
        return parts

    parts = side(plus)
    for i in range(2, count - 3):
        jump_before = parts[i][0] - parts[i - 1][0]
        jump_after = parts[i + 1][0] - parts[i][0]
        faces[i] = 6.0 * (half_flux[i] + half_flux[i + 1]) - parts[i][0] - upwind_term(
            parts[i - 1][1], parts[i][2], parts[i + 1][3], jump_before, jump_after
        )
    parts = side(minus)
    for i in range(3, count - 2):
        jump_before = parts[i][0] - parts[i - 1][0]
        jump_after = parts[i + 1][0] - parts[i][0]
        faces[i - 1] = faces[i - 1] + (
            upwind_term(parts[i + 1][3], parts[i][2], parts[i - 1][1], jump_after, jump_before)
            - parts[i][0]
        )
    return [faces[i] - faces[i - 1] for i in range(3, count - 3)]


def half_velocities(fields):
    density, mom_x, mom_y, mom_z, energy = fields
    over = 0.5 / density
    vel = (mom_x * over, mom_y * over, mom_z * over)
    kinetic = mom_x * vel[0] + mom_y * vel[1] + mom_z * vel[2]
    pressure = (gamma_gas - 1.0) * (energy - kinetic)
    return vel, pressure


def half_flux(fields, field, direction, speed, pressure):
    if field == 0:
        return 0.5 * fields[1 + direction]
    if field == 4:
        return (fields[4] + pressure) * speed
    flux = fields[field] * speed
    return flux + 0.5 * pressure if field == 1 + direction else flux


def side_planes(fields, half_speed):
    vel, pressure = half_velocities(fields)
    for field in range(FIELDS):
        scaled = half_speed * fields[field]
        along_y = periodic_divergence(
            half_flux(fields, field, 1, vel[1], pressure), scaled, y_up, y_up_two, y_down
        )
        flux = half_flux(fields, field, 2, vel[2], pressure)
        for first in range(0, ROWS, 8):
            rows = slice(first, first + 8)
            along_z = periodic_divergence(flux[rows], scaled[rows], z_up, z_up_two, z_down)
            yield field, rows, along_y[rows] + along_z


def plane_kernel(state, speed, out):
    half_speed = 0.5 * speed[0:1, :]

    def one_plane(plane, carry):
        fields = [state[f, plane] for f in range(FIELDS)]
        for field, rows, total in side_planes(fields, half_speed):
            out[field, plane, rows, :] = total
        return carry

    lax.fori_loop(0, state.shape[1], one_plane, 0)


def along_planes(state, speed):
    return pl.pallas_call(
        plane_kernel,
        out_shape=jax.ShapeDtypeStruct(state.shape, jnp.float32),
        in_specs=[VMEM, VMEM],
        out_specs=VMEM,
        compiler_params=params(),
        cost_estimate=cost(20_000_000, 1_000_000),
        name="planes",
    )(state, speed)


def across(get, half_speed):
    span = range(-3, BLOCK + 3)
    speeds, pressures = [], []
    for plane in span:
        vel, pressure = half_velocities([get(f, plane) for f in range(FIELDS)])
        speeds.append(vel[0])
        pressures.append(pressure)
    for field in range(FIELDS):
        fluxes, scaled = [], []
        for i, plane in enumerate(span):
            if field == 0:
                flux = 0.5 * get(1, plane)
            elif field == 4:
                flux = (get(4, plane) + pressures[i]) * speeds[i]
            else:
                flux = get(field, plane) * speeds[i]
                if field == 1:
                    flux = flux + 0.5 * pressures[i]
            fluxes.append(flux)
            scaled.append(half_speed * get(field, plane))
        yield field, open_divergence(fluxes, scaled)


def first_kernel(state, sides, below, above, speed, middle, low, high, top):
    half_speed = 0.5 * speed[0:1, :]
    factor = (courant / 6.0) / speed[0:1, :]

    def group(j, best):
        rows = pl.ds(pl.multiple_of(j * 8, 8), 8)

        def get(f, plane):
            if plane < 0:
                return below[f, plane + 3, rows, :]
            if plane >= BLOCK:
                return above[f, plane - BLOCK, rows, :]
            return state[f, plane, rows, :]

        for field, along_x in across(get, half_speed):
            for plane in range(BLOCK):
                total = along_x[plane] + sides[field, plane, rows, :]
                value = get(field, plane) - factor * total
                middle[field, plane, rows, :] = value
                if plane < 3:
                    low[field, plane, rows, :] = value
                if plane >= 5:
                    high[field, plane - 5, rows, :] = value
        for plane in range(BLOCK):
            best = jnp.maximum(
                best, wave_speed([middle[f, plane, rows, :] for f in range(FIELDS)])
            )
        return best

    best = lax.fori_loop(0, 4, group, jnp.zeros((8, LANES), jnp.float32))
    top[...] = jnp.full((8, LANES), jnp.max(best), jnp.float32)


def first_stage(*operands):
    whole = jax.ShapeDtypeStruct((FIELDS, BLOCK, ROWS, LANES), jnp.float32)
    halo = jax.ShapeDtypeStruct((FIELDS, 3, ROWS, LANES), jnp.float32)
    return pl.pallas_call(
        first_kernel,
        out_shape=(whole, halo, halo, jax.ShapeDtypeStruct((8, LANES), jnp.float32)),
        in_specs=[VMEM] * len(operands),
        out_specs=(VMEM,) * 4,
        compiler_params=params(),
        cost_estimate=cost(30_000_000, 3_000_000),
        name="first_stage",
    )(*operands)


def second_kernel(start, middle, sides, below, above, first_speed, speed, out):
    half_speed = 0.5 * speed[0:1, :]
    factor = (courant / 12.0) / first_speed[0:1, :]

    def group(j, carry):
        rows = pl.ds(pl.multiple_of(j * 8, 8), 8)
        spread = pl.ds(j, 8, stride=4)

        def get(f, plane):
            if plane < 0:
                return below[f, plane + 3, rows, :]
            if plane >= BLOCK:
                return above[f, plane - BLOCK, rows, :]
            return middle[f, plane, rows, :]

        for field, along_x in across(get, half_speed):
            for plane in range(BLOCK):
                total = along_x[plane] + sides[field, plane, rows, :]
                value = 0.5 * start[field, plane, rows, :] + (
                    0.5 * get(field, plane) - factor * total
                )
                out[field, plane, spread, :] = value
        return carry

    lax.fori_loop(0, 4, group, 0)


def second_stage(*operands):
    return pl.pallas_call(
        second_kernel,
        out_shape=jax.ShapeDtypeStruct((FIELDS, BLOCK, ROWS, LANES), jnp.float32),
        in_specs=[VMEM] * len(operands),
        out_specs=VMEM,
        compiler_params=params(),
        cost_estimate=cost(30_000_000, 3_000_000),
        name="second_stage",
    )(*operands)


def partners_values(value, axis, size, reach):
    turns = [reach * times for times in range(1, 4) if reach * times < size]
    return [lax.ppermute(value, axis, [(i, i ^ turn) for i in range(size)]) for turn in turns]


def per_device(blocks, owner_list, slot_list):
    size = lax.axis_size("gx")
    own = lax.axis_index("gx")
    per_dev = blocks.shape[0]
    cap = max(2, 2 * per_dev // size)
    up = [(i, (i + 1) % size) for i in range(size)]
    down = [(j, i) for i, j in up]

    parts = pack(tiled_rows(blocks), owner_list, size, cap, per_dev)
    parts, owner_list, slot_list = lax.optimization_barrier((parts, owner_list, slot_list))
    come = lax.all_to_all(parts, "gx", split_axis=0, concat_axis=0, tiled=True)
    table = arrival_spots(owner_list, slot_list, own, per_dev, size, cap)
    state, low, high, speed = unpack(table, come.reshape(-1, LANES), size, cap)
    below = lax.ppermute(high, "gx", up)
    above = lax.ppermute(low, "gx", down)
    sides = along_planes(state, speed)
    middle, low, high, top = first_stage(state, sides, below, above, speed)
    second, reach = top, 1
    while reach < size:
        come = partners_values(second, "gx", size, reach)
        if reach * 4 >= size:
            low, high, come[0] = lax.optimization_barrier((low, high, come[0]))
        second = functools.reduce(jnp.maximum, come, second)
        reach *= 4
    below = lax.ppermute(high, "gx", up)
    above = lax.ppermute(low, "gx", down)
    sides = along_planes(middle, second)
    return second_stage(state, middle, sides, below, above, speed, second)


def solution(mesh):
    return jax.shard_map(
        per_device,
        mesh=mesh,
        in_specs=(P(("runs", "gx"), None, None), P("runs"), P("runs")),
        out_specs=P(None, ("runs", "gx"), None, None),
        check_vma=False,
    )
```

```python
import functools

import jax
import jax.numpy as jnp
from jax import lax
from jax.experimental import pallas as pl
from jax.experimental.pallas import tpu as pltpu
from jax.sharding import PartitionSpec as P

BLOCK = 8
BY = 4
BZ = 16
FIELDS = 5
LANES = 128
ROWS = BY * BLOCK
PAIRS = BLOCK // 2
TILES = PAIRS * FIELDS

gamma_gas = 1.4
courant = 0.25
smooth_epsilon = 1e-06

VMEM = pl.BlockSpec(memory_space=pltpu.VMEM)
SMEM = pl.BlockSpec(memory_space=pltpu.SMEM)


def params(mebibytes=40):
    return pltpu.CompilerParams(vmem_limit_bytes=mebibytes * 1024 * 1024)


def cost(flops, size):
    return pl.CostEstimate(flops=flops, bytes_accessed=size, transcendentals=0)


def wave_speed(fields):
    density, mom_x, mom_y, mom_z, energy = fields
    inverse = 1.0 / density
    vel = (mom_x * inverse, mom_y * inverse, mom_z * inverse)
    kinetic = 0.5 * (mom_x * vel[0] + mom_y * vel[1] + mom_z * vel[2])
    pressure = (gamma_gas - 1.0) * (energy - kinetic)
    sound = jnp.sqrt(gamma_gas * pressure * inverse)
    fastest = jnp.maximum(jnp.maximum(jnp.abs(vel[0]), jnp.abs(vel[1])), jnp.abs(vel[2]))
    return fastest + sound


def tiled_rows(blocks):
    count = blocks.shape[0] // 8
    groups = blocks.reshape(count, 8, FIELDS, PAIRS, LANES).transpose(2, 0, 3, 1, 4)
    return groups.reshape(FIELDS * count * PAIRS * 8, LANES)


def pack_kernel(
    size, cap, per_dev, owner_hbm, rows_hbm, out_hbm, owner, rows, out, top, count, member, sems
):
    own = lax.axis_index("gx")
    fetch_owner = pltpu.make_async_copy(owner_hbm, owner, sems.at[0])
    fetch_rows = pltpu.make_async_copy(rows_hbm, rows, sems.at[1])
    fetch_owner.start()
    fetch_rows.start()

    def clear(dest, carry):
        count[dest] = 0
        return carry

    lax.fori_loop(0, size, clear, 0, unroll=8)
    fetch_owner.wait()

    def note(block, carry):
        dest = owner[own * per_dev + block]
        rank = count[dest]
        count[dest] = rank + 1
        member[dest * cap + rank] = lax.div(block, 8) * (PAIRS * 8) + lax.rem(block, 8)
        return carry

    lax.fori_loop(0, per_dev, note, 0, unroll=8)
    fetch_rows.wait()
    tiles = TILES * cap

    def message(dest, carry):
        @pl.when(count[dest] > 0)
        def _():
            for rank in range(cap):
                first = member[dest * cap + rank]
                for pair in range(PAIRS):
                    source = pl.ds(first + pair * 8, FIELDS, stride=per_dev * PAIRS)
                    to = dest * tiles + pair * (FIELDS * cap) + rank
                    out[pl.ds(to, FIELDS, stride=cap), :] = rows[source, :]
            part = out.at[pl.ds(pl.multiple_of(dest * tiles, tiles), tiles)]
            pltpu.make_async_copy(part, out_hbm.at[dest, pl.ds(0, tiles), 0], sems.at[2]).start()

        return carry

    lax.fori_loop(0, size, message, 0)
    best = jnp.zeros((8, LANES), jnp.float32)
    step = per_dev * PAIRS
    for first in range(0, step, 8):
        fields = [rows[f * step + first : f * step + first + 8, :] for f in range(FIELDS)]
        best = jnp.maximum(best, wave_speed(fields))
    top[...] = jnp.full(top.shape, jnp.max(best), jnp.float32)
    for dest in range(size):
        pltpu.make_async_copy(
            top.at[pl.ds(dest, 1)], out_hbm.at[dest, tiles], sems.at[3]
        ).start()
    half = out.at[pl.ds(0, per_dev * TILES)]
    pltpu.make_async_copy(half, half, sems.at[2]).wait()
    pltpu.make_async_copy(top, top, sems.at[3]).wait()


def pack(rows, owner_list, size, cap, per_dev):
    return pl.pallas_call(
        functools.partial(pack_kernel, size, cap, per_dev),
        out_shape=jax.ShapeDtypeStruct((size, TILES * cap + 1, 1, LANES), jnp.float32),
        in_specs=[pl.BlockSpec(memory_space=pltpu.HBM)] * 2,
        out_specs=pl.BlockSpec(memory_space=pltpu.HBM),
        scratch_shapes=[
            pltpu.SMEM(owner_list.shape, jnp.int32),
            pltpu.VMEM(rows.shape, jnp.float32),
            pltpu.VMEM((size * TILES * cap, LANES), jnp.float32),
            pltpu.VMEM((size, LANES), jnp.float32),
            pltpu.SMEM((size,), jnp.int32),
            pltpu.SMEM((size * cap,), jnp.int32),
            pltpu.SemaphoreType.DMA((4,)),
        ],
        compiler_params=params(62),
        cost_estimate=cost(1_000_000, 3_000_000),
        name="pack",
    )(owner_list, rows)


def arrival_spots(owner_list, slot_list, own, per_dev, size, cap):
    owners = owner_list.reshape(size, per_dev)
    slots = slot_list.reshape(size, per_dev)
    mine = owners == own
    spot = jnp.arange(per_dev, dtype=jnp.int32)
    earlier = spot[None, :] < spot[:, None]
    rank = jnp.sum((mine[:, None, :] & earlier[None]).astype(jnp.int32), axis=2)
    row = jnp.arange(size, dtype=jnp.int32)[:, None] * cap + rank
    key = jnp.where(mine, slots, -1)
    hit = key.reshape(1, -1) == spot[:, None]
    return jnp.max(jnp.where(hit, row.reshape(1, -1), 0), axis=1)


def exchanged_bits(rows, group):
    rows = list(rows)
    for bit in range(4):
        step = 1 << bit
        low = (group & step) == 0
        for index in range(16):
            if index & step:
                continue
            first, second = rows[index], rows[index | step]
            rows[index] = jnp.where(low, first, pltpu.roll(second, 8 * step, 1))
            rows[index | step] = jnp.where(low, pltpu.roll(first, LANES - 8 * step, 1), second)
    return rows


def unpack_kernel(size, cap, table, come, state, low_halo, high_halo, speed, scratch):
    message = TILES * cap + 1
    best = come[message - 1 : message, :]
    for source in range(1, size):
        best = jnp.maximum(best, come[(source + 1) * message - 1 : (source + 1) * message, :])
    speed[0] = best
    for slot in range(BY * BZ):
        p, q = divmod(slot, BZ)
        where = table[slot]
        source = lax.div(where, cap)
        rank = lax.rem(where, cap)
        for pair in range(PAIRS):
            couple, h = divmod(pair, 2)
            base = source * message + rank + pair * (FIELDS * cap)
            value = come[pl.ds(base, FIELDS, stride=cap), :]
            row = (couple * BZ + q) * 8 + 2 * p + h
            scratch[pl.ds(row, FIELDS, stride=PAIRS // 2 * BZ * 8), :] = value
    group = lax.broadcasted_iota(jnp.int32, (8, LANES), 1) // BLOCK
    even = lax.broadcasted_iota(jnp.int32, (8, LANES), 0) % 2 == 0

    for f in range(FIELDS):
        for couple in range(PAIRS // 2):
            first = (f * (PAIRS // 2) + couple) * BZ * 8
            rows = [scratch[first + q * 8 : first + q * 8 + 8, :] for q in range(BZ)]
            moved = exchanged_bits(rows, group)
            for second in range(2):
                for j in range(4):
                    lower = moved[second * BLOCK + j]
                    upper = moved[second * BLOCK + j + 4]
                    planes = (
                        jnp.where(even, lower, pltpu.roll(upper, 1, 0)),
                        jnp.where(even, pltpu.roll(lower, 7, 0), upper),
                    )
                    rows = slice(j * 8, j * 8 + 8)
                    for h in range(2):
                        plane = 4 * couple + 2 * h + second
                        state[f, plane, rows, :] = planes[h]
                        if plane < 3:
                            low_halo[f, plane, rows, :] = planes[h]
                        if plane >= 5:
                            high_halo[f, plane - 5, rows, :] = planes[h]


def unpack(table, come, size, cap):
    halo = jax.ShapeDtypeStruct((FIELDS, 3, ROWS, LANES), jnp.float32)
    return pl.pallas_call(
        functools.partial(unpack_kernel, size, cap),
        out_shape=(
            jax.ShapeDtypeStruct((FIELDS, BLOCK, ROWS, LANES), jnp.float32),
            halo,
            halo,
            jax.ShapeDtypeStruct((1, 1, LANES), jnp.float32),
        ),
        in_specs=[SMEM, VMEM],
        out_specs=(VMEM,) * 4,
        scratch_shapes=[pltpu.VMEM((FIELDS * (PAIRS // 2) * BZ * 8, LANES), jnp.float32)],
        compiler_params=params(),
        cost_estimate=cost(5_000_000, 2_000_000),
        name="unpack",
    )(table, come)


def y_up(x):
    return jnp.concatenate([x[8:], pltpu.roll(x[:8], 7, 0)], axis=0)


def y_down(x):
    return jnp.concatenate([pltpu.roll(x[24:], 1, 0), x[:24]], axis=0)


def y_up_two(x):
    return jnp.concatenate([x[16:], pltpu.roll(x[:8], 7, 0), pltpu.roll(x[8:16], 7, 0)], axis=0)


def z_up(x):
    return pltpu.roll(x, LANES - 1, 1)


def z_up_two(x):
    return pltpu.roll(x, LANES - 2, 1)


def z_down(x):
    return pltpu.roll(x, 1, 1)


def inverse(x):
    return 1.0 / x


def smoothness(before, after):
    curve = after - before
    middle = 0.5 * (after + before)
    base = curve * curve * (13.0 / 12.0) + smooth_epsilon
    plus = middle + curve
    minus = middle - curve
    left = inverse(base + plus * plus)
    centre = inverse(base + middle * middle)
    right = inverse(base + minus * minus)
    return curve, left * left, centre * centre, right * right


def upwind_term(left, centre, right, jump_before, jump_after):
    right = 3.0 * right
    top = left * (jump_before + jump_before) + right * jump_after
    return top * inverse(left + 6.0 * centre + right)


def periodic_divergence(half_flux, scaled, up, up_two, down):
    plus = half_flux + scaled
    minus = half_flux - scaled

    def side(values):
        after = up(values) - values
        curve, left, centre, right = smoothness(down(after), after)
        above = up(curve)
        return curve, above, left, centre, right, above - curve

    curve, _, left, centre, right, jump = side(plus)
    face = 6.0 * (half_flux + up(half_flux)) - curve
    face = face - upwind_term(down(left), centre, up(right), down(jump), jump)
    _, curve, left, centre, right, jump = side(minus)
    face = face + (upwind_term(up_two(right), up(centre), left, up(jump), jump) - curve)
    return face - down(face)


def open_divergence(half_flux, scaled):
    count = len(half_flux)
    plus = [a + b for a, b in zip(half_flux, scaled)]
    minus = [a - b for a, b in zip(half_flux, scaled)]
    faces = [None] * count

    def side(values):
        steps = [values[i + 1] - values[i] for i in range(count - 1)]
        parts = [None] + [smoothness(steps[i - 1], steps[i]) for i in range(1, count - 1)]
        return parts

    parts = side(plus)
    for i in range(2, count - 3):
        jump_before = parts[i][0] - parts[i - 1][0]
        jump_after = parts[i + 1][0] - parts[i][0]
        faces[i] = 6.0 * (half_flux[i] + half_flux[i + 1]) - parts[i][0] - upwind_term(
            parts[i - 1][1], parts[i][2], parts[i + 1][3], jump_before, jump_after
        )
    parts = side(minus)
    for i in range(3, count - 2):
        jump_before = parts[i][0] - parts[i - 1][0]
        jump_after = parts[i + 1][0] - parts[i][0]
        faces[i - 1] = faces[i - 1] + (
            upwind_term(parts[i + 1][3], parts[i][2], parts[i - 1][1], jump_after, jump_before)
            - parts[i][0]
        )
    return [faces[i] - faces[i - 1] for i in range(3, count - 3)]


def half_velocities(fields):
    density, mom_x, mom_y, mom_z, energy = fields
    over = 0.5 / density
    vel = (mom_x * over, mom_y * over, mom_z * over)
    kinetic = mom_x * vel[0] + mom_y * vel[1] + mom_z * vel[2]
    pressure = (gamma_gas - 1.0) * (energy - kinetic)
    return vel, pressure


def half_flux(fields, field, direction, speed, pressure):
    if field == 0:
        return 0.5 * fields[1 + direction]
    if field == 4:
        return (fields[4] + pressure) * speed
    flux = fields[field] * speed
    return flux + 0.5 * pressure if field == 1 + direction else flux


def side_planes(fields, half_speed):
    vel, pressure = half_velocities(fields)
    for field in range(FIELDS):
        scaled = half_speed * fields[field]
        along_y = periodic_divergence(
            half_flux(fields, field, 1, vel[1], pressure), scaled, y_up, y_up_two, y_down
        )
        flux = half_flux(fields, field, 2, vel[2], pressure)
        for first in range(0, ROWS, 8):
            rows = slice(first, first + 8)
            along_z = periodic_divergence(flux[rows], scaled[rows], z_up, z_up_two, z_down)
            yield field, rows, along_y[rows] + along_z


def fastest_of(speeds):
    best = speeds[0]
    for source in range(1, speeds.shape[0]):
        best = jnp.maximum(best, speeds[source])
    return best


def plane_kernel(state, speeds, out):
    half_speed = 0.5 * fastest_of(speeds)

    def one_plane(plane, carry):
        fields = [state[f, plane] for f in range(FIELDS)]
        for field, rows, total in side_planes(fields, half_speed):
            out[field, plane, rows, :] = total
        return carry

    lax.fori_loop(0, state.shape[1], one_plane, 0)


def along_planes(state, speed):
    return pl.pallas_call(
        plane_kernel,
        out_shape=jax.ShapeDtypeStruct(state.shape, jnp.float32),
        in_specs=[VMEM, VMEM],
        out_specs=VMEM,
        compiler_params=params(),
        cost_estimate=cost(20_000_000, 1_000_000),
        name="planes",
    )(state, speed)


def across(get, half_speed):
    span = range(-3, BLOCK + 3)
    speeds, pressures = [], []
    for plane in span:
        vel, pressure = half_velocities([get(f, plane) for f in range(FIELDS)])
        speeds.append(vel[0])
        pressures.append(pressure)
    for field in range(FIELDS):
        fluxes, scaled = [], []
        for i, plane in enumerate(span):
            if field == 0:
                flux = 0.5 * get(1, plane)
            elif field == 4:
                flux = (get(4, plane) + pressures[i]) * speeds[i]
            else:
                flux = get(field, plane) * speeds[i]
                if field == 1:
                    flux = flux + 0.5 * pressures[i]
            fluxes.append(flux)
            scaled.append(half_speed * get(field, plane))
        yield field, open_divergence(fluxes, scaled)


def first_kernel(state, sides, below, above, speed, middle, low, high, top):
    half_speed = 0.5 * speed[0]
    factor = (courant / 6.0) / speed[0]

    def group(j, best):
        rows = pl.ds(pl.multiple_of(j * 8, 8), 8)

        def get(f, plane):
            if plane < 0:
                return below[f, plane + 3, rows, :]
            if plane >= BLOCK:
                return above[f, plane - BLOCK, rows, :]
            return state[f, plane, rows, :]

        for field, along_x in across(get, half_speed):
            for plane in range(BLOCK):
                total = along_x[plane] + sides[field, plane, rows, :]
                value = get(field, plane) - factor * total
                middle[field, plane, rows, :] = value
                if plane < 3:
                    low[field, plane, rows, :] = value
                if plane >= 5:
                    high[field, plane - 5, rows, :] = value
        for plane in range(BLOCK):
            best = jnp.maximum(
                best, wave_speed([middle[f, plane, rows, :] for f in range(FIELDS)])
            )
        return best

    best = lax.fori_loop(0, 4, group, jnp.zeros((8, LANES), jnp.float32))
    most = jnp.full((1, LANES), jnp.max(best), jnp.float32)
    for dest in range(top.shape[0]):
        top[dest] = most


def first_stage(size, *operands):
    whole = jax.ShapeDtypeStruct((FIELDS, BLOCK, ROWS, LANES), jnp.float32)
    halo = jax.ShapeDtypeStruct((FIELDS, 3, ROWS, LANES), jnp.float32)
    return pl.pallas_call(
        first_kernel,
        out_shape=(whole, halo, halo, jax.ShapeDtypeStruct((size, 1, LANES), jnp.float32)),
        in_specs=[VMEM] * len(operands),
        out_specs=(VMEM,) * 4,
        compiler_params=params(),
        cost_estimate=cost(30_000_000, 3_000_000),
        name="first_stage",
    )(*operands)


def second_kernel(start, middle, sides, below, above, first_speed, speeds, out):
    half_speed = 0.5 * fastest_of(speeds)
    factor = (courant / 12.0) / first_speed[0]

    def group(j, carry):
        rows = pl.ds(pl.multiple_of(j * 8, 8), 8)
        spread = pl.ds(j, 8, stride=4)

        def get(f, plane):
            if plane < 0:
                return below[f, plane + 3, rows, :]
            if plane >= BLOCK:
                return above[f, plane - BLOCK, rows, :]
            return middle[f, plane, rows, :]

        for field, along_x in across(get, half_speed):
            for plane in range(BLOCK):
                total = along_x[plane] + sides[field, plane, rows, :]
                value = 0.5 * start[field, plane, rows, :] + (
                    0.5 * get(field, plane) - factor * total
                )
                out[field, plane, spread, :] = value
        return carry

    lax.fori_loop(0, 4, group, 0)


def second_stage(*operands):
    return pl.pallas_call(
        second_kernel,
        out_shape=jax.ShapeDtypeStruct((FIELDS, BLOCK, ROWS, LANES), jnp.float32),
        in_specs=[VMEM] * len(operands),
        out_specs=VMEM,
        compiler_params=params(),
        cost_estimate=cost(30_000_000, 3_000_000),
        name="second_stage",
    )(*operands)


def per_device(blocks, owner_list, slot_list):
    size = lax.axis_size("gx")
    own = lax.axis_index("gx")
    per_dev = blocks.shape[0]
    cap = max(2, 2 * per_dev // size)
    up = [(i, (i + 1) % size) for i in range(size)]
    down = [(j, i) for i, j in up]

    parts = pack(tiled_rows(blocks), owner_list, size, cap, per_dev)
    parts, owner_list, slot_list = lax.optimization_barrier((parts, owner_list, slot_list))
    come = lax.all_to_all(parts, "gx", split_axis=0, concat_axis=0, tiled=True)
    table = arrival_spots(owner_list, slot_list, own, per_dev, size, cap)
    state, low, high, speed = unpack(table, come.reshape(-1, LANES), size, cap)
    below = lax.ppermute(high, "gx", up)
    above = lax.ppermute(low, "gx", down)
    sides = along_planes(state, speed)
    middle, low, high, top = first_stage(size, state, sides, below, above, speed)
    second = lax.all_to_all(top, "gx", split_axis=0, concat_axis=0, tiled=True)
    low, high, second = lax.optimization_barrier((low, high, second))
    below = lax.ppermute(high, "gx", up)
    above = lax.ppermute(low, "gx", down)
    sides = along_planes(middle, second)
    return second_stage(state, middle, sides, below, above, speed, second)


def solution(mesh):
    return jax.shard_map(
        per_device,
        mesh=mesh,
        in_specs=(P(("runs", "gx"), None, None), P("runs"), P("runs")),
        out_specs=P(None, ("runs", "gx"), None, None),
        check_vma=False,
    )
```

```python
import functools

import jax
import jax.numpy as jnp
from jax import lax
from jax.experimental import pallas as pl
from jax.experimental.pallas import tpu as pltpu
from jax.sharding import PartitionSpec as P

BLOCK = 8
BY = 4
BZ = 16
FIELDS = 5
LANES = 128
ROWS = BY * BLOCK
PAIRS = BLOCK // 2
TILES = PAIRS * FIELDS

gamma_gas = 1.4
courant = 0.25
smooth_epsilon = 1e-06

VMEM = pl.BlockSpec(memory_space=pltpu.VMEM)
SMEM = pl.BlockSpec(memory_space=pltpu.SMEM)


def params(mebibytes=40):
    return pltpu.CompilerParams(vmem_limit_bytes=mebibytes * 1024 * 1024)


def cost(flops, size):
    return pl.CostEstimate(flops=flops, bytes_accessed=size, transcendentals=0)


def wave_speed(fields):
    density, mom_x, mom_y, mom_z, energy = fields
    inverse = 1.0 / density
    vel = (mom_x * inverse, mom_y * inverse, mom_z * inverse)
    kinetic = 0.5 * (mom_x * vel[0] + mom_y * vel[1] + mom_z * vel[2])
    pressure = (gamma_gas - 1.0) * (energy - kinetic)
    sound = jnp.sqrt(gamma_gas * pressure * inverse)
    fastest = jnp.maximum(jnp.maximum(jnp.abs(vel[0]), jnp.abs(vel[1])), jnp.abs(vel[2]))
    return fastest + sound


def tiled_rows(blocks):
    count = blocks.shape[0] // 8
    groups = blocks.reshape(count, 8, FIELDS, PAIRS, LANES).transpose(2, 0, 3, 1, 4)
    return groups.reshape(FIELDS * count * PAIRS * 8, LANES)


def pack_kernel(
    size, cap, per_dev, owner_hbm, rows_hbm, out_hbm, owner, rows, out, top, count, member, sems
):
    own = lax.axis_index("gx")
    fetch_owner = pltpu.make_async_copy(owner_hbm, owner, sems.at[0])
    fetch_rows = pltpu.make_async_copy(rows_hbm, rows, sems.at[1])
    fetch_owner.start()
    fetch_rows.start()

    def clear(dest, carry):
        count[dest] = 0
        return carry

    lax.fori_loop(0, size, clear, 0, unroll=8)
    fetch_owner.wait()

    def note(block, carry):
        dest = owner[own * per_dev + block]
        rank = count[dest]
        count[dest] = rank + 1
        member[dest * cap + rank] = lax.div(block, 8) * (PAIRS * 8) + lax.rem(block, 8)
        return carry

    lax.fori_loop(0, per_dev, note, 0, unroll=8)
    fetch_rows.wait()
    tiles = TILES * cap

    def message(dest, carry):
        @pl.when(count[dest] > 0)
        def _():
            for rank in range(cap):
                first = member[dest * cap + rank]
                for pair in range(PAIRS):
                    source = pl.ds(first + pair * 8, FIELDS, stride=per_dev * PAIRS)
                    to = dest * tiles + pair * (FIELDS * cap) + rank
                    out[pl.ds(to, FIELDS, stride=cap), :] = rows[source, :]
            part = out.at[pl.ds(pl.multiple_of(dest * tiles, tiles), tiles)]
            pltpu.make_async_copy(part, out_hbm.at[dest, pl.ds(0, tiles), 0], sems.at[2]).start()

        return carry

    lax.fori_loop(0, size, message, 0)
    best = jnp.zeros((8, LANES), jnp.float32)
    step = per_dev * PAIRS
    for first in range(0, step, 8):
        fields = [rows[f * step + first : f * step + first + 8, :] for f in range(FIELDS)]
        best = jnp.maximum(best, wave_speed(fields))
    top[...] = jnp.full(top.shape, jnp.max(best), jnp.float32)
    for dest in range(size):
        pltpu.make_async_copy(
            top.at[pl.ds(dest, 1)], out_hbm.at[dest, tiles], sems.at[3]
        ).start()
    half = out.at[pl.ds(0, per_dev * TILES)]
    pltpu.make_async_copy(half, half, sems.at[2]).wait()
    pltpu.make_async_copy(top, top, sems.at[3]).wait()


def pack(rows, owner_list, size, cap, per_dev):
    return pl.pallas_call(
        functools.partial(pack_kernel, size, cap, per_dev),
        out_shape=jax.ShapeDtypeStruct((size, TILES * cap + 1, 1, LANES), jnp.float32),
        in_specs=[pl.BlockSpec(memory_space=pltpu.HBM)] * 2,
        out_specs=pl.BlockSpec(memory_space=pltpu.HBM),
        scratch_shapes=[
            pltpu.SMEM(owner_list.shape, jnp.int32),
            pltpu.VMEM(rows.shape, jnp.float32),
            pltpu.VMEM((size * TILES * cap, LANES), jnp.float32),
            pltpu.VMEM((size, LANES), jnp.float32),
            pltpu.SMEM((size,), jnp.int32),
            pltpu.SMEM((size * cap,), jnp.int32),
            pltpu.SemaphoreType.DMA((4,)),
        ],
        compiler_params=params(62),
        cost_estimate=cost(1_000_000, 3_000_000),
        name="pack",
    )(owner_list, rows)


def arrival_spots(owner_list, slot_list, own, per_dev, size, cap):
    owners = owner_list.reshape(size, per_dev)
    slots = slot_list.reshape(size, per_dev)
    mine = owners == own
    spot = jnp.arange(per_dev, dtype=jnp.int32)
    earlier = spot[None, :] < spot[:, None]
    rank = jnp.sum((mine[:, None, :] & earlier[None]).astype(jnp.int32), axis=2)
    row = jnp.arange(size, dtype=jnp.int32)[:, None] * cap + rank
    key = jnp.where(mine, slots, -1)
    hit = key.reshape(1, -1) == spot[:, None]
    return jnp.max(jnp.where(hit, row.reshape(1, -1), 0), axis=1)


def exchanged_bits(rows, group):
    rows = list(rows)
    for bit in range(4):
        step = 1 << bit
        low = (group & step) == 0
        for index in range(16):
            if index & step:
                continue
            first, second = rows[index], rows[index | step]
            rows[index] = jnp.where(low, first, pltpu.roll(second, 8 * step, 1))
            rows[index | step] = jnp.where(low, pltpu.roll(first, LANES - 8 * step, 1), second)
    return rows


def unpack_kernel(size, cap, table, come, state, low_halo, high_halo, speed, scratch):
    message = TILES * cap + 1
    best = come[message - 1 : message, :]
    for source in range(1, size):
        best = jnp.maximum(best, come[(source + 1) * message - 1 : (source + 1) * message, :])
    speed[...] = jnp.broadcast_to(best, speed.shape)
    for slot in range(BY * BZ):
        p, q = divmod(slot, BZ)
        where = table[slot]
        source = lax.div(where, cap)
        rank = lax.rem(where, cap)
        for pair in range(PAIRS):
            couple, h = divmod(pair, 2)
            base = source * message + rank + pair * (FIELDS * cap)
            value = come[pl.ds(base, FIELDS, stride=cap), :]
            row = (couple * BZ + q) * 8 + 2 * p + h
            scratch[pl.ds(row, FIELDS, stride=PAIRS // 2 * BZ * 8), :] = value
    group = lax.broadcasted_iota(jnp.int32, (8, LANES), 1) // BLOCK
    even = lax.broadcasted_iota(jnp.int32, (8, LANES), 0) % 2 == 0

    for f in range(FIELDS):
        for couple in range(PAIRS // 2):
            first = (f * (PAIRS // 2) + couple) * BZ * 8
            rows = [scratch[first + q * 8 : first + q * 8 + 8, :] for q in range(BZ)]
            moved = exchanged_bits(rows, group)
            for second in range(2):
                for j in range(4):
                    lower = moved[second * BLOCK + j]
                    upper = moved[second * BLOCK + j + 4]
                    planes = (
                        jnp.where(even, lower, pltpu.roll(upper, 1, 0)),
                        jnp.where(even, pltpu.roll(lower, 7, 0), upper),
                    )
                    rows = slice(j * 8, j * 8 + 8)
                    for h in range(2):
                        plane = 4 * couple + 2 * h + second
                        state[f, plane, rows, :] = planes[h]
                        if plane < 3:
                            low_halo[f, plane, rows, :] = planes[h]
                        if plane >= 5:
                            high_halo[f, plane - 5, rows, :] = planes[h]


def unpack(table, come, size, cap):
    halo = jax.ShapeDtypeStruct((FIELDS, 3, ROWS, LANES), jnp.float32)
    return pl.pallas_call(
        functools.partial(unpack_kernel, size, cap),
        out_shape=(
            jax.ShapeDtypeStruct((FIELDS, BLOCK, ROWS, LANES), jnp.float32),
            halo,
            halo,
            jax.ShapeDtypeStruct((8, LANES), jnp.float32),
        ),
        in_specs=[SMEM, VMEM],
        out_specs=(VMEM,) * 4,
        scratch_shapes=[pltpu.VMEM((FIELDS * (PAIRS // 2) * BZ * 8, LANES), jnp.float32)],
        compiler_params=params(),
        cost_estimate=cost(5_000_000, 2_000_000),
        name="unpack",
    )(table, come)


def y_up(x):
    return jnp.concatenate([x[8:], pltpu.roll(x[:8], 7, 0)], axis=0)


def y_down(x):
    return jnp.concatenate([pltpu.roll(x[24:], 1, 0), x[:24]], axis=0)


def y_up_two(x):
    return jnp.concatenate([x[16:], pltpu.roll(x[:8], 7, 0), pltpu.roll(x[8:16], 7, 0)], axis=0)


def z_up(x):
    return pltpu.roll(x, LANES - 1, 1)


def z_up_two(x):
    return pltpu.roll(x, LANES - 2, 1)


def z_down(x):
    return pltpu.roll(x, 1, 1)


def inverse(x):
    return 1.0 / x


def smoothness(before, after):
    curve = after - before
    middle = 0.5 * (after + before)
    base = curve * curve * (13.0 / 12.0) + smooth_epsilon
    plus = middle + curve
    minus = middle - curve
    left = inverse(base + plus * plus)
    centre = inverse(base + middle * middle)
    right = inverse(base + minus * minus)
    return curve, left * left, centre * centre, right * right


def upwind_term(left, centre, right, jump_before, jump_after):
    right = 3.0 * right
    top = left * (jump_before + jump_before) + right * jump_after
    return top * inverse(left + 6.0 * centre + right)


def periodic_divergence(half_flux, scaled, up, up_two, down):
    plus = half_flux + scaled
    minus = half_flux - scaled

    def side(values):
        after = up(values) - values
        curve, left, centre, right = smoothness(down(after), after)
        above = up(curve)
        return curve, above, left, centre, right, above - curve

    curve, _, left, centre, right, jump = side(plus)
    face = 6.0 * (half_flux + up(half_flux)) - curve
    face = face - upwind_term(down(left), centre, up(right), down(jump), jump)
    _, curve, left, centre, right, jump = side(minus)
    face = face + (upwind_term(up_two(right), up(centre), left, up(jump), jump) - curve)
    return face - down(face)


def open_divergence(half_flux, scaled):
    count = len(half_flux)
    plus = [a + b for a, b in zip(half_flux, scaled)]
    minus = [a - b for a, b in zip(half_flux, scaled)]
    faces = [None] * count

    def side(values):
        steps = [values[i + 1] - values[i] for i in range(count - 1)]
        parts = [None] + [smoothness(steps[i - 1], steps[i]) for i in range(1, count - 1)]
        return parts

    parts = side(plus)
    for i in range(2, count - 3):
        jump_before = parts[i][0] - parts[i - 1][0]
        jump_after = parts[i + 1][0] - parts[i][0]
        faces[i] = 6.0 * (half_flux[i] + half_flux[i + 1]) - parts[i][0] - upwind_term(
            parts[i - 1][1], parts[i][2], parts[i + 1][3], jump_before, jump_after
        )
    parts = side(minus)
    for i in range(3, count - 2):
        jump_before = parts[i][0] - parts[i - 1][0]
        jump_after = parts[i + 1][0] - parts[i][0]
        faces[i - 1] = faces[i - 1] + (
            upwind_term(parts[i + 1][3], parts[i][2], parts[i - 1][1], jump_after, jump_before)
            - parts[i][0]
        )
    return [faces[i] - faces[i - 1] for i in range(3, count - 3)]


def half_velocities(fields):
    density, mom_x, mom_y, mom_z, energy = fields
    over = 0.5 / density
    vel = (mom_x * over, mom_y * over, mom_z * over)
    kinetic = mom_x * vel[0] + mom_y * vel[1] + mom_z * vel[2]
    pressure = (gamma_gas - 1.0) * (energy - kinetic)
    return vel, pressure


def half_flux(fields, field, direction, speed, pressure):
    if field == 0:
        return 0.5 * fields[1 + direction]
    if field == 4:
        return (fields[4] + pressure) * speed
    flux = fields[field] * speed
    return flux + 0.5 * pressure if field == 1 + direction else flux


def side_planes(fields, half_speed):
    vel, pressure = half_velocities(fields)
    for field in range(FIELDS):
        scaled = half_speed * fields[field]
        along_y = periodic_divergence(
            half_flux(fields, field, 1, vel[1], pressure), scaled, y_up, y_up_two, y_down
        )
        flux = half_flux(fields, field, 2, vel[2], pressure)
        for first in range(0, ROWS, 8):
            rows = slice(first, first + 8)
            along_z = periodic_divergence(flux[rows], scaled[rows], z_up, z_up_two, z_down)
            yield field, rows, along_y[rows] + along_z


def plane_kernel(state, speed, out):
    half_speed = 0.5 * speed[0:1, :]

    def one_plane(plane, carry):
        fields = [state[f, plane] for f in range(FIELDS)]
        for field, rows, total in side_planes(fields, half_speed):
            out[field, plane, rows, :] = total
        return carry

    lax.fori_loop(0, state.shape[1], one_plane, 0)


def along_planes(state, speed):
    return pl.pallas_call(
        plane_kernel,
        out_shape=jax.ShapeDtypeStruct(state.shape, jnp.float32),
        in_specs=[VMEM, VMEM],
        out_specs=VMEM,
        compiler_params=params(),
        cost_estimate=cost(20_000_000, 1_000_000),
        name="planes",
    )(state, speed)


def across(get, half_speed):
    span = range(-3, BLOCK + 3)
    speeds, pressures = [], []
    for plane in span:
        vel, pressure = half_velocities([get(f, plane) for f in range(FIELDS)])
        speeds.append(vel[0])
        pressures.append(pressure)
    for field in range(FIELDS):
        fluxes, scaled = [], []
        for i, plane in enumerate(span):
            if field == 0:
                flux = 0.5 * get(1, plane)
            elif field == 4:
                flux = (get(4, plane) + pressures[i]) * speeds[i]
            else:
                flux = get(field, plane) * speeds[i]
                if field == 1:
                    flux = flux + 0.5 * pressures[i]
            fluxes.append(flux)
            scaled.append(half_speed * get(field, plane))
        yield field, open_divergence(fluxes, scaled)


def first_kernel(state, sides, below, above, speed, middle, low, high, top):
    half_speed = 0.5 * speed[0:1, :]
    factor = (courant / 6.0) / speed[0:1, :]

    def group(j, best):
        rows = pl.ds(pl.multiple_of(j * 8, 8), 8)

        def get(f, plane):
            if plane < 0:
                return below[f, plane + 3, rows, :]
            if plane >= BLOCK:
                return above[f, plane - BLOCK, rows, :]
            return state[f, plane, rows, :]

        for field, along_x in across(get, half_speed):
            for plane in range(BLOCK):
                total = along_x[plane] + sides[field, plane, rows, :]
                value = get(field, plane) - factor * total
                middle[field, plane, rows, :] = value
                if plane < 3:
                    low[field, plane, rows, :] = value
                if plane >= 5:
                    high[field, plane - 5, rows, :] = value
        for plane in range(BLOCK):
            best = jnp.maximum(
                best, wave_speed([middle[f, plane, rows, :] for f in range(FIELDS)])
            )
        return best

    best = lax.fori_loop(0, 4, group, jnp.zeros((8, LANES), jnp.float32))
    top[...] = jnp.full((8, LANES), jnp.max(best), jnp.float32)


def first_stage(*operands):
    whole = jax.ShapeDtypeStruct((FIELDS, BLOCK, ROWS, LANES), jnp.float32)
    halo = jax.ShapeDtypeStruct((FIELDS, 3, ROWS, LANES), jnp.float32)
    return pl.pallas_call(
        first_kernel,
        out_shape=(whole, halo, halo, jax.ShapeDtypeStruct((8, LANES), jnp.float32)),
        in_specs=[VMEM] * len(operands),
        out_specs=(VMEM,) * 4,
        compiler_params=params(),
        cost_estimate=cost(30_000_000, 3_000_000),
        name="first_stage",
    )(*operands)


def second_kernel(start, middle, sides, below, above, first_speed, speed, out):
    half_speed = 0.5 * speed[0:1, :]
    factor = (courant / 12.0) / first_speed[0:1, :]

    def group(j, carry):
        rows = pl.ds(pl.multiple_of(j * 8, 8), 8)
        spread = pl.ds(j, 8, stride=4)

        def get(f, plane):
            if plane < 0:
                return below[f, plane + 3, rows, :]
            if plane >= BLOCK:
                return above[f, plane - BLOCK, rows, :]
            return middle[f, plane, rows, :]

        for field, along_x in across(get, half_speed):
            for plane in range(BLOCK):
                total = along_x[plane] + sides[field, plane, rows, :]
                value = 0.5 * start[field, plane, rows, :] + (
                    0.5 * get(field, plane) - factor * total
                )
                out[field, plane, spread, :] = value
        return carry

    lax.fori_loop(0, 4, group, 0)


def second_stage(*operands):
    return pl.pallas_call(
        second_kernel,
        out_shape=jax.ShapeDtypeStruct((FIELDS, BLOCK, ROWS, LANES), jnp.float32),
        in_specs=[VMEM] * len(operands),
        out_specs=VMEM,
        compiler_params=params(),
        cost_estimate=cost(30_000_000, 3_000_000),
        name="second_stage",
    )(*operands)


def everyone_max(value, axis, size):
    reach = 1
    while reach * 4 < size:
        reach *= 4
    while reach:
        copies = [value]
        for times in range(1, 4):
            turn = reach * times
            if turn < size:
                pairs = [(i, i ^ turn) for i in range(size)]
                copies.append(lax.ppermute(value, axis, pairs))
        value = functools.reduce(jnp.maximum, copies)
        reach //= 4
    return value


def per_device(blocks, owner_list, slot_list):
    size = lax.axis_size("gx")
    own = lax.axis_index("gx")
    per_dev = blocks.shape[0]
    cap = max(2, 2 * per_dev // size)
    up = [(i, (i + 1) % size) for i in range(size)]
    down = [(j, i) for i, j in up]

    parts = pack(tiled_rows(blocks), owner_list, size, cap, per_dev)
    parts, owner_list, slot_list = lax.optimization_barrier((parts, owner_list, slot_list))
    come = lax.all_to_all(parts, "gx", split_axis=0, concat_axis=0, tiled=True)
    table = arrival_spots(owner_list, slot_list, own, per_dev, size, cap)
    state, low, high, speed = unpack(table, come.reshape(-1, LANES), size, cap)
    below = lax.ppermute(high, "gx", up)
    above = lax.ppermute(low, "gx", down)
    sides = along_planes(state, speed)
    middle, low, high, top = first_stage(state, sides, below, above, speed)
    second = everyone_max(top, "gx", size)
    below = lax.ppermute(high, "gx", up)
    above = lax.ppermute(low, "gx", down)
    sides = along_planes(middle, second)
    return second_stage(state, middle, sides, below, above, speed, second)


def solution(mesh):
    return jax.shard_map(
        per_device,
        mesh=mesh,
        in_specs=(P(("runs", "gx"), None, None), P("runs"), P("runs")),
        out_specs=P(None, ("runs", "gx"), None, None),
        check_vma=False,
    )
```

```python
import functools

import jax
import jax.numpy as jnp
from jax import lax
from jax.experimental import pallas as pl
from jax.experimental.pallas import tpu as pltpu
from jax.sharding import PartitionSpec as P

BLOCK = 8
BY = 4
BZ = 16
FIELDS = 5
LANES = 128
ROWS = BY * BLOCK
PAIRS = BLOCK // 2
TILES = PAIRS * FIELDS

gamma_gas = 1.4
courant = 0.25
smooth_epsilon = 1e-06

VMEM = pl.BlockSpec(memory_space=pltpu.VMEM)
SMEM = pl.BlockSpec(memory_space=pltpu.SMEM)


def params(mebibytes=40):
    return pltpu.CompilerParams(vmem_limit_bytes=mebibytes * 1024 * 1024)


def cost(flops, size):
    return pl.CostEstimate(flops=flops, bytes_accessed=size, transcendentals=0)


def wave_speed(fields):
    density, mom_x, mom_y, mom_z, energy = fields
    inverse = 1.0 / density
    vel = (mom_x * inverse, mom_y * inverse, mom_z * inverse)
    kinetic = 0.5 * (mom_x * vel[0] + mom_y * vel[1] + mom_z * vel[2])
    pressure = (gamma_gas - 1.0) * (energy - kinetic)
    sound = jnp.sqrt(gamma_gas * pressure * inverse)
    fastest = jnp.maximum(jnp.maximum(jnp.abs(vel[0]), jnp.abs(vel[1])), jnp.abs(vel[2]))
    return fastest + sound


def tiled_rows(blocks):
    count = blocks.shape[0] // 8
    groups = blocks.reshape(count, 8, FIELDS, PAIRS, LANES).transpose(2, 0, 3, 1, 4)
    return groups.reshape(FIELDS * count * PAIRS * 8, LANES)


def pack_kernel(
    size, cap, per_dev, owner_hbm, rows_hbm, out_hbm, owner, rows, out, top, count, member, sems
):
    own = lax.axis_index("gx")
    fetch_owner = pltpu.make_async_copy(owner_hbm, owner, sems.at[0])
    fetch_rows = pltpu.make_async_copy(rows_hbm, rows, sems.at[1])
    fetch_owner.start()
    fetch_rows.start()

    def clear(dest, carry):
        count[dest] = 0
        return carry

    lax.fori_loop(0, size, clear, 0, unroll=8)
    fetch_owner.wait()

    def note(block, carry):
        dest = owner[own * per_dev + block]
        rank = count[dest]
        count[dest] = rank + 1
        member[dest * cap + rank] = lax.div(block, 8) * (PAIRS * 8) + lax.rem(block, 8)
        return carry

    lax.fori_loop(0, per_dev, note, 0, unroll=8)
    fetch_rows.wait()
    tiles = TILES * cap

    def message(dest, carry):
        @pl.when(count[dest] > 0)
        def _():
            for rank in range(cap):
                first = member[dest * cap + rank]
                for pair in range(PAIRS):
                    source = pl.ds(first + pair * 8, FIELDS, stride=per_dev * PAIRS)
                    to = dest * tiles + pair * (FIELDS * cap) + rank
                    out[pl.ds(to, FIELDS, stride=cap), :] = rows[source, :]
            part = out.at[pl.ds(pl.multiple_of(dest * tiles, tiles), tiles)]
            pltpu.make_async_copy(part, out_hbm.at[dest, pl.ds(0, tiles), 0], sems.at[2]).start()

        return carry

    lax.fori_loop(0, size, message, 0)
    best = jnp.zeros((8, LANES), jnp.float32)
    step = per_dev * PAIRS
    for first in range(0, step, 8):
        fields = [rows[f * step + first : f * step + first + 8, :] for f in range(FIELDS)]
        best = jnp.maximum(best, wave_speed(fields))
    top[...] = jnp.full(top.shape, jnp.max(best), jnp.float32)
    for dest in range(size):
        pltpu.make_async_copy(
            top.at[pl.ds(dest, 1)], out_hbm.at[dest, tiles], sems.at[3]
        ).start()
    half = out.at[pl.ds(0, per_dev * TILES)]
    pltpu.make_async_copy(half, half, sems.at[2]).wait()
    pltpu.make_async_copy(top, top, sems.at[3]).wait()


def pack(rows, owner_list, size, cap, per_dev):
    return pl.pallas_call(
        functools.partial(pack_kernel, size, cap, per_dev),
        out_shape=jax.ShapeDtypeStruct((size, TILES * cap + 1, 1, LANES), jnp.float32),
        in_specs=[pl.BlockSpec(memory_space=pltpu.HBM)] * 2,
        out_specs=pl.BlockSpec(memory_space=pltpu.HBM),
        scratch_shapes=[
            pltpu.SMEM(owner_list.shape, jnp.int32),
            pltpu.VMEM(rows.shape, jnp.float32),
            pltpu.VMEM((size * TILES * cap, LANES), jnp.float32),
            pltpu.VMEM((size, LANES), jnp.float32),
            pltpu.SMEM((size,), jnp.int32),
            pltpu.SMEM((size * cap,), jnp.int32),
            pltpu.SemaphoreType.DMA((4,)),
        ],
        compiler_params=params(62),
        cost_estimate=cost(1_000_000, 3_000_000),
        name="pack",
    )(owner_list, rows)


def arrival_spots(owner_list, slot_list, own, per_dev, size, cap):
    owners = owner_list.reshape(size, per_dev)
    slots = slot_list.reshape(size, per_dev)
    mine = owners == own
    spot = jnp.arange(per_dev, dtype=jnp.int32)
    earlier = spot[None, :] < spot[:, None]
    rank = jnp.sum((mine[:, None, :] & earlier[None]).astype(jnp.int32), axis=2)
    row = jnp.arange(size, dtype=jnp.int32)[:, None] * cap + rank
    key = jnp.where(mine, slots, -1)
    hit = key.reshape(1, -1) == spot[:, None]
    return jnp.max(jnp.where(hit, row.reshape(1, -1), 0), axis=1)


def exchanged_bits(rows, group):
    rows = list(rows)
    for bit in range(4):
        step = 1 << bit
        low = (group & step) == 0
        for index in range(16):
            if index & step:
                continue
            first, second = rows[index], rows[index | step]
            rows[index] = jnp.where(low, first, pltpu.roll(second, 8 * step, 1))
            rows[index | step] = jnp.where(low, pltpu.roll(first, LANES - 8 * step, 1), second)
    return rows


def unpack_kernel(size, cap, table, come, state, low_halo, high_halo, speed, scratch):
    message = TILES * cap + 1
    best = come[message - 1 : message, :]
    for source in range(1, size):
        best = jnp.maximum(best, come[(source + 1) * message - 1 : (source + 1) * message, :])
    speed[...] = jnp.broadcast_to(best, speed.shape)
    for slot in range(BY * BZ):
        p, q = divmod(slot, BZ)
        where = table[slot]
        source = lax.div(where, cap)
        rank = lax.rem(where, cap)
        for pair in range(PAIRS):
            couple, h = divmod(pair, 2)
            base = source * message + rank + pair * (FIELDS * cap)
            value = come[pl.ds(base, FIELDS, stride=cap), :]
            row = (couple * BZ + q) * 8 + 2 * p + h
            scratch[pl.ds(row, FIELDS, stride=PAIRS // 2 * BZ * 8), :] = value
    group = lax.broadcasted_iota(jnp.int32, (8, LANES), 1) // BLOCK
    even = lax.broadcasted_iota(jnp.int32, (8, LANES), 0) % 2 == 0

    for f in range(FIELDS):
        for couple in range(PAIRS // 2):
            first = (f * (PAIRS // 2) + couple) * BZ * 8
            rows = [scratch[first + q * 8 : first + q * 8 + 8, :] for q in range(BZ)]
            moved = exchanged_bits(rows, group)
            for second in range(2):
                for j in range(4):
                    lower = moved[second * BLOCK + j]
                    upper = moved[second * BLOCK + j + 4]
                    planes = (
                        jnp.where(even, lower, pltpu.roll(upper, 1, 0)),
                        jnp.where(even, pltpu.roll(lower, 7, 0), upper),
                    )
                    rows = slice(j * 8, j * 8 + 8)
                    for h in range(2):
                        plane = 4 * couple + 2 * h + second
                        state[f, plane, rows, :] = planes[h]
                        if plane < 3:
                            low_halo[f, plane, rows, :] = planes[h]
                        if plane >= 5:
                            high_halo[f, plane - 5, rows, :] = planes[h]


def unpack(table, come, size, cap):
    halo = jax.ShapeDtypeStruct((FIELDS, 3, ROWS, LANES), jnp.float32)
    return pl.pallas_call(
        functools.partial(unpack_kernel, size, cap),
        out_shape=(
            jax.ShapeDtypeStruct((FIELDS, BLOCK, ROWS, LANES), jnp.float32),
            halo,
            halo,
            jax.ShapeDtypeStruct((8, LANES), jnp.float32),
        ),
        in_specs=[SMEM, VMEM],
        out_specs=(VMEM,) * 4,
        scratch_shapes=[pltpu.VMEM((FIELDS * (PAIRS // 2) * BZ * 8, LANES), jnp.float32)],
        compiler_params=params(),
        cost_estimate=cost(5_000_000, 2_000_000),
        name="unpack",
    )(table, come)


def y_up(x):
    return jnp.concatenate([x[8:], pltpu.roll(x[:8], 7, 0)], axis=0)


def y_down(x):
    return jnp.concatenate([pltpu.roll(x[24:], 1, 0), x[:24]], axis=0)


def y_up_two(x):
    return jnp.concatenate([x[16:], pltpu.roll(x[:8], 7, 0), pltpu.roll(x[8:16], 7, 0)], axis=0)


def inverse(x):
    return 1.0 / x


def smoothness(before, after):
    curve = after - before
    middle = 0.5 * (after + before)
    base = curve * curve * (13.0 / 12.0) + smooth_epsilon
    plus = middle + curve
    minus = middle - curve
    left = inverse(base + plus * plus)
    centre = inverse(base + middle * middle)
    right = inverse(base + minus * minus)
    return curve, left * left, centre * centre, right * right


def upwind_term(left, centre, right, jump_before, jump_after):
    right = 3.0 * right
    top = left * (jump_before + jump_before) + right * jump_after
    return top * inverse(left + 6.0 * centre + right)


def periodic_divergence(half_flux, scaled, up, up_two, down):
    plus = half_flux + scaled
    minus = half_flux - scaled

    def side(values):
        after = up(values) - values
        curve, left, centre, right = smoothness(down(after), after)
        above = up(curve)
        return curve, above, left, centre, right, above - curve

    curve, _, left, centre, right, jump = side(plus)
    face = 6.0 * (half_flux + up(half_flux)) - curve
    face = face - upwind_term(down(left), centre, up(right), down(jump), jump)
    _, curve, left, centre, right, jump = side(minus)
    face = face + (upwind_term(up_two(right), up(centre), left, up(jump), jump) - curve)
    return face - down(face)


def ring_divergence(half_flux, scaled):
    count = len(half_flux)

    def up(values):
        return values[1:] + [pltpu.roll(values[0], 7, 0)]

    def down(values):
        return [pltpu.roll(values[-1], 1, 0)] + values[:-1]

    def side(values):
        after = [above - value for above, value in zip(up(values), values)]
        parts = [smoothness(before, step) for before, step in zip(down(after), after)]
        curve, left, centre, right = (list(part) for part in zip(*parts))
        jump = [above - value for above, value in zip(up(curve), curve)]
        return curve, left, centre, right, jump

    curve, left, centre, right, jump = side([a + b for a, b in zip(half_flux, scaled)])
    terms = zip(down(left), centre, up(right), down(jump), jump)
    face = [
        6.0 * (here + above) - bend - upwind_term(*term)
        for here, above, bend, term in zip(half_flux, up(half_flux), curve, terms)
    ]
    curve, left, centre, right, jump = side([a - b for a, b in zip(half_flux, scaled)])
    terms = zip(up(right), centre, down(left), jump, down(jump))
    other = [upwind_term(*term) - bend for bend, term in zip(curve, terms)]
    face = [one + two for one, two in zip(face, up(other))]
    return [here - below for here, below in zip(face, down(face))]


def open_divergence(half_flux, scaled):
    count = len(half_flux)
    plus = [a + b for a, b in zip(half_flux, scaled)]
    minus = [a - b for a, b in zip(half_flux, scaled)]
    faces = [None] * count

    def side(values):
        steps = [values[i + 1] - values[i] for i in range(count - 1)]
        parts = [None] + [smoothness(steps[i - 1], steps[i]) for i in range(1, count - 1)]
        return parts

    parts = side(plus)
    for i in range(2, count - 3):
        jump_before = parts[i][0] - parts[i - 1][0]
        jump_after = parts[i + 1][0] - parts[i][0]
        faces[i] = 6.0 * (half_flux[i] + half_flux[i + 1]) - parts[i][0] - upwind_term(
            parts[i - 1][1], parts[i][2], parts[i + 1][3], jump_before, jump_after
        )
    parts = side(minus)
    for i in range(3, count - 2):
        jump_before = parts[i][0] - parts[i - 1][0]
        jump_after = parts[i + 1][0] - parts[i][0]
        faces[i - 1] = faces[i - 1] + (
            upwind_term(parts[i + 1][3], parts[i][2], parts[i - 1][1], jump_after, jump_before)
            - parts[i][0]
        )
    return [faces[i] - faces[i - 1] for i in range(3, count - 3)]


def half_velocities(fields):
    density, mom_x, mom_y, mom_z, energy = fields
    over = 0.5 / density
    vel = (mom_x * over, mom_y * over, mom_z * over)
    kinetic = mom_x * vel[0] + mom_y * vel[1] + mom_z * vel[2]
    pressure = (gamma_gas - 1.0) * (energy - kinetic)
    return vel, pressure


def half_flux(fields, field, direction, speed, pressure):
    if field == 0:
        return 0.5 * fields[1 + direction]
    if field == 4:
        return (fields[4] + pressure) * speed
    flux = fields[field] * speed
    return flux + 0.5 * pressure if field == 1 + direction else flux


def plane_kernel(state, speed, out, turned):
    half_speed = 0.5 * speed[0:1, :]
    lane = lax.broadcasted_iota(jnp.int32, (LANES, LANES), 1)
    to_turned = (lane % 8) * 16 + lane // 8
    to_plain = (lane % 16) * 8 + lane // 16

    def four_planes(part, carry):
        planes = pl.ds(part * 4, 4)
        for f in range(FIELDS):
            plain = state[f, planes].reshape(LANES, LANES)
            turned[f] = jnp.take_along_axis(plain, to_turned, axis=1).T
        for place in range(4):
            fields = [state[f, part * 4 + place] for f in range(FIELDS)]
            vel, pressure = half_velocities(fields)
            for field in range(FIELDS):
                out[field, part * 4 + place] = periodic_divergence(
                    half_flux(fields, field, 1, vel[1], pressure),
                    half_speed * fields[field],
                    y_up,
                    y_up_two,
                    y_down,
                )
        columns = [
            [turned[f, row : row + 8] for row in range(0, LANES, 8)] for f in range(FIELDS)
        ]
        along = [half_velocities(fields) for fields in zip(*columns)]
        for field in range(FIELDS):
            fluxes = [
                half_flux(fields, field, 2, vel[2], pressure)
                for fields, (vel, pressure) in zip(zip(*columns), along)
            ]
            scaled = [half_speed * value for value in columns[field]]
            total = jnp.concatenate(ring_divergence(fluxes, scaled), axis=0)
            plain = jnp.take_along_axis(total.T, to_plain, axis=1)
            out[field, planes] += plain.reshape(4, ROWS, LANES)
        return carry

    lax.fori_loop(0, state.shape[1] // 4, four_planes, 0)


def along_planes(state, speed):
    return pl.pallas_call(
        plane_kernel,
        out_shape=jax.ShapeDtypeStruct(state.shape, jnp.float32),
        in_specs=[VMEM, VMEM],
        out_specs=VMEM,
        scratch_shapes=[pltpu.VMEM((FIELDS, LANES, LANES), jnp.float32)],
        compiler_params=params(),
        cost_estimate=cost(20_000_000, 1_000_000),
        name="planes",
    )(state, speed)


def across(get, half_speed):
    span = range(-3, BLOCK + 3)
    speeds, pressures = [], []
    for plane in span:
        vel, pressure = half_velocities([get(f, plane) for f in range(FIELDS)])
        speeds.append(vel[0])
        pressures.append(pressure)
    for field in range(FIELDS):
        fluxes, scaled = [], []
        for i, plane in enumerate(span):
            if field == 0:
                flux = 0.5 * get(1, plane)
            elif field == 4:
                flux = (get(4, plane) + pressures[i]) * speeds[i]
            else:
                flux = get(field, plane) * speeds[i]
                if field == 1:
                    flux = flux + 0.5 * pressures[i]
            fluxes.append(flux)
            scaled.append(half_speed * get(field, plane))
        yield field, open_divergence(fluxes, scaled)


def first_kernel(state, sides, below, above, speed, middle, low, high, top):
    half_speed = 0.5 * speed[0:1, :]
    factor = (courant / 6.0) / speed[0:1, :]

    def group(j, best):
        rows = pl.ds(pl.multiple_of(j * 8, 8), 8)

        def get(f, plane):
            if plane < 0:
                return below[f, plane + 3, rows, :]
            if plane >= BLOCK:
                return above[f, plane - BLOCK, rows, :]
            return state[f, plane, rows, :]

        for field, along_x in across(get, half_speed):
            for plane in range(BLOCK):
                total = along_x[plane] + sides[field, plane, rows, :]
                value = get(field, plane) - factor * total
                middle[field, plane, rows, :] = value
                if plane < 3:
                    low[field, plane, rows, :] = value
                if plane >= 5:
                    high[field, plane - 5, rows, :] = value
        for plane in range(BLOCK):
            best = jnp.maximum(
                best, wave_speed([middle[f, plane, rows, :] for f in range(FIELDS)])
            )
        return best

    best = lax.fori_loop(0, 4, group, jnp.zeros((8, LANES), jnp.float32))
    top[...] = jnp.full((8, LANES), jnp.max(best), jnp.float32)


def first_stage(*operands):
    whole = jax.ShapeDtypeStruct((FIELDS, BLOCK, ROWS, LANES), jnp.float32)
    halo = jax.ShapeDtypeStruct((FIELDS, 3, ROWS, LANES), jnp.float32)
    return pl.pallas_call(
        first_kernel,
        out_shape=(whole, halo, halo, jax.ShapeDtypeStruct((8, LANES), jnp.float32)),
        in_specs=[VMEM] * len(operands),
        out_specs=(VMEM,) * 4,
        compiler_params=params(),
        cost_estimate=cost(30_000_000, 3_000_000),
        name="first_stage",
    )(*operands)


def second_kernel(start, middle, sides, below, above, first_speed, speed, out):
    half_speed = 0.5 * speed[0:1, :]
    factor = (courant / 12.0) / first_speed[0:1, :]

    def group(j, carry):
        rows = pl.ds(pl.multiple_of(j * 8, 8), 8)
        spread = pl.ds(j, 8, stride=4)

        def get(f, plane):
            if plane < 0:
                return below[f, plane + 3, rows, :]
            if plane >= BLOCK:
                return above[f, plane - BLOCK, rows, :]
            return middle[f, plane, rows, :]

        for field, along_x in across(get, half_speed):
            for plane in range(BLOCK):
                total = along_x[plane] + sides[field, plane, rows, :]
                value = 0.5 * start[field, plane, rows, :] + (
                    0.5 * get(field, plane) - factor * total
                )
                out[field, plane, spread, :] = value
        return carry

    lax.fori_loop(0, 4, group, 0)


def second_stage(*operands):
    return pl.pallas_call(
        second_kernel,
        out_shape=jax.ShapeDtypeStruct((FIELDS, BLOCK, ROWS, LANES), jnp.float32),
        in_specs=[VMEM] * len(operands),
        out_specs=VMEM,
        compiler_params=params(),
        cost_estimate=cost(30_000_000, 3_000_000),
        name="second_stage",
    )(*operands)


def everyone_max(value, axis, size):
    reach = 1
    while reach * 4 < size:
        reach *= 4
    while reach:
        copies = [value]
        for times in range(1, 4):
            turn = reach * times
            if turn < size:
                pairs = [(i, i ^ turn) for i in range(size)]
                copies.append(lax.ppermute(value, axis, pairs))
        value = functools.reduce(jnp.maximum, copies)
        reach //= 4
    return value


def per_device(blocks, owner_list, slot_list):
    size = lax.axis_size("gx")
    own = lax.axis_index("gx")
    per_dev = blocks.shape[0]
    cap = max(2, 2 * per_dev // size)
    up = [(i, (i + 1) % size) for i in range(size)]
    down = [(j, i) for i, j in up]

    parts = pack(tiled_rows(blocks), owner_list, size, cap, per_dev)
    parts, owner_list, slot_list = lax.optimization_barrier((parts, owner_list, slot_list))
    come = lax.all_to_all(parts, "gx", split_axis=0, concat_axis=0, tiled=True)
    table = arrival_spots(owner_list, slot_list, own, per_dev, size, cap)
    state, low, high, speed = unpack(table, come.reshape(-1, LANES), size, cap)
    below = lax.ppermute(high, "gx", up)
    above = lax.ppermute(low, "gx", down)
    sides = along_planes(state, speed)
    middle, low, high, top = first_stage(state, sides, below, above, speed)
    second = everyone_max(top, "gx", size)
    below = lax.ppermute(high, "gx", up)
    above = lax.ppermute(low, "gx", down)
    sides = along_planes(middle, second)
    return second_stage(state, middle, sides, below, above, speed, second)


def solution(mesh):
    return jax.shard_map(
        per_device,
        mesh=mesh,
        in_specs=(P(("runs", "gx"), None, None), P("runs"), P("runs")),
        out_specs=P(None, ("runs", "gx"), None, None),
        check_vma=False,
    )
```

```python
import functools

import jax
import jax.numpy as jnp
from jax import lax
from jax.experimental import pallas as pl
from jax.experimental.pallas import tpu as pltpu
from jax.sharding import PartitionSpec as P

BLOCK = 8
BY = 4
BZ = 16
FIELDS = 5
LANES = 128
ROWS = BY * BLOCK
PAIRS = BLOCK // 2
TILES = PAIRS * FIELDS

gamma_gas = 1.4
courant = 0.25
smooth_epsilon = 1e-06

VMEM = pl.BlockSpec(memory_space=pltpu.VMEM)
SMEM = pl.BlockSpec(memory_space=pltpu.SMEM)


def params(mebibytes=40):
    return pltpu.CompilerParams(vmem_limit_bytes=mebibytes * 1024 * 1024)


def cost(flops, size):
    return pl.CostEstimate(flops=flops, bytes_accessed=size, transcendentals=0)


def wave_speed(fields):
    density, mom_x, mom_y, mom_z, energy = fields
    inverse = 1.0 / density
    vel = (mom_x * inverse, mom_y * inverse, mom_z * inverse)
    kinetic = 0.5 * (mom_x * vel[0] + mom_y * vel[1] + mom_z * vel[2])
    pressure = (gamma_gas - 1.0) * (energy - kinetic)
    sound = jnp.sqrt(gamma_gas * pressure * inverse)
    fastest = jnp.maximum(jnp.maximum(jnp.abs(vel[0]), jnp.abs(vel[1])), jnp.abs(vel[2]))
    return fastest + sound


def device_at(place, size):
    if size < 4 or size & (size - 1):
        return place
    return (place % 2) * (size // 2) + (place // 2 % 2) * (size // 4) + place // 4


def exchange_order(size):
    return [device_at(place, size) for place in range(size)]


def tiled_rows(blocks):
    count = blocks.shape[0] // 8
    groups = blocks.reshape(count, 8, FIELDS, PAIRS, LANES).transpose(2, 0, 3, 1, 4)
    return groups.reshape(FIELDS * count * PAIRS * 8, LANES)


def pack_kernel(
    size, cap, per_dev, owner_hbm, rows_hbm, out_hbm, owner, rows, out, top, count, member, sems
):
    own = lax.axis_index("gx")
    fetch_owner = pltpu.make_async_copy(owner_hbm, owner, sems.at[0])
    fetch_rows = pltpu.make_async_copy(rows_hbm, rows, sems.at[1])
    fetch_owner.start()
    fetch_rows.start()

    def clear(dest, carry):
        count[dest] = 0
        return carry

    lax.fori_loop(0, size, clear, 0, unroll=8)
    fetch_owner.wait()

    def note(block, carry):
        dest = owner[own * per_dev + block]
        rank = count[dest]
        count[dest] = rank + 1
        member[dest * cap + rank] = lax.div(block, 8) * (PAIRS * 8) + lax.rem(block, 8)
        return carry

    lax.fori_loop(0, per_dev, note, 0, unroll=8)
    fetch_rows.wait()
    tiles = TILES * cap

    def message(place, carry):
        dest = device_at(place, size)

        @pl.when(count[dest] > 0)
        def _():
            for rank in range(cap):
                first = member[dest * cap + rank]
                for pair in range(PAIRS):
                    source = pl.ds(first + pair * 8, FIELDS, stride=per_dev * PAIRS)
                    to = place * tiles + pair * (FIELDS * cap) + rank
                    out[pl.ds(to, FIELDS, stride=cap), :] = rows[source, :]
            part = out.at[pl.ds(pl.multiple_of(place * tiles, tiles), tiles)]
            pltpu.make_async_copy(part, out_hbm.at[place, pl.ds(0, tiles), 0], sems.at[2]).start()

        return carry

    lax.fori_loop(0, size, message, 0)
    best = jnp.zeros((8, LANES), jnp.float32)
    step = per_dev * PAIRS
    for first in range(0, step, 8):
        fields = [rows[f * step + first : f * step + first + 8, :] for f in range(FIELDS)]
        best = jnp.maximum(best, wave_speed(fields))
    top[...] = jnp.full(top.shape, jnp.max(best), jnp.float32)
    for dest in range(size):
        pltpu.make_async_copy(
            top.at[pl.ds(dest, 1)], out_hbm.at[dest, tiles], sems.at[3]
        ).start()
    half = out.at[pl.ds(0, per_dev * TILES)]
    pltpu.make_async_copy(half, half, sems.at[2]).wait()
    pltpu.make_async_copy(top, top, sems.at[3]).wait()


def pack(rows, owner_list, size, cap, per_dev):
    return pl.pallas_call(
        functools.partial(pack_kernel, size, cap, per_dev),
        out_shape=jax.ShapeDtypeStruct((size, TILES * cap + 1, 1, LANES), jnp.float32),
        in_specs=[pl.BlockSpec(memory_space=pltpu.HBM)] * 2,
        out_specs=pl.BlockSpec(memory_space=pltpu.HBM),
        scratch_shapes=[
            pltpu.SMEM(owner_list.shape, jnp.int32),
            pltpu.VMEM(rows.shape, jnp.float32),
            pltpu.VMEM((size * TILES * cap, LANES), jnp.float32),
            pltpu.VMEM((size, LANES), jnp.float32),
            pltpu.SMEM((size,), jnp.int32),
            pltpu.SMEM((size * cap,), jnp.int32),
            pltpu.SemaphoreType.DMA((4,)),
        ],
        compiler_params=params(62),
        cost_estimate=cost(1_000_000, 3_000_000),
        name="pack",
    )(owner_list, rows)


def arrival_spots(owner_list, slot_list, own, per_dev, size, cap):
    owners = owner_list.reshape(size, per_dev)
    slots = slot_list.reshape(size, per_dev)
    mine = owners == own
    spot = jnp.arange(per_dev, dtype=jnp.int32)
    earlier = spot[None, :] < spot[:, None]
    rank = jnp.sum((mine[:, None, :] & earlier[None]).astype(jnp.int32), axis=2)
    order = exchange_order(size)
    places = jnp.array([order.index(source) for source in range(size)], jnp.int32)
    row = places[:, None] * cap + rank
    key = jnp.where(mine, slots, -1)
    hit = key.reshape(1, -1) == spot[:, None]
    return jnp.max(jnp.where(hit, row.reshape(1, -1), 0), axis=1)


def exchanged_bits(rows, group):
    rows = list(rows)
    for bit in range(4):
        step = 1 << bit
        low = (group & step) == 0
        for index in range(16):
            if index & step:
                continue
            first, second = rows[index], rows[index | step]
            rows[index] = jnp.where(low, first, pltpu.roll(second, 8 * step, 1))
            rows[index | step] = jnp.where(low, pltpu.roll(first, LANES - 8 * step, 1), second)
    return rows


def unpack_kernel(size, cap, table, come, state, low_halo, high_halo, speed, scratch):
    message = TILES * cap + 1
    best = come[message - 1 : message, :]
    for source in range(1, size):
        best = jnp.maximum(best, come[(source + 1) * message - 1 : (source + 1) * message, :])
    speed[...] = jnp.broadcast_to(best, speed.shape)
    for slot in range(BY * BZ):
        p, q = divmod(slot, BZ)
        where = table[slot]
        source = lax.div(where, cap)
        rank = lax.rem(where, cap)
        for pair in range(PAIRS):
            couple, h = divmod(pair, 2)
            base = source * message + rank + pair * (FIELDS * cap)
            value = come[pl.ds(base, FIELDS, stride=cap), :]
            row = (couple * BZ + q) * 8 + 2 * p + h
            scratch[pl.ds(row, FIELDS, stride=PAIRS // 2 * BZ * 8), :] = value
    group = lax.broadcasted_iota(jnp.int32, (8, LANES), 1) // BLOCK
    even = lax.broadcasted_iota(jnp.int32, (8, LANES), 0) % 2 == 0

    for f in range(FIELDS):
        for couple in range(PAIRS // 2):
            first = (f * (PAIRS // 2) + couple) * BZ * 8
            rows = [scratch[first + q * 8 : first + q * 8 + 8, :] for q in range(BZ)]
            moved = exchanged_bits(rows, group)
            for second in range(2):
                for j in range(4):
                    lower = moved[second * BLOCK + j]
                    upper = moved[second * BLOCK + j + 4]
                    planes = (
                        jnp.where(even, lower, pltpu.roll(upper, 1, 0)),
                        jnp.where(even, pltpu.roll(lower, 7, 0), upper),
                    )
                    rows = slice(j * 8, j * 8 + 8)
                    for h in range(2):
                        plane = 4 * couple + 2 * h + second
                        state[f, plane, rows, :] = planes[h]
                        if plane < 3:
                            low_halo[f, plane, rows, :] = planes[h]
                        if plane >= 5:
                            high_halo[f, plane - 5, rows, :] = planes[h]


def unpack(table, come, size, cap):
    halo = jax.ShapeDtypeStruct((FIELDS, 3, ROWS, LANES), jnp.float32)
    return pl.pallas_call(
        functools.partial(unpack_kernel, size, cap),
        out_shape=(
            jax.ShapeDtypeStruct((FIELDS, BLOCK, ROWS, LANES), jnp.float32),
            halo,
            halo,
            jax.ShapeDtypeStruct((8, LANES), jnp.float32),
        ),
        in_specs=[SMEM, VMEM],
        out_specs=(VMEM,) * 4,
        scratch_shapes=[pltpu.VMEM((FIELDS * (PAIRS // 2) * BZ * 8, LANES), jnp.float32)],
        compiler_params=params(),
        cost_estimate=cost(5_000_000, 2_000_000),
        name="unpack",
    )(table, come)


def y_up(x):
    return jnp.concatenate([x[8:], pltpu.roll(x[:8], 7, 0)], axis=0)


def y_down(x):
    return jnp.concatenate([pltpu.roll(x[24:], 1, 0), x[:24]], axis=0)


def y_up_two(x):
    return jnp.concatenate([x[16:], pltpu.roll(x[:8], 7, 0), pltpu.roll(x[8:16], 7, 0)], axis=0)


def inverse(x):
    return 1.0 / x


def smoothness(before, after):
    curve = after - before
    middle = 0.5 * (after + before)
    base = curve * curve * (13.0 / 12.0) + smooth_epsilon
    plus = middle + curve
    minus = middle - curve
    left = inverse(base + plus * plus)
    centre = inverse(base + middle * middle)
    right = inverse(base + minus * minus)
    return curve, left * left, centre * centre, right * right


def upwind_term(left, centre, right, jump_before, jump_after):
    right = 3.0 * right
    top = left * (jump_before + jump_before) + right * jump_after
    return top * inverse(left + 6.0 * centre + right)


def periodic_divergence(half_flux, scaled, up, up_two, down):
    plus = half_flux + scaled
    minus = half_flux - scaled

    def side(values):
        after = up(values) - values
        curve, left, centre, right = smoothness(down(after), after)
        above = up(curve)
        return curve, above, left, centre, right, above - curve

    curve, _, left, centre, right, jump = side(plus)
    face = 6.0 * (half_flux + up(half_flux)) - curve
    face = face - upwind_term(down(left), centre, up(right), down(jump), jump)
    _, curve, left, centre, right, jump = side(minus)
    face = face + (upwind_term(up_two(right), up(centre), left, up(jump), jump) - curve)
    return face - down(face)


def ring_divergence(half_flux, scaled):
    count = len(half_flux)

    def up(values):
        return values[1:] + [pltpu.roll(values[0], 7, 0)]

    def down(values):
        return [pltpu.roll(values[-1], 1, 0)] + values[:-1]

    def side(values):
        after = [above - value for above, value in zip(up(values), values)]
        parts = [smoothness(before, step) for before, step in zip(down(after), after)]
        curve, left, centre, right = (list(part) for part in zip(*parts))
        jump = [above - value for above, value in zip(up(curve), curve)]
        return curve, left, centre, right, jump

    curve, left, centre, right, jump = side([a + b for a, b in zip(half_flux, scaled)])
    terms = zip(down(left), centre, up(right), down(jump), jump)
    face = [
        6.0 * (here + above) - bend - upwind_term(*term)
        for here, above, bend, term in zip(half_flux, up(half_flux), curve, terms)
    ]
    curve, left, centre, right, jump = side([a - b for a, b in zip(half_flux, scaled)])
    terms = zip(up(right), centre, down(left), jump, down(jump))
    other = [upwind_term(*term) - bend for bend, term in zip(curve, terms)]
    face = [one + two for one, two in zip(face, up(other))]
    return [here - below for here, below in zip(face, down(face))]


def open_divergence(half_flux, scaled):
    count = len(half_flux)
    plus = [a + b for a, b in zip(half_flux, scaled)]
    minus = [a - b for a, b in zip(half_flux, scaled)]
    faces = [None] * count

    def side(values):
        steps = [values[i + 1] - values[i] for i in range(count - 1)]
        parts = [None] + [smoothness(steps[i - 1], steps[i]) for i in range(1, count - 1)]
        return parts

    parts = side(plus)
    for i in range(2, count - 3):
        jump_before = parts[i][0] - parts[i - 1][0]
        jump_after = parts[i + 1][0] - parts[i][0]
        faces[i] = 6.0 * (half_flux[i] + half_flux[i + 1]) - parts[i][0] - upwind_term(
            parts[i - 1][1], parts[i][2], parts[i + 1][3], jump_before, jump_after
        )
    parts = side(minus)
    for i in range(3, count - 2):
        jump_before = parts[i][0] - parts[i - 1][0]
        jump_after = parts[i + 1][0] - parts[i][0]
        faces[i - 1] = faces[i - 1] + (
            upwind_term(parts[i + 1][3], parts[i][2], parts[i - 1][1], jump_after, jump_before)
            - parts[i][0]
        )
    return [faces[i] - faces[i - 1] for i in range(3, count - 3)]


def half_velocities(fields):
    density, mom_x, mom_y, mom_z, energy = fields
    over = 0.5 / density
    vel = (mom_x * over, mom_y * over, mom_z * over)
    kinetic = mom_x * vel[0] + mom_y * vel[1] + mom_z * vel[2]
    pressure = (gamma_gas - 1.0) * (energy - kinetic)
    return vel, pressure


def half_flux(fields, field, direction, speed, pressure):
    if field == 0:
        return 0.5 * fields[1 + direction]
    if field == 4:
        return (fields[4] + pressure) * speed
    flux = fields[field] * speed
    return flux + 0.5 * pressure if field == 1 + direction else flux


def plane_kernel(state, speed, out, turned):
    half_speed = 0.5 * speed[0:1, :]
    lane = lax.broadcasted_iota(jnp.int32, (LANES, LANES), 1)
    to_turned = (lane % 8) * 16 + lane // 8
    to_plain = (lane % 16) * 8 + lane // 16

    def four_planes(part, carry):
        planes = pl.ds(part * 4, 4)
        for f in range(FIELDS):
            plain = state[f, planes].reshape(LANES, LANES)
            turned[f] = jnp.take_along_axis(plain, to_turned, axis=1).T
        for place in range(4):
            fields = [state[f, part * 4 + place] for f in range(FIELDS)]
            vel, pressure = half_velocities(fields)
            for field in range(FIELDS):
                out[field, part * 4 + place] = periodic_divergence(
                    half_flux(fields, field, 1, vel[1], pressure),
                    half_speed * fields[field],
                    y_up,
                    y_up_two,
                    y_down,
                )
        columns = [
            [turned[f, row : row + 8] for row in range(0, LANES, 8)] for f in range(FIELDS)
        ]
        along = [half_velocities(fields) for fields in zip(*columns)]
        for field in range(FIELDS):
            fluxes = [
                half_flux(fields, field, 2, vel[2], pressure)
                for fields, (vel, pressure) in zip(zip(*columns), along)
            ]
            scaled = [half_speed * value for value in columns[field]]
            total = jnp.concatenate(ring_divergence(fluxes, scaled), axis=0)
            plain = jnp.take_along_axis(total.T, to_plain, axis=1)
            out[field, planes] += plain.reshape(4, ROWS, LANES)
        return carry

    lax.fori_loop(0, state.shape[1] // 4, four_planes, 0)


def along_planes(state, speed):
    return pl.pallas_call(
        plane_kernel,
        out_shape=jax.ShapeDtypeStruct(state.shape, jnp.float32),
        in_specs=[VMEM, VMEM],
        out_specs=VMEM,
        scratch_shapes=[pltpu.VMEM((FIELDS, LANES, LANES), jnp.float32)],
        compiler_params=params(),
        cost_estimate=cost(20_000_000, 1_000_000),
        name="planes",
    )(state, speed)


def across(get, half_speed):
    span = range(-3, BLOCK + 3)
    speeds, pressures = [], []
    for plane in span:
        vel, pressure = half_velocities([get(f, plane) for f in range(FIELDS)])
        speeds.append(vel[0])
        pressures.append(pressure)
    for field in range(FIELDS):
        fluxes, scaled = [], []
        for i, plane in enumerate(span):
            if field == 0:
                flux = 0.5 * get(1, plane)
            elif field == 4:
                flux = (get(4, plane) + pressures[i]) * speeds[i]
            else:
                flux = get(field, plane) * speeds[i]
                if field == 1:
                    flux = flux + 0.5 * pressures[i]
            fluxes.append(flux)
            scaled.append(half_speed * get(field, plane))
        yield field, open_divergence(fluxes, scaled)


def first_kernel(state, sides, below, above, speed, middle, low, high, top):
    half_speed = 0.5 * speed[0:1, :]
    factor = (courant / 6.0) / speed[0:1, :]

    def group(j, best):
        rows = pl.ds(pl.multiple_of(j * 8, 8), 8)

        def get(f, plane):
            if plane < 0:
                return below[f, plane + 3, rows, :]
            if plane >= BLOCK:
                return above[f, plane - BLOCK, rows, :]
            return state[f, plane, rows, :]

        for field, along_x in across(get, half_speed):
            for plane in range(BLOCK):
                total = along_x[plane] + sides[field, plane, rows, :]
                value = get(field, plane) - factor * total
                middle[field, plane, rows, :] = value
                if plane < 3:
                    low[field, plane, rows, :] = value
                if plane >= 5:
                    high[field, plane - 5, rows, :] = value
        for plane in range(BLOCK):
            best = jnp.maximum(
                best, wave_speed([middle[f, plane, rows, :] for f in range(FIELDS)])
            )
        return best

    best = lax.fori_loop(0, 4, group, jnp.zeros((8, LANES), jnp.float32))
    top[...] = jnp.full((8, LANES), jnp.max(best), jnp.float32)


def first_stage(*operands):
    whole = jax.ShapeDtypeStruct((FIELDS, BLOCK, ROWS, LANES), jnp.float32)
    halo = jax.ShapeDtypeStruct((FIELDS, 3, ROWS, LANES), jnp.float32)
    return pl.pallas_call(
        first_kernel,
        out_shape=(whole, halo, halo, jax.ShapeDtypeStruct((8, LANES), jnp.float32)),
        in_specs=[VMEM] * len(operands),
        out_specs=(VMEM,) * 4,
        compiler_params=params(),
        cost_estimate=cost(30_000_000, 3_000_000),
        name="first_stage",
    )(*operands)


def second_kernel(start, middle, sides, below, above, first_speed, speed, out):
    half_speed = 0.5 * speed[0:1, :]
    factor = (courant / 12.0) / first_speed[0:1, :]

    def group(j, carry):
        rows = pl.ds(pl.multiple_of(j * 8, 8), 8)
        spread = pl.ds(j, 8, stride=4)

        def get(f, plane):
            if plane < 0:
                return below[f, plane + 3, rows, :]
            if plane >= BLOCK:
                return above[f, plane - BLOCK, rows, :]
            return middle[f, plane, rows, :]

        for field, along_x in across(get, half_speed):
            for plane in range(BLOCK):
                total = along_x[plane] + sides[field, plane, rows, :]
                value = 0.5 * start[field, plane, rows, :] + (
                    0.5 * get(field, plane) - factor * total
                )
                out[field, plane, spread, :] = value
        return carry

    lax.fori_loop(0, 4, group, 0)


def second_stage(*operands):
    return pl.pallas_call(
        second_kernel,
        out_shape=jax.ShapeDtypeStruct((FIELDS, BLOCK, ROWS, LANES), jnp.float32),
        in_specs=[VMEM] * len(operands),
        out_specs=VMEM,
        compiler_params=params(),
        cost_estimate=cost(30_000_000, 3_000_000),
        name="second_stage",
    )(*operands)


def everyone_max(value, axis, size):
    reach = 1
    while reach * 4 < size:
        reach *= 4
    while reach:
        copies = [value]
        for times in range(1, 4):
            turn = reach * times
            if turn < size:
                pairs = [(i, i ^ turn) for i in range(size)]
                copies.append(lax.ppermute(value, axis, pairs))
        value = functools.reduce(jnp.maximum, copies)
        reach //= 4
    return value


def per_device(blocks, owner_list, slot_list):
    size = lax.axis_size("gx")
    own = lax.axis_index("gx")
    per_dev = blocks.shape[0]
    cap = max(2, 2 * per_dev // size)
    up = [(i, (i + 1) % size) for i in range(size)]
    down = [(j, i) for i, j in up]

    parts = pack(tiled_rows(blocks), owner_list, size, cap, per_dev)
    parts, owner_list, slot_list = lax.optimization_barrier((parts, owner_list, slot_list))
    come = lax.all_to_all(
        parts,
        "gx",
        split_axis=0,
        concat_axis=0,
        tiled=True,
        axis_index_groups=[exchange_order(size)],
    )
    table = arrival_spots(owner_list, slot_list, own, per_dev, size, cap)
    state, low, high, speed = unpack(table, come.reshape(-1, LANES), size, cap)
    below = lax.ppermute(high, "gx", up)
    above = lax.ppermute(low, "gx", down)
    sides = along_planes(state, speed)
    middle, low, high, top = first_stage(state, sides, below, above, speed)
    second = everyone_max(top, "gx", size)
    below = lax.ppermute(high, "gx", up)
    above = lax.ppermute(low, "gx", down)
    sides = along_planes(middle, second)
    return second_stage(state, middle, sides, below, above, speed, second)


def solution(mesh):
    return jax.shard_map(
        per_device,
        mesh=mesh,
        in_specs=(P(("runs", "gx"), None, None), P("runs"), P("runs")),
        out_specs=P(None, ("runs", "gx"), None, None),
        check_vma=False,
    )
```

```python
import functools

import jax
import jax.numpy as jnp
from jax import lax
from jax.experimental import pallas as pl
from jax.experimental.pallas import tpu as pltpu
from jax.sharding import PartitionSpec as P

BLOCK = 8
BY = 4
BZ = 16
FIELDS = 5
LANES = 128
ROWS = BY * BLOCK
PAIRS = BLOCK // 2
TILES = PAIRS * FIELDS

gamma_gas = 1.4
courant = 0.25
smooth_epsilon = 1e-06

VMEM = pl.BlockSpec(memory_space=pltpu.VMEM)
SMEM = pl.BlockSpec(memory_space=pltpu.SMEM)


def params(mebibytes=40):
    return pltpu.CompilerParams(vmem_limit_bytes=mebibytes * 1024 * 1024)


def cost(flops, size):
    return pl.CostEstimate(flops=flops, bytes_accessed=size, transcendentals=0)


def wave_speed(fields):
    density, mom_x, mom_y, mom_z, energy = fields
    inverse = 1.0 / density
    vel = (mom_x * inverse, mom_y * inverse, mom_z * inverse)
    kinetic = 0.5 * (mom_x * vel[0] + mom_y * vel[1] + mom_z * vel[2])
    pressure = (gamma_gas - 1.0) * (energy - kinetic)
    sound = jnp.sqrt(gamma_gas * pressure * inverse)
    fastest = jnp.maximum(jnp.maximum(jnp.abs(vel[0]), jnp.abs(vel[1])), jnp.abs(vel[2]))
    return fastest + sound


def tiled_rows(blocks):
    count = blocks.shape[0] // 8
    groups = blocks.reshape(count, 8, FIELDS, PAIRS, LANES).transpose(2, 0, 3, 1, 4)
    return groups.reshape(FIELDS * count * PAIRS * 8, LANES)


def pack_kernel(
    size, cap, per_dev, owner_hbm, rows_hbm, out_hbm, owner, rows, out, top, count, member, sems
):
    own = lax.axis_index("gx")
    fetch_owner = pltpu.make_async_copy(owner_hbm, owner, sems.at[0])
    fetch_rows = pltpu.make_async_copy(rows_hbm, rows, sems.at[1])
    fetch_owner.start()
    fetch_rows.start()

    def clear(dest, carry):
        count[dest] = 0
        return carry

    lax.fori_loop(0, size, clear, 0, unroll=8)
    fetch_owner.wait()

    def note(block, carry):
        dest = owner[own * per_dev + block]
        rank = count[dest]
        count[dest] = rank + 1
        member[dest * cap + rank] = lax.div(block, 8) * (PAIRS * 8) + lax.rem(block, 8)
        return carry

    lax.fori_loop(0, per_dev, note, 0, unroll=8)
    fetch_rows.wait()
    tiles = TILES * cap

    def message(dest, carry):
        @pl.when(count[dest] > 0)
        def _():
            for rank in range(cap):
                first = member[dest * cap + rank]
                for pair in range(PAIRS):
                    source = pl.ds(first + pair * 8, FIELDS, stride=per_dev * PAIRS)
                    to = dest * tiles + pair * (FIELDS * cap) + rank
                    out[pl.ds(to, FIELDS, stride=cap), :] = rows[source, :]
            part = out.at[pl.ds(pl.multiple_of(dest * tiles, tiles), tiles)]
            pltpu.make_async_copy(part, out_hbm.at[dest, pl.ds(0, tiles), 0], sems.at[2]).start()

        return carry

    lax.fori_loop(0, size, message, 0)
    best = jnp.zeros((8, LANES), jnp.float32)
    step = per_dev * PAIRS
    for first in range(0, step, 8):
        fields = [rows[f * step + first : f * step + first + 8, :] for f in range(FIELDS)]
        best = jnp.maximum(best, wave_speed(fields))
    top[...] = jnp.full(top.shape, jnp.max(best), jnp.float32)
    for dest in range(size):
        pltpu.make_async_copy(
            top.at[pl.ds(dest, 1)], out_hbm.at[dest, tiles], sems.at[3]
        ).start()
    half = out.at[pl.ds(0, per_dev * TILES)]
    pltpu.make_async_copy(half, half, sems.at[2]).wait()
    pltpu.make_async_copy(top, top, sems.at[3]).wait()


def pack(rows, owner_list, size, cap, per_dev):
    return pl.pallas_call(
        functools.partial(pack_kernel, size, cap, per_dev),
        out_shape=jax.ShapeDtypeStruct((size, TILES * cap + 1, 1, LANES), jnp.float32),
        in_specs=[pl.BlockSpec(memory_space=pltpu.HBM)] * 2,
        out_specs=pl.BlockSpec(memory_space=pltpu.HBM),
        scratch_shapes=[
            pltpu.SMEM(owner_list.shape, jnp.int32),
            pltpu.VMEM(rows.shape, jnp.float32),
            pltpu.VMEM((size * TILES * cap, LANES), jnp.float32),
            pltpu.VMEM((size, LANES), jnp.float32),
            pltpu.SMEM((size,), jnp.int32),
            pltpu.SMEM((size * cap,), jnp.int32),
            pltpu.SemaphoreType.DMA((4,)),
        ],
        compiler_params=params(62),
        cost_estimate=cost(1_000_000, 3_000_000),
        name="pack",
    )(owner_list, rows)


def arrival_spots(owner_list, slot_list, own, per_dev, size, cap):
    owners = owner_list.reshape(size, per_dev)
    slots = slot_list.reshape(size, per_dev)
    mine = owners == own
    spot = jnp.arange(per_dev, dtype=jnp.int32)
    earlier = spot[None, :] < spot[:, None]
    rank = jnp.sum((mine[:, None, :] & earlier[None]).astype(jnp.int32), axis=2)
    row = jnp.arange(size, dtype=jnp.int32)[:, None] * cap + rank
    key = jnp.where(mine, slots, -1)
    hit = key.reshape(1, -1) == spot[:, None]
    return jnp.max(jnp.where(hit, row.reshape(1, -1), 0), axis=1)


def exchanged_bits(rows, group):
    rows = list(rows)
    for bit in range(4):
        step = 1 << bit
        low = (group & step) == 0
        for index in range(16):
            if index & step:
                continue
            first, second = rows[index], rows[index | step]
            rows[index] = jnp.where(low, first, pltpu.roll(second, 8 * step, 1))
            rows[index | step] = jnp.where(low, pltpu.roll(first, LANES - 8 * step, 1), second)
    return rows


def unpack_kernel(size, cap, couple, table, come, state, halo, *refs):
    message = TILES * cap + 1
    scratch = refs[-1]
    if couple == 0:
        best = come[message - 1 : message, :]
        for source in range(1, size):
            best = jnp.maximum(best, come[(source + 1) * message - 1 : (source + 1) * message, :])
        refs[0][...] = jnp.broadcast_to(best, refs[0].shape)
    for slot in range(BY * BZ):
        p, q = divmod(slot, BZ)
        where = table[slot]
        source = lax.div(where, cap)
        rank = lax.rem(where, cap)
        for h in range(2):
            base = source * message + rank + (2 * couple + h) * (FIELDS * cap)
            value = come[pl.ds(base, FIELDS, stride=cap), :]
            scratch[pl.ds(q * 8 + 2 * p + h, FIELDS, stride=BZ * 8), :] = value
    group = lax.broadcasted_iota(jnp.int32, (8, LANES), 1) // BLOCK
    even = lax.broadcasted_iota(jnp.int32, (8, LANES), 0) % 2 == 0

    for f in range(FIELDS):
        first = f * BZ * 8
        rows = [scratch[first + q * 8 : first + q * 8 + 8, :] for q in range(BZ)]
        moved = exchanged_bits(rows, group)
        for second in range(2):
            for j in range(4):
                lower = moved[second * BLOCK + j]
                upper = moved[second * BLOCK + j + 4]
                planes = (
                    jnp.where(even, lower, pltpu.roll(upper, 1, 0)),
                    jnp.where(even, pltpu.roll(lower, 7, 0), upper),
                )
                rows = slice(j * 8, j * 8 + 8)
                for h in range(2):
                    plane = 2 * h + second
                    state[f, plane, rows, :] = planes[h]
                    at = plane - couple
                    if 0 <= at < 3:
                        halo[f, at, rows, :] = planes[h]


def unpack(table, come, couple, size, cap):
    shapes = [
        jax.ShapeDtypeStruct((FIELDS, 4, ROWS, LANES), jnp.float32),
        jax.ShapeDtypeStruct((FIELDS, 3, ROWS, LANES), jnp.float32),
    ]
    if couple == 0:
        shapes.append(jax.ShapeDtypeStruct((8, LANES), jnp.float32))
    return pl.pallas_call(
        functools.partial(unpack_kernel, size, cap, couple),
        out_shape=shapes,
        in_specs=[SMEM, VMEM],
        out_specs=[VMEM] * len(shapes),
        scratch_shapes=[pltpu.VMEM((FIELDS * BZ * 8, LANES), jnp.float32)],
        compiler_params=params(),
        cost_estimate=cost(5_000_000, 2_000_000),
        name="unpack",
    )(table, come)


def y_up(x):
    return jnp.concatenate([x[8:], pltpu.roll(x[:8], 7, 0)], axis=0)


def y_down(x):
    return jnp.concatenate([pltpu.roll(x[24:], 1, 0), x[:24]], axis=0)


def y_up_two(x):
    return jnp.concatenate([x[16:], pltpu.roll(x[:8], 7, 0), pltpu.roll(x[8:16], 7, 0)], axis=0)


def inverse(x):
    return 1.0 / x


def smoothness(before, after):
    curve = after - before
    middle = 0.5 * (after + before)
    base = curve * curve * (13.0 / 12.0) + smooth_epsilon
    plus = middle + curve
    minus = middle - curve
    left = inverse(base + plus * plus)
    centre = inverse(base + middle * middle)
    right = inverse(base + minus * minus)
    return curve, left * left, centre * centre, right * right


def upwind_term(left, centre, right, jump_before, jump_after):
    right = 3.0 * right
    top = left * (jump_before + jump_before) + right * jump_after
    return top * inverse(left + 6.0 * centre + right)


def periodic_divergence(half_flux, scaled, up, up_two, down):
    plus = half_flux + scaled
    minus = half_flux - scaled

    def side(values):
        after = up(values) - values
        curve, left, centre, right = smoothness(down(after), after)
        above = up(curve)
        return curve, above, left, centre, right, above - curve

    curve, _, left, centre, right, jump = side(plus)
    face = 6.0 * (half_flux + up(half_flux)) - curve
    face = face - upwind_term(down(left), centre, up(right), down(jump), jump)
    _, curve, left, centre, right, jump = side(minus)
    face = face + (upwind_term(up_two(right), up(centre), left, up(jump), jump) - curve)
    return face - down(face)


def ring_divergence(half_flux, scaled):
    count = len(half_flux)

    def up(values):
        return values[1:] + [pltpu.roll(values[0], 7, 0)]

    def down(values):
        return [pltpu.roll(values[-1], 1, 0)] + values[:-1]

    def side(values):
        after = [above - value for above, value in zip(up(values), values)]
        parts = [smoothness(before, step) for before, step in zip(down(after), after)]
        curve, left, centre, right = (list(part) for part in zip(*parts))
        jump = [above - value for above, value in zip(up(curve), curve)]
        return curve, left, centre, right, jump

    curve, left, centre, right, jump = side([a + b for a, b in zip(half_flux, scaled)])
    terms = zip(down(left), centre, up(right), down(jump), jump)
    face = [
        6.0 * (here + above) - bend - upwind_term(*term)
        for here, above, bend, term in zip(half_flux, up(half_flux), curve, terms)
    ]
    curve, left, centre, right, jump = side([a - b for a, b in zip(half_flux, scaled)])
    terms = zip(up(right), centre, down(left), jump, down(jump))
    other = [upwind_term(*term) - bend for bend, term in zip(curve, terms)]
    face = [one + two for one, two in zip(face, up(other))]
    return [here - below for here, below in zip(face, down(face))]


def open_divergence(half_flux, scaled):
    count = len(half_flux)
    plus = [a + b for a, b in zip(half_flux, scaled)]
    minus = [a - b for a, b in zip(half_flux, scaled)]
    faces = [None] * count

    def side(values):
        steps = [values[i + 1] - values[i] for i in range(count - 1)]
        parts = [None] + [smoothness(steps[i - 1], steps[i]) for i in range(1, count - 1)]
        return parts

    parts = side(plus)
    for i in range(2, count - 3):
        jump_before = parts[i][0] - parts[i - 1][0]
        jump_after = parts[i + 1][0] - parts[i][0]
        faces[i] = 6.0 * (half_flux[i] + half_flux[i + 1]) - parts[i][0] - upwind_term(
            parts[i - 1][1], parts[i][2], parts[i + 1][3], jump_before, jump_after
        )
    parts = side(minus)
    for i in range(3, count - 2):
        jump_before = parts[i][0] - parts[i - 1][0]
        jump_after = parts[i + 1][0] - parts[i][0]
        faces[i - 1] = faces[i - 1] + (
            upwind_term(parts[i + 1][3], parts[i][2], parts[i - 1][1], jump_after, jump_before)
            - parts[i][0]
        )
    return [faces[i] - faces[i - 1] for i in range(3, count - 3)]


def half_velocities(fields):
    density, mom_x, mom_y, mom_z, energy = fields
    over = 0.5 / density
    vel = (mom_x * over, mom_y * over, mom_z * over)
    kinetic = mom_x * vel[0] + mom_y * vel[1] + mom_z * vel[2]
    pressure = (gamma_gas - 1.0) * (energy - kinetic)
    return vel, pressure


def half_flux(fields, field, direction, speed, pressure):
    if field == 0:
        return 0.5 * fields[1 + direction]
    if field == 4:
        return (fields[4] + pressure) * speed
    flux = fields[field] * speed
    return flux + 0.5 * pressure if field == 1 + direction else flux


def plane_kernel(state_low, state_high, speed, out, turned):
    half_speed = 0.5 * speed[0:1, :]
    lane = lax.broadcasted_iota(jnp.int32, (LANES, LANES), 1)
    to_turned = (lane % 8) * 16 + lane // 8
    to_plain = (lane % 16) * 8 + lane // 16

    for part, state in enumerate((state_low, state_high)):
        for f in range(FIELDS):
            plain = state[f].reshape(LANES, LANES)
            turned[f] = jnp.take_along_axis(plain, to_turned, axis=1).T
        for place in range(4):
            fields = [state[f, place] for f in range(FIELDS)]
            vel, pressure = half_velocities(fields)
            for field in range(FIELDS):
                out[field, part * 4 + place] = periodic_divergence(
                    half_flux(fields, field, 1, vel[1], pressure),
                    half_speed * fields[field],
                    y_up,
                    y_up_two,
                    y_down,
                )
        columns = [
            [turned[f, row : row + 8] for row in range(0, LANES, 8)] for f in range(FIELDS)
        ]
        along = [half_velocities(fields) for fields in zip(*columns)]
        for field in range(FIELDS):
            fluxes = [
                half_flux(fields, field, 2, vel[2], pressure)
                for fields, (vel, pressure) in zip(zip(*columns), along)
            ]
            scaled = [half_speed * value for value in columns[field]]
            total = jnp.concatenate(ring_divergence(fluxes, scaled), axis=0)
            plain = jnp.take_along_axis(total.T, to_plain, axis=1)
            out[field, part * 4 : part * 4 + 4] += plain.reshape(4, ROWS, LANES)


def along_planes(state_low, state_high, speed):
    return pl.pallas_call(
        plane_kernel,
        out_shape=jax.ShapeDtypeStruct((FIELDS, BLOCK, ROWS, LANES), jnp.float32),
        in_specs=[VMEM] * 3,
        out_specs=VMEM,
        scratch_shapes=[pltpu.VMEM((FIELDS, LANES, LANES), jnp.float32)],
        compiler_params=params(),
        cost_estimate=cost(20_000_000, 1_000_000),
        name="planes",
    )(state_low, state_high, speed)


def across(get, half_speed):
    span = range(-3, BLOCK + 3)
    speeds, pressures = [], []
    for plane in span:
        vel, pressure = half_velocities([get(f, plane) for f in range(FIELDS)])
        speeds.append(vel[0])
        pressures.append(pressure)
    for field in range(FIELDS):
        fluxes, scaled = [], []
        for i, plane in enumerate(span):
            if field == 0:
                flux = 0.5 * get(1, plane)
            elif field == 4:
                flux = (get(4, plane) + pressures[i]) * speeds[i]
            else:
                flux = get(field, plane) * speeds[i]
                if field == 1:
                    flux = flux + 0.5 * pressures[i]
            fluxes.append(flux)
            scaled.append(half_speed * get(field, plane))
        yield field, open_divergence(fluxes, scaled)


def slab(state_low, state_high, below, above, rows):
    def get(f, plane):
        if plane < 0:
            return below[f, plane + 3, rows, :]
        if plane >= BLOCK:
            return above[f, plane - BLOCK, rows, :]
        return (state_low, state_high)[plane // 4][f, plane % 4, rows, :]

    return get


def first_kernel(
    state_low, state_high, sides, below, above, speed, middle_low, middle_high, low, high
):
    half_speed = 0.5 * speed[0:1, :]
    factor = (courant / 6.0) / speed[0:1, :]
    middle = (middle_low, middle_high)

    def group(j, carry):
        rows = pl.ds(pl.multiple_of(j * 8, 8), 8)
        get = slab(state_low, state_high, below, above, rows)
        for field, along_x in across(get, half_speed):
            for plane in range(BLOCK):
                total = along_x[plane] + sides[field, plane, rows, :]
                value = get(field, plane) - factor * total
                middle[plane // 4][field, plane % 4, rows, :] = value
                if plane < 3:
                    low[field, plane, rows, :] = value
                if plane >= 5:
                    high[field, plane - 5, rows, :] = value
        return carry

    lax.fori_loop(0, 4, group, 0)


def first_stage(*operands):
    part = jax.ShapeDtypeStruct((FIELDS, 4, ROWS, LANES), jnp.float32)
    halo = jax.ShapeDtypeStruct((FIELDS, 3, ROWS, LANES), jnp.float32)
    return pl.pallas_call(
        first_kernel,
        out_shape=(part, part, halo, halo),
        in_specs=[VMEM] * len(operands),
        out_specs=(VMEM,) * 4,
        compiler_params=params(),
        cost_estimate=cost(30_000_000, 3_000_000),
        name="first_stage",
    )(*operands)


def fastest_kernel(middle_low, middle_high, top):
    best = jnp.zeros((8, LANES), jnp.float32)
    for part in (middle_low, middle_high):
        for plane in range(4):
            for row in range(0, ROWS, 8):
                fields = [part[f, plane, row : row + 8, :] for f in range(FIELDS)]
                best = jnp.maximum(best, wave_speed(fields))
    top[...] = jnp.full(top.shape, jnp.max(best), jnp.float32)


def fastest(*parts):
    return pl.pallas_call(
        fastest_kernel,
        out_shape=jax.ShapeDtypeStruct((8, LANES), jnp.float32),
        in_specs=[VMEM] * 2,
        out_specs=VMEM,
        compiler_params=params(),
        cost_estimate=cost(1_000_000_000, 100_000_000),
        name="fastest",
    )(*parts)


def second_kernel(
    state_low, state_high, middle_low, middle_high, sides, below, above, first_speed, speed, out
):
    half_speed = 0.5 * speed[0:1, :]
    factor = (courant / 12.0) / first_speed[0:1, :]

    def group(j, carry):
        rows = pl.ds(pl.multiple_of(j * 8, 8), 8)
        spread = pl.ds(j, 8, stride=4)

        get = slab(middle_low, middle_high, below, above, rows)
        for field, along_x in across(get, half_speed):
            for plane in range(BLOCK):
                total = along_x[plane] + sides[field, plane, rows, :]
                start = (state_low, state_high)[plane // 4][field, plane % 4, rows, :]
                value = 0.5 * start + (0.5 * get(field, plane) - factor * total)
                out[field, plane, spread, :] = value
        return carry

    lax.fori_loop(0, 4, group, 0)


def second_stage(*operands):
    return pl.pallas_call(
        second_kernel,
        out_shape=jax.ShapeDtypeStruct((FIELDS, BLOCK, ROWS, LANES), jnp.float32),
        in_specs=[VMEM] * len(operands),
        out_specs=VMEM,
        compiler_params=params(),
        cost_estimate=cost(30_000_000, 3_000_000),
        name="second_stage",
    )(*operands)


def everyone_max(value, axis, size):
    reach = 1
    while reach * 4 < size:
        reach *= 4
    while reach:
        copies = [value]
        for times in range(1, 4):
            turn = reach * times
            if turn < size:
                pairs = [(i, i ^ turn) for i in range(size)]
                copies.append(lax.ppermute(value, axis, pairs))
        value = functools.reduce(jnp.maximum, copies)
        reach //= 4
    return value


def per_device(blocks, owner_list, slot_list):
    size = lax.axis_size("gx")
    own = lax.axis_index("gx")
    per_dev = blocks.shape[0]
    cap = max(2, 2 * per_dev // size)
    up = [(i, (i + 1) % size) for i in range(size)]
    down = [(j, i) for i, j in up]

    parts = pack(tiled_rows(blocks), owner_list, size, cap, per_dev)
    parts, owner_list, slot_list = lax.optimization_barrier((parts, owner_list, slot_list))
    come = lax.all_to_all(parts, "gx", split_axis=0, concat_axis=0, tiled=True)
    table = arrival_spots(owner_list, slot_list, own, per_dev, size, cap)
    come = come.reshape(-1, LANES)
    state_low, low, speed = unpack(table, come, 0, size, cap)
    above = lax.ppermute(low, "gx", down)
    state_high, high = unpack(table, come, 1, size, cap)
    below = lax.ppermute(high, "gx", up)
    state = (state_low, state_high)
    sides = along_planes(*state, speed)
    *middle, low, high = first_stage(*state, sides, below, above, speed)
    below = lax.ppermute(high, "gx", up)
    above = lax.ppermute(low, "gx", down)
    second = everyone_max(fastest(*middle), "gx", size)
    sides = along_planes(*middle, second)
    return second_stage(*state, *middle, sides, below, above, speed, second)


def solution(mesh):
    return jax.shard_map(
        per_device,
        mesh=mesh,
        in_specs=(P(("runs", "gx"), None, None), P("runs"), P("runs")),
        out_specs=P(None, ("runs", "gx"), None, None),
        check_vma=False,
    )
```

```python
import functools

import jax
import jax.numpy as jnp
from jax import lax
from jax.experimental import pallas as pl
from jax.experimental.pallas import tpu as pltpu
from jax.sharding import PartitionSpec as P

BLOCK = 8
BY = 4
BZ = 16
FIELDS = 5
LANES = 128
ROWS = BY * BLOCK
PAIRS = BLOCK // 2
TILES = PAIRS * FIELDS

gamma_gas = 1.4
courant = 0.25
smooth_epsilon = 1e-06

VMEM = pl.BlockSpec(memory_space=pltpu.VMEM)
SMEM = pl.BlockSpec(memory_space=pltpu.SMEM)


def params(mebibytes=40):
    return pltpu.CompilerParams(vmem_limit_bytes=mebibytes * 1024 * 1024)


def cost(flops, size):
    return pl.CostEstimate(flops=flops, bytes_accessed=size, transcendentals=0)


def wave_speed(fields):
    density, mom_x, mom_y, mom_z, energy = fields
    inverse = 1.0 / density
    vel = (mom_x * inverse, mom_y * inverse, mom_z * inverse)
    kinetic = 0.5 * (mom_x * vel[0] + mom_y * vel[1] + mom_z * vel[2])
    pressure = (gamma_gas - 1.0) * (energy - kinetic)
    sound = jnp.sqrt(gamma_gas * pressure * inverse)
    fastest = jnp.maximum(jnp.maximum(jnp.abs(vel[0]), jnp.abs(vel[1])), jnp.abs(vel[2]))
    return fastest + sound


def tiled_rows(blocks):
    count = blocks.shape[0] // 8
    groups = blocks.reshape(count, 8, FIELDS, PAIRS, LANES).transpose(2, 0, 3, 1, 4)
    return groups.reshape(FIELDS * count * PAIRS * 8, LANES)


def pack_kernel(
    size, cap, per_dev, owner_hbm, rows_hbm, out_hbm, owner, rows, out, top, count, member, sems
):
    own = lax.axis_index("gx")
    fetch_owner = pltpu.make_async_copy(owner_hbm, owner, sems.at[0])
    fetch_rows = pltpu.make_async_copy(rows_hbm, rows, sems.at[1])
    fetch_owner.start()
    fetch_rows.start()

    def clear(dest, carry):
        count[dest] = 0
        return carry

    lax.fori_loop(0, size, clear, 0, unroll=8)
    fetch_owner.wait()

    def note(block, carry):
        dest = owner[own * per_dev + block]
        rank = count[dest]
        count[dest] = rank + 1
        member[dest * cap + rank] = lax.div(block, 8) * (PAIRS * 8) + lax.rem(block, 8)
        return carry

    lax.fori_loop(0, per_dev, note, 0, unroll=8)
    fetch_rows.wait()
    tiles = TILES * cap

    def message(dest, carry):
        @pl.when(count[dest] > 0)
        def _():
            for rank in range(cap):
                first = member[dest * cap + rank]
                for pair in range(PAIRS):
                    source = pl.ds(first + pair * 8, FIELDS, stride=per_dev * PAIRS)
                    to = dest * tiles + pair * (FIELDS * cap) + rank
                    out[pl.ds(to, FIELDS, stride=cap), :] = rows[source, :]
            part = out.at[pl.ds(pl.multiple_of(dest * tiles, tiles), tiles)]
            pltpu.make_async_copy(part, out_hbm.at[dest, pl.ds(0, tiles), 0], sems.at[2]).start()

        return carry

    lax.fori_loop(0, size, message, 0)
    best = jnp.zeros((8, LANES), jnp.float32)
    step = per_dev * PAIRS
    for first in range(0, step, 8):
        fields = [rows[f * step + first : f * step + first + 8, :] for f in range(FIELDS)]
        best = jnp.maximum(best, wave_speed(fields))
    top[...] = jnp.full(top.shape, jnp.max(best), jnp.float32)
    for dest in range(size):
        pltpu.make_async_copy(
            top.at[pl.ds(dest, 1)], out_hbm.at[dest, tiles], sems.at[3]
        ).start()
    half = out.at[pl.ds(0, per_dev * TILES)]
    pltpu.make_async_copy(half, half, sems.at[2]).wait()
    pltpu.make_async_copy(top, top, sems.at[3]).wait()


def pack(rows, owner_list, size, cap, per_dev):
    return pl.pallas_call(
        functools.partial(pack_kernel, size, cap, per_dev),
        out_shape=jax.ShapeDtypeStruct((size, TILES * cap + 1, 1, LANES), jnp.float32),
        in_specs=[pl.BlockSpec(memory_space=pltpu.HBM)] * 2,
        out_specs=pl.BlockSpec(memory_space=pltpu.HBM),
        scratch_shapes=[
            pltpu.SMEM(owner_list.shape, jnp.int32),
            pltpu.VMEM(rows.shape, jnp.float32),
            pltpu.VMEM((size * TILES * cap, LANES), jnp.float32),
            pltpu.VMEM((size, LANES), jnp.float32),
            pltpu.SMEM((size,), jnp.int32),
            pltpu.SMEM((size * cap,), jnp.int32),
            pltpu.SemaphoreType.DMA((4,)),
        ],
        compiler_params=params(62),
        cost_estimate=cost(1_000_000, 3_000_000),
        name="pack",
    )(owner_list, rows)


def arrival_spots(owner_list, slot_list, own, per_dev, size, cap):
    owners = owner_list.reshape(size, per_dev)
    slots = slot_list.reshape(size, per_dev)
    mine = owners == own
    spot = jnp.arange(per_dev, dtype=jnp.int32)
    earlier = spot[None, :] < spot[:, None]
    rank = jnp.sum((mine[:, None, :] & earlier[None]).astype(jnp.int32), axis=2)
    row = jnp.arange(size, dtype=jnp.int32)[:, None] * cap + rank
    key = jnp.where(mine, slots, -1)
    hit = key.reshape(1, -1) == spot[:, None]
    return jnp.max(jnp.where(hit, row.reshape(1, -1), 0), axis=1)


def exchanged_bits(rows, group):
    rows = list(rows)
    for bit in range(4):
        step = 1 << bit
        low = (group & step) == 0
        for index in range(16):
            if index & step:
                continue
            first, second = rows[index], rows[index | step]
            rows[index] = jnp.where(low, first, pltpu.roll(second, 8 * step, 1))
            rows[index | step] = jnp.where(low, pltpu.roll(first, LANES - 8 * step, 1), second)
    return rows


def unpack_kernel(size, cap, couple, table, come, state, halo, *refs):
    message = TILES * cap + 1
    scratch = refs[-1]
    if couple == 0:
        best = come[message - 1 : message, :]
        for source in range(1, size):
            best = jnp.maximum(best, come[(source + 1) * message - 1 : (source + 1) * message, :])
        refs[0][...] = jnp.broadcast_to(best, refs[0].shape)
    for slot in range(BY * BZ):
        p, q = divmod(slot, BZ)
        where = table[slot]
        source = lax.div(where, cap)
        rank = lax.rem(where, cap)
        for h in range(2):
            base = source * message + rank + (2 * couple + h) * (FIELDS * cap)
            value = come[pl.ds(base, FIELDS, stride=cap), :]
            scratch[pl.ds(q * 8 + 2 * p + h, FIELDS, stride=BZ * 8), :] = value
    group = lax.broadcasted_iota(jnp.int32, (8, LANES), 1) // BLOCK
    even = lax.broadcasted_iota(jnp.int32, (8, LANES), 0) % 2 == 0

    for f in range(FIELDS):
        first = f * BZ * 8
        rows = [scratch[first + q * 8 : first + q * 8 + 8, :] for q in range(BZ)]
        moved = exchanged_bits(rows, group)
        for second in range(2):
            for j in range(4):
                lower = moved[second * BLOCK + j]
                upper = moved[second * BLOCK + j + 4]
                planes = (
                    jnp.where(even, lower, pltpu.roll(upper, 1, 0)),
                    jnp.where(even, pltpu.roll(lower, 7, 0), upper),
                )
                rows = slice(j * 8, j * 8 + 8)
                for h in range(2):
                    plane = 2 * h + second
                    state[f, plane, rows, :] = planes[h]
                    at = plane - couple
                    if 0 <= at < 3:
                        halo[f, at, rows, :] = planes[h]


def unpack(table, come, couple, size, cap):
    shapes = [
        jax.ShapeDtypeStruct((FIELDS, 4, ROWS, LANES), jnp.float32),
        jax.ShapeDtypeStruct((FIELDS, 3, ROWS, LANES), jnp.float32),
    ]
    if couple == 0:
        shapes.append(jax.ShapeDtypeStruct((8, LANES), jnp.float32))
    return pl.pallas_call(
        functools.partial(unpack_kernel, size, cap, couple),
        out_shape=shapes,
        in_specs=[SMEM, VMEM],
        out_specs=[VMEM] * len(shapes),
        scratch_shapes=[pltpu.VMEM((FIELDS * BZ * 8, LANES), jnp.float32)],
        compiler_params=params(),
        cost_estimate=cost(1_000_000_000, 100_000_000),
        name="unpack",
    )(table, come)


def y_up(x):
    return jnp.concatenate([x[8:], pltpu.roll(x[:8], 7, 0)], axis=0)


def y_down(x):
    return jnp.concatenate([pltpu.roll(x[24:], 1, 0), x[:24]], axis=0)


def y_up_two(x):
    return jnp.concatenate([x[16:], pltpu.roll(x[:8], 7, 0), pltpu.roll(x[8:16], 7, 0)], axis=0)


def inverse(x):
    return 1.0 / x


def smoothness(before, after):
    curve = after - before
    middle = 0.5 * (after + before)
    base = curve * curve * (13.0 / 12.0) + smooth_epsilon
    plus = middle + curve
    minus = middle - curve
    left = inverse(base + plus * plus)
    centre = inverse(base + middle * middle)
    right = inverse(base + minus * minus)
    return curve, left * left, centre * centre, right * right


def upwind_term(left, centre, right, jump_before, jump_after):
    right = 3.0 * right
    top = left * (jump_before + jump_before) + right * jump_after
    return top * inverse(left + 6.0 * centre + right)


def periodic_divergence(half_flux, scaled, up, up_two, down):
    plus = half_flux + scaled
    minus = half_flux - scaled

    def side(values):
        after = up(values) - values
        curve, left, centre, right = smoothness(down(after), after)
        above = up(curve)
        return curve, above, left, centre, right, above - curve

    curve, _, left, centre, right, jump = side(plus)
    face = 6.0 * (half_flux + up(half_flux)) - curve
    face = face - upwind_term(down(left), centre, up(right), down(jump), jump)
    _, curve, left, centre, right, jump = side(minus)
    face = face + (upwind_term(up_two(right), up(centre), left, up(jump), jump) - curve)
    return face - down(face)


def ring_divergence(half_flux, scaled):
    count = len(half_flux)

    def up(values):
        return values[1:] + [pltpu.roll(values[0], 7, 0)]

    def down(values):
        return [pltpu.roll(values[-1], 1, 0)] + values[:-1]

    def side(values):
        after = [above - value for above, value in zip(up(values), values)]
        parts = [smoothness(before, step) for before, step in zip(down(after), after)]
        curve, left, centre, right = (list(part) for part in zip(*parts))
        jump = [above - value for above, value in zip(up(curve), curve)]
        return curve, left, centre, right, jump

    curve, left, centre, right, jump = side([a + b for a, b in zip(half_flux, scaled)])
    terms = zip(down(left), centre, up(right), down(jump), jump)
    face = [
        6.0 * (here + above) - bend - upwind_term(*term)
        for here, above, bend, term in zip(half_flux, up(half_flux), curve, terms)
    ]
    curve, left, centre, right, jump = side([a - b for a, b in zip(half_flux, scaled)])
    terms = zip(up(right), centre, down(left), jump, down(jump))
    other = [upwind_term(*term) - bend for bend, term in zip(curve, terms)]
    face = [one + two for one, two in zip(face, up(other))]
    return [here - below for here, below in zip(face, down(face))]


def open_divergence(half_flux, scaled):
    count = len(half_flux)
    plus = [a + b for a, b in zip(half_flux, scaled)]
    minus = [a - b for a, b in zip(half_flux, scaled)]
    faces = [None] * count

    def side(values):
        steps = [values[i + 1] - values[i] for i in range(count - 1)]
        parts = [None] + [smoothness(steps[i - 1], steps[i]) for i in range(1, count - 1)]
        return parts

    parts = side(plus)
    for i in range(2, count - 3):
        jump_before = parts[i][0] - parts[i - 1][0]
        jump_after = parts[i + 1][0] - parts[i][0]
        faces[i] = 6.0 * (half_flux[i] + half_flux[i + 1]) - parts[i][0] - upwind_term(
            parts[i - 1][1], parts[i][2], parts[i + 1][3], jump_before, jump_after
        )
    parts = side(minus)
    for i in range(3, count - 2):
        jump_before = parts[i][0] - parts[i - 1][0]
        jump_after = parts[i + 1][0] - parts[i][0]
        faces[i - 1] = faces[i - 1] + (
            upwind_term(parts[i + 1][3], parts[i][2], parts[i - 1][1], jump_after, jump_before)
            - parts[i][0]
        )
    return [faces[i] - faces[i - 1] for i in range(3, count - 3)]


def half_velocities(fields):
    density, mom_x, mom_y, mom_z, energy = fields
    over = 0.5 / density
    vel = (mom_x * over, mom_y * over, mom_z * over)
    kinetic = mom_x * vel[0] + mom_y * vel[1] + mom_z * vel[2]
    pressure = (gamma_gas - 1.0) * (energy - kinetic)
    return vel, pressure


def half_flux(fields, field, direction, speed, pressure):
    if field == 0:
        return 0.5 * fields[1 + direction]
    if field == 4:
        return (fields[4] + pressure) * speed
    flux = fields[field] * speed
    return flux + 0.5 * pressure if field == 1 + direction else flux


def plane_kernel(state_low, state_high, speed, out, turned):
    half_speed = 0.5 * speed[0:1, :]
    lane = lax.broadcasted_iota(jnp.int32, (LANES, LANES), 1)
    to_turned = (lane % 8) * 16 + lane // 8
    to_plain = (lane % 16) * 8 + lane // 16

    for part, state in enumerate((state_low, state_high)):
        for f in range(FIELDS):
            plain = state[f].reshape(LANES, LANES)
            turned[f] = jnp.take_along_axis(plain, to_turned, axis=1).T
        for place in range(4):
            fields = [state[f, place] for f in range(FIELDS)]
            vel, pressure = half_velocities(fields)
            for field in range(FIELDS):
                out[field, part * 4 + place] = periodic_divergence(
                    half_flux(fields, field, 1, vel[1], pressure),
                    half_speed * fields[field],
                    y_up,
                    y_up_two,
                    y_down,
                )
        columns = [
            [turned[f, row : row + 8] for row in range(0, LANES, 8)] for f in range(FIELDS)
        ]
        along = [half_velocities(fields) for fields in zip(*columns)]
        for field in range(FIELDS):
            fluxes = [
                half_flux(fields, field, 2, vel[2], pressure)
                for fields, (vel, pressure) in zip(zip(*columns), along)
            ]
            scaled = [half_speed * value for value in columns[field]]
            total = jnp.concatenate(ring_divergence(fluxes, scaled), axis=0)
            plain = jnp.take_along_axis(total.T, to_plain, axis=1)
            out[field, part * 4 : part * 4 + 4] += plain.reshape(4, ROWS, LANES)


def along_planes(state_low, state_high, speed):
    return pl.pallas_call(
        plane_kernel,
        out_shape=jax.ShapeDtypeStruct((FIELDS, BLOCK, ROWS, LANES), jnp.float32),
        in_specs=[VMEM] * 3,
        out_specs=VMEM,
        scratch_shapes=[pltpu.VMEM((FIELDS, LANES, LANES), jnp.float32)],
        compiler_params=params(),
        cost_estimate=cost(1, 1),
        name="planes",
    )(state_low, state_high, speed)


def across(get, half_speed):
    span = range(-3, BLOCK + 3)
    speeds, pressures = [], []
    for plane in span:
        vel, pressure = half_velocities([get(f, plane) for f in range(FIELDS)])
        speeds.append(vel[0])
        pressures.append(pressure)
    for field in range(FIELDS):
        fluxes, scaled = [], []
        for i, plane in enumerate(span):
            if field == 0:
                flux = 0.5 * get(1, plane)
            elif field == 4:
                flux = (get(4, plane) + pressures[i]) * speeds[i]
            else:
                flux = get(field, plane) * speeds[i]
                if field == 1:
                    flux = flux + 0.5 * pressures[i]
            fluxes.append(flux)
            scaled.append(half_speed * get(field, plane))
        yield field, open_divergence(fluxes, scaled)


def slab(state_low, state_high, below, above, rows):
    def get(f, plane):
        if plane < 0:
            return below[f, plane + 3, rows, :]
        if plane >= BLOCK:
            return above[f, plane - BLOCK, rows, :]
        return (state_low, state_high)[plane // 4][f, plane % 4, rows, :]

    return get


def first_kernel(
    state_low, state_high, sides, below, above, speed, middle_low, middle_high, low, high
):
    half_speed = 0.5 * speed[0:1, :]
    factor = (courant / 6.0) / speed[0:1, :]
    middle = (middle_low, middle_high)

    def group(j, carry):
        rows = pl.ds(pl.multiple_of(j * 8, 8), 8)
        get = slab(state_low, state_high, below, above, rows)
        for field, along_x in across(get, half_speed):
            for plane in range(BLOCK):
                total = along_x[plane] + sides[field, plane, rows, :]
                value = get(field, plane) - factor * total
                middle[plane // 4][field, plane % 4, rows, :] = value
                if plane < 3:
                    low[field, plane, rows, :] = value
                if plane >= 5:
                    high[field, plane - 5, rows, :] = value
        return carry

    lax.fori_loop(0, 4, group, 0)


def first_stage(*operands):
    part = jax.ShapeDtypeStruct((FIELDS, 4, ROWS, LANES), jnp.float32)
    halo = jax.ShapeDtypeStruct((FIELDS, 3, ROWS, LANES), jnp.float32)
    return pl.pallas_call(
        first_kernel,
        out_shape=(part, part, halo, halo),
        in_specs=[VMEM] * len(operands),
        out_specs=(VMEM,) * 4,
        compiler_params=params(),
        cost_estimate=cost(30_000_000, 3_000_000),
        name="first_stage",
    )(*operands)


def fastest_kernel(middle_low, middle_high, top):
    best = jnp.zeros((8, LANES), jnp.float32)
    for part in (middle_low, middle_high):
        for plane in range(4):
            for row in range(0, ROWS, 8):
                fields = [part[f, plane, row : row + 8, :] for f in range(FIELDS)]
                best = jnp.maximum(best, wave_speed(fields))
    top[...] = jnp.full(top.shape, jnp.max(best), jnp.float32)


def fastest(*parts):
    return pl.pallas_call(
        fastest_kernel,
        out_shape=jax.ShapeDtypeStruct((8, LANES), jnp.float32),
        in_specs=[VMEM] * 2,
        out_specs=VMEM,
        compiler_params=params(),
        cost_estimate=cost(1_000_000_000, 100_000_000),
        name="fastest",
    )(*parts)


def second_kernel(
    state_low, state_high, middle_low, middle_high, sides, below, above, first_speed, speed, out
):
    half_speed = 0.5 * speed[0:1, :]
    factor = (courant / 12.0) / first_speed[0:1, :]

    def group(j, carry):
        rows = pl.ds(pl.multiple_of(j * 8, 8), 8)
        spread = pl.ds(j, 8, stride=4)

        get = slab(middle_low, middle_high, below, above, rows)
        for field, along_x in across(get, half_speed):
            for plane in range(BLOCK):
                total = along_x[plane] + sides[field, plane, rows, :]
                start = (state_low, state_high)[plane // 4][field, plane % 4, rows, :]
                value = 0.5 * start + (0.5 * get(field, plane) - factor * total)
                out[field, plane, spread, :] = value
        return carry

    lax.fori_loop(0, 4, group, 0)


def second_stage(*operands):
    return pl.pallas_call(
        second_kernel,
        out_shape=jax.ShapeDtypeStruct((FIELDS, BLOCK, ROWS, LANES), jnp.float32),
        in_specs=[VMEM] * len(operands),
        out_specs=VMEM,
        compiler_params=params(),
        cost_estimate=cost(30_000_000, 3_000_000),
        name="second_stage",
    )(*operands)


def everyone_max(value, axis, size):
    reach = 1
    while reach * 4 < size:
        reach *= 4
    while reach:
        copies = [value]
        for times in range(1, 4):
            turn = reach * times
            if turn < size:
                pairs = [(i, i ^ turn) for i in range(size)]
                copies.append(lax.ppermute(value, axis, pairs))
        value = functools.reduce(jnp.maximum, copies)
        reach //= 4
    return value


def per_device(blocks, owner_list, slot_list):
    size = lax.axis_size("gx")
    own = lax.axis_index("gx")
    per_dev = blocks.shape[0]
    cap = max(2, 2 * per_dev // size)
    up = [(i, (i + 1) % size) for i in range(size)]
    down = [(j, i) for i, j in up]

    parts = pack(tiled_rows(blocks), owner_list, size, cap, per_dev)
    parts, owner_list, slot_list = lax.optimization_barrier((parts, owner_list, slot_list))
    come = lax.all_to_all(parts, "gx", split_axis=0, concat_axis=0, tiled=True)
    table = arrival_spots(owner_list, slot_list, own, per_dev, size, cap)
    come = come.reshape(-1, LANES)
    state_low, low, speed = unpack(table, come, 0, size, cap)
    above = lax.ppermute(low, "gx", down)
    state_high, high = unpack(table, come, 1, size, cap)
    below = lax.ppermute(high, "gx", up)
    state = (state_low, state_high)
    sides = along_planes(*state, speed)
    *middle, low, high = first_stage(*state, sides, below, above, speed)
    below = lax.ppermute(high, "gx", up)
    above = lax.ppermute(low, "gx", down)
    second = everyone_max(fastest(*middle), "gx", size)
    sides = along_planes(*middle, second)
    return second_stage(*state, *middle, sides, below, above, speed, second)


def solution(mesh):
    return jax.shard_map(
        per_device,
        mesh=mesh,
        in_specs=(P(("runs", "gx"), None, None), P("runs"), P("runs")),
        out_specs=P(None, ("runs", "gx"), None, None),
        check_vma=False,
    )
```

```python
import functools

import jax
import jax.numpy as jnp
from jax import lax
from jax.experimental import pallas as pl
from jax.experimental.pallas import tpu as pltpu
from jax.sharding import PartitionSpec as P

BLOCK = 8
BY = 4
BZ = 16
FIELDS = 5
LANES = 128
ROWS = BY * BLOCK
PAIRS = BLOCK // 2
TILES = PAIRS * FIELDS

gamma_gas = 1.4
courant = 0.25
smooth_epsilon = 1e-06

VMEM = pl.BlockSpec(memory_space=pltpu.VMEM)
SMEM = pl.BlockSpec(memory_space=pltpu.SMEM)


def params(mebibytes=40):
    return pltpu.CompilerParams(vmem_limit_bytes=mebibytes * 1024 * 1024)


def cost(flops, size):
    return pl.CostEstimate(flops=flops, bytes_accessed=size, transcendentals=0)


def wave_speed(fields):
    density, mom_x, mom_y, mom_z, energy = fields
    inverse = 1.0 / density
    vel = (mom_x * inverse, mom_y * inverse, mom_z * inverse)
    kinetic = 0.5 * (mom_x * vel[0] + mom_y * vel[1] + mom_z * vel[2])
    pressure = (gamma_gas - 1.0) * (energy - kinetic)
    sound = jnp.sqrt(gamma_gas * pressure * inverse)
    fastest = jnp.maximum(jnp.maximum(jnp.abs(vel[0]), jnp.abs(vel[1])), jnp.abs(vel[2]))
    return fastest + sound


def tiled_rows(blocks):
    count = blocks.shape[0] // 8
    groups = blocks.reshape(count, 8, FIELDS, PAIRS, LANES).transpose(2, 0, 3, 1, 4)
    return groups.reshape(FIELDS * count * PAIRS * 8, LANES)


def pack_kernel(
    size, cap, per_dev, owner_hbm, rows_hbm, out_hbm, owner, rows, out, top, count, member, sems
):
    own = lax.axis_index("gx")
    fetch_owner = pltpu.make_async_copy(owner_hbm, owner, sems.at[0])
    fetch_rows = pltpu.make_async_copy(rows_hbm, rows, sems.at[1])
    fetch_owner.start()
    fetch_rows.start()

    def clear(dest, carry):
        count[dest] = 0
        return carry

    lax.fori_loop(0, size, clear, 0, unroll=8)
    fetch_owner.wait()

    def note(block, carry):
        dest = owner[own * per_dev + block]
        rank = count[dest]
        count[dest] = rank + 1
        member[dest * cap + rank] = lax.div(block, 8) * (PAIRS * 8) + lax.rem(block, 8)
        return carry

    lax.fori_loop(0, per_dev, note, 0, unroll=8)
    fetch_rows.wait()
    tiles = TILES * cap

    def message(dest, carry):
        @pl.when(count[dest] > 0)
        def _():
            for rank in range(cap):
                first = member[dest * cap + rank]
                for pair in range(PAIRS):
                    source = pl.ds(first + pair * 8, FIELDS, stride=per_dev * PAIRS)
                    to = dest * tiles + pair * (FIELDS * cap) + rank
                    out[pl.ds(to, FIELDS, stride=cap), :] = rows[source, :]
            part = out.at[pl.ds(pl.multiple_of(dest * tiles, tiles), tiles)]
            pltpu.make_async_copy(part, out_hbm.at[dest, pl.ds(0, tiles), 0], sems.at[2]).start()

        return carry

    lax.fori_loop(0, size, message, 0)
    best = jnp.zeros((8, LANES), jnp.float32)
    step = per_dev * PAIRS
    for first in range(0, step, 8):
        fields = [rows[f * step + first : f * step + first + 8, :] for f in range(FIELDS)]
        best = jnp.maximum(best, wave_speed(fields))
    top[...] = jnp.full(top.shape, jnp.max(best), jnp.float32)
    for dest in range(size):
        pltpu.make_async_copy(
            top.at[pl.ds(dest, 1)], out_hbm.at[dest, tiles], sems.at[3]
        ).start()
    half = out.at[pl.ds(0, per_dev * TILES)]
    pltpu.make_async_copy(half, half, sems.at[2]).wait()
    pltpu.make_async_copy(top, top, sems.at[3]).wait()


def pack(rows, owner_list, size, cap, per_dev):
    return pl.pallas_call(
        functools.partial(pack_kernel, size, cap, per_dev),
        out_shape=jax.ShapeDtypeStruct((size, TILES * cap + 1, 1, LANES), jnp.float32),
        in_specs=[pl.BlockSpec(memory_space=pltpu.HBM)] * 2,
        out_specs=pl.BlockSpec(memory_space=pltpu.HBM),
        scratch_shapes=[
            pltpu.SMEM(owner_list.shape, jnp.int32),
            pltpu.VMEM(rows.shape, jnp.float32),
            pltpu.VMEM((size * TILES * cap, LANES), jnp.float32),
            pltpu.VMEM((size, LANES), jnp.float32),
            pltpu.SMEM((size,), jnp.int32),
            pltpu.SMEM((size * cap,), jnp.int32),
            pltpu.SemaphoreType.DMA((4,)),
        ],
        compiler_params=params(62),
        cost_estimate=cost(1_000_000, 3_000_000),
        name="pack",
    )(owner_list, rows)


def own_is_even():
    return lax.axis_index("gx") % 2 == 0


def swapped(far_side, near_side, size):
    apart = [(i, (i - 1 if i % 2 == 0 else i + 1) % size) for i in range(size)]
    chip = [(i, i ^ 1) for i in range(size)]
    return lax.ppermute(far_side, "gx", apart), lax.ppermute(near_side, "gx", chip)


def sort_halos(far, near, below, above):
    lower_first = own_is_even()
    for f in range(FIELDS):
        for plane in range(3):
            one, two = far[f, plane], near[f, plane]
            below[f, plane] = jnp.where(lower_first, one, two)
            above[f, plane] = jnp.where(lower_first, two, one)


HALO = (FIELDS, 3, ROWS, LANES)


def arrival_spots(owner_list, slot_list, own, per_dev, size, cap):
    owners = owner_list.reshape(size, per_dev)
    slots = slot_list.reshape(size, per_dev)
    mine = owners == own
    spot = jnp.arange(per_dev, dtype=jnp.int32)
    earlier = spot[None, :] < spot[:, None]
    rank = jnp.sum((mine[:, None, :] & earlier[None]).astype(jnp.int32), axis=2)
    row = jnp.arange(size, dtype=jnp.int32)[:, None] * cap + rank
    key = jnp.where(mine, slots, -1)
    hit = key.reshape(1, -1) == spot[:, None]
    return jnp.max(jnp.where(hit, row.reshape(1, -1), 0), axis=1)


def exchanged_bits(rows, group):
    rows = list(rows)
    for bit in range(4):
        step = 1 << bit
        low = (group & step) == 0
        for index in range(16):
            if index & step:
                continue
            first, second = rows[index], rows[index | step]
            rows[index] = jnp.where(low, first, pltpu.roll(second, 8 * step, 1))
            rows[index | step] = jnp.where(low, pltpu.roll(first, LANES - 8 * step, 1), second)
    return rows


def unpack_kernel(size, cap, table, come, state, far_side, near_side, speed, scratch):
    message = TILES * cap + 1
    best = come[message - 1 : message, :]
    for source in range(1, size):
        best = jnp.maximum(best, come[(source + 1) * message - 1 : (source + 1) * message, :])
    speed[...] = jnp.broadcast_to(best, speed.shape)
    for slot in range(BY * BZ):
        p, q = divmod(slot, BZ)
        where = table[slot]
        source = lax.div(where, cap)
        rank = lax.rem(where, cap)
        for pair in range(PAIRS):
            couple, h = divmod(pair, 2)
            base = source * message + rank + pair * (FIELDS * cap)
            value = come[pl.ds(base, FIELDS, stride=cap), :]
            row = (couple * BZ + q) * 8 + 2 * p + h
            scratch[pl.ds(row, FIELDS, stride=PAIRS // 2 * BZ * 8), :] = value
    group = lax.broadcasted_iota(jnp.int32, (8, LANES), 1) // BLOCK
    even = lax.broadcasted_iota(jnp.int32, (8, LANES), 0) % 2 == 0

    for f in range(FIELDS):
        for couple in range(PAIRS // 2):
            first = (f * (PAIRS // 2) + couple) * BZ * 8
            rows = [scratch[first + q * 8 : first + q * 8 + 8, :] for q in range(BZ)]
            moved = exchanged_bits(rows, group)
            for second in range(2):
                for j in range(4):
                    lower = moved[second * BLOCK + j]
                    upper = moved[second * BLOCK + j + 4]
                    planes = (
                        jnp.where(even, lower, pltpu.roll(upper, 1, 0)),
                        jnp.where(even, pltpu.roll(lower, 7, 0), upper),
                    )
                    rows = slice(j * 8, j * 8 + 8)
                    for h in range(2):
                        plane = 4 * couple + 2 * h + second
                        state[f, plane, rows, :] = planes[h]
    lower_first = own_is_even()
    for f in range(FIELDS):
        for plane in range(3):
            low, high = state[f, plane], state[f, BLOCK - 3 + plane]
            far_side[f, plane] = jnp.where(lower_first, low, high)
            near_side[f, plane] = jnp.where(lower_first, high, low)


def unpack(table, come, size, cap):
    halo = jax.ShapeDtypeStruct(HALO, jnp.float32)
    return pl.pallas_call(
        functools.partial(unpack_kernel, size, cap),
        out_shape=(
            jax.ShapeDtypeStruct((FIELDS, BLOCK, ROWS, LANES), jnp.float32),
            halo,
            halo,
            jax.ShapeDtypeStruct((8, LANES), jnp.float32),
        ),
        in_specs=[SMEM, VMEM],
        out_specs=(VMEM,) * 4,
        scratch_shapes=[pltpu.VMEM((FIELDS * (PAIRS // 2) * BZ * 8, LANES), jnp.float32)],
        compiler_params=params(),
        cost_estimate=cost(5_000_000, 2_000_000),
        name="unpack",
    )(table, come)


def y_up(x):
    return jnp.concatenate([x[8:], pltpu.roll(x[:8], 7, 0)], axis=0)


def y_down(x):
    return jnp.concatenate([pltpu.roll(x[24:], 1, 0), x[:24]], axis=0)


def y_up_two(x):
    return jnp.concatenate([x[16:], pltpu.roll(x[:8], 7, 0), pltpu.roll(x[8:16], 7, 0)], axis=0)


def inverse(x):
    return 1.0 / x


def smoothness(before, after):
    curve = after - before
    middle = 0.5 * (after + before)
    base = curve * curve * (13.0 / 12.0) + smooth_epsilon
    plus = middle + curve
    minus = middle - curve
    left = inverse(base + plus * plus)
    centre = inverse(base + middle * middle)
    right = inverse(base + minus * minus)
    return curve, left * left, centre * centre, right * right


def upwind_term(left, centre, right, jump_before, jump_after):
    right = 3.0 * right
    top = left * (jump_before + jump_before) + right * jump_after
    return top * inverse(left + 6.0 * centre + right)


def periodic_divergence(half_flux, scaled, up, up_two, down):
    plus = half_flux + scaled
    minus = half_flux - scaled

    def side(values):
        after = up(values) - values
        curve, left, centre, right = smoothness(down(after), after)
        above = up(curve)
        return curve, above, left, centre, right, above - curve

    curve, _, left, centre, right, jump = side(plus)
    face = 6.0 * (half_flux + up(half_flux)) - curve
    face = face - upwind_term(down(left), centre, up(right), down(jump), jump)
    _, curve, left, centre, right, jump = side(minus)
    face = face + (upwind_term(up_two(right), up(centre), left, up(jump), jump) - curve)
    return face - down(face)


def ring_divergence(half_flux, scaled):
    count = len(half_flux)

    def up(values):
        return values[1:] + [pltpu.roll(values[0], 7, 0)]

    def down(values):
        return [pltpu.roll(values[-1], 1, 0)] + values[:-1]

    def side(values):
        after = [above - value for above, value in zip(up(values), values)]
        parts = [smoothness(before, step) for before, step in zip(down(after), after)]
        curve, left, centre, right = (list(part) for part in zip(*parts))
        jump = [above - value for above, value in zip(up(curve), curve)]
        return curve, left, centre, right, jump

    curve, left, centre, right, jump = side([a + b for a, b in zip(half_flux, scaled)])
    terms = zip(down(left), centre, up(right), down(jump), jump)
    face = [
        6.0 * (here + above) - bend - upwind_term(*term)
        for here, above, bend, term in zip(half_flux, up(half_flux), curve, terms)
    ]
    curve, left, centre, right, jump = side([a - b for a, b in zip(half_flux, scaled)])
    terms = zip(up(right), centre, down(left), jump, down(jump))
    other = [upwind_term(*term) - bend for bend, term in zip(curve, terms)]
    face = [one + two for one, two in zip(face, up(other))]
    return [here - below for here, below in zip(face, down(face))]


def open_divergence(half_flux, scaled):
    count = len(half_flux)
    plus = [a + b for a, b in zip(half_flux, scaled)]
    minus = [a - b for a, b in zip(half_flux, scaled)]
    faces = [None] * count

    def side(values):
        steps = [values[i + 1] - values[i] for i in range(count - 1)]
        parts = [None] + [smoothness(steps[i - 1], steps[i]) for i in range(1, count - 1)]
        return parts

    parts = side(plus)
    for i in range(2, count - 3):
        jump_before = parts[i][0] - parts[i - 1][0]
        jump_after = parts[i + 1][0] - parts[i][0]
        faces[i] = 6.0 * (half_flux[i] + half_flux[i + 1]) - parts[i][0] - upwind_term(
            parts[i - 1][1], parts[i][2], parts[i + 1][3], jump_before, jump_after
        )
    parts = side(minus)
    for i in range(3, count - 2):
        jump_before = parts[i][0] - parts[i - 1][0]
        jump_after = parts[i + 1][0] - parts[i][0]
        faces[i - 1] = faces[i - 1] + (
            upwind_term(parts[i + 1][3], parts[i][2], parts[i - 1][1], jump_after, jump_before)
            - parts[i][0]
        )
    return [faces[i] - faces[i - 1] for i in range(3, count - 3)]


def half_velocities(fields):
    density, mom_x, mom_y, mom_z, energy = fields
    over = 0.5 / density
    vel = (mom_x * over, mom_y * over, mom_z * over)
    kinetic = mom_x * vel[0] + mom_y * vel[1] + mom_z * vel[2]
    pressure = (gamma_gas - 1.0) * (energy - kinetic)
    return vel, pressure


def half_flux(fields, field, direction, speed, pressure):
    if field == 0:
        return 0.5 * fields[1 + direction]
    if field == 4:
        return (fields[4] + pressure) * speed
    flux = fields[field] * speed
    return flux + 0.5 * pressure if field == 1 + direction else flux


def plane_kernel(state, speed, out, turned):
    half_speed = 0.5 * speed[0:1, :]
    lane = lax.broadcasted_iota(jnp.int32, (LANES, LANES), 1)
    to_turned = (lane % 8) * 16 + lane // 8
    to_plain = (lane % 16) * 8 + lane // 16

    def four_planes(part, carry):
        planes = pl.ds(part * 4, 4)
        for f in range(FIELDS):
            plain = state[f, planes].reshape(LANES, LANES)
            turned[f] = jnp.take_along_axis(plain, to_turned, axis=1).T
        for place in range(4):
            fields = [state[f, part * 4 + place] for f in range(FIELDS)]
            vel, pressure = half_velocities(fields)
            for field in range(FIELDS):
                out[field, part * 4 + place] = periodic_divergence(
                    half_flux(fields, field, 1, vel[1], pressure),
                    half_speed * fields[field],
                    y_up,
                    y_up_two,
                    y_down,
                )
        columns = [
            [turned[f, row : row + 8] for row in range(0, LANES, 8)] for f in range(FIELDS)
        ]
        along = [half_velocities(fields) for fields in zip(*columns)]
        for field in range(FIELDS):
            fluxes = [
                half_flux(fields, field, 2, vel[2], pressure)
                for fields, (vel, pressure) in zip(zip(*columns), along)
            ]
            scaled = [half_speed * value for value in columns[field]]
            total = jnp.concatenate(ring_divergence(fluxes, scaled), axis=0)
            plain = jnp.take_along_axis(total.T, to_plain, axis=1)
            out[field, planes] += plain.reshape(4, ROWS, LANES)
        return carry

    lax.fori_loop(0, state.shape[1] // 4, four_planes, 0)


def along_planes(state, speed):
    return pl.pallas_call(
        plane_kernel,
        out_shape=jax.ShapeDtypeStruct(state.shape, jnp.float32),
        in_specs=[VMEM, VMEM],
        out_specs=VMEM,
        scratch_shapes=[pltpu.VMEM((FIELDS, LANES, LANES), jnp.float32)],
        compiler_params=params(),
        cost_estimate=cost(20_000_000, 1_000_000),
        name="planes",
    )(state, speed)


def across(get, half_speed):
    span = range(-3, BLOCK + 3)
    speeds, pressures = [], []
    for plane in span:
        vel, pressure = half_velocities([get(f, plane) for f in range(FIELDS)])
        speeds.append(vel[0])
        pressures.append(pressure)
    for field in range(FIELDS):
        fluxes, scaled = [], []
        for i, plane in enumerate(span):
            if field == 0:
                flux = 0.5 * get(1, plane)
            elif field == 4:
                flux = (get(4, plane) + pressures[i]) * speeds[i]
            else:
                flux = get(field, plane) * speeds[i]
                if field == 1:
                    flux = flux + 0.5 * pressures[i]
            fluxes.append(flux)
            scaled.append(half_speed * get(field, plane))
        yield field, open_divergence(fluxes, scaled)


def first_kernel(
    state, sides, far, near, speed, middle, far_side, near_side, top, below, above
):
    sort_halos(far, near, below, above)
    lower_first = own_is_even()
    half_speed = 0.5 * speed[0:1, :]
    factor = (courant / 6.0) / speed[0:1, :]

    def group(j, best):
        rows = pl.ds(pl.multiple_of(j * 8, 8), 8)

        def get(f, plane):
            if plane < 0:
                return below[f, plane + 3, rows, :]
            if plane >= BLOCK:
                return above[f, plane - BLOCK, rows, :]
            return state[f, plane, rows, :]

        for field, along_x in across(get, half_speed):
            values = []
            for plane in range(BLOCK):
                total = along_x[plane] + sides[field, plane, rows, :]
                values.append(get(field, plane) - factor * total)
                middle[field, plane, rows, :] = values[plane]
            for plane in range(3):
                low, high = values[plane], values[BLOCK - 3 + plane]
                far_side[field, plane, rows, :] = jnp.where(lower_first, low, high)
                near_side[field, plane, rows, :] = jnp.where(lower_first, high, low)
        for plane in range(BLOCK):
            best = jnp.maximum(
                best, wave_speed([middle[f, plane, rows, :] for f in range(FIELDS)])
            )
        return best

    best = lax.fori_loop(0, 4, group, jnp.zeros((8, LANES), jnp.float32))
    top[...] = jnp.full((8, LANES), jnp.max(best), jnp.float32)


def first_stage(*operands):
    whole = jax.ShapeDtypeStruct((FIELDS, BLOCK, ROWS, LANES), jnp.float32)
    halo = jax.ShapeDtypeStruct(HALO, jnp.float32)
    return pl.pallas_call(
        first_kernel,
        out_shape=(whole, halo, halo, jax.ShapeDtypeStruct((8, LANES), jnp.float32)),
        in_specs=[VMEM] * len(operands),
        out_specs=(VMEM,) * 4,
        scratch_shapes=[pltpu.VMEM(HALO, jnp.float32)] * 2,
        compiler_params=params(),
        cost_estimate=cost(30_000_000, 3_000_000),
        name="first_stage",
    )(*operands)


def second_kernel(start, middle, sides, far, near, first_speed, speed, out, below, above):
    sort_halos(far, near, below, above)
    half_speed = 0.5 * speed[0:1, :]
    factor = (courant / 12.0) / first_speed[0:1, :]

    def group(j, carry):
        rows = pl.ds(pl.multiple_of(j * 8, 8), 8)
        spread = pl.ds(j, 8, stride=4)

        def get(f, plane):
            if plane < 0:
                return below[f, plane + 3, rows, :]
            if plane >= BLOCK:
                return above[f, plane - BLOCK, rows, :]
            return middle[f, plane, rows, :]

        for field, along_x in across(get, half_speed):
            for plane in range(BLOCK):
                total = along_x[plane] + sides[field, plane, rows, :]
                value = 0.5 * start[field, plane, rows, :] + (
                    0.5 * get(field, plane) - factor * total
                )
                out[field, plane, spread, :] = value
        return carry

    lax.fori_loop(0, 4, group, 0)


def second_stage(*operands):
    return pl.pallas_call(
        second_kernel,
        out_shape=jax.ShapeDtypeStruct((FIELDS, BLOCK, ROWS, LANES), jnp.float32),
        in_specs=[VMEM] * len(operands),
        out_specs=VMEM,
        scratch_shapes=[pltpu.VMEM(HALO, jnp.float32)] * 2,
        compiler_params=params(),
        cost_estimate=cost(30_000_000, 3_000_000),
        name="second_stage",
    )(*operands)


def everyone_max(value, axis, size):
    reach = 1
    while reach * 4 < size:
        reach *= 4
    while reach:
        copies = [value]
        for times in range(1, 4):
            turn = reach * times
            if turn < size:
                pairs = [(i, i ^ turn) for i in range(size)]
                copies.append(lax.ppermute(value, axis, pairs))
        value = functools.reduce(jnp.maximum, copies)
        reach //= 4
    return value


def per_device(blocks, owner_list, slot_list):
    size = lax.axis_size("gx")
    own = lax.axis_index("gx")
    per_dev = blocks.shape[0]
    cap = max(2, 2 * per_dev // size)

    parts = pack(tiled_rows(blocks), owner_list, size, cap, per_dev)
    parts, owner_list, slot_list = lax.optimization_barrier((parts, owner_list, slot_list))
    come = lax.all_to_all(parts, "gx", split_axis=0, concat_axis=0, tiled=True)
    table = arrival_spots(owner_list, slot_list, own, per_dev, size, cap)
    state, far_side, near_side, speed = unpack(table, come.reshape(-1, LANES), size, cap)
    far, near = swapped(far_side, near_side, size)
    sides = along_planes(state, speed)
    middle, far_side, near_side, top = first_stage(state, sides, far, near, speed)
    far, near = swapped(far_side, near_side, size)
    second = everyone_max(top, "gx", size)
    sides = along_planes(middle, second)
    return second_stage(state, middle, sides, far, near, speed, second)


def solution(mesh):
    return jax.shard_map(
        per_device,
        mesh=mesh,
        in_specs=(P(("runs", "gx"), None, None), P("runs"), P("runs")),
        out_specs=P(None, ("runs", "gx"), None, None),
        check_vma=False,
    )
```

```python
import functools

import jax
import jax.numpy as jnp
from jax import lax
from jax.experimental import pallas as pl
from jax.experimental.pallas import tpu as pltpu
from jax.sharding import PartitionSpec as P

BLOCK = 8
BY = 4
BZ = 16
FIELDS = 5
LANES = 128
ROWS = BY * BLOCK
PAIRS = BLOCK // 2
TILES = PAIRS * FIELDS

gamma_gas = 1.4
courant = 0.25
smooth_epsilon = 1e-06

VMEM = pl.BlockSpec(memory_space=pltpu.VMEM)
SMEM = pl.BlockSpec(memory_space=pltpu.SMEM)


def params(mebibytes=40):
    return pltpu.CompilerParams(vmem_limit_bytes=mebibytes * 1024 * 1024)


def cost(flops, size):
    return pl.CostEstimate(flops=flops, bytes_accessed=size, transcendentals=0)


def wave_speed(fields):
    density, mom_x, mom_y, mom_z, energy = fields
    inverse = 1.0 / density
    vel = (mom_x * inverse, mom_y * inverse, mom_z * inverse)
    kinetic = 0.5 * (mom_x * vel[0] + mom_y * vel[1] + mom_z * vel[2])
    pressure = (gamma_gas - 1.0) * (energy - kinetic)
    sound = jnp.sqrt(gamma_gas * pressure * inverse)
    fastest = jnp.maximum(jnp.maximum(jnp.abs(vel[0]), jnp.abs(vel[1])), jnp.abs(vel[2]))
    return fastest + sound


def tiled_rows(blocks):
    count = blocks.shape[0] // 8
    groups = blocks.reshape(count, 8, FIELDS, PAIRS, LANES).transpose(2, 0, 3, 1, 4)
    return groups.reshape(FIELDS * count * PAIRS * 8, LANES)


def pack_kernel(
    size, cap, per_dev, owner_hbm, rows_hbm, out_hbm, owner, rows, out, top, count, member, sems
):
    own = lax.axis_index("gx")
    fetch_owner = pltpu.make_async_copy(owner_hbm, owner, sems.at[0])
    fetch_rows = pltpu.make_async_copy(rows_hbm, rows, sems.at[1])
    fetch_owner.start()
    fetch_rows.start()

    def clear(dest, carry):
        count[dest] = 0
        return carry

    lax.fori_loop(0, size, clear, 0, unroll=8)
    fetch_owner.wait()

    def note(block, carry):
        dest = owner[own * per_dev + block]
        rank = count[dest]
        count[dest] = rank + 1
        member[dest * cap + rank] = lax.div(block, 8) * (PAIRS * 8) + lax.rem(block, 8)
        return carry

    lax.fori_loop(0, per_dev, note, 0, unroll=8)
    fetch_rows.wait()
    tiles = TILES * cap

    def message(dest, carry):
        @pl.when(count[dest] > 0)
        def _():
            for rank in range(cap):
                first = member[dest * cap + rank]
                for pair in range(PAIRS):
                    source = pl.ds(first + pair * 8, FIELDS, stride=per_dev * PAIRS)
                    to = dest * tiles + pair * (FIELDS * cap) + rank
                    out[pl.ds(to, FIELDS, stride=cap), :] = rows[source, :]
            part = out.at[pl.ds(pl.multiple_of(dest * tiles, tiles), tiles)]
            pltpu.make_async_copy(part, out_hbm.at[dest, pl.ds(0, tiles), 0], sems.at[2]).start()

        return carry

    lax.fori_loop(0, size, message, 0)
    best = jnp.zeros((8, LANES), jnp.float32)
    step = per_dev * PAIRS
    for first in range(0, step, 8):
        fields = [rows[f * step + first : f * step + first + 8, :] for f in range(FIELDS)]
        best = jnp.maximum(best, wave_speed(fields))
    top[...] = jnp.full(top.shape, jnp.max(best), jnp.float32)
    for dest in range(size):
        pltpu.make_async_copy(
            top.at[pl.ds(dest, 1)], out_hbm.at[dest, tiles], sems.at[3]
        ).start()
    half = out.at[pl.ds(0, per_dev * TILES)]
    pltpu.make_async_copy(half, half, sems.at[2]).wait()
    pltpu.make_async_copy(top, top, sems.at[3]).wait()


def pack(rows, owner_list, size, cap, per_dev):
    return pl.pallas_call(
        functools.partial(pack_kernel, size, cap, per_dev),
        out_shape=jax.ShapeDtypeStruct((size, TILES * cap + 1, 1, LANES), jnp.float32),
        in_specs=[pl.BlockSpec(memory_space=pltpu.HBM)] * 2,
        out_specs=pl.BlockSpec(memory_space=pltpu.HBM),
        scratch_shapes=[
            pltpu.SMEM(owner_list.shape, jnp.int32),
            pltpu.VMEM(rows.shape, jnp.float32),
            pltpu.VMEM((size * TILES * cap, LANES), jnp.float32),
            pltpu.VMEM((size, LANES), jnp.float32),
            pltpu.SMEM((size,), jnp.int32),
            pltpu.SMEM((size * cap,), jnp.int32),
            pltpu.SemaphoreType.DMA((4,)),
        ],
        compiler_params=params(62),
        cost_estimate=cost(1_000_000, 3_000_000),
        name="pack",
    )(owner_list, rows)


def own_is_even():
    return lax.axis_index("gx") % 2 == 0


def swapped(far_side, near_side, size):
    apart = [(i, (i - 1 if i % 2 == 0 else i + 1) % size) for i in range(size)]
    chip = [(i, i ^ 1) for i in range(size)]
    return lax.ppermute(far_side, "gx", apart), lax.ppermute(near_side, "gx", chip)


def sort_halos(far, near, below, above):
    lower_first = own_is_even()
    for f in range(FIELDS):
        for plane in range(3):
            one, two = far[f, plane], near[f, plane]
            below[f, plane] = jnp.where(lower_first, one, two)
            above[f, plane] = jnp.where(lower_first, two, one)


HALO = (FIELDS, 3, ROWS, LANES)


def arrival_spots(owner_list, slot_list, own, per_dev, size, cap):
    owners = owner_list.reshape(size, per_dev)
    slots = slot_list.reshape(size, per_dev)
    mine = owners == own
    spot = jnp.arange(per_dev, dtype=jnp.int32)
    earlier = spot[None, :] < spot[:, None]
    rank = jnp.sum((mine[:, None, :] & earlier[None]).astype(jnp.int32), axis=2)
    row = jnp.arange(size, dtype=jnp.int32)[:, None] * cap + rank
    key = jnp.where(mine, slots, -1)
    hit = key.reshape(1, -1) == spot[:, None]
    return jnp.max(jnp.where(hit, row.reshape(1, -1), 0), axis=1)


def exchanged_bits(rows, group):
    rows = list(rows)
    for bit in range(4):
        step = 1 << bit
        low = (group & step) == 0
        for index in range(16):
            if index & step:
                continue
            first, second = rows[index], rows[index | step]
            rows[index] = jnp.where(low, first, pltpu.roll(second, 8 * step, 1))
            rows[index | step] = jnp.where(low, pltpu.roll(first, LANES - 8 * step, 1), second)
    return rows


def unpack_kernel(size, cap, table, come, state, far_side, near_side, speed, scratch):
    message = TILES * cap + 1
    best = come[message - 1 : message, :]
    for source in range(1, size):
        best = jnp.maximum(best, come[(source + 1) * message - 1 : (source + 1) * message, :])
    speed[...] = jnp.broadcast_to(best, speed.shape)
    for slot in range(BY * BZ):
        p, q = divmod(slot, BZ)
        where = table[slot]
        source = lax.div(where, cap)
        rank = lax.rem(where, cap)
        for pair in range(PAIRS):
            couple, h = divmod(pair, 2)
            base = source * message + rank + pair * (FIELDS * cap)
            value = come[pl.ds(base, FIELDS, stride=cap), :]
            row = (couple * BZ + q) * 8 + 2 * p + h
            scratch[pl.ds(row, FIELDS, stride=PAIRS // 2 * BZ * 8), :] = value
    group = lax.broadcasted_iota(jnp.int32, (8, LANES), 1) // BLOCK
    even = lax.broadcasted_iota(jnp.int32, (8, LANES), 0) % 2 == 0

    for f in range(FIELDS):
        for couple in range(PAIRS // 2):
            first = (f * (PAIRS // 2) + couple) * BZ * 8
            rows = [scratch[first + q * 8 : first + q * 8 + 8, :] for q in range(BZ)]
            moved = exchanged_bits(rows, group)
            for second in range(2):
                for j in range(4):
                    lower = moved[second * BLOCK + j]
                    upper = moved[second * BLOCK + j + 4]
                    planes = (
                        jnp.where(even, lower, pltpu.roll(upper, 1, 0)),
                        jnp.where(even, pltpu.roll(lower, 7, 0), upper),
                    )
                    rows = slice(j * 8, j * 8 + 8)
                    for h in range(2):
                        plane = 4 * couple + 2 * h + second
                        state[f, plane, rows, :] = planes[h]
    lower_first = own_is_even()
    for f in range(FIELDS):
        for plane in range(3):
            low, high = state[f, plane], state[f, BLOCK - 3 + plane]
            far_side[f, plane] = jnp.where(lower_first, low, high)
            near_side[f, plane] = jnp.where(lower_first, high, low)


def unpack(table, come, size, cap):
    halo = jax.ShapeDtypeStruct(HALO, jnp.float32)
    return pl.pallas_call(
        functools.partial(unpack_kernel, size, cap),
        out_shape=(
            jax.ShapeDtypeStruct((FIELDS, BLOCK, ROWS, LANES), jnp.float32),
            halo,
            halo,
            jax.ShapeDtypeStruct((8, LANES), jnp.float32),
        ),
        in_specs=[SMEM, VMEM],
        out_specs=(VMEM,) * 4,
        scratch_shapes=[pltpu.VMEM((FIELDS * (PAIRS // 2) * BZ * 8, LANES), jnp.float32)],
        compiler_params=params(),
        cost_estimate=cost(5_000_000, 2_000_000),
        name="unpack",
    )(table, come)


def y_up(x):
    return jnp.concatenate([x[8:], pltpu.roll(x[:8], 7, 0)], axis=0)


def y_down(x):
    return jnp.concatenate([pltpu.roll(x[24:], 1, 0), x[:24]], axis=0)


def y_up_two(x):
    return jnp.concatenate([x[16:], pltpu.roll(x[:8], 7, 0), pltpu.roll(x[8:16], 7, 0)], axis=0)


def inverse(x):
    return 1.0 / x


def smoothness(before, after):
    curve = after - before
    middle = 0.5 * (after + before)
    base = curve * curve * (13.0 / 12.0) + smooth_epsilon
    plus = middle + curve
    minus = middle - curve
    left = inverse(base + plus * plus)
    centre = inverse(base + middle * middle)
    right = inverse(base + minus * minus)
    return curve, left * left, centre * centre, right * right


def upwind_term(left, centre, right, jump_before, jump_after):
    right = 3.0 * right
    top = left * (jump_before + jump_before) + right * jump_after
    return top * inverse(left + 6.0 * centre + right)


def periodic_divergence(half_flux, scaled, up, up_two, down):
    plus = half_flux + scaled
    minus = half_flux - scaled

    def side(values):
        after = up(values) - values
        curve, left, centre, right = smoothness(down(after), after)
        above = up(curve)
        return curve, above, left, centre, right, above - curve

    curve, _, left, centre, right, jump = side(plus)
    face = 6.0 * (half_flux + up(half_flux)) - curve
    face = face - upwind_term(down(left), centre, up(right), down(jump), jump)
    _, curve, left, centre, right, jump = side(minus)
    face = face + (upwind_term(up_two(right), up(centre), left, up(jump), jump) - curve)
    return face - down(face)


def ring_divergence(half_flux, scaled):
    count = len(half_flux)

    def up(values):
        return values[1:] + [pltpu.roll(values[0], 7, 0)]

    def down(values):
        return [pltpu.roll(values[-1], 1, 0)] + values[:-1]

    def side(values):
        after = [above - value for above, value in zip(up(values), values)]
        parts = [smoothness(before, step) for before, step in zip(down(after), after)]
        curve, left, centre, right = (list(part) for part in zip(*parts))
        jump = [above - value for above, value in zip(up(curve), curve)]
        return curve, left, centre, right, jump

    curve, left, centre, right, jump = side([a + b for a, b in zip(half_flux, scaled)])
    terms = zip(down(left), centre, up(right), down(jump), jump)
    face = [
        6.0 * (here + above) - bend - upwind_term(*term)
        for here, above, bend, term in zip(half_flux, up(half_flux), curve, terms)
    ]
    curve, left, centre, right, jump = side([a - b for a, b in zip(half_flux, scaled)])
    terms = zip(up(right), centre, down(left), jump, down(jump))
    other = [upwind_term(*term) - bend for bend, term in zip(curve, terms)]
    face = [one + two for one, two in zip(face, up(other))]
    return [here - below for here, below in zip(face, down(face))]


def x_divergence(half_flux, scaled, plus_at, minus_at, centre_at):
    faces = {i: 6.0 * (half_flux[i] + half_flux[i + 1]) for i in centre_at}

    def add(i, value):
        faces[i] = faces[i] + value if i in faces else value

    def side(sign):
        values = {i: half_flux[i] + sign * scaled[i] for i in half_flux}
        steps = {i: values[i + 1] - values[i] for i in values if i + 1 in values}
        return {i: smoothness(steps[i - 1], steps[i]) for i in steps if i - 1 in steps}

    parts = side(1)
    for i in plus_at:
        curve, left, centre, right = zip(parts[i - 1], parts[i], parts[i + 1])
        term = upwind_term(left[0], centre[1], right[2], curve[1] - curve[0], curve[2] - curve[1])
        add(i, -(curve[1] + term))
    parts = side(-1)
    for i in minus_at:
        curve, left, centre, right = zip(parts[i - 1], parts[i], parts[i + 1])
        term = upwind_term(right[2], centre[1], left[0], curve[2] - curve[1], curve[1] - curve[0])
        add(i - 1, term - curve[1])
    total = {}
    for i in range(BLOCK):
        if i in faces:
            total[i] = faces[i]
        if i - 1 in faces:
            total[i] = total[i] - faces[i - 1] if i in total else -faces[i - 1]
    return total


INNER = (range(2, 6), range(2, 6), range(0, 7))
OUTER = ((-1, 0, 1, 6, 7), (0, 1, 6, 7, 8), (-1, 7))
EVERY = (range(-1, 8), range(0, 9), range(-1, 8))


def ring_divergence(half_flux, scaled):
    count = len(half_flux)

    def up(values):
        return values[1:] + [pltpu.roll(values[0], 7, 0)]

    def down(values):
        return [pltpu.roll(values[-1], 1, 0)] + values[:-1]

    def side(values):
        after = [above - value for above, value in zip(up(values), values)]
        parts = [smoothness(before, step) for before, step in zip(down(after), after)]
        curve, left, centre, right = (list(part) for part in zip(*parts))
        jump = [above - value for above, value in zip(up(curve), curve)]
        return curve, left, centre, right, jump

    curve, left, centre, right, jump = side([a + b for a, b in zip(half_flux, scaled)])
    terms = zip(down(left), centre, up(right), down(jump), jump)
    face = [
        6.0 * (here + above) - bend - upwind_term(*term)
        for here, above, bend, term in zip(half_flux, up(half_flux), curve, terms)
    ]
    curve, left, centre, right, jump = side([a - b for a, b in zip(half_flux, scaled)])
    terms = zip(up(right), centre, down(left), jump, down(jump))
    other = [upwind_term(*term) - bend for bend, term in zip(curve, terms)]
    face = [one + two for one, two in zip(face, up(other))]
    return [here - below for here, below in zip(face, down(face))]


def open_divergence(half_flux, scaled):
    count = len(half_flux)
    plus = [a + b for a, b in zip(half_flux, scaled)]
    minus = [a - b for a, b in zip(half_flux, scaled)]
    faces = [None] * count

    def side(values):
        steps = [values[i + 1] - values[i] for i in range(count - 1)]
        parts = [None] + [smoothness(steps[i - 1], steps[i]) for i in range(1, count - 1)]
        return parts

    parts = side(plus)
    for i in range(2, count - 3):
        jump_before = parts[i][0] - parts[i - 1][0]
        jump_after = parts[i + 1][0] - parts[i][0]
        faces[i] = 6.0 * (half_flux[i] + half_flux[i + 1]) - parts[i][0] - upwind_term(
            parts[i - 1][1], parts[i][2], parts[i + 1][3], jump_before, jump_after
        )
    parts = side(minus)
    for i in range(3, count - 2):
        jump_before = parts[i][0] - parts[i - 1][0]
        jump_after = parts[i + 1][0] - parts[i][0]
        faces[i - 1] = faces[i - 1] + (
            upwind_term(parts[i + 1][3], parts[i][2], parts[i - 1][1], jump_after, jump_before)
            - parts[i][0]
        )
    return [faces[i] - faces[i - 1] for i in range(3, count - 3)]


def half_velocities(fields):
    density, mom_x, mom_y, mom_z, energy = fields
    over = 0.5 / density
    vel = (mom_x * over, mom_y * over, mom_z * over)
    kinetic = mom_x * vel[0] + mom_y * vel[1] + mom_z * vel[2]
    pressure = (gamma_gas - 1.0) * (energy - kinetic)
    return vel, pressure


def half_flux(fields, field, direction, speed, pressure):
    if field == 0:
        return 0.5 * fields[1 + direction]
    if field == 4:
        return (fields[4] + pressure) * speed
    flux = fields[field] * speed
    return flux + 0.5 * pressure if field == 1 + direction else flux


def plane_kernel(with_inner, state, speed, out, turned):
    half_speed = 0.5 * speed[0:1, :]
    lane = lax.broadcasted_iota(jnp.int32, (LANES, LANES), 1)
    to_turned = (lane % 8) * 16 + lane // 8
    to_plain = (lane % 16) * 8 + lane // 16

    def four_planes(part, carry):
        planes = pl.ds(part * 4, 4)
        for f in range(FIELDS):
            plain = state[f, planes].reshape(LANES, LANES)
            turned[f] = jnp.take_along_axis(plain, to_turned, axis=1).T
        for place in range(4):
            fields = [state[f, part * 4 + place] for f in range(FIELDS)]
            vel, pressure = half_velocities(fields)
            for field in range(FIELDS):
                out[field, part * 4 + place] = periodic_divergence(
                    half_flux(fields, field, 1, vel[1], pressure),
                    half_speed * fields[field],
                    y_up,
                    y_up_two,
                    y_down,
                )
        columns = [
            [turned[f, row : row + 8] for row in range(0, LANES, 8)] for f in range(FIELDS)
        ]
        along = [half_velocities(fields) for fields in zip(*columns)]
        for field in range(FIELDS):
            fluxes = [
                half_flux(fields, field, 2, vel[2], pressure)
                for fields, (vel, pressure) in zip(zip(*columns), along)
            ]
            scaled = [half_speed * value for value in columns[field]]
            total = jnp.concatenate(ring_divergence(fluxes, scaled), axis=0)
            plain = jnp.take_along_axis(total.T, to_plain, axis=1)
            out[field, planes] += plain.reshape(4, ROWS, LANES)
        return carry

    lax.fori_loop(0, state.shape[1] // 4, four_planes, 0)

    def group(j, carry):
        rows = pl.ds(pl.multiple_of(j * 8, 8), 8)

        def get(f, plane):
            return state[f, plane, rows, :]

        for field, along_x in across(get, half_speed, range(BLOCK), INNER):
            for plane in range(BLOCK):
                out[field, plane, rows, :] += along_x[plane]
        return carry

    if with_inner:
        lax.fori_loop(0, 4, group, 0)


def along_planes(state, speed, with_inner):
    return pl.pallas_call(
        functools.partial(plane_kernel, with_inner),
        out_shape=jax.ShapeDtypeStruct(state.shape, jnp.float32),
        in_specs=[VMEM, VMEM],
        out_specs=VMEM,
        scratch_shapes=[pltpu.VMEM((FIELDS, LANES, LANES), jnp.float32)],
        compiler_params=params(),
        cost_estimate=cost(20_000_000, 1_000_000),
        name="planes",
    )(state, speed)


def across(get, half_speed, span, parts):
    speeds, pressures = {}, {}
    for plane in span:
        vel, pressure = half_velocities([get(f, plane) for f in range(FIELDS)])
        speeds[plane] = vel[0]
        pressures[plane] = pressure
    for field in range(FIELDS):
        fluxes, scaled = {}, {}
        for plane in span:
            if field == 0:
                flux = 0.5 * get(1, plane)
            elif field == 4:
                flux = (get(4, plane) + pressures[plane]) * speeds[plane]
            else:
                flux = get(field, plane) * speeds[plane]
                if field == 1:
                    flux = flux + 0.5 * pressures[plane]
            fluxes[plane] = flux
            scaled[plane] = half_speed * get(field, plane)
        yield field, x_divergence(fluxes, scaled, *parts)


WITH_HALOS = range(-3, BLOCK + 3)


def first_kernel(
    state, sides, far, near, speed, middle, far_side, near_side, top, below, above
):
    sort_halos(far, near, below, above)
    lower_first = own_is_even()
    half_speed = 0.5 * speed[0:1, :]
    factor = (courant / 6.0) / speed[0:1, :]

    def group(j, best):
        rows = pl.ds(pl.multiple_of(j * 8, 8), 8)

        def get(f, plane):
            if plane < 0:
                return below[f, plane + 3, rows, :]
            if plane >= BLOCK:
                return above[f, plane - BLOCK, rows, :]
            return state[f, plane, rows, :]

        for field, along_x in across(get, half_speed, WITH_HALOS, OUTER):
            values = []
            for plane in range(BLOCK):
                total = sides[field, plane, rows, :]
                if plane in along_x:
                    total = total + along_x[plane]
                values.append(get(field, plane) - factor * total)
                middle[field, plane, rows, :] = values[plane]
            for plane in range(3):
                low, high = values[plane], values[BLOCK - 3 + plane]
                far_side[field, plane, rows, :] = jnp.where(lower_first, low, high)
                near_side[field, plane, rows, :] = jnp.where(lower_first, high, low)
        for plane in range(BLOCK):
            best = jnp.maximum(
                best, wave_speed([middle[f, plane, rows, :] for f in range(FIELDS)])
            )
        return best

    best = lax.fori_loop(0, 4, group, jnp.zeros((8, LANES), jnp.float32))
    top[...] = jnp.full((8, LANES), jnp.max(best), jnp.float32)


def first_stage(*operands):
    whole = jax.ShapeDtypeStruct((FIELDS, BLOCK, ROWS, LANES), jnp.float32)
    halo = jax.ShapeDtypeStruct(HALO, jnp.float32)
    return pl.pallas_call(
        first_kernel,
        out_shape=(whole, halo, halo, jax.ShapeDtypeStruct((8, LANES), jnp.float32)),
        in_specs=[VMEM] * len(operands),
        out_specs=(VMEM,) * 4,
        scratch_shapes=[pltpu.VMEM(HALO, jnp.float32)] * 2,
        compiler_params=params(),
        cost_estimate=cost(30_000_000, 3_000_000),
        name="first_stage",
    )(*operands)


def second_kernel(start, middle, sides, far, near, first_speed, speed, out, below, above):
    sort_halos(far, near, below, above)
    half_speed = 0.5 * speed[0:1, :]
    factor = (courant / 12.0) / first_speed[0:1, :]

    def group(j, carry):
        rows = pl.ds(pl.multiple_of(j * 8, 8), 8)
        spread = pl.ds(j, 8, stride=4)

        def get(f, plane):
            if plane < 0:
                return below[f, plane + 3, rows, :]
            if plane >= BLOCK:
                return above[f, plane - BLOCK, rows, :]
            return middle[f, plane, rows, :]

        for field, along_x in across(get, half_speed, WITH_HALOS, EVERY):
            for plane in range(BLOCK):
                total = along_x[plane] + sides[field, plane, rows, :]
                value = 0.5 * start[field, plane, rows, :] + (
                    0.5 * get(field, plane) - factor * total
                )
                out[field, plane, spread, :] = value
        return carry

    lax.fori_loop(0, 4, group, 0)


def second_stage(*operands):
    return pl.pallas_call(
        second_kernel,
        out_shape=jax.ShapeDtypeStruct((FIELDS, BLOCK, ROWS, LANES), jnp.float32),
        in_specs=[VMEM] * len(operands),
        out_specs=VMEM,
        scratch_shapes=[pltpu.VMEM(HALO, jnp.float32)] * 2,
        compiler_params=params(),
        cost_estimate=cost(30_000_000, 3_000_000),
        name="second_stage",
    )(*operands)


def everyone_max(value, axis, size):
    reach = 1
    while reach * 4 < size:
        reach *= 4
    while reach:
        copies = [value]
        for times in range(1, 4):
            turn = reach * times
            if turn < size:
                pairs = [(i, i ^ turn) for i in range(size)]
                copies.append(lax.ppermute(value, axis, pairs))
        value = functools.reduce(jnp.maximum, copies)
        reach //= 4
    return value


def per_device(blocks, owner_list, slot_list):
    size = lax.axis_size("gx")
    own = lax.axis_index("gx")
    per_dev = blocks.shape[0]
    cap = max(2, 2 * per_dev // size)

    parts = pack(tiled_rows(blocks), owner_list, size, cap, per_dev)
    parts, owner_list, slot_list = lax.optimization_barrier((parts, owner_list, slot_list))
    come = lax.all_to_all(parts, "gx", split_axis=0, concat_axis=0, tiled=True)
    table = arrival_spots(owner_list, slot_list, own, per_dev, size, cap)
    state, far_side, near_side, speed = unpack(table, come.reshape(-1, LANES), size, cap)
    far, near = swapped(far_side, near_side, size)
    sides = along_planes(state, speed, True)
    middle, far_side, near_side, top = first_stage(state, sides, far, near, speed)
    far, near = swapped(far_side, near_side, size)
    second = everyone_max(top, "gx", size)
    sides = along_planes(middle, second, False)
    return second_stage(state, middle, sides, far, near, speed, second)


def solution(mesh):
    return jax.shard_map(
        per_device,
        mesh=mesh,
        in_specs=(P(("runs", "gx"), None, None), P("runs"), P("runs")),
        out_specs=P(None, ("runs", "gx"), None, None),
        check_vma=False,
    )
```

```python
import functools

import jax
import jax.numpy as jnp
from jax import lax
from jax.experimental import pallas as pl
from jax.experimental.pallas import tpu as pltpu
from jax.sharding import PartitionSpec as P

BLOCK = 8
BY = 4
BZ = 16
FIELDS = 5
LANES = 128
ROWS = BY * BLOCK
PAIRS = BLOCK // 2
TILES = PAIRS * FIELDS

gamma_gas = 1.4
courant = 0.25
smooth_epsilon = 1e-06

VMEM = pl.BlockSpec(memory_space=pltpu.VMEM)
SMEM = pl.BlockSpec(memory_space=pltpu.SMEM)


def params(mebibytes=40):
    return pltpu.CompilerParams(vmem_limit_bytes=mebibytes * 1024 * 1024)


def cost(flops, size):
    return pl.CostEstimate(flops=flops, bytes_accessed=size, transcendentals=0)


def wave_speed(fields):
    density, mom_x, mom_y, mom_z, energy = fields
    inverse = 1.0 / density
    vel = (mom_x * inverse, mom_y * inverse, mom_z * inverse)
    kinetic = 0.5 * (mom_x * vel[0] + mom_y * vel[1] + mom_z * vel[2])
    pressure = (gamma_gas - 1.0) * (energy - kinetic)
    sound = jnp.sqrt(gamma_gas * pressure * inverse)
    fastest = jnp.maximum(jnp.maximum(jnp.abs(vel[0]), jnp.abs(vel[1])), jnp.abs(vel[2]))
    return fastest + sound


def tiled_rows(blocks):
    count = blocks.shape[0] // 8
    groups = blocks.reshape(count, 8, FIELDS, PAIRS, LANES).transpose(2, 0, 3, 1, 4)
    return groups.reshape(FIELDS * count * PAIRS * 8, LANES)


def pack_kernel(
    size, cap, per_dev, owner_hbm, rows_hbm, out_hbm, owner, rows, out, top, count, member, sems
):
    own = lax.axis_index("gx")
    fetch_owner = pltpu.make_async_copy(owner_hbm, owner, sems.at[0])
    fetch_rows = pltpu.make_async_copy(rows_hbm, rows, sems.at[1])
    fetch_owner.start()
    fetch_rows.start()

    def clear(dest, carry):
        count[dest] = 0
        return carry

    lax.fori_loop(0, size, clear, 0, unroll=8)
    fetch_owner.wait()

    def note(block, carry):
        dest = owner[own * per_dev + block]
        rank = count[dest]
        count[dest] = rank + 1
        member[dest * cap + rank] = lax.div(block, 8) * (PAIRS * 8) + lax.rem(block, 8)
        return carry

    lax.fori_loop(0, per_dev, note, 0, unroll=8)
    fetch_rows.wait()
    tiles = TILES * cap

    def message(dest, carry):
        @pl.when(count[dest] > 0)
        def _():
            for rank in range(cap):
                first = member[dest * cap + rank]
                for pair in range(PAIRS):
                    source = pl.ds(first + pair * 8, FIELDS, stride=per_dev * PAIRS)
                    to = dest * tiles + pair * (FIELDS * cap) + rank
                    out[pl.ds(to, FIELDS, stride=cap), :] = rows[source, :]
            part = out.at[pl.ds(pl.multiple_of(dest * tiles, tiles), tiles)]
            pltpu.make_async_copy(part, out_hbm.at[dest, pl.ds(0, tiles), 0], sems.at[2]).start()

        return carry

    lax.fori_loop(0, size, message, 0)
    best = jnp.zeros((8, LANES), jnp.float32)
    step = per_dev * PAIRS
    for first in range(0, step, 8):
        fields = [rows[f * step + first : f * step + first + 8, :] for f in range(FIELDS)]
        best = jnp.maximum(best, wave_speed(fields))
    top[...] = jnp.full(top.shape, jnp.max(best), jnp.float32)
    for dest in range(size):
        pltpu.make_async_copy(
            top.at[pl.ds(dest, 1)], out_hbm.at[dest, tiles], sems.at[3]
        ).start()
    half = out.at[pl.ds(0, per_dev * TILES)]
    pltpu.make_async_copy(half, half, sems.at[2]).wait()
    pltpu.make_async_copy(top, top, sems.at[3]).wait()


def pack(rows, owner_list, size, cap, per_dev):
    return pl.pallas_call(
        functools.partial(pack_kernel, size, cap, per_dev),
        out_shape=jax.ShapeDtypeStruct((size, TILES * cap + 1, 1, LANES), jnp.float32),
        in_specs=[pl.BlockSpec(memory_space=pltpu.HBM)] * 2,
        out_specs=pl.BlockSpec(memory_space=pltpu.HBM),
        scratch_shapes=[
            pltpu.SMEM(owner_list.shape, jnp.int32),
            pltpu.VMEM(rows.shape, jnp.float32),
            pltpu.VMEM((size * TILES * cap, LANES), jnp.float32),
            pltpu.VMEM((size, LANES), jnp.float32),
            pltpu.SMEM((size,), jnp.int32),
            pltpu.SMEM((size * cap,), jnp.int32),
            pltpu.SemaphoreType.DMA((4,)),
        ],
        compiler_params=params(62),
        cost_estimate=cost(1_000_000, 3_000_000),
        name="pack",
    )(owner_list, rows)


def own_is_even():
    return lax.axis_index("gx") % 2 == 0


def swapped(far_side, near_side, size):
    apart = [(i, (i - 1 if i % 2 == 0 else i + 1) % size) for i in range(size)]
    chip = [(i, i ^ 1) for i in range(size)]
    return lax.ppermute(far_side, "gx", apart), lax.ppermute(near_side, "gx", chip)


def sort_halos(far, near, below, above):
    lower_first = own_is_even()
    for f in range(FIELDS):
        for plane in range(3):
            one, two = far[f, plane], near[f, plane]
            below[f, plane] = jnp.where(lower_first, one, two)
            above[f, plane] = jnp.where(lower_first, two, one)


HALO = (FIELDS, 3, ROWS, LANES)


def arrival_spots(owner_list, slot_list, own, per_dev, size, cap):
    owners = owner_list.reshape(size, per_dev)
    slots = slot_list.reshape(size, per_dev)
    mine = owners == own
    spot = jnp.arange(per_dev, dtype=jnp.int32)
    earlier = spot[None, :] < spot[:, None]
    rank = jnp.sum((mine[:, None, :] & earlier[None]).astype(jnp.int32), axis=2)
    row = jnp.arange(size, dtype=jnp.int32)[:, None] * cap + rank
    key = jnp.where(mine, slots, -1)
    hit = key.reshape(1, -1) == spot[:, None]
    return jnp.max(jnp.where(hit, row.reshape(1, -1), 0), axis=1)


def exchanged_bits(rows, group):
    rows = list(rows)
    for bit in range(4):
        step = 1 << bit
        low = (group & step) == 0
        for index in range(16):
            if index & step:
                continue
            first, second = rows[index], rows[index | step]
            rows[index] = jnp.where(low, first, pltpu.roll(second, 8 * step, 1))
            rows[index | step] = jnp.where(low, pltpu.roll(first, LANES - 8 * step, 1), second)
    return rows


def unpack_kernel(size, cap, table, come, state, far_side, near_side, speed, scratch):
    message = TILES * cap + 1
    best = come[message - 1 : message, :]
    for source in range(1, size):
        best = jnp.maximum(best, come[(source + 1) * message - 1 : (source + 1) * message, :])
    speed[...] = jnp.broadcast_to(best, speed.shape)
    for slot in range(BY * BZ):
        p, q = divmod(slot, BZ)
        where = table[slot]
        source = lax.div(where, cap)
        rank = lax.rem(where, cap)
        for pair in range(PAIRS):
            couple, h = divmod(pair, 2)
            base = source * message + rank + pair * (FIELDS * cap)
            value = come[pl.ds(base, FIELDS, stride=cap), :]
            row = (couple * BZ + q) * 8 + 2 * p + h
            scratch[pl.ds(row, FIELDS, stride=PAIRS // 2 * BZ * 8), :] = value
    group = lax.broadcasted_iota(jnp.int32, (8, LANES), 1) // BLOCK
    even = lax.broadcasted_iota(jnp.int32, (8, LANES), 0) % 2 == 0

    for f in range(FIELDS):
        for couple in range(PAIRS // 2):
            first = (f * (PAIRS // 2) + couple) * BZ * 8
            rows = [scratch[first + q * 8 : first + q * 8 + 8, :] for q in range(BZ)]
            moved = exchanged_bits(rows, group)
            for second in range(2):
                for j in range(4):
                    lower = moved[second * BLOCK + j]
                    upper = moved[second * BLOCK + j + 4]
                    planes = (
                        jnp.where(even, lower, pltpu.roll(upper, 1, 0)),
                        jnp.where(even, pltpu.roll(lower, 7, 0), upper),
                    )
                    rows = slice(j * 8, j * 8 + 8)
                    for h in range(2):
                        plane = 4 * couple + 2 * h + second
                        state[f, plane, rows, :] = planes[h]
    lower_first = own_is_even()
    for f in range(FIELDS):
        for plane in range(3):
            low, high = state[f, plane], state[f, BLOCK - 3 + plane]
            far_side[f, plane] = jnp.where(lower_first, low, high)
            near_side[f, plane] = jnp.where(lower_first, high, low)


def unpack(table, come, size, cap):
    halo = jax.ShapeDtypeStruct(HALO, jnp.float32)
    return pl.pallas_call(
        functools.partial(unpack_kernel, size, cap),
        out_shape=(
            jax.ShapeDtypeStruct((FIELDS, BLOCK, ROWS, LANES), jnp.float32),
            halo,
            halo,
            jax.ShapeDtypeStruct((8, LANES), jnp.float32),
        ),
        in_specs=[SMEM, VMEM],
        out_specs=(VMEM,) * 4,
        scratch_shapes=[pltpu.VMEM((FIELDS * (PAIRS // 2) * BZ * 8, LANES), jnp.float32)],
        compiler_params=params(),
        cost_estimate=cost(5_000_000, 2_000_000),
        name="unpack",
    )(table, come)


def y_up(x):
    return jnp.concatenate([x[8:], pltpu.roll(x[:8], 7, 0)], axis=0)


def y_down(x):
    return jnp.concatenate([pltpu.roll(x[24:], 1, 0), x[:24]], axis=0)


def y_up_two(x):
    return jnp.concatenate([x[16:], pltpu.roll(x[:8], 7, 0), pltpu.roll(x[8:16], 7, 0)], axis=0)


def inverse(x):
    return 1.0 / x


def smoothness(before, after):
    curve = after - before
    middle = 0.5 * (after + before)
    base = curve * curve * (13.0 / 12.0) + smooth_epsilon
    plus = middle + curve
    minus = middle - curve
    left = inverse(base + plus * plus)
    centre = inverse(base + middle * middle)
    right = inverse(base + minus * minus)
    return curve, left * left, centre * centre, right * right


def upwind_term(left, centre, right, jump_before, jump_after):
    right = 3.0 * right
    top = left * (jump_before + jump_before) + right * jump_after
    return top * inverse(left + 6.0 * centre + right)


def periodic_divergence(half_flux, scaled, up, up_two, down):
    plus = half_flux + scaled
    minus = half_flux - scaled

    def side(values):
        after = up(values) - values
        curve, left, centre, right = smoothness(down(after), after)
        above = up(curve)
        return curve, above, left, centre, right, above - curve

    curve, _, left, centre, right, jump = side(plus)
    face = 6.0 * (half_flux + up(half_flux)) - curve
    face = face - upwind_term(down(left), centre, up(right), down(jump), jump)
    _, curve, left, centre, right, jump = side(minus)
    face = face + (upwind_term(up_two(right), up(centre), left, up(jump), jump) - curve)
    return face - down(face)


def ring_divergence(half_flux, scaled):
    count = len(half_flux)

    def up(values):
        return values[1:] + [pltpu.roll(values[0], 7, 0)]

    def down(values):
        return [pltpu.roll(values[-1], 1, 0)] + values[:-1]

    def side(values):
        after = [above - value for above, value in zip(up(values), values)]
        parts = [smoothness(before, step) for before, step in zip(down(after), after)]
        curve, left, centre, right = (list(part) for part in zip(*parts))
        jump = [above - value for above, value in zip(up(curve), curve)]
        return curve, left, centre, right, jump

    curve, left, centre, right, jump = side([a + b for a, b in zip(half_flux, scaled)])
    terms = zip(down(left), centre, up(right), down(jump), jump)
    face = [
        6.0 * (here + above) - bend - upwind_term(*term)
        for here, above, bend, term in zip(half_flux, up(half_flux), curve, terms)
    ]
    curve, left, centre, right, jump = side([a - b for a, b in zip(half_flux, scaled)])
    terms = zip(up(right), centre, down(left), jump, down(jump))
    other = [upwind_term(*term) - bend for bend, term in zip(curve, terms)]
    face = [one + two for one, two in zip(face, up(other))]
    return [here - below for here, below in zip(face, down(face))]


def x_divergence(half_flux, scaled, plus_at, minus_at, centre_at):
    faces = {i: 6.0 * (half_flux[i] + half_flux[i + 1]) for i in centre_at}

    def add(i, value):
        faces[i] = faces[i] + value if i in faces else value

    def side(sign):
        values = {i: half_flux[i] + sign * scaled[i] for i in half_flux}
        steps = {i: values[i + 1] - values[i] for i in values if i + 1 in values}
        return {i: smoothness(steps[i - 1], steps[i]) for i in steps if i - 1 in steps}

    parts = side(1)
    for i in plus_at:
        curve, left, centre, right = zip(parts[i - 1], parts[i], parts[i + 1])
        term = upwind_term(left[0], centre[1], right[2], curve[1] - curve[0], curve[2] - curve[1])
        add(i, -(curve[1] + term))
    parts = side(-1)
    for i in minus_at:
        curve, left, centre, right = zip(parts[i - 1], parts[i], parts[i + 1])
        term = upwind_term(right[2], centre[1], left[0], curve[2] - curve[1], curve[1] - curve[0])
        add(i - 1, term - curve[1])
    total = {}
    for i in range(BLOCK):
        if i in faces:
            total[i] = faces[i]
        if i - 1 in faces:
            total[i] = total[i] - faces[i - 1] if i in total else -faces[i - 1]
    return total


INNER = (range(2, 6), range(2, 6), range(0, 7))
OUTER = ((-1, 0, 1, 6, 7), (0, 1, 6, 7, 8), (-1, 7))
EVERY = (range(-1, 8), range(0, 9), range(-1, 8))


def ring_divergence(half_flux, scaled):
    count = len(half_flux)

    def up(values):
        return values[1:] + [pltpu.roll(values[0], 7, 0)]

    def down(values):
        return [pltpu.roll(values[-1], 1, 0)] + values[:-1]

    def side(values):
        after = [above - value for above, value in zip(up(values), values)]
        parts = [smoothness(before, step) for before, step in zip(down(after), after)]
        curve, left, centre, right = (list(part) for part in zip(*parts))
        jump = [above - value for above, value in zip(up(curve), curve)]
        return curve, left, centre, right, jump

    curve, left, centre, right, jump = side([a + b for a, b in zip(half_flux, scaled)])
    terms = zip(down(left), centre, up(right), down(jump), jump)
    face = [
        6.0 * (here + above) - bend - upwind_term(*term)
        for here, above, bend, term in zip(half_flux, up(half_flux), curve, terms)
    ]
    curve, left, centre, right, jump = side([a - b for a, b in zip(half_flux, scaled)])
    terms = zip(up(right), centre, down(left), jump, down(jump))
    other = [upwind_term(*term) - bend for bend, term in zip(curve, terms)]
    face = [one + two for one, two in zip(face, up(other))]
    return [here - below for here, below in zip(face, down(face))]


def open_divergence(half_flux, scaled):
    count = len(half_flux)
    plus = [a + b for a, b in zip(half_flux, scaled)]
    minus = [a - b for a, b in zip(half_flux, scaled)]
    faces = [None] * count

    def side(values):
        steps = [values[i + 1] - values[i] for i in range(count - 1)]
        parts = [None] + [smoothness(steps[i - 1], steps[i]) for i in range(1, count - 1)]
        return parts

    parts = side(plus)
    for i in range(2, count - 3):
        jump_before = parts[i][0] - parts[i - 1][0]
        jump_after = parts[i + 1][0] - parts[i][0]
        faces[i] = 6.0 * (half_flux[i] + half_flux[i + 1]) - parts[i][0] - upwind_term(
            parts[i - 1][1], parts[i][2], parts[i + 1][3], jump_before, jump_after
        )
    parts = side(minus)
    for i in range(3, count - 2):
        jump_before = parts[i][0] - parts[i - 1][0]
        jump_after = parts[i + 1][0] - parts[i][0]
        faces[i - 1] = faces[i - 1] + (
            upwind_term(parts[i + 1][3], parts[i][2], parts[i - 1][1], jump_after, jump_before)
            - parts[i][0]
        )
    return [faces[i] - faces[i - 1] for i in range(3, count - 3)]


def half_velocities(fields):
    density, mom_x, mom_y, mom_z, energy = fields
    over = 0.5 / density
    vel = (mom_x * over, mom_y * over, mom_z * over)
    kinetic = mom_x * vel[0] + mom_y * vel[1] + mom_z * vel[2]
    pressure = (gamma_gas - 1.0) * (energy - kinetic)
    return vel, pressure


def half_flux(fields, field, direction, speed, pressure):
    if field == 0:
        return 0.5 * fields[1 + direction]
    if field == 4:
        return (fields[4] + pressure) * speed
    flux = fields[field] * speed
    return flux + 0.5 * pressure if field == 1 + direction else flux


def plane_kernel(with_inner, state, speed, out, turned):
    half_speed = 0.5 * speed[0:1, :]
    lane = lax.broadcasted_iota(jnp.int32, (LANES, LANES), 1)
    to_turned = (lane % 8) * 16 + lane // 8
    to_plain = (lane % 16) * 8 + lane // 16

    def four_planes(part, carry):
        planes = pl.ds(part * 4, 4)
        for f in range(FIELDS):
            plain = state[f, planes].reshape(LANES, LANES)
            turned[f] = jnp.take_along_axis(plain, to_turned, axis=1).T
        for place in range(4):
            fields = [state[f, part * 4 + place] for f in range(FIELDS)]
            vel, pressure = half_velocities(fields)
            for field in range(FIELDS):
                out[field, part * 4 + place] = periodic_divergence(
                    half_flux(fields, field, 1, vel[1], pressure),
                    half_speed * fields[field],
                    y_up,
                    y_up_two,
                    y_down,
                )
        columns = [
            [turned[f, row : row + 8] for row in range(0, LANES, 8)] for f in range(FIELDS)
        ]
        along = [half_velocities(fields) for fields in zip(*columns)]
        for field in range(FIELDS):
            fluxes = [
                half_flux(fields, field, 2, vel[2], pressure)
                for fields, (vel, pressure) in zip(zip(*columns), along)
            ]
            scaled = [half_speed * value for value in columns[field]]
            total = jnp.concatenate(ring_divergence(fluxes, scaled), axis=0)
            plain = jnp.take_along_axis(total.T, to_plain, axis=1)
            out[field, planes] += plain.reshape(4, ROWS, LANES)
        return carry

    lax.fori_loop(0, state.shape[1] // 4, four_planes, 0)

    def group(j, carry):
        rows = pl.ds(pl.multiple_of(j * 8, 8), 8)

        def get(f, plane):
            return state[f, plane, rows, :]

        for field, along_x in across(get, half_speed, range(BLOCK), INNER):
            for plane in range(BLOCK):
                out[field, plane, rows, :] += along_x[plane]
        return carry

    if with_inner:
        lax.fori_loop(0, 4, group, 0)


def along_planes(state, speed, with_inner):
    return pl.pallas_call(
        functools.partial(plane_kernel, with_inner),
        out_shape=jax.ShapeDtypeStruct(state.shape, jnp.float32),
        in_specs=[VMEM, VMEM],
        out_specs=VMEM,
        scratch_shapes=[pltpu.VMEM((FIELDS, LANES, LANES), jnp.float32)],
        compiler_params=params(),
        cost_estimate=cost(20_000_000, 1_000_000),
        name="planes",
    )(state, speed)


def across(get, half_speed, span, parts):
    speeds, pressures = {}, {}
    for plane in span:
        vel, pressure = half_velocities([get(f, plane) for f in range(FIELDS)])
        speeds[plane] = vel[0]
        pressures[plane] = pressure
    for field in range(FIELDS):
        fluxes, scaled = {}, {}
        for plane in span:
            if field == 0:
                flux = 0.5 * get(1, plane)
            elif field == 4:
                flux = (get(4, plane) + pressures[plane]) * speeds[plane]
            else:
                flux = get(field, plane) * speeds[plane]
                if field == 1:
                    flux = flux + 0.5 * pressures[plane]
            fluxes[plane] = flux
            scaled[plane] = half_speed * get(field, plane)
        yield field, x_divergence(fluxes, scaled, *parts)


WITH_HALOS = range(-3, BLOCK + 3)


def first_kernel(
    state, sides, far, near, speed, middle, far_side, near_side, top, below, above
):
    sort_halos(far, near, below, above)
    lower_first = own_is_even()
    half_speed = 0.5 * speed[0:1, :]
    factor = (courant / 6.0) / speed[0:1, :]

    def group(j, best):
        rows = pl.ds(pl.multiple_of(j * 8, 8), 8)

        def get(f, plane):
            if plane < 0:
                return below[f, plane + 3, rows, :]
            if plane >= BLOCK:
                return above[f, plane - BLOCK, rows, :]
            return state[f, plane, rows, :]

        for field, along_x in across(get, half_speed, WITH_HALOS, OUTER):
            values = []
            for plane in range(BLOCK):
                total = sides[field, plane, rows, :]
                if plane in along_x:
                    total = total + along_x[plane]
                values.append(get(field, plane) - factor * total)
                middle[field, plane, rows, :] = values[plane]
            for plane in range(3):
                low, high = values[plane], values[BLOCK - 3 + plane]
                far_side[field, plane, rows, :] = jnp.where(lower_first, low, high)
                near_side[field, plane, rows, :] = jnp.where(lower_first, high, low)
        for plane in range(BLOCK):
            best = jnp.maximum(
                best, wave_speed([middle[f, plane, rows, :] for f in range(FIELDS)])
            )
        return best

    best = lax.fori_loop(0, 4, group, jnp.zeros((8, LANES), jnp.float32))
    top[...] = jnp.full((8, LANES), jnp.max(best), jnp.float32)


def first_stage(*operands):
    whole = jax.ShapeDtypeStruct((FIELDS, BLOCK, ROWS, LANES), jnp.float32)
    halo = jax.ShapeDtypeStruct(HALO, jnp.float32)
    return pl.pallas_call(
        first_kernel,
        out_shape=(whole, halo, halo, jax.ShapeDtypeStruct((8, LANES), jnp.float32)),
        in_specs=[VMEM] * len(operands),
        out_specs=(VMEM,) * 4,
        scratch_shapes=[pltpu.VMEM(HALO, jnp.float32)] * 2,
        compiler_params=params(),
        cost_estimate=cost(30_000_000, 3_000_000),
        name="first_stage",
    )(*operands)


def second_kernel(start, middle, sides, far, near, first_speed, speed, out, below, above):
    sort_halos(far, near, below, above)
    half_speed = 0.5 * speed[0:1, :]
    factor = (courant / 12.0) / first_speed[0:1, :]

    def group(j, carry):
        rows = pl.ds(pl.multiple_of(j * 8, 8), 8)
        spread = pl.ds(j, 8, stride=4)

        def get(f, plane):
            if plane < 0:
                return below[f, plane + 3, rows, :]
            if plane >= BLOCK:
                return above[f, plane - BLOCK, rows, :]
            return middle[f, plane, rows, :]

        for field, along_x in across(get, half_speed, WITH_HALOS, EVERY):
            for plane in range(BLOCK):
                total = along_x[plane] + sides[field, plane, rows, :]
                value = 0.5 * start[field, plane, rows, :] + (
                    0.5 * get(field, plane) - factor * total
                )
                out[field, plane, spread, :] = value
        return carry

    lax.fori_loop(0, 4, group, 0)


def second_stage(*operands):
    return pl.pallas_call(
        second_kernel,
        out_shape=jax.ShapeDtypeStruct((FIELDS, BLOCK, ROWS, LANES), jnp.float32),
        in_specs=[VMEM] * len(operands),
        out_specs=VMEM,
        scratch_shapes=[pltpu.VMEM(HALO, jnp.float32)] * 2,
        compiler_params=params(),
        cost_estimate=cost(30_000_000, 3_000_000),
        name="second_stage",
    )(*operands)


def max_rounds(size):
    rounds = []
    while size > 4:
        width = 4 if size >= 16 else 2
        size //= width
        rounds.append([size * times for times in range(1, width)])
    return rounds + [[size // 2]] * (size == 4) + [[1]] * (size > 1)


def everyone_max(value, axis, size):
    for turns in max_rounds(size):
        copies = [value]
        for turn in turns:
            pairs = [(i, i ^ turn) for i in range(size)]
            copies.append(lax.ppermute(value, axis, pairs))
        value = functools.reduce(jnp.maximum, copies)
    return value


def per_device(blocks, owner_list, slot_list):
    size = lax.axis_size("gx")
    own = lax.axis_index("gx")
    per_dev = blocks.shape[0]
    cap = max(2, 2 * per_dev // size)

    parts = pack(tiled_rows(blocks), owner_list, size, cap, per_dev)
    parts, owner_list, slot_list = lax.optimization_barrier((parts, owner_list, slot_list))
    come = lax.all_to_all(parts, "gx", split_axis=0, concat_axis=0, tiled=True)
    table = arrival_spots(owner_list, slot_list, own, per_dev, size, cap)
    state, far_side, near_side, speed = unpack(table, come.reshape(-1, LANES), size, cap)
    far, near = swapped(far_side, near_side, size)
    sides = along_planes(state, speed, True)
    middle, far_side, near_side, top = first_stage(state, sides, far, near, speed)
    far, near = swapped(far_side, near_side, size)
    second = everyone_max(top, "gx", size)
    sides = along_planes(middle, second, False)
    return second_stage(state, middle, sides, far, near, speed, second)


def solution(mesh):
    return jax.shard_map(
        per_device,
        mesh=mesh,
        in_specs=(P(("runs", "gx"), None, None), P("runs"), P("runs")),
        out_specs=P(None, ("runs", "gx"), None, None),
        check_vma=False,
    )
```

```python
import functools

import jax
import jax.numpy as jnp
from jax import lax
from jax.experimental import pallas as pl
from jax.experimental.pallas import tpu as pltpu
from jax.sharding import PartitionSpec as P

BLOCK = 8
BY = 4
BZ = 16
FIELDS = 5
LANES = 128
ROWS = BY * BLOCK
PAIRS = BLOCK // 2
TILES = PAIRS * FIELDS

gamma_gas = 1.4
courant = 0.25
smooth_epsilon = 1e-06

VMEM = pl.BlockSpec(memory_space=pltpu.VMEM)
SMEM = pl.BlockSpec(memory_space=pltpu.SMEM)


def params(mebibytes=40):
    return pltpu.CompilerParams(vmem_limit_bytes=mebibytes * 1024 * 1024)


def cost(flops, size):
    return pl.CostEstimate(flops=flops, bytes_accessed=size, transcendentals=0)


def wave_speed(fields):
    density, mom_x, mom_y, mom_z, energy = fields
    inverse = 1.0 / density
    vel = (mom_x * inverse, mom_y * inverse, mom_z * inverse)
    kinetic = 0.5 * (mom_x * vel[0] + mom_y * vel[1] + mom_z * vel[2])
    pressure = (gamma_gas - 1.0) * (energy - kinetic)
    sound = jnp.sqrt(gamma_gas * pressure * inverse)
    fastest = jnp.maximum(jnp.maximum(jnp.abs(vel[0]), jnp.abs(vel[1])), jnp.abs(vel[2]))
    return fastest + sound


def tiled_rows(blocks):
    count = blocks.shape[0] // 8
    groups = blocks.reshape(count, 8, FIELDS, PAIRS, LANES).transpose(2, 0, 3, 1, 4)
    return groups.reshape(FIELDS * count * PAIRS * 8, LANES)


def pack_kernel(
    size, cap, per_dev, owner_hbm, rows_hbm, out_hbm, owner, rows, out, top, count, member, sems
):
    own = lax.axis_index("gx")
    fetch_owner = pltpu.make_async_copy(owner_hbm, owner, sems.at[0])
    fetch_rows = pltpu.make_async_copy(rows_hbm, rows, sems.at[1])
    fetch_owner.start()
    fetch_rows.start()

    def clear(dest, carry):
        count[dest] = 0
        return carry

    lax.fori_loop(0, size, clear, 0, unroll=8)
    fetch_owner.wait()

    def note(block, carry):
        dest = owner[own * per_dev + block]
        rank = count[dest]
        count[dest] = rank + 1
        member[dest * cap + rank] = lax.div(block, 8) * (PAIRS * 8) + lax.rem(block, 8)
        return carry

    lax.fori_loop(0, per_dev, note, 0, unroll=8)
    fetch_rows.wait()
    tiles = TILES * cap

    def message(dest, carry):
        @pl.when(count[dest] > 0)
        def _():
            for rank in range(cap):
                first = member[dest * cap + rank]
                for pair in range(PAIRS):
                    source = pl.ds(first + pair * 8, FIELDS, stride=per_dev * PAIRS)
                    to = dest * tiles + pair * (FIELDS * cap) + rank
                    out[pl.ds(to, FIELDS, stride=cap), :] = rows[source, :]
            part = out.at[pl.ds(pl.multiple_of(dest * tiles, tiles), tiles)]
            pltpu.make_async_copy(part, out_hbm.at[dest, pl.ds(0, tiles), 0], sems.at[2]).start()

        return carry

    lax.fori_loop(0, size, message, 0)
    best = jnp.zeros((8, LANES), jnp.float32)
    step = per_dev * PAIRS
    for first in range(0, step, 8):
        fields = [rows[f * step + first : f * step + first + 8, :] for f in range(FIELDS)]
        best = jnp.maximum(best, wave_speed(fields))
    top[...] = jnp.full(top.shape, jnp.max(best), jnp.float32)
    for dest in range(size):
        pltpu.make_async_copy(
            top.at[pl.ds(dest, 1)], out_hbm.at[dest, tiles], sems.at[3]
        ).start()
    half = out.at[pl.ds(0, per_dev * TILES)]
    pltpu.make_async_copy(half, half, sems.at[2]).wait()
    pltpu.make_async_copy(top, top, sems.at[3]).wait()


def pack(rows, owner_list, size, cap, per_dev):
    return pl.pallas_call(
        functools.partial(pack_kernel, size, cap, per_dev),
        out_shape=jax.ShapeDtypeStruct((size, TILES * cap + 1, 1, LANES), jnp.float32),
        in_specs=[pl.BlockSpec(memory_space=pltpu.HBM)] * 2,
        out_specs=pl.BlockSpec(memory_space=pltpu.HBM),
        scratch_shapes=[
            pltpu.SMEM(owner_list.shape, jnp.int32),
            pltpu.VMEM(rows.shape, jnp.float32),
            pltpu.VMEM((size * TILES * cap, LANES), jnp.float32),
            pltpu.VMEM((size, LANES), jnp.float32),
            pltpu.SMEM((size,), jnp.int32),
            pltpu.SMEM((size * cap,), jnp.int32),
            pltpu.SemaphoreType.DMA((4,)),
        ],
        compiler_params=params(62),
        cost_estimate=cost(1_000_000, 3_000_000),
        name="pack",
    )(owner_list, rows)


def own_is_even():
    return lax.axis_index("gx") % 2 == 0


def swapped(far_side, near_side, size):
    apart = [(i, (i - 1 if i % 2 == 0 else i + 1) % size) for i in range(size)]
    chip = [(i, i ^ 1) for i in range(size)]
    return lax.ppermute(far_side, "gx", apart), lax.ppermute(near_side, "gx", chip)


def sort_halos(far, near, below, above):
    lower_first = own_is_even()
    for f in range(FIELDS):
        for plane in range(3):
            one, two = far[f, plane], near[f, plane]
            below[f, plane] = jnp.where(lower_first, one, two)
            above[f, plane] = jnp.where(lower_first, two, one)


HALO = (FIELDS, 3, ROWS, LANES)


def arrival_spots(owner_list, slot_list, own, per_dev, size, cap):
    owners = owner_list.reshape(size, per_dev)
    slots = slot_list.reshape(size, per_dev)
    mine = owners == own
    spot = jnp.arange(per_dev, dtype=jnp.int32)
    earlier = spot[None, :] < spot[:, None]
    rank = jnp.sum((mine[:, None, :] & earlier[None]).astype(jnp.int32), axis=2)
    row = jnp.arange(size, dtype=jnp.int32)[:, None] * (TILES * cap + 1) + rank
    key = jnp.where(mine, slots, -1)
    hit = key.reshape(1, -1) == spot[:, None]
    return jnp.max(jnp.where(hit, row.reshape(1, -1), 0), axis=1)


def exchanged_bits(rows, group):
    rows = list(rows)
    for bit in range(4):
        step = 1 << bit
        low = (group & step) == 0
        for index in range(16):
            if index & step:
                continue
            first, second = rows[index], rows[index | step]
            rows[index] = jnp.where(low, first, pltpu.roll(second, 8 * step, 1))
            rows[index | step] = jnp.where(low, pltpu.roll(first, LANES - 8 * step, 1), second)
    return rows


def unpack_kernel(size, cap, table, come, state, far_side, near_side, speed, scratch):
    message = TILES * cap + 1
    best = come[message - 1 : message, :]
    for source in range(1, size):
        best = jnp.maximum(best, come[(source + 1) * message - 1 : (source + 1) * message, :])
    speed[...] = jnp.broadcast_to(best, speed.shape)
    group = lax.broadcasted_iota(jnp.int32, (8, LANES), 1) // BLOCK
    even = lax.broadcasted_iota(jnp.int32, (8, LANES), 0) % 2 == 0
    half = FIELDS * BZ * 8

    def gather(couple, slot):
        p, q = divmod(slot, BZ)
        for h in range(2):
            base = table[slot] + (2 * couple + h) * (FIELDS * cap)
            value = come[pl.ds(base, FIELDS, stride=cap), :]
            scratch[pl.ds(couple * half + q * 8 + 2 * p + h, FIELDS, stride=BZ * 8), :] = value

    def arrange(couple, f):
        first = couple * half + f * BZ * 8
        moved = exchanged_bits(
            [scratch[first + q * 8 : first + q * 8 + 8, :] for q in range(BZ)], group
        )
        for second in range(2):
            for j in range(4):
                lower = moved[second * BLOCK + j]
                upper = moved[second * BLOCK + j + 4]
                planes = (
                    jnp.where(even, lower, pltpu.roll(upper, 1, 0)),
                    jnp.where(even, pltpu.roll(lower, 7, 0), upper),
                )
                for h in range(2):
                    state[f, 4 * couple + 2 * h + second, j * 8 : j * 8 + 8, :] = planes[h]

    for slot in range(BY * BZ):
        gather(0, slot)
    for f in range(FIELDS):
        for slot in range(f, BY * BZ, FIELDS):
            gather(1, slot)
        arrange(0, f)
    for f in range(FIELDS):
        arrange(1, f)
    lower_first = own_is_even()
    for f in range(FIELDS):
        for plane in range(3):
            low, high = state[f, plane], state[f, BLOCK - 3 + plane]
            far_side[f, plane] = jnp.where(lower_first, low, high)
            near_side[f, plane] = jnp.where(lower_first, high, low)


def unpack(table, come, size, cap):
    halo = jax.ShapeDtypeStruct(HALO, jnp.float32)
    return pl.pallas_call(
        functools.partial(unpack_kernel, size, cap),
        out_shape=(
            jax.ShapeDtypeStruct((FIELDS, BLOCK, ROWS, LANES), jnp.float32),
            halo,
            halo,
            jax.ShapeDtypeStruct((8, LANES), jnp.float32),
        ),
        in_specs=[SMEM, VMEM],
        out_specs=(VMEM,) * 4,
        scratch_shapes=[pltpu.VMEM((FIELDS * (PAIRS // 2) * BZ * 8, LANES), jnp.float32)],
        compiler_params=params(),
        cost_estimate=cost(5_000_000, 2_000_000),
        name="unpack",
    )(table, come)


def y_up(x):
    return jnp.concatenate([x[8:], pltpu.roll(x[:8], 7, 0)], axis=0)


def y_down(x):
    return jnp.concatenate([pltpu.roll(x[24:], 1, 0), x[:24]], axis=0)


def y_up_two(x):
    return jnp.concatenate([x[16:], pltpu.roll(x[:8], 7, 0), pltpu.roll(x[8:16], 7, 0)], axis=0)


def inverse(x):
    return 1.0 / x


def smoothness(before, after):
    curve = after - before
    middle = 0.5 * (after + before)
    base = curve * curve * (13.0 / 12.0) + smooth_epsilon
    plus = middle + curve
    minus = middle - curve
    left = inverse(base + plus * plus)
    centre = inverse(base + middle * middle)
    right = inverse(base + minus * minus)
    return curve, left * left, centre * centre, right * right


def upwind_term(left, centre, right, jump_before, jump_after):
    right = 3.0 * right
    top = left * (jump_before + jump_before) + right * jump_after
    return top * inverse(left + 6.0 * centre + right)


def periodic_divergence(half_flux, scaled, up, up_two, down):
    plus = half_flux + scaled
    minus = half_flux - scaled

    def side(values):
        after = up(values) - values
        curve, left, centre, right = smoothness(down(after), after)
        above = up(curve)
        return curve, above, left, centre, right, above - curve

    curve, _, left, centre, right, jump = side(plus)
    face = 6.0 * (half_flux + up(half_flux)) - curve
    face = face - upwind_term(down(left), centre, up(right), down(jump), jump)
    _, curve, left, centre, right, jump = side(minus)
    face = face + (upwind_term(up_two(right), up(centre), left, up(jump), jump) - curve)
    return face - down(face)


def ring_divergence(half_flux, scaled):
    count = len(half_flux)

    def up(values):
        return values[1:] + [pltpu.roll(values[0], 7, 0)]

    def down(values):
        return [pltpu.roll(values[-1], 1, 0)] + values[:-1]

    def side(values):
        after = [above - value for above, value in zip(up(values), values)]
        parts = [smoothness(before, step) for before, step in zip(down(after), after)]
        curve, left, centre, right = (list(part) for part in zip(*parts))
        jump = [above - value for above, value in zip(up(curve), curve)]
        return curve, left, centre, right, jump

    curve, left, centre, right, jump = side([a + b for a, b in zip(half_flux, scaled)])
    terms = zip(down(left), centre, up(right), down(jump), jump)
    face = [
        6.0 * (here + above) - bend - upwind_term(*term)
        for here, above, bend, term in zip(half_flux, up(half_flux), curve, terms)
    ]
    curve, left, centre, right, jump = side([a - b for a, b in zip(half_flux, scaled)])
    terms = zip(up(right), centre, down(left), jump, down(jump))
    other = [upwind_term(*term) - bend for bend, term in zip(curve, terms)]
    face = [one + two for one, two in zip(face, up(other))]
    return [here - below for here, below in zip(face, down(face))]


def x_divergence(half_flux, scaled, plus_at, minus_at, centre_at):
    faces = {i: 6.0 * (half_flux[i] + half_flux[i + 1]) for i in centre_at}

    def add(i, value):
        faces[i] = faces[i] + value if i in faces else value

    def side(sign):
        values = {i: half_flux[i] + sign * scaled[i] for i in half_flux}
        steps = {i: values[i + 1] - values[i] for i in values if i + 1 in values}
        return {i: smoothness(steps[i - 1], steps[i]) for i in steps if i - 1 in steps}

    parts = side(1)
    for i in plus_at:
        curve, left, centre, right = zip(parts[i - 1], parts[i], parts[i + 1])
        term = upwind_term(left[0], centre[1], right[2], curve[1] - curve[0], curve[2] - curve[1])
        add(i, -(curve[1] + term))
    parts = side(-1)
    for i in minus_at:
        curve, left, centre, right = zip(parts[i - 1], parts[i], parts[i + 1])
        term = upwind_term(right[2], centre[1], left[0], curve[2] - curve[1], curve[1] - curve[0])
        add(i - 1, term - curve[1])
    total = {}
    for i in range(BLOCK):
        if i in faces:
            total[i] = faces[i]
        if i - 1 in faces:
            total[i] = total[i] - faces[i - 1] if i in total else -faces[i - 1]
    return total


INNER = (range(2, 6), range(2, 6), range(0, 7))
OUTER = ((-1, 0, 1, 6, 7), (0, 1, 6, 7, 8), (-1, 7))
EVERY = (range(-1, 8), range(0, 9), range(-1, 8))


def ring_divergence(half_flux, scaled):
    count = len(half_flux)

    def up(values):
        return values[1:] + [pltpu.roll(values[0], 7, 0)]

    def down(values):
        return [pltpu.roll(values[-1], 1, 0)] + values[:-1]

    def side(values):
        after = [above - value for above, value in zip(up(values), values)]
        parts = [smoothness(before, step) for before, step in zip(down(after), after)]
        curve, left, centre, right = (list(part) for part in zip(*parts))
        jump = [above - value for above, value in zip(up(curve), curve)]
        return curve, left, centre, right, jump

    curve, left, centre, right, jump = side([a + b for a, b in zip(half_flux, scaled)])
    terms = zip(down(left), centre, up(right), down(jump), jump)
    face = [
        6.0 * (here + above) - bend - upwind_term(*term)
        for here, above, bend, term in zip(half_flux, up(half_flux), curve, terms)
    ]
    curve, left, centre, right, jump = side([a - b for a, b in zip(half_flux, scaled)])
    terms = zip(up(right), centre, down(left), jump, down(jump))
    other = [upwind_term(*term) - bend for bend, term in zip(curve, terms)]
    face = [one + two for one, two in zip(face, up(other))]
    return [here - below for here, below in zip(face, down(face))]


def open_divergence(half_flux, scaled):
    count = len(half_flux)
    plus = [a + b for a, b in zip(half_flux, scaled)]
    minus = [a - b for a, b in zip(half_flux, scaled)]
    faces = [None] * count

    def side(values):
        steps = [values[i + 1] - values[i] for i in range(count - 1)]
        parts = [None] + [smoothness(steps[i - 1], steps[i]) for i in range(1, count - 1)]
        return parts

    parts = side(plus)
    for i in range(2, count - 3):
        jump_before = parts[i][0] - parts[i - 1][0]
        jump_after = parts[i + 1][0] - parts[i][0]
        faces[i] = 6.0 * (half_flux[i] + half_flux[i + 1]) - parts[i][0] - upwind_term(
            parts[i - 1][1], parts[i][2], parts[i + 1][3], jump_before, jump_after
        )
    parts = side(minus)
    for i in range(3, count - 2):
        jump_before = parts[i][0] - parts[i - 1][0]
        jump_after = parts[i + 1][0] - parts[i][0]
        faces[i - 1] = faces[i - 1] + (
            upwind_term(parts[i + 1][3], parts[i][2], parts[i - 1][1], jump_after, jump_before)
            - parts[i][0]
        )
    return [faces[i] - faces[i - 1] for i in range(3, count - 3)]


def half_velocities(fields):
    density, mom_x, mom_y, mom_z, energy = fields
    over = 0.5 / density
    vel = (mom_x * over, mom_y * over, mom_z * over)
    kinetic = mom_x * vel[0] + mom_y * vel[1] + mom_z * vel[2]
    pressure = (gamma_gas - 1.0) * (energy - kinetic)
    return vel, pressure


def half_flux(fields, field, direction, speed, pressure):
    if field == 0:
        return 0.5 * fields[1 + direction]
    if field == 4:
        return (fields[4] + pressure) * speed
    flux = fields[field] * speed
    return flux + 0.5 * pressure if field == 1 + direction else flux


def plane_kernel(with_inner, state, speed, out, turned):
    half_speed = 0.5 * speed[0:1, :]
    lane = lax.broadcasted_iota(jnp.int32, (LANES, LANES), 1)
    to_turned = (lane % 8) * 16 + lane // 8
    to_plain = (lane % 16) * 8 + lane // 16

    def four_planes(part, carry):
        planes = pl.ds(part * 4, 4)
        for f in range(FIELDS):
            plain = state[f, planes].reshape(LANES, LANES)
            turned[f] = jnp.take_along_axis(plain, to_turned, axis=1).T
        for place in range(4):
            fields = [state[f, part * 4 + place] for f in range(FIELDS)]
            vel, pressure = half_velocities(fields)
            for field in range(FIELDS):
                out[field, part * 4 + place] = periodic_divergence(
                    half_flux(fields, field, 1, vel[1], pressure),
                    half_speed * fields[field],
                    y_up,
                    y_up_two,
                    y_down,
                )
        columns = [
            [turned[f, row : row + 8] for row in range(0, LANES, 8)] for f in range(FIELDS)
        ]
        along = [half_velocities(fields) for fields in zip(*columns)]
        for field in range(FIELDS):
            fluxes = [
                half_flux(fields, field, 2, vel[2], pressure)
                for fields, (vel, pressure) in zip(zip(*columns), along)
            ]
            scaled = [half_speed * value for value in columns[field]]
            total = jnp.concatenate(ring_divergence(fluxes, scaled), axis=0)
            plain = jnp.take_along_axis(total.T, to_plain, axis=1)
            out[field, planes] += plain.reshape(4, ROWS, LANES)
        return carry

    lax.fori_loop(0, state.shape[1] // 4, four_planes, 0)

    def group(j, carry):
        rows = pl.ds(pl.multiple_of(j * 8, 8), 8)

        def get(f, plane):
            return state[f, plane, rows, :]

        for field, along_x in across(get, half_speed, range(BLOCK), INNER):
            for plane in range(BLOCK):
                out[field, plane, rows, :] += along_x[plane]
        return carry

    if with_inner:
        lax.fori_loop(0, 4, group, 0)


def along_planes(state, speed, with_inner):
    return pl.pallas_call(
        functools.partial(plane_kernel, with_inner),
        out_shape=jax.ShapeDtypeStruct(state.shape, jnp.float32),
        in_specs=[VMEM, VMEM],
        out_specs=VMEM,
        scratch_shapes=[pltpu.VMEM((FIELDS, LANES, LANES), jnp.float32)],
        compiler_params=params(),
        cost_estimate=cost(20_000_000, 1_000_000),
        name="planes",
    )(state, speed)


def across(get, half_speed, span, parts):
    speeds, pressures = {}, {}
    for plane in span:
        vel, pressure = half_velocities([get(f, plane) for f in range(FIELDS)])
        speeds[plane] = vel[0]
        pressures[plane] = pressure
    for field in range(FIELDS):
        fluxes, scaled = {}, {}
        for plane in span:
            if field == 0:
                flux = 0.5 * get(1, plane)
            elif field == 4:
                flux = (get(4, plane) + pressures[plane]) * speeds[plane]
            else:
                flux = get(field, plane) * speeds[plane]
                if field == 1:
                    flux = flux + 0.5 * pressures[plane]
            fluxes[plane] = flux
            scaled[plane] = half_speed * get(field, plane)
        yield field, x_divergence(fluxes, scaled, *parts)


WITH_HALOS = range(-3, BLOCK + 3)


def first_kernel(
    state, sides, far, near, speed, middle, far_side, near_side, top, below, above
):
    sort_halos(far, near, below, above)
    lower_first = own_is_even()
    half_speed = 0.5 * speed[0:1, :]
    factor = (courant / 6.0) / speed[0:1, :]

    def group(j, best):
        rows = pl.ds(pl.multiple_of(j * 8, 8), 8)

        def get(f, plane):
            if plane < 0:
                return below[f, plane + 3, rows, :]
            if plane >= BLOCK:
                return above[f, plane - BLOCK, rows, :]
            return state[f, plane, rows, :]

        for field, along_x in across(get, half_speed, WITH_HALOS, OUTER):
            values = []
            for plane in range(BLOCK):
                total = sides[field, plane, rows, :]
                if plane in along_x:
                    total = total + along_x[plane]
                values.append(get(field, plane) - factor * total)
                middle[field, plane, rows, :] = values[plane]
            for plane in range(3):
                low, high = values[plane], values[BLOCK - 3 + plane]
                far_side[field, plane, rows, :] = jnp.where(lower_first, low, high)
                near_side[field, plane, rows, :] = jnp.where(lower_first, high, low)
        for plane in range(BLOCK):
            best = jnp.maximum(
                best, wave_speed([middle[f, plane, rows, :] for f in range(FIELDS)])
            )
        return best

    best = lax.fori_loop(0, 4, group, jnp.zeros((8, LANES), jnp.float32))
    top[...] = jnp.full((8, LANES), jnp.max(best), jnp.float32)


def first_stage(*operands):
    whole = jax.ShapeDtypeStruct((FIELDS, BLOCK, ROWS, LANES), jnp.float32)
    halo = jax.ShapeDtypeStruct(HALO, jnp.float32)
    return pl.pallas_call(
        first_kernel,
        out_shape=(whole, halo, halo, jax.ShapeDtypeStruct((8, LANES), jnp.float32)),
        in_specs=[VMEM] * len(operands),
        out_specs=(VMEM,) * 4,
        scratch_shapes=[pltpu.VMEM(HALO, jnp.float32)] * 2,
        compiler_params=params(),
        cost_estimate=cost(30_000_000, 3_000_000),
        name="first_stage",
    )(*operands)


def second_kernel(start, middle, sides, far, near, first_speed, speed, out, below, above):
    sort_halos(far, near, below, above)
    half_speed = 0.5 * speed[0:1, :]
    factor = (courant / 12.0) / first_speed[0:1, :]

    def group(j, carry):
        rows = pl.ds(pl.multiple_of(j * 8, 8), 8)
        spread = pl.ds(j, 8, stride=4)

        def get(f, plane):
            if plane < 0:
                return below[f, plane + 3, rows, :]
            if plane >= BLOCK:
                return above[f, plane - BLOCK, rows, :]
            return middle[f, plane, rows, :]

        for field, along_x in across(get, half_speed, WITH_HALOS, EVERY):
            for plane in range(BLOCK):
                total = along_x[plane] + sides[field, plane, rows, :]
                value = 0.5 * start[field, plane, rows, :] + (
                    0.5 * get(field, plane) - factor * total
                )
                out[field, plane, spread, :] = value
        return carry

    lax.fori_loop(0, 4, group, 0)


def second_stage(*operands):
    return pl.pallas_call(
        second_kernel,
        out_shape=jax.ShapeDtypeStruct((FIELDS, BLOCK, ROWS, LANES), jnp.float32),
        in_specs=[VMEM] * len(operands),
        out_specs=VMEM,
        scratch_shapes=[pltpu.VMEM(HALO, jnp.float32)] * 2,
        compiler_params=params(),
        cost_estimate=cost(30_000_000, 3_000_000),
        name="second_stage",
    )(*operands)


def everyone_max(value, axis, size):
    reach = 1
    while reach * 4 < size:
        reach *= 4
    while reach:
        copies = [value]
        for times in range(1, 4):
            turn = reach * times
            if turn < size:
                pairs = [(i, i ^ turn) for i in range(size)]
                copies.append(lax.ppermute(value, axis, pairs))
        value = functools.reduce(jnp.maximum, copies)
        reach //= 4
    return value


def per_device(blocks, owner_list, slot_list):
    size = lax.axis_size("gx")
    own = lax.axis_index("gx")
    per_dev = blocks.shape[0]
    cap = max(2, 2 * per_dev // size)

    parts = pack(tiled_rows(blocks), owner_list, size, cap, per_dev)
    parts, owner_list, slot_list = lax.optimization_barrier((parts, owner_list, slot_list))
    come = lax.all_to_all(parts, "gx", split_axis=0, concat_axis=0, tiled=True)
    table = arrival_spots(owner_list, slot_list, own, per_dev, size, cap)
    state, far_side, near_side, speed = unpack(table, come.reshape(-1, LANES), size, cap)
    far, near = swapped(far_side, near_side, size)
    sides = along_planes(state, speed, True)
    middle, far_side, near_side, top = first_stage(state, sides, far, near, speed)
    far, near = swapped(far_side, near_side, size)
    second = everyone_max(top, "gx", size)
    sides = along_planes(middle, second, False)
    return second_stage(state, middle, sides, far, near, speed, second)


def solution(mesh):
    return jax.shard_map(
        per_device,
        mesh=mesh,
        in_specs=(P(("runs", "gx"), None, None), P("runs"), P("runs")),
        out_specs=P(None, ("runs", "gx"), None, None),
        check_vma=False,
    )
```

```python
import functools

import jax
import jax.numpy as jnp
from jax import lax
from jax.experimental import pallas as pl
from jax.experimental.pallas import tpu as pltpu
from jax.sharding import PartitionSpec as P

BLOCK = 8
BY = 4
BZ = 16
FIELDS = 5
LANES = 128
ROWS = BY * BLOCK
PAIRS = BLOCK // 2
TILES = PAIRS * FIELDS

gamma_gas = 1.4
courant = 0.25
smooth_epsilon = 1e-06

VMEM = pl.BlockSpec(memory_space=pltpu.VMEM)
SMEM = pl.BlockSpec(memory_space=pltpu.SMEM)


def params(mebibytes=40):
    return pltpu.CompilerParams(vmem_limit_bytes=mebibytes * 1024 * 1024)


def cost(flops, size):
    return pl.CostEstimate(flops=flops, bytes_accessed=size, transcendentals=0)


def wave_speed(fields):
    density, mom_x, mom_y, mom_z, energy = fields
    inverse = 1.0 / density
    vel = (mom_x * inverse, mom_y * inverse, mom_z * inverse)
    kinetic = 0.5 * (mom_x * vel[0] + mom_y * vel[1] + mom_z * vel[2])
    pressure = (gamma_gas - 1.0) * (energy - kinetic)
    sound = jnp.sqrt(gamma_gas * pressure * inverse)
    fastest = jnp.maximum(jnp.maximum(jnp.abs(vel[0]), jnp.abs(vel[1])), jnp.abs(vel[2]))
    return fastest + sound


def tiled_rows(blocks):
    count = blocks.shape[0] // 8
    groups = blocks.reshape(count, 8, FIELDS, PAIRS, LANES).transpose(2, 0, 3, 1, 4)
    return groups.reshape(FIELDS * count * PAIRS * 8, 1, LANES)


def pack_kernel(
    size, cap, per_dev, owner_hbm, rows_hbm, out_hbm, owner, rows, tiled, out, top, count, member, sems
):
    own = lax.axis_index("gx")
    fetch_owner = pltpu.make_async_copy(owner_hbm, owner, sems.at[0])
    fetch_rows = pltpu.make_async_copy(rows_hbm, rows, sems.at[1])
    fetch_tiled = pltpu.make_async_copy(rows_hbm.at[:, 0], tiled, sems.at[4])
    fetch_owner.start()
    fetch_rows.start()
    fetch_tiled.start()

    def clear(dest, carry):
        count[dest] = 0
        return carry

    lax.fori_loop(0, size, clear, 0, unroll=8)
    fetch_owner.wait()

    def note(block, carry):
        dest = owner[own * per_dev + block]
        rank = count[dest]
        count[dest] = rank + 1
        member[dest * cap + rank] = lax.div(block, 8) * (PAIRS * 8) + lax.rem(block, 8)
        return carry

    lax.fori_loop(0, per_dev, note, 0, unroll=8)
    fetch_rows.wait()
    tiles = TILES * cap

    def message(dest, carry):
        @pl.when(count[dest] > 0)
        def _():
            for rank in range(cap):
                first = member[dest * cap + rank]
                for pair in range(PAIRS):
                    for f in range(FIELDS):
                        to = dest * tiles + (pair * FIELDS + f) * cap + rank
                        out[to] = rows[first + f * (per_dev * PAIRS) + pair * 8]
            part = out.at[pl.ds(dest * tiles, tiles)]
            pltpu.make_async_copy(part, out_hbm.at[dest, pl.ds(0, tiles)], sems.at[2]).start()

        return carry

    lax.fori_loop(0, size, message, 0)
    fetch_tiled.wait()
    best = jnp.zeros((8, LANES), jnp.float32)
    step = per_dev * PAIRS
    for first in range(0, step, 8):
        fields = [tiled[f * step + first : f * step + first + 8, :] for f in range(FIELDS)]
        best = jnp.maximum(best, wave_speed(fields))
    top[...] = jnp.full(top.shape, jnp.max(best), jnp.float32)
    for dest in range(size):
        pltpu.make_async_copy(
            top.at[pl.ds(dest, 1)], out_hbm.at[dest, tiles], sems.at[3]
        ).start()
    half = out.at[pl.ds(0, per_dev * TILES)]
    pltpu.make_async_copy(half, half, sems.at[2]).wait()
    pltpu.make_async_copy(top, top, sems.at[3]).wait()


def pack(rows, owner_list, size, cap, per_dev):
    return pl.pallas_call(
        functools.partial(pack_kernel, size, cap, per_dev),
        out_shape=jax.ShapeDtypeStruct((size, TILES * cap + 1, 1, LANES), jnp.float32),
        in_specs=[pl.BlockSpec(memory_space=pltpu.HBM)] * 2,
        out_specs=pl.BlockSpec(memory_space=pltpu.HBM),
        scratch_shapes=[
            pltpu.SMEM(owner_list.shape, jnp.int32),
            pltpu.VMEM(rows.shape, jnp.float32),
            pltpu.VMEM((rows.shape[0], LANES), jnp.float32),
            pltpu.VMEM((size * TILES * cap, 1, LANES), jnp.float32),
            pltpu.VMEM((size, LANES), jnp.float32),
            pltpu.SMEM((size,), jnp.int32),
            pltpu.SMEM((size * cap,), jnp.int32),
            pltpu.SemaphoreType.DMA((5,)),
        ],
        compiler_params=params(62),
        cost_estimate=cost(1_000_000, 3_000_000),
        name="pack",
    )(owner_list, rows)


def own_is_even():
    return lax.axis_index("gx") % 2 == 0


def swapped(far_side, near_side, size):
    apart = [(i, (i - 1 if i % 2 == 0 else i + 1) % size) for i in range(size)]
    chip = [(i, i ^ 1) for i in range(size)]
    return lax.ppermute(far_side, "gx", apart), lax.ppermute(near_side, "gx", chip)


def sort_halos(far, near, below, above):
    lower_first = own_is_even()
    for f in range(FIELDS):
        for plane in range(3):
            one, two = far[f, plane], near[f, plane]
            below[f, plane] = jnp.where(lower_first, one, two)
            above[f, plane] = jnp.where(lower_first, two, one)


HALO = (FIELDS, 3, ROWS, LANES)


def arrival_spots(owner_list, slot_list, own, per_dev, size, cap):
    owners = owner_list.reshape(size, per_dev)
    slots = slot_list.reshape(size, per_dev)
    mine = owners == own
    spot = jnp.arange(per_dev, dtype=jnp.int32)
    earlier = spot[None, :] < spot[:, None]
    rank = jnp.sum((mine[:, None, :] & earlier[None]).astype(jnp.int32), axis=2)
    row = jnp.arange(size, dtype=jnp.int32)[:, None] * (TILES * cap + 1) + rank
    key = jnp.where(mine, slots, -1)
    hit = key.reshape(1, -1) == spot[:, None]
    return jnp.max(jnp.where(hit, row.reshape(1, -1), 0), axis=1)


def exchanged_bits(rows, group):
    rows = list(rows)
    for bit in range(4):
        step = 1 << bit
        low = (group & step) == 0
        for index in range(16):
            if index & step:
                continue
            first, second = rows[index], rows[index | step]
            rows[index] = jnp.where(low, first, pltpu.roll(second, 8 * step, 1))
            rows[index | step] = jnp.where(low, pltpu.roll(first, LANES - 8 * step, 1), second)
    return rows


def unpack_kernel(size, cap, table, come, state, far_side, near_side, speed, scratch):
    message = TILES * cap + 1
    best = come[message - 1]
    for source in range(1, size):
        best = jnp.maximum(best, come[(source + 1) * message - 1])
    speed[...] = jnp.broadcast_to(best, speed.shape)
    group = lax.broadcasted_iota(jnp.int32, (8, LANES), 1) // BLOCK
    even = lax.broadcasted_iota(jnp.int32, (8, LANES), 0) % 2 == 0
    half = FIELDS * BZ * 8

    def gather(couple, slot):
        p, q = divmod(slot, BZ)
        first = table[slot]
        for h in range(2):
            for f in range(FIELDS):
                row = couple * half + (f * BZ + q) * 8 + 2 * p + h
                value = come[first + ((2 * couple + h) * FIELDS + f) * cap]
                scratch[row : row + 1, :] = value

    def arrange(couple, f):
        first = couple * half + f * BZ * 8
        moved = exchanged_bits(
            [scratch[first + q * 8 : first + q * 8 + 8, :] for q in range(BZ)], group
        )
        for second in range(2):
            for j in range(4):
                lower = moved[second * BLOCK + j]
                upper = moved[second * BLOCK + j + 4]
                planes = (
                    jnp.where(even, lower, pltpu.roll(upper, 1, 0)),
                    jnp.where(even, pltpu.roll(lower, 7, 0), upper),
                )
                for h in range(2):
                    state[f, 4 * couple + 2 * h + second, j * 8 : j * 8 + 8, :] = planes[h]

    for slot in range(BY * BZ):
        gather(0, slot)
    for f in range(FIELDS):
        for slot in range(f, BY * BZ, FIELDS):
            gather(1, slot)
        arrange(0, f)
    for f in range(FIELDS):
        arrange(1, f)
    lower_first = own_is_even()
    for f in range(FIELDS):
        for plane in range(3):
            low, high = state[f, plane], state[f, BLOCK - 3 + plane]
            far_side[f, plane] = jnp.where(lower_first, low, high)
            near_side[f, plane] = jnp.where(lower_first, high, low)


def unpack(table, come, size, cap):
    halo = jax.ShapeDtypeStruct(HALO, jnp.float32)
    return pl.pallas_call(
        functools.partial(unpack_kernel, size, cap),
        out_shape=(
            jax.ShapeDtypeStruct((FIELDS, BLOCK, ROWS, LANES), jnp.float32),
            halo,
            halo,
            jax.ShapeDtypeStruct((8, LANES), jnp.float32),
        ),
        in_specs=[SMEM, VMEM],
        out_specs=(VMEM,) * 4,
        scratch_shapes=[pltpu.VMEM((FIELDS * (PAIRS // 2) * BZ * 8, LANES), jnp.float32)],
        compiler_params=params(),
        cost_estimate=cost(5_000_000, 2_000_000),
        name="unpack",
    )(table, come)


def y_up(x):
    return jnp.concatenate([x[8:], pltpu.roll(x[:8], 7, 0)], axis=0)


def y_down(x):
    return jnp.concatenate([pltpu.roll(x[24:], 1, 0), x[:24]], axis=0)


def y_up_two(x):
    return jnp.concatenate([x[16:], pltpu.roll(x[:8], 7, 0), pltpu.roll(x[8:16], 7, 0)], axis=0)


def inverse(x):
    return 1.0 / x


def smoothness(before, after):
    curve = after - before
    middle = 0.5 * (after + before)
    base = curve * curve * (13.0 / 12.0) + smooth_epsilon
    plus = middle + curve
    minus = middle - curve
    left = inverse(base + plus * plus)
    centre = inverse(base + middle * middle)
    right = inverse(base + minus * minus)
    return curve, left * left, centre * centre, right * right


def upwind_term(left, centre, right, jump_before, jump_after):
    right = 3.0 * right
    top = left * (jump_before + jump_before) + right * jump_after
    return top * inverse(left + 6.0 * centre + right)


def periodic_divergence(half_flux, scaled, up, up_two, down):
    plus = half_flux + scaled
    minus = half_flux - scaled

    def side(values):
        after = up(values) - values
        curve, left, centre, right = smoothness(down(after), after)
        above = up(curve)
        return curve, above, left, centre, right, above - curve

    curve, _, left, centre, right, jump = side(plus)
    face = 6.0 * (half_flux + up(half_flux)) - curve
    face = face - upwind_term(down(left), centre, up(right), down(jump), jump)
    _, curve, left, centre, right, jump = side(minus)
    face = face + (upwind_term(up_two(right), up(centre), left, up(jump), jump) - curve)
    return face - down(face)


def ring_divergence(half_flux, scaled):
    count = len(half_flux)

    def up(values):
        return values[1:] + [pltpu.roll(values[0], 7, 0)]

    def down(values):
        return [pltpu.roll(values[-1], 1, 0)] + values[:-1]

    def side(values):
        after = [above - value for above, value in zip(up(values), values)]
        parts = [smoothness(before, step) for before, step in zip(down(after), after)]
        curve, left, centre, right = (list(part) for part in zip(*parts))
        jump = [above - value for above, value in zip(up(curve), curve)]
        return curve, left, centre, right, jump

    curve, left, centre, right, jump = side([a + b for a, b in zip(half_flux, scaled)])
    terms = zip(down(left), centre, up(right), down(jump), jump)
    face = [
        6.0 * (here + above) - bend - upwind_term(*term)
        for here, above, bend, term in zip(half_flux, up(half_flux), curve, terms)
    ]
    curve, left, centre, right, jump = side([a - b for a, b in zip(half_flux, scaled)])
    terms = zip(up(right), centre, down(left), jump, down(jump))
    other = [upwind_term(*term) - bend for bend, term in zip(curve, terms)]
    face = [one + two for one, two in zip(face, up(other))]
    return [here - below for here, below in zip(face, down(face))]


def x_divergence(half_flux, scaled, plus_at, minus_at, centre_at):
    faces = {i: 6.0 * (half_flux[i] + half_flux[i + 1]) for i in centre_at}

    def add(i, value):
        faces[i] = faces[i] + value if i in faces else value

    def side(sign):
        values = {i: half_flux[i] + sign * scaled[i] for i in half_flux}
        steps = {i: values[i + 1] - values[i] for i in values if i + 1 in values}
        return {i: smoothness(steps[i - 1], steps[i]) for i in steps if i - 1 in steps}

    parts = side(1)
    for i in plus_at:
        curve, left, centre, right = zip(parts[i - 1], parts[i], parts[i + 1])
        term = upwind_term(left[0], centre[1], right[2], curve[1] - curve[0], curve[2] - curve[1])
        add(i, -(curve[1] + term))
    parts = side(-1)
    for i in minus_at:
        curve, left, centre, right = zip(parts[i - 1], parts[i], parts[i + 1])
        term = upwind_term(right[2], centre[1], left[0], curve[2] - curve[1], curve[1] - curve[0])
        add(i - 1, term - curve[1])
    total = {}
    for i in range(BLOCK):
        if i in faces:
            total[i] = faces[i]
        if i - 1 in faces:
            total[i] = total[i] - faces[i - 1] if i in total else -faces[i - 1]
    return total


INNER = (range(2, 6), range(2, 6), range(0, 7))
OUTER = ((-1, 0, 1, 6, 7), (0, 1, 6, 7, 8), (-1, 7))
EVERY = (range(-1, 8), range(0, 9), range(-1, 8))


def ring_divergence(half_flux, scaled):
    count = len(half_flux)

    def up(values):
        return values[1:] + [pltpu.roll(values[0], 7, 0)]

    def down(values):
        return [pltpu.roll(values[-1], 1, 0)] + values[:-1]

    def side(values):
        after = [above - value for above, value in zip(up(values), values)]
        parts = [smoothness(before, step) for before, step in zip(down(after), after)]
        curve, left, centre, right = (list(part) for part in zip(*parts))
        jump = [above - value for above, value in zip(up(curve), curve)]
        return curve, left, centre, right, jump

    curve, left, centre, right, jump = side([a + b for a, b in zip(half_flux, scaled)])
    terms = zip(down(left), centre, up(right), down(jump), jump)
    face = [
        6.0 * (here + above) - bend - upwind_term(*term)
        for here, above, bend, term in zip(half_flux, up(half_flux), curve, terms)
    ]
    curve, left, centre, right, jump = side([a - b for a, b in zip(half_flux, scaled)])
    terms = zip(up(right), centre, down(left), jump, down(jump))
    other = [upwind_term(*term) - bend for bend, term in zip(curve, terms)]
    face = [one + two for one, two in zip(face, up(other))]
    return [here - below for here, below in zip(face, down(face))]


def open_divergence(half_flux, scaled):
    count = len(half_flux)
    plus = [a + b for a, b in zip(half_flux, scaled)]
    minus = [a - b for a, b in zip(half_flux, scaled)]
    faces = [None] * count

    def side(values):
        steps = [values[i + 1] - values[i] for i in range(count - 1)]
        parts = [None] + [smoothness(steps[i - 1], steps[i]) for i in range(1, count - 1)]
        return parts

    parts = side(plus)
    for i in range(2, count - 3):
        jump_before = parts[i][0] - parts[i - 1][0]
        jump_after = parts[i + 1][0] - parts[i][0]
        faces[i] = 6.0 * (half_flux[i] + half_flux[i + 1]) - parts[i][0] - upwind_term(
            parts[i - 1][1], parts[i][2], parts[i + 1][3], jump_before, jump_after
        )
    parts = side(minus)
    for i in range(3, count - 2):
        jump_before = parts[i][0] - parts[i - 1][0]
        jump_after = parts[i + 1][0] - parts[i][0]
        faces[i - 1] = faces[i - 1] + (
            upwind_term(parts[i + 1][3], parts[i][2], parts[i - 1][1], jump_after, jump_before)
            - parts[i][0]
        )
    return [faces[i] - faces[i - 1] for i in range(3, count - 3)]


def half_velocities(fields):
    density, mom_x, mom_y, mom_z, energy = fields
    over = 0.5 / density
    vel = (mom_x * over, mom_y * over, mom_z * over)
    kinetic = mom_x * vel[0] + mom_y * vel[1] + mom_z * vel[2]
    pressure = (gamma_gas - 1.0) * (energy - kinetic)
    return vel, pressure


def half_flux(fields, field, direction, speed, pressure):
    if field == 0:
        return 0.5 * fields[1 + direction]
    if field == 4:
        return (fields[4] + pressure) * speed
    flux = fields[field] * speed
    return flux + 0.5 * pressure if field == 1 + direction else flux


def plane_kernel(with_inner, state, speed, out, turned):
    half_speed = 0.5 * speed[0:1, :]
    lane = lax.broadcasted_iota(jnp.int32, (LANES, LANES), 1)
    to_turned = (lane % 8) * 16 + lane // 8
    to_plain = (lane % 16) * 8 + lane // 16

    def four_planes(part, carry):
        planes = pl.ds(part * 4, 4)
        for f in range(FIELDS):
            plain = state[f, planes].reshape(LANES, LANES)
            turned[f] = jnp.take_along_axis(plain, to_turned, axis=1).T
        for place in range(4):
            fields = [state[f, part * 4 + place] for f in range(FIELDS)]
            vel, pressure = half_velocities(fields)
            for field in range(FIELDS):
                out[field, part * 4 + place] = periodic_divergence(
                    half_flux(fields, field, 1, vel[1], pressure),
                    half_speed * fields[field],
                    y_up,
                    y_up_two,
                    y_down,
                )
        columns = [
            [turned[f, row : row + 8] for row in range(0, LANES, 8)] for f in range(FIELDS)
        ]
        along = [half_velocities(fields) for fields in zip(*columns)]
        for field in range(FIELDS):
            fluxes = [
                half_flux(fields, field, 2, vel[2], pressure)
                for fields, (vel, pressure) in zip(zip(*columns), along)
            ]
            scaled = [half_speed * value for value in columns[field]]
            total = jnp.concatenate(ring_divergence(fluxes, scaled), axis=0)
            plain = jnp.take_along_axis(total.T, to_plain, axis=1)
            out[field, planes] += plain.reshape(4, ROWS, LANES)
        return carry

    lax.fori_loop(0, state.shape[1] // 4, four_planes, 0)

    def group(j, carry):
        rows = pl.ds(pl.multiple_of(j * 8, 8), 8)

        def get(f, plane):
            return state[f, plane, rows, :]

        for field, along_x in across(get, half_speed, range(BLOCK), INNER):
            for plane in range(BLOCK):
                out[field, plane, rows, :] += along_x[plane]
        return carry

    if with_inner:
        lax.fori_loop(0, 4, group, 0)


def along_planes(state, speed, with_inner):
    return pl.pallas_call(
        functools.partial(plane_kernel, with_inner),
        out_shape=jax.ShapeDtypeStruct(state.shape, jnp.float32),
        in_specs=[VMEM, VMEM],
        out_specs=VMEM,
        scratch_shapes=[pltpu.VMEM((FIELDS, LANES, LANES), jnp.float32)],
        compiler_params=params(),
        cost_estimate=cost(20_000_000, 1_000_000),
        name="planes",
    )(state, speed)


def across(get, half_speed, span, parts):
    speeds, pressures = {}, {}
    for plane in span:
        vel, pressure = half_velocities([get(f, plane) for f in range(FIELDS)])
        speeds[plane] = vel[0]
        pressures[plane] = pressure
    for field in range(FIELDS):
        fluxes, scaled = {}, {}
        for plane in span:
            if field == 0:
                flux = 0.5 * get(1, plane)
            elif field == 4:
                flux = (get(4, plane) + pressures[plane]) * speeds[plane]
            else:
                flux = get(field, plane) * speeds[plane]
                if field == 1:
                    flux = flux + 0.5 * pressures[plane]
            fluxes[plane] = flux
            scaled[plane] = half_speed * get(field, plane)
        yield field, x_divergence(fluxes, scaled, *parts)


WITH_HALOS = range(-3, BLOCK + 3)


def first_kernel(
    state, sides, far, near, speed, middle, far_side, near_side, top, below, above
):
    sort_halos(far, near, below, above)
    lower_first = own_is_even()
    half_speed = 0.5 * speed[0:1, :]
    factor = (courant / 6.0) / speed[0:1, :]

    def group(j, best):
        rows = pl.ds(pl.multiple_of(j * 8, 8), 8)

        def get(f, plane):
            if plane < 0:
                return below[f, plane + 3, rows, :]
            if plane >= BLOCK:
                return above[f, plane - BLOCK, rows, :]
            return state[f, plane, rows, :]

        for field, along_x in across(get, half_speed, WITH_HALOS, OUTER):
            values = []
            for plane in range(BLOCK):
                total = sides[field, plane, rows, :]
                if plane in along_x:
                    total = total + along_x[plane]
                values.append(get(field, plane) - factor * total)
                middle[field, plane, rows, :] = values[plane]
            for plane in range(3):
                low, high = values[plane], values[BLOCK - 3 + plane]
                far_side[field, plane, rows, :] = jnp.where(lower_first, low, high)
                near_side[field, plane, rows, :] = jnp.where(lower_first, high, low)
        for plane in range(BLOCK):
            best = jnp.maximum(
                best, wave_speed([middle[f, plane, rows, :] for f in range(FIELDS)])
            )
        return best

    best = lax.fori_loop(0, 4, group, jnp.zeros((8, LANES), jnp.float32))
    top[...] = jnp.full((8, LANES), jnp.max(best), jnp.float32)


def first_stage(*operands):
    whole = jax.ShapeDtypeStruct((FIELDS, BLOCK, ROWS, LANES), jnp.float32)
    halo = jax.ShapeDtypeStruct(HALO, jnp.float32)
    return pl.pallas_call(
        first_kernel,
        out_shape=(whole, halo, halo, jax.ShapeDtypeStruct((8, LANES), jnp.float32)),
        in_specs=[VMEM] * len(operands),
        out_specs=(VMEM,) * 4,
        scratch_shapes=[pltpu.VMEM(HALO, jnp.float32)] * 2,
        compiler_params=params(),
        cost_estimate=cost(30_000_000, 3_000_000),
        name="first_stage",
    )(*operands)


def second_kernel(start, middle, sides, far, near, first_speed, speed, out, below, above):
    sort_halos(far, near, below, above)
    half_speed = 0.5 * speed[0:1, :]
    factor = (courant / 12.0) / first_speed[0:1, :]

    def group(j, carry):
        rows = pl.ds(pl.multiple_of(j * 8, 8), 8)
        spread = pl.ds(j, 8, stride=4)

        def get(f, plane):
            if plane < 0:
                return below[f, plane + 3, rows, :]
            if plane >= BLOCK:
                return above[f, plane - BLOCK, rows, :]
            return middle[f, plane, rows, :]

        for field, along_x in across(get, half_speed, WITH_HALOS, EVERY):
            for plane in range(BLOCK):
                total = along_x[plane] + sides[field, plane, rows, :]
                value = 0.5 * start[field, plane, rows, :] + (
                    0.5 * get(field, plane) - factor * total
                )
                out[field, plane, spread, :] = value
        return carry

    lax.fori_loop(0, 4, group, 0)


def second_stage(*operands):
    return pl.pallas_call(
        second_kernel,
        out_shape=jax.ShapeDtypeStruct((FIELDS, BLOCK, ROWS, LANES), jnp.float32),
        in_specs=[VMEM] * len(operands),
        out_specs=VMEM,
        scratch_shapes=[pltpu.VMEM(HALO, jnp.float32)] * 2,
        compiler_params=params(),
        cost_estimate=cost(30_000_000, 3_000_000),
        name="second_stage",
    )(*operands)


def everyone_max(value, axis, size):
    reach = 1
    while reach * 4 < size:
        reach *= 4
    while reach:
        copies = [value]
        for times in range(1, 4):
            turn = reach * times
            if turn < size:
                pairs = [(i, i ^ turn) for i in range(size)]
                copies.append(lax.ppermute(value, axis, pairs))
        value = functools.reduce(jnp.maximum, copies)
        reach //= 4
    return value


def per_device(blocks, owner_list, slot_list):
    size = lax.axis_size("gx")
    own = lax.axis_index("gx")
    per_dev = blocks.shape[0]
    cap = max(2, 2 * per_dev // size)

    parts = pack(tiled_rows(blocks), owner_list, size, cap, per_dev)
    parts, owner_list, slot_list = lax.optimization_barrier((parts, owner_list, slot_list))
    come = lax.all_to_all(parts, "gx", split_axis=0, concat_axis=0, tiled=True)
    table = arrival_spots(owner_list, slot_list, own, per_dev, size, cap)
    state, far_side, near_side, speed = unpack(table, come.reshape(-1, 1, LANES), size, cap)
    far, near = swapped(far_side, near_side, size)
    sides = along_planes(state, speed, True)
    middle, far_side, near_side, top = first_stage(state, sides, far, near, speed)
    far, near = swapped(far_side, near_side, size)
    second = everyone_max(top, "gx", size)
    sides = along_planes(middle, second, False)
    return second_stage(state, middle, sides, far, near, speed, second)


def solution(mesh):
    return jax.shard_map(
        per_device,
        mesh=mesh,
        in_specs=(P(("runs", "gx"), None, None), P("runs"), P("runs")),
        out_specs=P(None, ("runs", "gx"), None, None),
        check_vma=False,
    )
```

```python
import functools

import jax
import jax.numpy as jnp
from jax import lax
from jax.experimental import pallas as pl
from jax.experimental.pallas import tpu as pltpu
from jax.sharding import PartitionSpec as P

BLOCK = 8
BY = 4
BZ = 16
FIELDS = 5
LANES = 128
ROWS = BY * BLOCK
PAIRS = BLOCK // 2
TILES = PAIRS * FIELDS

gamma_gas = 1.4
courant = 0.25
smooth_epsilon = 1e-06

VMEM = pl.BlockSpec(memory_space=pltpu.VMEM)
SMEM = pl.BlockSpec(memory_space=pltpu.SMEM)


def params(mebibytes=40):
    return pltpu.CompilerParams(vmem_limit_bytes=mebibytes * 1024 * 1024)


def cost(flops, size):
    return pl.CostEstimate(flops=flops, bytes_accessed=size, transcendentals=0)


def wave_speed(fields):
    density, mom_x, mom_y, mom_z, energy = fields
    inverse = 1.0 / density
    vel = (mom_x * inverse, mom_y * inverse, mom_z * inverse)
    kinetic = 0.5 * (mom_x * vel[0] + mom_y * vel[1] + mom_z * vel[2])
    pressure = (gamma_gas - 1.0) * (energy - kinetic)
    sound = jnp.sqrt(gamma_gas * pressure * inverse)
    fastest = jnp.maximum(jnp.maximum(jnp.abs(vel[0]), jnp.abs(vel[1])), jnp.abs(vel[2]))
    return fastest + sound


def tiled_rows(blocks):
    count = blocks.shape[0] // 8
    groups = blocks.reshape(count, 8, FIELDS, PAIRS, LANES).transpose(2, 0, 3, 1, 4)
    return groups.reshape(FIELDS * count * PAIRS * 8, 1, LANES)


def pack_kernel(
    size, cap, per_dev, owner_hbm, rows_hbm, out_hbm, owner, rows, tiled, out, top, count, member, sems
):
    own = lax.axis_index("gx")
    fetch_owner = pltpu.make_async_copy(owner_hbm, owner, sems.at[0])
    fetch_rows = pltpu.make_async_copy(rows_hbm, rows, sems.at[1])
    fetch_tiled = pltpu.make_async_copy(rows_hbm.at[:, 0], tiled, sems.at[4])
    fetch_owner.start()
    fetch_rows.start()
    fetch_tiled.start()

    def clear(dest, carry):
        count[dest] = 0
        return carry

    lax.fori_loop(0, size, clear, 0, unroll=8)
    fetch_owner.wait()

    fetch_tiled.wait()
    best = jnp.zeros((8, LANES), jnp.float32)
    step = per_dev * PAIRS
    for first in range(0, step, 8):
        fields = [tiled[f * step + first : f * step + first + 8, :] for f in range(FIELDS)]
        best = jnp.maximum(best, wave_speed(fields))
    for block in range(per_dev):
        dest = owner[own * per_dev + block]
        rank = count[dest]
        count[dest] = rank + 1
        member[dest * cap + rank] = block // 8 * (PAIRS * 8) + block % 8
    most = jnp.full((1, LANES), jnp.max(best), jnp.float32)
    for dest in range(size):
        top[dest] = most
    send_top = pltpu.make_async_copy(top, out_hbm.at[:, TILES * cap], sems.at[3])
    send_top.start()
    fetch_rows.wait()
    tiles = TILES * cap

    def message(dest, carry):
        @pl.when(count[dest] > 0)
        def _():
            for rank in range(cap):
                first = member[dest * cap + rank]
                for pair in range(PAIRS):
                    for f in range(FIELDS):
                        to = dest * tiles + (pair * FIELDS + f) * cap + rank
                        out[to] = rows[first + f * (per_dev * PAIRS) + pair * 8]
            part = out.at[pl.ds(dest * tiles, tiles)]
            pltpu.make_async_copy(part, out_hbm.at[dest, pl.ds(0, tiles)], sems.at[2]).start()

        return carry

    lax.fori_loop(0, size, message, 0)
    half = out.at[pl.ds(0, per_dev * TILES)]
    pltpu.make_async_copy(half, half, sems.at[2]).wait()
    send_top.wait()


def pack(rows, owner_list, size, cap, per_dev):
    return pl.pallas_call(
        functools.partial(pack_kernel, size, cap, per_dev),
        out_shape=jax.ShapeDtypeStruct((size, TILES * cap + 1, 1, LANES), jnp.float32),
        in_specs=[pl.BlockSpec(memory_space=pltpu.HBM)] * 2,
        out_specs=pl.BlockSpec(memory_space=pltpu.HBM),
        scratch_shapes=[
            pltpu.SMEM(owner_list.shape, jnp.int32),
            pltpu.VMEM(rows.shape, jnp.float32),
            pltpu.VMEM((rows.shape[0], LANES), jnp.float32),
            pltpu.VMEM((size * TILES * cap, 1, LANES), jnp.float32),
            pltpu.VMEM((size, 1, LANES), jnp.float32),
            pltpu.SMEM((size,), jnp.int32),
            pltpu.SMEM((size * cap,), jnp.int32),
            pltpu.SemaphoreType.DMA((5,)),
        ],
        compiler_params=params(62),
        cost_estimate=cost(1_000_000, 3_000_000),
        name="pack",
    )(owner_list, rows)


def turned_round():
    return lax.axis_index("gx") % 2


def place_of(plane):
    return jnp.where(turned_round() == 0, plane, BLOCK - 1 - plane)


def sign_of_x():
    return jnp.where(turned_round() == 0, 1.0, -1.0).astype(jnp.float32)


def from_far(far_side, size):
    pairs = [(i, (i - 1 if i % 2 == 0 else i + 1) % size) for i in range(size)]
    return lax.ppermute(far_side, "gx", pairs)


def from_near(near_side, size):
    return lax.ppermute(near_side, "gx", [(i, i ^ 1) for i in range(size)])


HALO = (FIELDS, 3, ROWS, LANES)


def arrival_spots(owner_list, slot_list, own, per_dev, size, cap):
    owners = owner_list.reshape(size, per_dev)
    slots = slot_list.reshape(size, per_dev)
    mine = owners == own
    spot = jnp.arange(per_dev, dtype=jnp.int32)
    earlier = spot[None, :] < spot[:, None]
    rank = jnp.sum((mine[:, None, :] & earlier[None]).astype(jnp.int32), axis=2)
    row = jnp.arange(size, dtype=jnp.int32)[:, None] * (TILES * cap + 1) + rank
    key = jnp.where(mine, slots, -1)
    hit = key.reshape(1, -1) == spot[:, None]
    return jnp.max(jnp.where(hit, row.reshape(1, -1), 0), axis=1)


def exchanged_bits(rows, group):
    rows = list(rows)
    for bit in range(4):
        step = 1 << bit
        low = (group & step) == 0
        for index in range(16):
            if index & step:
                continue
            first, second = rows[index], rows[index | step]
            rows[index] = jnp.where(low, first, pltpu.roll(second, 8 * step, 1))
            rows[index | step] = jnp.where(low, pltpu.roll(first, LANES - 8 * step, 1), second)
    return rows


def unpack_kernel(size, cap, table, come, state, far_side, near_side, speed, scratch):
    message = TILES * cap + 1
    best = come[message - 1]
    for source in range(1, size):
        best = jnp.maximum(best, come[(source + 1) * message - 1])
    speed[...] = jnp.broadcast_to(best, speed.shape)
    group = lax.broadcasted_iota(jnp.int32, (8, LANES), 1) // BLOCK
    even = lax.broadcasted_iota(jnp.int32, (8, LANES), 0) % 2 == 0
    half = FIELDS * BZ * 8
    places = [place_of(plane) for plane in range(BLOCK)]

    def gather(couple, slot):
        p, q = divmod(slot, BZ)
        first = table[slot]
        for h in range(2):
            for f in range(FIELDS):
                row = couple * half + (f * BZ + q) * 8 + 2 * p + h
                value = come[first + ((2 * couple + h) * FIELDS + f) * cap]
                scratch[row : row + 1, :] = value

    def arrange(couple, f):
        first = couple * half + f * BZ * 8
        moved = exchanged_bits(
            [scratch[first + q * 8 : first + q * 8 + 8, :] for q in range(BZ)], group
        )
        for second in range(2):
            for j in range(4):
                lower = moved[second * BLOCK + j]
                upper = moved[second * BLOCK + j + 4]
                planes = (
                    jnp.where(even, lower, pltpu.roll(upper, 1, 0)),
                    jnp.where(even, pltpu.roll(lower, 7, 0), upper),
                )
                for h in range(2):
                    state[f, places[4 * couple + 2 * h + second], j * 8 : j * 8 + 8, :] = planes[h]

    for slot in range(BY * BZ):
        gather(0, slot)
    for f in range(FIELDS):
        for slot in range(f, BY * BZ, FIELDS):
            gather(1, slot)
        arrange(0, f)
    for f in range(FIELDS):
        arrange(1, f)
    for f in range(FIELDS):
        for place in range(3):
            far_side[f, place] = state[f, place]
            near_side[f, place] = state[f, BLOCK - 3 + place]


def unpack(table, come, size, cap):
    halo = jax.ShapeDtypeStruct(HALO, jnp.float32)
    return pl.pallas_call(
        functools.partial(unpack_kernel, size, cap),
        out_shape=(
            jax.ShapeDtypeStruct((FIELDS, BLOCK, ROWS, LANES), jnp.float32),
            halo,
            halo,
            jax.ShapeDtypeStruct((8, LANES), jnp.float32),
        ),
        in_specs=[SMEM, VMEM],
        out_specs=(VMEM,) * 4,
        scratch_shapes=[pltpu.VMEM((FIELDS * (PAIRS // 2) * BZ * 8, LANES), jnp.float32)],
        compiler_params=params(),
        cost_estimate=cost(5_000_000, 2_000_000),
        name="unpack",
    )(table, come)


def y_up(x):
    return jnp.concatenate([x[8:], pltpu.roll(x[:8], 7, 0)], axis=0)


def y_down(x):
    return jnp.concatenate([pltpu.roll(x[24:], 1, 0), x[:24]], axis=0)


def y_up_two(x):
    return jnp.concatenate([x[16:], pltpu.roll(x[:8], 7, 0), pltpu.roll(x[8:16], 7, 0)], axis=0)


def inverse(x):
    return 1.0 / x


def smoothness(before, after):
    curve = after - before
    middle = 0.5 * (after + before)
    base = curve * curve * (13.0 / 12.0) + smooth_epsilon
    plus = middle + curve
    minus = middle - curve
    left = inverse(base + plus * plus)
    centre = inverse(base + middle * middle)
    right = inverse(base + minus * minus)
    return curve, left * left, centre * centre, right * right


def upwind_term(left, centre, right, jump_before, jump_after):
    right = 3.0 * right
    top = left * (jump_before + jump_before) + right * jump_after
    return top * inverse(left + 6.0 * centre + right)


def periodic_divergence(half_flux, scaled, up, up_two, down):
    plus = half_flux + scaled
    minus = half_flux - scaled

    def side(values):
        after = up(values) - values
        curve, left, centre, right = smoothness(down(after), after)
        above = up(curve)
        return curve, above, left, centre, right, above - curve

    curve, _, left, centre, right, jump = side(plus)
    face = 6.0 * (half_flux + up(half_flux)) - curve
    face = face - upwind_term(down(left), centre, up(right), down(jump), jump)
    _, curve, left, centre, right, jump = side(minus)
    face = face + (upwind_term(up_two(right), up(centre), left, up(jump), jump) - curve)
    return face - down(face)


def ring_divergence(half_flux, scaled):
    count = len(half_flux)

    def up(values):
        return values[1:] + [pltpu.roll(values[0], 7, 0)]

    def down(values):
        return [pltpu.roll(values[-1], 1, 0)] + values[:-1]

    def side(values):
        after = [above - value for above, value in zip(up(values), values)]
        parts = [smoothness(before, step) for before, step in zip(down(after), after)]
        curve, left, centre, right = (list(part) for part in zip(*parts))
        jump = [above - value for above, value in zip(up(curve), curve)]
        return curve, left, centre, right, jump

    curve, left, centre, right, jump = side([a + b for a, b in zip(half_flux, scaled)])
    terms = zip(down(left), centre, up(right), down(jump), jump)
    face = [
        6.0 * (here + above) - bend - upwind_term(*term)
        for here, above, bend, term in zip(half_flux, up(half_flux), curve, terms)
    ]
    curve, left, centre, right, jump = side([a - b for a, b in zip(half_flux, scaled)])
    terms = zip(up(right), centre, down(left), jump, down(jump))
    other = [upwind_term(*term) - bend for bend, term in zip(curve, terms)]
    face = [one + two for one, two in zip(face, up(other))]
    return [here - below for here, below in zip(face, down(face))]


def x_divergence(half_flux, scaled, plus_at, minus_at, centre_at):
    faces = {i: 6.0 * (half_flux[i] + half_flux[i + 1]) for i in centre_at}

    def add(i, value):
        faces[i] = faces[i] + value if i in faces else value

    def side(sign):
        values = {i: half_flux[i] + sign * scaled[i] for i in half_flux}
        steps = {i: values[i + 1] - values[i] for i in values if i + 1 in values}
        return {i: smoothness(steps[i - 1], steps[i]) for i in steps if i - 1 in steps}

    parts = side(1)
    for i in plus_at:
        curve, left, centre, right = zip(parts[i - 1], parts[i], parts[i + 1])
        term = upwind_term(left[0], centre[1], right[2], curve[1] - curve[0], curve[2] - curve[1])
        add(i, -(curve[1] + term))
    parts = side(-1)
    for i in minus_at:
        curve, left, centre, right = zip(parts[i - 1], parts[i], parts[i + 1])
        term = upwind_term(right[2], centre[1], left[0], curve[2] - curve[1], curve[1] - curve[0])
        add(i - 1, term - curve[1])
    total = {}
    for i in range(BLOCK):
        if i in faces:
            total[i] = faces[i]
        if i - 1 in faces:
            total[i] = total[i] - faces[i - 1] if i in total else -faces[i - 1]
    return total


INNER = (range(2, 6), range(2, 6), range(0, 7))
FAR = ((-1, 0, 1), (0, 1), (-1,))
NEAR = ((6, 7), (6, 7, 8), (7,))
EVERY = (range(-1, 8), range(0, 9), range(-1, 8))


def ring_divergence(half_flux, scaled):
    count = len(half_flux)

    def up(values):
        return values[1:] + [pltpu.roll(values[0], 7, 0)]

    def down(values):
        return [pltpu.roll(values[-1], 1, 0)] + values[:-1]

    def side(values):
        after = [above - value for above, value in zip(up(values), values)]
        parts = [smoothness(before, step) for before, step in zip(down(after), after)]
        curve, left, centre, right = (list(part) for part in zip(*parts))
        jump = [above - value for above, value in zip(up(curve), curve)]
        return curve, left, centre, right, jump

    curve, left, centre, right, jump = side([a + b for a, b in zip(half_flux, scaled)])
    terms = zip(down(left), centre, up(right), down(jump), jump)
    face = [
        6.0 * (here + above) - bend - upwind_term(*term)
        for here, above, bend, term in zip(half_flux, up(half_flux), curve, terms)
    ]
    curve, left, centre, right, jump = side([a - b for a, b in zip(half_flux, scaled)])
    terms = zip(up(right), centre, down(left), jump, down(jump))
    other = [upwind_term(*term) - bend for bend, term in zip(curve, terms)]
    face = [one + two for one, two in zip(face, up(other))]
    return [here - below for here, below in zip(face, down(face))]


def open_divergence(half_flux, scaled):
    count = len(half_flux)
    plus = [a + b for a, b in zip(half_flux, scaled)]
    minus = [a - b for a, b in zip(half_flux, scaled)]
    faces = [None] * count

    def side(values):
        steps = [values[i + 1] - values[i] for i in range(count - 1)]
        parts = [None] + [smoothness(steps[i - 1], steps[i]) for i in range(1, count - 1)]
        return parts

    parts = side(plus)
    for i in range(2, count - 3):
        jump_before = parts[i][0] - parts[i - 1][0]
        jump_after = parts[i + 1][0] - parts[i][0]
        faces[i] = 6.0 * (half_flux[i] + half_flux[i + 1]) - parts[i][0] - upwind_term(
            parts[i - 1][1], parts[i][2], parts[i + 1][3], jump_before, jump_after
        )
    parts = side(minus)
    for i in range(3, count - 2):
        jump_before = parts[i][0] - parts[i - 1][0]
        jump_after = parts[i + 1][0] - parts[i][0]
        faces[i - 1] = faces[i - 1] + (
            upwind_term(parts[i + 1][3], parts[i][2], parts[i - 1][1], jump_after, jump_before)
            - parts[i][0]
        )
    return [faces[i] - faces[i - 1] for i in range(3, count - 3)]


def half_velocities(fields):
    density, mom_x, mom_y, mom_z, energy = fields
    over = 0.5 / density
    vel = (mom_x * over, mom_y * over, mom_z * over)
    kinetic = mom_x * vel[0] + mom_y * vel[1] + mom_z * vel[2]
    pressure = (gamma_gas - 1.0) * (energy - kinetic)
    return vel, pressure


def half_flux(fields, field, direction, speed, pressure):
    if field == 0:
        return 0.5 * fields[1 + direction]
    if field == 4:
        return (fields[4] + pressure) * speed
    flux = fields[field] * speed
    return flux + 0.5 * pressure if field == 1 + direction else flux


def plane_kernel(with_inner, *refs):
    *states, speed, out, turned = refs
    half_speed = 0.5 * speed[0:1, :]
    lane = lax.broadcasted_iota(jnp.int32, (LANES, LANES), 1)
    to_turned = (lane % 8) * 16 + lane // 8
    to_plain = (lane % 16) * 8 + lane // 16

    for part in range(2):
        state, first = (states[0], 4 * part) if len(states) == 1 else (states[part], 0)
        for f in range(FIELDS):
            plain = state[f, first : first + 4].reshape(LANES, LANES)
            turned[f] = jnp.take_along_axis(plain, to_turned, axis=1).T
        for place in range(4):
            fields = [state[f, first + place] for f in range(FIELDS)]
            vel, pressure = half_velocities(fields)
            for field in range(FIELDS):
                out[field, part * 4 + place] = periodic_divergence(
                    half_flux(fields, field, 1, vel[1], pressure),
                    half_speed * fields[field],
                    y_up,
                    y_up_two,
                    y_down,
                )
        columns = [
            [turned[f, row : row + 8] for row in range(0, LANES, 8)] for f in range(FIELDS)
        ]
        along = [half_velocities(fields) for fields in zip(*columns)]
        for field in range(FIELDS):
            fluxes = [
                half_flux(fields, field, 2, vel[2], pressure)
                for fields, (vel, pressure) in zip(zip(*columns), along)
            ]
            scaled = [half_speed * value for value in columns[field]]
            total = jnp.concatenate(ring_divergence(fluxes, scaled), axis=0)
            plain = jnp.take_along_axis(total.T, to_plain, axis=1)
            out[field, part * 4 : part * 4 + 4] += plain.reshape(4, ROWS, LANES)

    def group(j, carry):
        rows = pl.ds(pl.multiple_of(j * 8, 8), 8)

        def get(f, place):
            return states[0][f, place, rows, :]

        for field, along_x in across(get, half_speed, range(BLOCK), INNER):
            for place in range(BLOCK):
                out[field, place, rows, :] += along_x[place]
        return carry

    if with_inner:
        lax.fori_loop(0, 4, group, 0)


def along_planes(states, speed, with_inner):
    return pl.pallas_call(
        functools.partial(plane_kernel, with_inner),
        out_shape=jax.ShapeDtypeStruct((FIELDS, BLOCK, ROWS, LANES), jnp.float32),
        in_specs=[VMEM] * (len(states) + 1),
        out_specs=VMEM,
        scratch_shapes=[pltpu.VMEM((FIELDS, LANES, LANES), jnp.float32)],
        compiler_params=params(),
        cost_estimate=cost(20_000_000, 1_000_000),
        name="planes",
    )(*states, speed)


def across(get, half_speed, span, parts):
    sign = sign_of_x()
    speeds, pressures = {}, {}
    for place in span:
        vel, pressure = half_velocities([get(f, place) for f in range(FIELDS)])
        speeds[place] = sign * vel[0]
        pressures[place] = pressure
    for field in range(FIELDS):
        fluxes, scaled = {}, {}
        for place in span:
            if field == 0:
                flux = (0.5 * sign) * get(1, place)
            elif field == 4:
                flux = (get(4, place) + pressures[place]) * speeds[place]
            else:
                flux = get(field, place) * speeds[place]
                if field == 1:
                    flux = flux + (0.5 * sign) * pressures[place]
            fluxes[place] = flux
            scaled[place] = half_speed * get(field, place)
        yield field, x_divergence(fluxes, scaled, *parts)


WITH_HALOS = range(-3, BLOCK + 3)


def with_halos(far, near, inside, rows):
    def get(f, place):
        if place < 0:
            return far[f, -1 - place, rows, :]
        if place >= BLOCK:
            return near[f, BLOCK + 2 - place, rows, :]
        return inside(f, place)

    return get


def first_kernel(is_far, *refs):
    if is_far:
        state, sides, halo, speed, other, middle, side, top = refs
    else:
        state, sides, halo, speed, middle, side, top = refs
    first, parts, span = (0, FAR, range(-3, 4)) if is_far else (4, NEAR, range(4, 11))
    half_speed = 0.5 * speed[0:1, :]
    factor = (courant / 6.0) / speed[0:1, :]

    def group(j, best):
        rows = pl.ds(pl.multiple_of(j * 8, 8), 8)

        def inside(f, place):
            return state[f, place, rows, :]

        get = with_halos(halo, halo, inside, rows)
        for field, along_x in across(get, half_speed, span, parts):
            for k in range(4):
                total = sides[field, first + k, rows, :]
                if first + k in along_x:
                    total = total + along_x[first + k]
                value = get(field, first + k) - factor * total
                middle[field, k, rows, :] = value
                at = k if is_far else k - 1
                if 0 <= at < 3:
                    side[field, at, rows, :] = value
        for k in range(4):
            best = jnp.maximum(best, wave_speed([middle[f, k, rows, :] for f in range(FIELDS)]))
        return best

    start = other[...] if is_far else jnp.zeros((8, LANES), jnp.float32)
    best = lax.fori_loop(0, 4, group, start)
    top[...] = jnp.full((8, LANES), jnp.max(best), jnp.float32) if is_far else best


def first_stage(is_far, *operands):
    return pl.pallas_call(
        functools.partial(first_kernel, is_far),
        out_shape=(
            jax.ShapeDtypeStruct((FIELDS, 4, ROWS, LANES), jnp.float32),
            jax.ShapeDtypeStruct(HALO, jnp.float32),
            jax.ShapeDtypeStruct((8, LANES), jnp.float32),
        ),
        in_specs=[VMEM] * len(operands),
        out_specs=(VMEM,) * 3,
        compiler_params=params(),
        cost_estimate=cost(15_000_000, 2_000_000),
        name="first_far" if is_far else "first_near",
    )(*operands)


def second_kernel(state, middle_far, middle_near, sides, far, near, first_speed, speed, out):
    half_speed = 0.5 * speed[0:1, :]
    factor = (courant / 12.0) / first_speed[0:1, :]
    planes = [place_of(place) for place in range(BLOCK)]

    def group(j, carry):
        rows = pl.ds(pl.multiple_of(j * 8, 8), 8)
        spread = pl.ds(j, 8, stride=4)

        def inside(f, place):
            return (middle_far, middle_near)[place // 4][f, place % 4, rows, :]

        get = with_halos(far, near, inside, rows)
        for field, along_x in across(get, half_speed, WITH_HALOS, EVERY):
            for place in range(BLOCK):
                total = along_x[place] + sides[field, place, rows, :]
                value = 0.5 * state[field, place, rows, :] + (
                    0.5 * get(field, place) - factor * total
                )
                out[field, planes[place], spread, :] = value
        return carry

    lax.fori_loop(0, 4, group, 0)


def second_stage(*operands):
    return pl.pallas_call(
        second_kernel,
        out_shape=jax.ShapeDtypeStruct((FIELDS, BLOCK, ROWS, LANES), jnp.float32),
        in_specs=[VMEM] * len(operands),
        out_specs=VMEM,
        compiler_params=params(),
        cost_estimate=cost(30_000_000, 3_000_000),
        name="second_stage",
    )(*operands)


def everyone_max(value, axis, size):
    reach = 1
    while reach * 4 < size:
        reach *= 4
    while reach:
        copies = [value]
        for times in range(1, 4):
            turn = reach * times
            if turn < size:
                pairs = [(i, i ^ turn) for i in range(size)]
                copies.append(lax.ppermute(value, axis, pairs))
        value = functools.reduce(jnp.maximum, copies)
        reach //= 4
    return value


def per_device(blocks, owner_list, slot_list):
    size = lax.axis_size("gx")
    own = lax.axis_index("gx")
    per_dev = blocks.shape[0]
    cap = max(2, 2 * per_dev // size)

    parts = pack(tiled_rows(blocks), owner_list, size, cap, per_dev)
    parts, owner_list, slot_list = lax.optimization_barrier((parts, owner_list, slot_list))
    come = lax.all_to_all(parts, "gx", split_axis=0, concat_axis=0, tiled=True)
    table = arrival_spots(owner_list, slot_list, own, per_dev, size, cap)
    state, far_side, near_side, speed = unpack(table, come.reshape(-1, 1, LANES), size, cap)
    far = from_far(far_side, size)
    near = from_near(near_side, size)
    sides = along_planes((state,), speed, True)
    middle_near, near_side, top = first_stage(False, state, sides, near, speed)
    middle_far, far_side, top = first_stage(True, state, sides, far, speed, top)
    far = from_far(far_side, size)
    near = from_near(near_side, size)
    second = everyone_max(top, "gx", size)
    sides = along_planes((middle_far, middle_near), second, False)
    return second_stage(state, middle_far, middle_near, sides, far, near, speed, second)


def solution(mesh):
    return jax.shard_map(
        per_device,
        mesh=mesh,
        in_specs=(P(("runs", "gx"), None, None), P("runs"), P("runs")),
        out_specs=P(None, ("runs", "gx"), None, None),
        check_vma=False,
    )
```

```python
import functools

import jax
import jax.numpy as jnp
from jax import lax
from jax.experimental import pallas as pl
from jax.experimental.pallas import tpu as pltpu
from jax.sharding import PartitionSpec as P

BLOCK = 8
BY = 4
BZ = 16
FIELDS = 5
LANES = 128
ROWS = BY * BLOCK
PAIRS = BLOCK // 2
TILES = PAIRS * FIELDS

gamma_gas = 1.4
courant = 0.25
smooth_epsilon = 1e-06

VMEM = pl.BlockSpec(memory_space=pltpu.VMEM)
SMEM = pl.BlockSpec(memory_space=pltpu.SMEM)


def params(mebibytes=40):
    return pltpu.CompilerParams(vmem_limit_bytes=mebibytes * 1024 * 1024)


def cost(flops, size):
    return pl.CostEstimate(flops=flops, bytes_accessed=size, transcendentals=0)


def wave_speed(fields):
    density, mom_x, mom_y, mom_z, energy = fields
    inverse = 1.0 / density
    vel = (mom_x * inverse, mom_y * inverse, mom_z * inverse)
    kinetic = 0.5 * (mom_x * vel[0] + mom_y * vel[1] + mom_z * vel[2])
    pressure = (gamma_gas - 1.0) * (energy - kinetic)
    sound = jnp.sqrt(gamma_gas * pressure * inverse)
    fastest = jnp.maximum(jnp.maximum(jnp.abs(vel[0]), jnp.abs(vel[1])), jnp.abs(vel[2]))
    return fastest + sound


def tiled_rows(blocks):
    count = blocks.shape[0] // 8
    groups = blocks.reshape(count, 8, FIELDS, PAIRS, LANES).transpose(2, 0, 3, 1, 4)
    return groups.reshape(FIELDS * count * PAIRS * 8, 1, LANES)


def pack_kernel(
    size, cap, per_dev, owner_hbm, rows_hbm, out_hbm, owner, rows, tiled, out, top, count, member, sems
):
    own = lax.axis_index("gx")
    fetch_owner = pltpu.make_async_copy(owner_hbm, owner, sems.at[0])
    fetch_rows = pltpu.make_async_copy(rows_hbm, rows, sems.at[1])
    fetch_tiled = pltpu.make_async_copy(rows_hbm.at[:, 0], tiled, sems.at[4])
    fetch_owner.start()
    fetch_rows.start()
    fetch_tiled.start()

    def clear(dest, carry):
        count[dest] = 0
        return carry

    lax.fori_loop(0, size, clear, 0, unroll=8)
    fetch_owner.wait()

    def note(block, carry):
        dest = owner[own * per_dev + block]
        rank = count[dest]
        count[dest] = rank + 1
        member[dest * cap + rank] = lax.div(block, 8) * (PAIRS * 8) + lax.rem(block, 8)
        return carry

    lax.fori_loop(0, per_dev, note, 0, unroll=8)
    fetch_rows.wait()
    tiles = TILES * cap

    def message(dest, carry):
        @pl.when(count[dest] > 0)
        def _():
            for rank in range(cap):
                first = member[dest * cap + rank]
                for pair in range(PAIRS):
                    for f in range(FIELDS):
                        to = dest * tiles + (pair * FIELDS + f) * cap + rank
                        out[to] = rows[first + f * (per_dev * PAIRS) + pair * 8]
            part = out.at[pl.ds(dest * tiles, tiles)]
            pltpu.make_async_copy(part, out_hbm.at[dest, pl.ds(0, tiles)], sems.at[2]).start()

        return carry

    lax.fori_loop(0, size, message, 0)
    fetch_tiled.wait()
    best = jnp.zeros((8, LANES), jnp.float32)
    step = per_dev * PAIRS
    for first in range(0, step, 8):
        fields = [tiled[f * step + first : f * step + first + 8, :] for f in range(FIELDS)]
        best = jnp.maximum(best, wave_speed(fields))
    most = jnp.full((1, LANES), jnp.max(best), jnp.float32)
    for dest in range(size):
        top[dest] = most
    send_top = pltpu.make_async_copy(top, out_hbm.at[:, tiles], sems.at[3])
    send_top.start()
    half = out.at[pl.ds(0, per_dev * TILES)]
    pltpu.make_async_copy(half, half, sems.at[2]).wait()
    send_top.wait()


def pack(rows, owner_list, size, cap, per_dev):
    return pl.pallas_call(
        functools.partial(pack_kernel, size, cap, per_dev),
        out_shape=jax.ShapeDtypeStruct((size, TILES * cap + 1, 1, LANES), jnp.float32),
        in_specs=[pl.BlockSpec(memory_space=pltpu.HBM)] * 2,
        out_specs=pl.BlockSpec(memory_space=pltpu.HBM),
        scratch_shapes=[
            pltpu.SMEM(owner_list.shape, jnp.int32),
            pltpu.VMEM(rows.shape, jnp.float32),
            pltpu.VMEM((rows.shape[0], LANES), jnp.float32),
            pltpu.VMEM((size * TILES * cap, 1, LANES), jnp.float32),
            pltpu.VMEM((size, 1, LANES), jnp.float32),
            pltpu.SMEM((size,), jnp.int32),
            pltpu.SMEM((size * cap,), jnp.int32),
            pltpu.SemaphoreType.DMA((5,)),
        ],
        compiler_params=params(62),
        cost_estimate=cost(1_000_000, 3_000_000),
        name="pack",
    )(owner_list, rows)


def turned_round():
    return lax.axis_index("gx") % 2


def place_of(plane):
    return jnp.where(turned_round() == 0, plane, BLOCK - 1 - plane)


def sign_of_x():
    return jnp.where(turned_round() == 0, 1.0, -1.0).astype(jnp.float32)


def from_far(far_side, size):
    pairs = [(i, (i - 1 if i % 2 == 0 else i + 1) % size) for i in range(size)]
    return lax.ppermute(far_side, "gx", pairs)


def from_near(near_side, size):
    return lax.ppermute(near_side, "gx", [(i, i ^ 1) for i in range(size)])


HALO = (FIELDS, 3, ROWS, LANES)


def arrival_spots(owner_list, slot_list, own, per_dev, size, cap):
    owners = owner_list.reshape(size, per_dev)
    slots = slot_list.reshape(size, per_dev)
    mine = owners == own
    spot = jnp.arange(per_dev, dtype=jnp.int32)
    earlier = spot[None, :] < spot[:, None]
    rank = jnp.sum((mine[:, None, :] & earlier[None]).astype(jnp.int32), axis=2)
    row = jnp.arange(size, dtype=jnp.int32)[:, None] * (TILES * cap + 1) + rank
    key = jnp.where(mine, slots, -1)
    hit = key.reshape(1, -1) == spot[:, None]
    return jnp.max(jnp.where(hit, row.reshape(1, -1), 0), axis=1)


def exchanged_bits(rows, group):
    rows = list(rows)
    for bit in range(4):
        step = 1 << bit
        low = (group & step) == 0
        for index in range(16):
            if index & step:
                continue
            first, second = rows[index], rows[index | step]
            rows[index] = jnp.where(low, first, pltpu.roll(second, 8 * step, 1))
            rows[index | step] = jnp.where(low, pltpu.roll(first, LANES - 8 * step, 1), second)
    return rows


def unpack_kernel(size, cap, table, come, state, far_side, near_side, speed, scratch):
    message = TILES * cap + 1
    best = come[message - 1]
    for source in range(1, size):
        best = jnp.maximum(best, come[(source + 1) * message - 1])
    speed[...] = jnp.broadcast_to(best, speed.shape)
    group = lax.broadcasted_iota(jnp.int32, (8, LANES), 1) // BLOCK
    even = lax.broadcasted_iota(jnp.int32, (8, LANES), 0) % 2 == 0
    half = FIELDS * BZ * 8
    places = [place_of(plane) for plane in range(BLOCK)]

    def gather(couple, slot):
        p, q = divmod(slot, BZ)
        first = table[slot]
        for h in range(2):
            for f in range(FIELDS):
                row = couple * half + (f * BZ + q) * 8 + 2 * p + h
                value = come[first + ((2 * couple + h) * FIELDS + f) * cap]
                scratch[row : row + 1, :] = value

    def arrange(couple, f):
        first = couple * half + f * BZ * 8
        moved = exchanged_bits(
            [scratch[first + q * 8 : first + q * 8 + 8, :] for q in range(BZ)], group
        )
        for second in range(2):
            for j in range(4):
                lower = moved[second * BLOCK + j]
                upper = moved[second * BLOCK + j + 4]
                planes = (
                    jnp.where(even, lower, pltpu.roll(upper, 1, 0)),
                    jnp.where(even, pltpu.roll(lower, 7, 0), upper),
                )
                for h in range(2):
                    state[f, places[4 * couple + 2 * h + second], j * 8 : j * 8 + 8, :] = planes[h]

    for slot in range(BY * BZ):
        gather(0, slot)
    for f in range(FIELDS):
        for slot in range(f, BY * BZ, FIELDS):
            gather(1, slot)
        arrange(0, f)
    for f in range(FIELDS):
        arrange(1, f)
    for f in range(FIELDS):
        for place in range(3):
            far_side[f, place] = state[f, place]
            near_side[f, place] = state[f, BLOCK - 3 + place]


def unpack(table, come, size, cap):
    halo = jax.ShapeDtypeStruct(HALO, jnp.float32)
    return pl.pallas_call(
        functools.partial(unpack_kernel, size, cap),
        out_shape=(
            jax.ShapeDtypeStruct((FIELDS, BLOCK, ROWS, LANES), jnp.float32),
            halo,
            halo,
            jax.ShapeDtypeStruct((8, LANES), jnp.float32),
        ),
        in_specs=[SMEM, VMEM],
        out_specs=(VMEM,) * 4,
        scratch_shapes=[pltpu.VMEM((FIELDS * (PAIRS // 2) * BZ * 8, LANES), jnp.float32)],
        compiler_params=params(),
        cost_estimate=cost(5_000_000, 2_000_000),
        name="unpack",
    )(table, come)


def y_up(x):
    return jnp.concatenate([x[8:], pltpu.roll(x[:8], 7, 0)], axis=0)


def y_down(x):
    return jnp.concatenate([pltpu.roll(x[24:], 1, 0), x[:24]], axis=0)


def y_up_two(x):
    return jnp.concatenate([x[16:], pltpu.roll(x[:8], 7, 0), pltpu.roll(x[8:16], 7, 0)], axis=0)


def inverse(x):
    return 1.0 / x


def smoothness(before, after):
    curve = after - before
    middle = 0.5 * (after + before)
    base = curve * curve * (13.0 / 12.0) + smooth_epsilon
    plus = middle + curve
    minus = middle - curve
    left = inverse(base + plus * plus)
    centre = inverse(base + middle * middle)
    right = inverse(base + minus * minus)
    return curve, left * left, centre * centre, right * right


def upwind_term(left, centre, right, jump_before, jump_after):
    right = 3.0 * right
    top = left * (jump_before + jump_before) + right * jump_after
    return top * inverse(left + 6.0 * centre + right)


def periodic_divergence(half_flux, scaled, up, up_two, down):
    plus = half_flux + scaled
    minus = half_flux - scaled

    def side(values):
        after = up(values) - values
        curve, left, centre, right = smoothness(down(after), after)
        above = up(curve)
        return curve, above, left, centre, right, above - curve

    curve, _, left, centre, right, jump = side(plus)
    face = 6.0 * (half_flux + up(half_flux)) - curve
    face = face - upwind_term(down(left), centre, up(right), down(jump), jump)
    _, curve, left, centre, right, jump = side(minus)
    face = face + (upwind_term(up_two(right), up(centre), left, up(jump), jump) - curve)
    return face - down(face)


def ring_divergence(half_flux, scaled):
    count = len(half_flux)

    def up(values):
        return values[1:] + [pltpu.roll(values[0], 7, 0)]

    def down(values):
        return [pltpu.roll(values[-1], 1, 0)] + values[:-1]

    def side(values):
        after = [above - value for above, value in zip(up(values), values)]
        parts = [smoothness(before, step) for before, step in zip(down(after), after)]
        curve, left, centre, right = (list(part) for part in zip(*parts))
        jump = [above - value for above, value in zip(up(curve), curve)]
        return curve, left, centre, right, jump

    curve, left, centre, right, jump = side([a + b for a, b in zip(half_flux, scaled)])
    terms = zip(down(left), centre, up(right), down(jump), jump)
    face = [
        6.0 * (here + above) - bend - upwind_term(*term)
        for here, above, bend, term in zip(half_flux, up(half_flux), curve, terms)
    ]
    curve, left, centre, right, jump = side([a - b for a, b in zip(half_flux, scaled)])
    terms = zip(up(right), centre, down(left), jump, down(jump))
    other = [upwind_term(*term) - bend for bend, term in zip(curve, terms)]
    face = [one + two for one, two in zip(face, up(other))]
    return [here - below for here, below in zip(face, down(face))]


def x_divergence(half_flux, scaled, plus_at, minus_at, centre_at):
    faces = {i: 6.0 * (half_flux[i] + half_flux[i + 1]) for i in centre_at}

    def add(i, value):
        faces[i] = faces[i] + value if i in faces else value

    def side(sign):
        values = {i: half_flux[i] + sign * scaled[i] for i in half_flux}
        steps = {i: values[i + 1] - values[i] for i in values if i + 1 in values}
        return {i: smoothness(steps[i - 1], steps[i]) for i in steps if i - 1 in steps}

    parts = side(1)
    for i in plus_at:
        curve, left, centre, right = zip(parts[i - 1], parts[i], parts[i + 1])
        term = upwind_term(left[0], centre[1], right[2], curve[1] - curve[0], curve[2] - curve[1])
        add(i, -(curve[1] + term))
    parts = side(-1)
    for i in minus_at:
        curve, left, centre, right = zip(parts[i - 1], parts[i], parts[i + 1])
        term = upwind_term(right[2], centre[1], left[0], curve[2] - curve[1], curve[1] - curve[0])
        add(i - 1, term - curve[1])
    total = {}
    for i in range(BLOCK):
        if i in faces:
            total[i] = faces[i]
        if i - 1 in faces:
            total[i] = total[i] - faces[i - 1] if i in total else -faces[i - 1]
    return total


INNER = (range(2, 6), range(2, 6), range(0, 7))
FAR = ((-1, 0, 1), (0, 1), (-1,))
NEAR = ((6, 7), (6, 7, 8), (7,))


def ring_divergence(half_flux, scaled):
    count = len(half_flux)

    def up(values):
        return values[1:] + [pltpu.roll(values[0], 7, 0)]

    def down(values):
        return [pltpu.roll(values[-1], 1, 0)] + values[:-1]

    def side(values):
        after = [above - value for above, value in zip(up(values), values)]
        parts = [smoothness(before, step) for before, step in zip(down(after), after)]
        curve, left, centre, right = (list(part) for part in zip(*parts))
        jump = [above - value for above, value in zip(up(curve), curve)]
        return curve, left, centre, right, jump

    curve, left, centre, right, jump = side([a + b for a, b in zip(half_flux, scaled)])
    terms = zip(down(left), centre, up(right), down(jump), jump)
    face = [
        6.0 * (here + above) - bend - upwind_term(*term)
        for here, above, bend, term in zip(half_flux, up(half_flux), curve, terms)
    ]
    curve, left, centre, right, jump = side([a - b for a, b in zip(half_flux, scaled)])
    terms = zip(up(right), centre, down(left), jump, down(jump))
    other = [upwind_term(*term) - bend for bend, term in zip(curve, terms)]
    face = [one + two for one, two in zip(face, up(other))]
    return [here - below for here, below in zip(face, down(face))]


def open_divergence(half_flux, scaled):
    count = len(half_flux)
    plus = [a + b for a, b in zip(half_flux, scaled)]
    minus = [a - b for a, b in zip(half_flux, scaled)]
    faces = [None] * count

    def side(values):
        steps = [values[i + 1] - values[i] for i in range(count - 1)]
        parts = [None] + [smoothness(steps[i - 1], steps[i]) for i in range(1, count - 1)]
        return parts

    parts = side(plus)
    for i in range(2, count - 3):
        jump_before = parts[i][0] - parts[i - 1][0]
        jump_after = parts[i + 1][0] - parts[i][0]
        faces[i] = 6.0 * (half_flux[i] + half_flux[i + 1]) - parts[i][0] - upwind_term(
            parts[i - 1][1], parts[i][2], parts[i + 1][3], jump_before, jump_after
        )
    parts = side(minus)
    for i in range(3, count - 2):
        jump_before = parts[i][0] - parts[i - 1][0]
        jump_after = parts[i + 1][0] - parts[i][0]
        faces[i - 1] = faces[i - 1] + (
            upwind_term(parts[i + 1][3], parts[i][2], parts[i - 1][1], jump_after, jump_before)
            - parts[i][0]
        )
    return [faces[i] - faces[i - 1] for i in range(3, count - 3)]


def half_velocities(fields):
    density, mom_x, mom_y, mom_z, energy = fields
    over = 0.5 / density
    vel = (mom_x * over, mom_y * over, mom_z * over)
    kinetic = mom_x * vel[0] + mom_y * vel[1] + mom_z * vel[2]
    pressure = (gamma_gas - 1.0) * (energy - kinetic)
    return vel, pressure


def half_flux(fields, field, direction, speed, pressure):
    if field == 0:
        return 0.5 * fields[1 + direction]
    if field == 4:
        return (fields[4] + pressure) * speed
    flux = fields[field] * speed
    return flux + 0.5 * pressure if field == 1 + direction else flux


def plane_kernel(*refs):
    *states, speed, out, turned = refs
    half_speed = 0.5 * speed[0:1, :]
    lane = lax.broadcasted_iota(jnp.int32, (LANES, LANES), 1)
    to_turned = (lane % 8) * 16 + lane // 8
    to_plain = (lane % 16) * 8 + lane // 16

    for part in range(2):
        state, first = (states[0], 4 * part) if len(states) == 1 else (states[part], 0)
        for f in range(FIELDS):
            plain = state[f, first : first + 4].reshape(LANES, LANES)
            turned[f] = jnp.take_along_axis(plain, to_turned, axis=1).T
        for place in range(4):
            fields = [state[f, first + place] for f in range(FIELDS)]
            vel, pressure = half_velocities(fields)
            for field in range(FIELDS):
                out[field, part * 4 + place] = periodic_divergence(
                    half_flux(fields, field, 1, vel[1], pressure),
                    half_speed * fields[field],
                    y_up,
                    y_up_two,
                    y_down,
                )
        columns = [
            [turned[f, row : row + 8] for row in range(0, LANES, 8)] for f in range(FIELDS)
        ]
        along = [half_velocities(fields) for fields in zip(*columns)]
        for field in range(FIELDS):
            fluxes = [
                half_flux(fields, field, 2, vel[2], pressure)
                for fields, (vel, pressure) in zip(zip(*columns), along)
            ]
            scaled = [half_speed * value for value in columns[field]]
            total = jnp.concatenate(ring_divergence(fluxes, scaled), axis=0)
            plain = jnp.take_along_axis(total.T, to_plain, axis=1)
            out[field, part * 4 : part * 4 + 4] += plain.reshape(4, ROWS, LANES)

    def group(j, carry):
        rows = pl.ds(pl.multiple_of(j * 8, 8), 8)

        def get(f, place):
            if len(states) == 1:
                return states[0][f, place, rows, :]
            return states[place // 4][f, place % 4, rows, :]

        for field, along_x in across(get, half_speed, range(BLOCK), INNER):
            for place in range(BLOCK):
                out[field, place, rows, :] += along_x[place]
        return carry

    lax.fori_loop(0, 4, group, 0)


def along_planes(states, speed):
    return pl.pallas_call(
        plane_kernel,
        out_shape=jax.ShapeDtypeStruct((FIELDS, BLOCK, ROWS, LANES), jnp.float32),
        in_specs=[VMEM] * (len(states) + 1),
        out_specs=VMEM,
        scratch_shapes=[pltpu.VMEM((FIELDS, LANES, LANES), jnp.float32)],
        compiler_params=params(),
        cost_estimate=cost(20_000_000, 1_000_000),
        name="planes",
    )(*states, speed)


def across(get, half_speed, span, parts):
    sign = sign_of_x()
    speeds, pressures = {}, {}
    for place in span:
        vel, pressure = half_velocities([get(f, place) for f in range(FIELDS)])
        speeds[place] = sign * vel[0]
        pressures[place] = pressure
    for field in range(FIELDS):
        fluxes, scaled = {}, {}
        for place in span:
            if field == 0:
                flux = (0.5 * sign) * get(1, place)
            elif field == 4:
                flux = (get(4, place) + pressures[place]) * speeds[place]
            else:
                flux = get(field, place) * speeds[place]
                if field == 1:
                    flux = flux + (0.5 * sign) * pressures[place]
            fluxes[place] = flux
            scaled[place] = half_speed * get(field, place)
        yield field, x_divergence(fluxes, scaled, *parts)


def with_halo(halo, inside, rows):
    def get(f, place):
        if place < 0:
            return halo[f, -1 - place, rows, :]
        if place >= BLOCK:
            return halo[f, BLOCK + 2 - place, rows, :]
        return inside(f, place)

    return get


def half_of(is_far):
    return (0, FAR, range(-3, 4)) if is_far else (4, NEAR, range(4, 11))


def first_kernel(is_far, *refs):
    if is_far:
        state, sides, halo, speed, other, middle, side, top = refs
    else:
        state, sides, halo, speed, middle, side, top = refs
    first, parts, span = half_of(is_far)
    half_speed = 0.5 * speed[0:1, :]
    factor = (courant / 6.0) / speed[0:1, :]

    def group(j, best):
        rows = pl.ds(pl.multiple_of(j * 8, 8), 8)

        def inside(f, place):
            return state[f, place, rows, :]

        get = with_halo(halo, inside, rows)
        for field, along_x in across(get, half_speed, span, parts):
            for k in range(4):
                total = sides[field, first + k, rows, :]
                if first + k in along_x:
                    total = total + along_x[first + k]
                value = get(field, first + k) - factor * total
                middle[field, k, rows, :] = value
                at = k if is_far else k - 1
                if 0 <= at < 3:
                    side[field, at, rows, :] = value
        for k in range(4):
            best = jnp.maximum(best, wave_speed([middle[f, k, rows, :] for f in range(FIELDS)]))
        return best

    start = other[...] if is_far else jnp.zeros((8, LANES), jnp.float32)
    best = lax.fori_loop(0, 4, group, start)
    top[...] = jnp.full((8, LANES), jnp.max(best), jnp.float32) if is_far else best


def first_stage(is_far, *operands):
    return pl.pallas_call(
        functools.partial(first_kernel, is_far),
        out_shape=(
            jax.ShapeDtypeStruct((FIELDS, 4, ROWS, LANES), jnp.float32),
            jax.ShapeDtypeStruct(HALO, jnp.float32),
            jax.ShapeDtypeStruct((8, LANES), jnp.float32),
        ),
        in_specs=[VMEM] * len(operands),
        out_specs=(VMEM,) * 3,
        compiler_params=params(),
        cost_estimate=cost(15_000_000, 2_000_000),
        name="first_far" if is_far else "first_near",
    )(*operands)


def second_kernel(is_far, *refs):
    if is_far:
        state, middle, sides, halo, first_speed, speed, other, out = refs
    else:
        state, middle, sides, halo, first_speed, speed, out = refs
    first, parts, span = half_of(is_far)
    half_speed = 0.5 * speed[0:1, :]
    factor = (courant / 12.0) / first_speed[0:1, :]
    if is_far:
        for k in range(4):
            plane = place_of(4 + k)
            for f in range(FIELDS):
                out[f, plane] = other[f, k]

    def group(j, carry):
        rows = pl.ds(pl.multiple_of(j * 8, 8), 8)
        spread = pl.ds(j, 8, stride=4)

        def inside(f, place):
            return middle[f, place - first, rows, :]

        get = with_halo(halo, inside, rows)
        for field, along_x in across(get, half_speed, span, parts):
            for k in range(4):
                total = sides[field, first + k, rows, :]
                if first + k in along_x:
                    total = total + along_x[first + k]
                value = 0.5 * state[field, first + k, rows, :] + (
                    0.5 * get(field, first + k) - factor * total
                )
                out[field, place_of(k) if is_far else k, spread, :] = value
        return carry

    lax.fori_loop(0, 4, group, 0)


def second_stage(is_far, *operands):
    places = BLOCK if is_far else 4
    return pl.pallas_call(
        functools.partial(second_kernel, is_far),
        out_shape=jax.ShapeDtypeStruct((FIELDS, places, ROWS, LANES), jnp.float32),
        in_specs=[VMEM] * len(operands),
        out_specs=VMEM,
        compiler_params=params(),
        cost_estimate=cost(15_000_000, 2_000_000),
        name="second_far" if is_far else "second_near",
    )(*operands)


def everyone_max(value, axis, size):
    reach = 1
    while reach * 4 < size:
        reach *= 4
    while reach:
        copies = [value]
        for times in range(1, 4):
            turn = reach * times
            if turn < size:
                pairs = [(i, i ^ turn) for i in range(size)]
                copies.append(lax.ppermute(value, axis, pairs))
        value = functools.reduce(jnp.maximum, copies)
        reach //= 4
    return value


def per_device(blocks, owner_list, slot_list):
    size = lax.axis_size("gx")
    own = lax.axis_index("gx")
    per_dev = blocks.shape[0]
    cap = max(2, 2 * per_dev // size)

    parts = pack(tiled_rows(blocks), owner_list, size, cap, per_dev)
    parts, owner_list, slot_list = lax.optimization_barrier((parts, owner_list, slot_list))
    come = lax.all_to_all(parts, "gx", split_axis=0, concat_axis=0, tiled=True)
    table = arrival_spots(owner_list, slot_list, own, per_dev, size, cap)
    state, far_side, near_side, speed = unpack(table, come.reshape(-1, 1, LANES), size, cap)
    far = from_far(far_side, size)
    near = from_near(near_side, size)
    sides = along_planes((state,), speed)
    middle_near, near_side, top = first_stage(False, state, sides, near, speed)
    middle_far, far_side, top = first_stage(True, state, sides, far, speed, top)
    near = from_near(near_side, size)
    second = everyone_max(top, "gx", size)
    far_side, second = lax.optimization_barrier((far_side, second))
    far = from_far(far_side, size)
    sides = along_planes((middle_far, middle_near), second)
    part = second_stage(False, state, middle_near, sides, near, speed, second)
    return second_stage(True, state, middle_far, sides, far, speed, second, part)


def solution(mesh):
    return jax.shard_map(
        per_device,
        mesh=mesh,
        in_specs=(P(("runs", "gx"), None, None), P("runs"), P("runs")),
        out_specs=P(None, ("runs", "gx"), None, None),
        check_vma=False,
    )
```

```python
import functools

import jax
import jax.numpy as jnp
from jax import lax
from jax.experimental import pallas as pl
from jax.experimental.pallas import tpu as pltpu
from jax.sharding import PartitionSpec as P

BLOCK = 8
BY = 4
BZ = 16
FIELDS = 5
LANES = 128
ROWS = BY * BLOCK
PAIRS = BLOCK // 2
TILES = PAIRS * FIELDS

gamma_gas = 1.4
courant = 0.25
smooth_epsilon = 1e-06

VMEM = pl.BlockSpec(memory_space=pltpu.VMEM)
SMEM = pl.BlockSpec(memory_space=pltpu.SMEM)


def params(mebibytes=40):
    return pltpu.CompilerParams(vmem_limit_bytes=mebibytes * 1024 * 1024)


def cost(flops, size):
    return pl.CostEstimate(flops=flops, bytes_accessed=size, transcendentals=0)


def wave_speed(fields):
    density, mom_x, mom_y, mom_z, energy = fields
    inverse = 1.0 / density
    vel = (mom_x * inverse, mom_y * inverse, mom_z * inverse)
    kinetic = 0.5 * (mom_x * vel[0] + mom_y * vel[1] + mom_z * vel[2])
    pressure = (gamma_gas - 1.0) * (energy - kinetic)
    sound = jnp.sqrt(gamma_gas * pressure * inverse)
    fastest = jnp.maximum(jnp.maximum(jnp.abs(vel[0]), jnp.abs(vel[1])), jnp.abs(vel[2]))
    return fastest + sound


def tiled_rows(blocks):
    count = blocks.shape[0] // 8
    groups = blocks.reshape(count, 8, FIELDS, PAIRS, LANES).transpose(2, 0, 3, 1, 4)
    return groups.reshape(FIELDS * count * PAIRS * 8, 1, LANES)


def pack_kernel(
    size, cap, per_dev, owner_hbm, rows_hbm, out_hbm, owner, rows, tiled, out, top, count, member, sems
):
    own = lax.axis_index("gx")
    fetch_owner = pltpu.make_async_copy(owner_hbm, owner, sems.at[0])
    fetch_rows = pltpu.make_async_copy(rows_hbm, rows, sems.at[1])
    fetch_tiled = pltpu.make_async_copy(rows_hbm.at[:, 0], tiled, sems.at[4])
    fetch_owner.start()
    fetch_rows.start()
    fetch_tiled.start()

    def clear(dest, carry):
        count[dest] = 0
        return carry

    lax.fori_loop(0, size, clear, 0, unroll=8)
    fetch_owner.wait()

    def note(block, carry):
        dest = owner[own * per_dev + block]
        rank = count[dest]
        count[dest] = rank + 1
        member[dest * cap + rank] = lax.div(block, 8) * (PAIRS * 8) + lax.rem(block, 8)
        return carry

    lax.fori_loop(0, per_dev, note, 0, unroll=8)
    fetch_rows.wait()
    tiles = TILES * cap

    def message(dest, carry):
        @pl.when(count[dest] > 0)
        def _():
            for rank in range(cap):
                first = member[dest * cap + rank]
                for pair in range(PAIRS):
                    for f in range(FIELDS):
                        to = dest * tiles + (pair * FIELDS + f) * cap + rank
                        out[to] = rows[first + f * (per_dev * PAIRS) + pair * 8]
            part = out.at[pl.ds(dest * tiles, tiles)]
            pltpu.make_async_copy(part, out_hbm.at[dest, pl.ds(0, tiles)], sems.at[2]).start()

        return carry

    lax.fori_loop(0, size, message, 0)
    fetch_tiled.wait()
    best = jnp.zeros((8, LANES), jnp.float32)
    step = per_dev * PAIRS
    for first in range(0, step, 8):
        fields = [tiled[f * step + first : f * step + first + 8, :] for f in range(FIELDS)]
        best = jnp.maximum(best, wave_speed(fields))
    most = jnp.full((1, LANES), jnp.max(best), jnp.float32)
    for dest in range(size):
        top[dest] = most
    send_top = pltpu.make_async_copy(top, out_hbm.at[:, tiles], sems.at[3])
    send_top.start()
    half = out.at[pl.ds(0, per_dev * TILES)]
    pltpu.make_async_copy(half, half, sems.at[2]).wait()
    send_top.wait()


def pack(rows, owner_list, size, cap, per_dev):
    return pl.pallas_call(
        functools.partial(pack_kernel, size, cap, per_dev),
        out_shape=jax.ShapeDtypeStruct((size, TILES * cap + 1, 1, LANES), jnp.float32),
        in_specs=[pl.BlockSpec(memory_space=pltpu.HBM)] * 2,
        out_specs=pl.BlockSpec(memory_space=pltpu.HBM),
        scratch_shapes=[
            pltpu.SMEM(owner_list.shape, jnp.int32),
            pltpu.VMEM(rows.shape, jnp.float32),
            pltpu.VMEM((rows.shape[0], LANES), jnp.float32),
            pltpu.VMEM((size * TILES * cap, 1, LANES), jnp.float32),
            pltpu.VMEM((size, 1, LANES), jnp.float32),
            pltpu.SMEM((size,), jnp.int32),
            pltpu.SMEM((size * cap,), jnp.int32),
            pltpu.SemaphoreType.DMA((5,)),
        ],
        compiler_params=params(62),
        cost_estimate=cost(1_000_000, 3_000_000),
        name="pack",
    )(owner_list, rows)


def turned_round():
    return lax.axis_index("gx") % 2


def place_of(plane):
    return jnp.where(turned_round() == 0, plane, BLOCK - 1 - plane)


def sign_of_x():
    return jnp.where(turned_round() == 0, 1.0, -1.0).astype(jnp.float32)


def from_far(far_side, size):
    pairs = [(i, (i - 1 if i % 2 == 0 else i + 1) % size) for i in range(size)]
    return lax.ppermute(far_side, "gx", pairs)


def from_near(near_side, size):
    return lax.ppermute(near_side, "gx", [(i, i ^ 1) for i in range(size)])


HALO = (FIELDS, 3, ROWS, LANES)


def arrival_spots(owner_list, slot_list, own, per_dev, size, cap):
    owners = owner_list.reshape(size, per_dev)
    slots = slot_list.reshape(size, per_dev)
    mine = owners == own
    spot = jnp.arange(per_dev, dtype=jnp.int32)
    earlier = spot[None, :] < spot[:, None]
    rank = jnp.sum((mine[:, None, :] & earlier[None]).astype(jnp.int32), axis=2)
    row = jnp.arange(size, dtype=jnp.int32)[:, None] * (TILES * cap + 1) + rank
    key = jnp.where(mine, slots, -1)
    hit = key.reshape(1, -1) == spot[:, None]
    return jnp.max(jnp.where(hit, row.reshape(1, -1), 0), axis=1)


def exchanged_bits(rows, group):
    rows = list(rows)
    for bit in range(4):
        step = 1 << bit
        low = (group & step) == 0
        for index in range(16):
            if index & step:
                continue
            first, second = rows[index], rows[index | step]
            rows[index] = jnp.where(low, first, pltpu.roll(second, 8 * step, 1))
            rows[index | step] = jnp.where(low, pltpu.roll(first, LANES - 8 * step, 1), second)
    return rows


def unpack_kernel(size, cap, table, come, state, far_side, near_side, speed, scratch):
    message = TILES * cap + 1
    best = come[message - 1]
    for source in range(1, size):
        best = jnp.maximum(best, come[(source + 1) * message - 1])
    speed[...] = jnp.broadcast_to(best, speed.shape)
    group = lax.broadcasted_iota(jnp.int32, (8, LANES), 1) // BLOCK
    even = lax.broadcasted_iota(jnp.int32, (8, LANES), 0) % 2 == 0
    half = FIELDS * BZ * 8
    places = [place_of(plane) for plane in range(BLOCK)]

    def gather(couple, slot):
        p, q = divmod(slot, BZ)
        first = table[slot]
        for h in range(2):
            for f in range(FIELDS):
                row = couple * half + (f * BZ + q) * 8 + 2 * p + h
                value = come[first + ((2 * couple + h) * FIELDS + f) * cap]
                scratch[row : row + 1, :] = value

    def arrange(couple, f):
        first = couple * half + f * BZ * 8
        moved = exchanged_bits(
            [scratch[first + q * 8 : first + q * 8 + 8, :] for q in range(BZ)], group
        )
        for second in range(2):
            for j in range(4):
                lower = moved[second * BLOCK + j]
                upper = moved[second * BLOCK + j + 4]
                planes = (
                    jnp.where(even, lower, pltpu.roll(upper, 1, 0)),
                    jnp.where(even, pltpu.roll(lower, 7, 0), upper),
                )
                for h in range(2):
                    state[f, places[4 * couple + 2 * h + second], j * 8 : j * 8 + 8, :] = planes[h]

    for slot in range(BY * BZ):
        gather(0, slot)
    for f in range(FIELDS):
        for slot in range(f, BY * BZ, FIELDS):
            gather(1, slot)
        arrange(0, f)
    for f in range(FIELDS):
        arrange(1, f)
    for f in range(FIELDS):
        for place in range(3):
            far_side[f, place] = state[f, place]
            near_side[f, place] = state[f, BLOCK - 3 + place]


def unpack(table, come, size, cap):
    halo = jax.ShapeDtypeStruct(HALO, jnp.float32)
    return pl.pallas_call(
        functools.partial(unpack_kernel, size, cap),
        out_shape=(
            jax.ShapeDtypeStruct((FIELDS, BLOCK, ROWS, LANES), jnp.float32),
            halo,
            halo,
            jax.ShapeDtypeStruct((8, LANES), jnp.float32),
        ),
        in_specs=[SMEM, VMEM],
        out_specs=(VMEM,) * 4,
        scratch_shapes=[pltpu.VMEM((FIELDS * (PAIRS // 2) * BZ * 8, LANES), jnp.float32)],
        compiler_params=params(),
        cost_estimate=cost(5_000_000, 2_000_000),
        name="unpack",
    )(table, come)


def y_up(x):
    return jnp.concatenate([x[8:], pltpu.roll(x[:8], 7, 0)], axis=0)


def y_down(x):
    return jnp.concatenate([pltpu.roll(x[24:], 1, 0), x[:24]], axis=0)


def y_up_two(x):
    return jnp.concatenate([x[16:], pltpu.roll(x[:8], 7, 0), pltpu.roll(x[8:16], 7, 0)], axis=0)


def inverse(x):
    return 1.0 / x


def smoothness(before, after):
    curve = after - before
    middle = 0.5 * (after + before)
    base = curve * curve * (13.0 / 12.0) + smooth_epsilon
    plus = middle + curve
    minus = middle - curve
    left = inverse(base + plus * plus)
    centre = inverse(base + middle * middle)
    right = inverse(base + minus * minus)
    return curve, left * left, centre * centre, right * right


def upwind_term(left, centre, right, jump_before, jump_after):
    right = 3.0 * right
    top = left * (jump_before + jump_before) + right * jump_after
    return top * inverse(left + 6.0 * centre + right)


def periodic_divergence(half_flux, scaled, up, up_two, down):
    plus = half_flux + scaled
    minus = half_flux - scaled

    def side(values):
        after = up(values) - values
        curve, left, centre, right = smoothness(down(after), after)
        above = up(curve)
        return curve, above, left, centre, right, above - curve

    curve, _, left, centre, right, jump = side(plus)
    face = 6.0 * (half_flux + up(half_flux)) - curve
    face = face - upwind_term(down(left), centre, up(right), down(jump), jump)
    _, curve, left, centre, right, jump = side(minus)
    face = face + (upwind_term(up_two(right), up(centre), left, up(jump), jump) - curve)
    return face - down(face)


def ring_divergence(half_flux, scaled):
    count = len(half_flux)

    def up(values):
        return values[1:] + [pltpu.roll(values[0], 7, 0)]

    def down(values):
        return [pltpu.roll(values[-1], 1, 0)] + values[:-1]

    def side(values):
        after = [above - value for above, value in zip(up(values), values)]
        parts = [smoothness(before, step) for before, step in zip(down(after), after)]
        curve, left, centre, right = (list(part) for part in zip(*parts))
        jump = [above - value for above, value in zip(up(curve), curve)]
        return curve, left, centre, right, jump

    curve, left, centre, right, jump = side([a + b for a, b in zip(half_flux, scaled)])
    terms = zip(down(left), centre, up(right), down(jump), jump)
    face = [
        6.0 * (here + above) - bend - upwind_term(*term)
        for here, above, bend, term in zip(half_flux, up(half_flux), curve, terms)
    ]
    curve, left, centre, right, jump = side([a - b for a, b in zip(half_flux, scaled)])
    terms = zip(up(right), centre, down(left), jump, down(jump))
    other = [upwind_term(*term) - bend for bend, term in zip(curve, terms)]
    face = [one + two for one, two in zip(face, up(other))]
    return [here - below for here, below in zip(face, down(face))]


def x_divergence(half_flux, scaled, plus_at, minus_at, centre_at):
    faces = {i: 6.0 * (half_flux[i] + half_flux[i + 1]) for i in centre_at}

    def add(i, value):
        faces[i] = faces[i] + value if i in faces else value

    def side(sign):
        values = {i: half_flux[i] + sign * scaled[i] for i in half_flux}
        steps = {i: values[i + 1] - values[i] for i in values if i + 1 in values}
        return {i: smoothness(steps[i - 1], steps[i]) for i in steps if i - 1 in steps}

    parts = side(1)
    for i in plus_at:
        curve, left, centre, right = zip(parts[i - 1], parts[i], parts[i + 1])
        term = upwind_term(left[0], centre[1], right[2], curve[1] - curve[0], curve[2] - curve[1])
        add(i, -(curve[1] + term))
    parts = side(-1)
    for i in minus_at:
        curve, left, centre, right = zip(parts[i - 1], parts[i], parts[i + 1])
        term = upwind_term(right[2], centre[1], left[0], curve[2] - curve[1], curve[1] - curve[0])
        add(i - 1, term - curve[1])
    total = {}
    for i in range(BLOCK):
        if i in faces:
            total[i] = faces[i]
        if i - 1 in faces:
            total[i] = total[i] - faces[i - 1] if i in total else -faces[i - 1]
    return total


INNER = (range(2, 6), range(2, 6), range(0, 7))
FAR = ((-1, 0, 1), (0, 1), (-1,))
NEAR = ((6, 7), (6, 7, 8), (7,))
EVERY = (range(-1, 8), range(0, 9), range(-1, 8))


def ring_divergence(half_flux, scaled):
    count = len(half_flux)

    def up(values):
        return values[1:] + [pltpu.roll(values[0], 7, 0)]

    def down(values):
        return [pltpu.roll(values[-1], 1, 0)] + values[:-1]

    def side(values):
        after = [above - value for above, value in zip(up(values), values)]
        parts = [smoothness(before, step) for before, step in zip(down(after), after)]
        curve, left, centre, right = (list(part) for part in zip(*parts))
        jump = [above - value for above, value in zip(up(curve), curve)]
        return curve, left, centre, right, jump

    curve, left, centre, right, jump = side([a + b for a, b in zip(half_flux, scaled)])
    terms = zip(down(left), centre, up(right), down(jump), jump)
    face = [
        6.0 * (here + above) - bend - upwind_term(*term)
        for here, above, bend, term in zip(half_flux, up(half_flux), curve, terms)
    ]
    curve, left, centre, right, jump = side([a - b for a, b in zip(half_flux, scaled)])
    terms = zip(up(right), centre, down(left), jump, down(jump))
    other = [upwind_term(*term) - bend for bend, term in zip(curve, terms)]
    face = [one + two for one, two in zip(face, up(other))]
    return [here - below for here, below in zip(face, down(face))]


def open_divergence(half_flux, scaled):
    count = len(half_flux)
    plus = [a + b for a, b in zip(half_flux, scaled)]
    minus = [a - b for a, b in zip(half_flux, scaled)]
    faces = [None] * count

    def side(values):
        steps = [values[i + 1] - values[i] for i in range(count - 1)]
        parts = [None] + [smoothness(steps[i - 1], steps[i]) for i in range(1, count - 1)]
        return parts

    parts = side(plus)
    for i in range(2, count - 3):
        jump_before = parts[i][0] - parts[i - 1][0]
        jump_after = parts[i + 1][0] - parts[i][0]
        faces[i] = 6.0 * (half_flux[i] + half_flux[i + 1]) - parts[i][0] - upwind_term(
            parts[i - 1][1], parts[i][2], parts[i + 1][3], jump_before, jump_after
        )
    parts = side(minus)
    for i in range(3, count - 2):
        jump_before = parts[i][0] - parts[i - 1][0]
        jump_after = parts[i + 1][0] - parts[i][0]
        faces[i - 1] = faces[i - 1] + (
            upwind_term(parts[i + 1][3], parts[i][2], parts[i - 1][1], jump_after, jump_before)
            - parts[i][0]
        )
    return [faces[i] - faces[i - 1] for i in range(3, count - 3)]


def half_velocities(fields):
    density, mom_x, mom_y, mom_z, energy = fields
    over = 0.5 / density
    vel = (mom_x * over, mom_y * over, mom_z * over)
    kinetic = mom_x * vel[0] + mom_y * vel[1] + mom_z * vel[2]
    pressure = (gamma_gas - 1.0) * (energy - kinetic)
    return vel, pressure


def half_flux(fields, field, direction, speed, pressure):
    if field == 0:
        return 0.5 * fields[1 + direction]
    if field == 4:
        return (fields[4] + pressure) * speed
    flux = fields[field] * speed
    return flux + 0.5 * pressure if field == 1 + direction else flux


def plane_kernel(with_inner, *refs):
    *states, speed, out, turned = refs
    half_speed = 0.5 * speed[0:1, :]
    lane = lax.broadcasted_iota(jnp.int32, (LANES, LANES), 1)
    to_turned = (lane % 8) * 16 + lane // 8
    to_plain = (lane % 16) * 8 + lane // 16

    for part in range(2):
        state, first = (states[0], 4 * part) if len(states) == 1 else (states[part], 0)
        for f in range(FIELDS):
            plain = state[f, first : first + 4].reshape(LANES, LANES)
            turned[f] = jnp.take_along_axis(plain, to_turned, axis=1).T
        for place in range(4):
            fields = [state[f, first + place] for f in range(FIELDS)]
            vel, pressure = half_velocities(fields)
            for field in range(FIELDS):
                out[field, part * 4 + place] = periodic_divergence(
                    half_flux(fields, field, 1, vel[1], pressure),
                    half_speed * fields[field],
                    y_up,
                    y_up_two,
                    y_down,
                )
        columns = [
            [turned[f, row : row + 8] for row in range(0, LANES, 8)] for f in range(FIELDS)
        ]
        along = [half_velocities(fields) for fields in zip(*columns)]
        for field in range(FIELDS):
            fluxes = [
                half_flux(fields, field, 2, vel[2], pressure)
                for fields, (vel, pressure) in zip(zip(*columns), along)
            ]
            scaled = [half_speed * value for value in columns[field]]
            total = jnp.concatenate(ring_divergence(fluxes, scaled), axis=0)
            plain = jnp.take_along_axis(total.T, to_plain, axis=1)
            out[field, part * 4 : part * 4 + 4] += plain.reshape(4, ROWS, LANES)

    def group(j, carry):
        rows = pl.ds(pl.multiple_of(j * 8, 8), 8)

        def get(f, place):
            return states[0][f, place, rows, :]

        for field, along_x in across(get, half_speed, range(BLOCK), INNER):
            for place in range(BLOCK):
                out[field, place, rows, :] += along_x[place]
        return carry

    if with_inner:
        lax.fori_loop(0, 4, group, 0)


def along_planes(states, speed, with_inner):
    return pl.pallas_call(
        functools.partial(plane_kernel, with_inner),
        out_shape=jax.ShapeDtypeStruct((FIELDS, BLOCK, ROWS, LANES), jnp.float32),
        in_specs=[VMEM] * (len(states) + 1),
        out_specs=VMEM,
        scratch_shapes=[pltpu.VMEM((FIELDS, LANES, LANES), jnp.float32)],
        compiler_params=params(),
        cost_estimate=cost(20_000_000, 1_000_000),
        name="planes",
    )(*states, speed)


def across(get, half_speed, span, parts):
    sign = sign_of_x()
    speeds, pressures = {}, {}
    for place in span:
        vel, pressure = half_velocities([get(f, place) for f in range(FIELDS)])
        speeds[place] = sign * vel[0]
        pressures[place] = pressure
    for field in range(FIELDS):
        fluxes, scaled = {}, {}
        for place in span:
            if field == 0:
                flux = (0.5 * sign) * get(1, place)
            elif field == 4:
                flux = (get(4, place) + pressures[place]) * speeds[place]
            else:
                flux = get(field, place) * speeds[place]
                if field == 1:
                    flux = flux + (0.5 * sign) * pressures[place]
            fluxes[place] = flux
            scaled[place] = half_speed * get(field, place)
        yield field, x_divergence(fluxes, scaled, *parts)


WITH_HALOS = range(-3, BLOCK + 3)


def with_halos(far, near, inside, rows):
    def get(f, place):
        if place < 0:
            return far[f, -1 - place, rows, :]
        if place >= BLOCK:
            return near[f, BLOCK + 2 - place, rows, :]
        return inside(f, place)

    return get


def first_kernel(is_far, *refs):
    if is_far:
        state, sides, halo, speed, other, middle, side, top = refs
    else:
        state, sides, halo, speed, middle, side, top = refs
    first, parts, span = (0, FAR, range(-3, 4)) if is_far else (4, NEAR, range(4, 11))
    half_speed = 0.5 * speed[0:1, :]
    factor = (courant / 6.0) / speed[0:1, :]

    def group(j, best):
        rows = pl.ds(pl.multiple_of(j * 8, 8), 8)

        def inside(f, place):
            return state[f, place, rows, :]

        get = with_halos(halo, halo, inside, rows)
        for field, along_x in across(get, half_speed, span, parts):
            for k in range(4):
                total = sides[field, first + k, rows, :]
                if first + k in along_x:
                    total = total + along_x[first + k]
                value = get(field, first + k) - factor * total
                middle[field, k, rows, :] = value
                at = k if is_far else k - 1
                if 0 <= at < 3:
                    side[field, at, rows, :] = value
        for k in range(4):
            best = jnp.maximum(best, wave_speed([middle[f, k, rows, :] for f in range(FIELDS)]))
        return best

    start = other[...] if is_far else jnp.zeros((8, LANES), jnp.float32)
    best = lax.fori_loop(0, 4, group, start)
    top[...] = jnp.full((8, LANES), jnp.max(best), jnp.float32) if is_far else best


def first_stage(is_far, *operands):
    return pl.pallas_call(
        functools.partial(first_kernel, is_far),
        out_shape=(
            jax.ShapeDtypeStruct((FIELDS, 4, ROWS, LANES), jnp.float32),
            jax.ShapeDtypeStruct(HALO, jnp.float32),
            jax.ShapeDtypeStruct((8, LANES), jnp.float32),
        ),
        in_specs=[VMEM] * len(operands),
        out_specs=(VMEM,) * 3,
        compiler_params=params(),
        cost_estimate=cost(15_000_000, 2_000_000),
        name="first_far" if is_far else "first_near",
    )(*operands)


def second_kernel(state, middle_far, middle_near, sides, far, near, first_speed, speed, out):
    half_speed = 0.5 * speed[0:1, :]
    factor = (courant / 12.0) / first_speed[0:1, :]
    planes = [place_of(place) for place in range(BLOCK)]

    def group(j, carry):
        rows = pl.ds(pl.multiple_of(j * 8, 8), 8)
        spread = pl.ds(j, 8, stride=4)

        def inside(f, place):
            return (middle_far, middle_near)[place // 4][f, place % 4, rows, :]

        get = with_halos(far, near, inside, rows)
        for field, along_x in across(get, half_speed, WITH_HALOS, EVERY):
            for place in range(BLOCK):
                total = along_x[place] + sides[field, place, rows, :]
                value = 0.5 * state[field, place, rows, :] + (
                    0.5 * get(field, place) - factor * total
                )
                out[field, planes[place], spread, :] = value
        return carry

    lax.fori_loop(0, 4, group, 0)


def second_stage(*operands):
    return pl.pallas_call(
        second_kernel,
        out_shape=jax.ShapeDtypeStruct((FIELDS, BLOCK, ROWS, LANES), jnp.float32),
        in_specs=[VMEM] * len(operands),
        out_specs=VMEM,
        compiler_params=params(),
        cost_estimate=cost(30_000_000, 3_000_000),
        name="second_stage",
    )(*operands)


def everyone_max(value, axis, size):
    reach = 1
    while reach * 4 < size:
        reach *= 4
    while reach:
        copies = [value]
        for times in range(3, 0, -1):
            turn = reach * times
            if turn < size:
                pairs = [(i, i ^ turn) for i in range(size)]
                copies.append(lax.ppermute(value, axis, pairs))
        value = functools.reduce(jnp.maximum, copies)
        reach //= 4
    return value


def per_device(blocks, owner_list, slot_list):
    size = lax.axis_size("gx")
    own = lax.axis_index("gx")
    per_dev = blocks.shape[0]
    cap = max(2, 2 * per_dev // size)

    parts = pack(tiled_rows(blocks), owner_list, size, cap, per_dev)
    parts, owner_list, slot_list = lax.optimization_barrier((parts, owner_list, slot_list))
    come = lax.all_to_all(parts, "gx", split_axis=0, concat_axis=0, tiled=True)
    table = arrival_spots(owner_list, slot_list, own, per_dev, size, cap)
    state, far_side, near_side, speed = unpack(table, come.reshape(-1, 1, LANES), size, cap)
    far = from_far(far_side, size)
    near = from_near(near_side, size)
    sides = along_planes((state,), speed, True)
    middle_near, near_side, top = first_stage(False, state, sides, near, speed)
    middle_far, far_side, top = first_stage(True, state, sides, far, speed, top)
    far = from_far(far_side, size)
    near = from_near(near_side, size)
    second = everyone_max(top, "gx", size)
    sides = along_planes((middle_far, middle_near), second, False)
    return second_stage(state, middle_far, middle_near, sides, far, near, speed, second)


def solution(mesh):
    return jax.shard_map(
        per_device,
        mesh=mesh,
        in_specs=(P(("runs", "gx"), None, None), P("runs"), P("runs")),
        out_specs=P(None, ("runs", "gx"), None, None),
        check_vma=False,
    )
```

```python
import functools

import jax
import jax.numpy as jnp
from jax import lax
from jax.experimental import pallas as pl
from jax.experimental.pallas import tpu as pltpu
from jax.sharding import PartitionSpec as P

BLOCK = 8
BY = 4
BZ = 16
FIELDS = 5
LANES = 128
ROWS = BY * BLOCK
PAIRS = BLOCK // 2
TILES = PAIRS * FIELDS

gamma_gas = 1.4
courant = 0.25
smooth_epsilon = 1e-06

VMEM = pl.BlockSpec(memory_space=pltpu.VMEM)
SMEM = pl.BlockSpec(memory_space=pltpu.SMEM)


def params(mebibytes=40):
    return pltpu.CompilerParams(vmem_limit_bytes=mebibytes * 1024 * 1024)


def cost(flops, size):
    return pl.CostEstimate(flops=flops, bytes_accessed=size, transcendentals=0)


def wave_speed(fields):
    density, mom_x, mom_y, mom_z, energy = fields
    inverse = 1.0 / density
    vel = (mom_x * inverse, mom_y * inverse, mom_z * inverse)
    kinetic = 0.5 * (mom_x * vel[0] + mom_y * vel[1] + mom_z * vel[2])
    pressure = (gamma_gas - 1.0) * (energy - kinetic)
    sound = jnp.sqrt(gamma_gas * pressure * inverse)
    fastest = jnp.maximum(jnp.maximum(jnp.abs(vel[0]), jnp.abs(vel[1])), jnp.abs(vel[2]))
    return fastest + sound


def tiled_rows(blocks):
    count = blocks.shape[0] // 8
    groups = blocks.reshape(count, 8, FIELDS, PAIRS, LANES).transpose(2, 0, 3, 1, 4)
    return groups.reshape(FIELDS * count * PAIRS * 8, 1, LANES)


def pack_kernel(
    size, cap, per_dev, owner_hbm, rows_hbm, out_hbm, owner, rows, tiled, out, top, count, member, sems
):
    own = lax.axis_index("gx")
    fetch_owner = pltpu.make_async_copy(owner_hbm, owner, sems.at[0])
    fetch_rows = pltpu.make_async_copy(rows_hbm, rows, sems.at[1])
    fetch_tiled = pltpu.make_async_copy(rows_hbm.at[:, 0], tiled, sems.at[4])
    fetch_owner.start()
    fetch_rows.start()
    fetch_tiled.start()

    def clear(dest, carry):
        count[dest] = 0
        return carry

    lax.fori_loop(0, size, clear, 0, unroll=8)
    fetch_owner.wait()

    def note(block, carry):
        dest = owner[own * per_dev + block]
        rank = count[dest]
        count[dest] = rank + 1
        member[dest * cap + rank] = lax.div(block, 8) * (PAIRS * 8) + lax.rem(block, 8)
        return carry

    lax.fori_loop(0, per_dev, note, 0, unroll=8)
    fetch_rows.wait()
    tiles = TILES * cap

    def message(dest, carry):
        @pl.when(count[dest] > 0)
        def _():
            for rank in range(cap):
                first = member[dest * cap + rank]
                for pair in range(PAIRS):
                    for f in range(FIELDS):
                        to = dest * tiles + (pair * FIELDS + f) * cap + rank
                        out[to] = rows[first + f * (per_dev * PAIRS) + pair * 8]
            part = out.at[pl.ds(dest * tiles, tiles)]
            pltpu.make_async_copy(part, out_hbm.at[dest, pl.ds(0, tiles)], sems.at[2]).start()

        return carry

    lax.fori_loop(0, size, message, 0)
    fetch_tiled.wait()
    best = jnp.zeros((8, LANES), jnp.float32)
    step = per_dev * PAIRS
    for first in range(0, step, 8):
        fields = [tiled[f * step + first : f * step + first + 8, :] for f in range(FIELDS)]
        best = jnp.maximum(best, wave_speed(fields))
    most = jnp.full((1, LANES), jnp.max(best), jnp.float32)
    for dest in range(size):
        top[dest] = most
    send_top = pltpu.make_async_copy(top, out_hbm.at[:, tiles], sems.at[3])
    send_top.start()
    half = out.at[pl.ds(0, per_dev * TILES)]
    pltpu.make_async_copy(half, half, sems.at[2]).wait()
    send_top.wait()


def pack(rows, owner_list, size, cap, per_dev):
    return pl.pallas_call(
        functools.partial(pack_kernel, size, cap, per_dev),
        out_shape=jax.ShapeDtypeStruct((size, TILES * cap + 1, 1, LANES), jnp.float32),
        in_specs=[pl.BlockSpec(memory_space=pltpu.HBM)] * 2,
        out_specs=pl.BlockSpec(memory_space=pltpu.HBM),
        scratch_shapes=[
            pltpu.SMEM(owner_list.shape, jnp.int32),
            pltpu.VMEM(rows.shape, jnp.float32),
            pltpu.VMEM((rows.shape[0], LANES), jnp.float32),
            pltpu.VMEM((size * TILES * cap, 1, LANES), jnp.float32),
            pltpu.VMEM((size, 1, LANES), jnp.float32),
            pltpu.SMEM((size,), jnp.int32),
            pltpu.SMEM((size * cap,), jnp.int32),
            pltpu.SemaphoreType.DMA((5,)),
        ],
        compiler_params=params(62),
        cost_estimate=cost(1_000_000, 3_000_000),
        name="pack",
    )(owner_list, rows)


def turned_round():
    return lax.axis_index("gx") % 2


def place_of(plane):
    return jnp.where(turned_round() == 0, plane, BLOCK - 1 - plane)


def sign_of_x():
    return jnp.where(turned_round() == 0, 1.0, -1.0).astype(jnp.float32)


def from_far(far_side, size):
    pairs = [(i, (i - 1 if i % 2 == 0 else i + 1) % size) for i in range(size)]
    return lax.ppermute(far_side, "gx", pairs)


def from_near(near_side, size):
    return lax.ppermute(near_side, "gx", [(i, i ^ 1) for i in range(size)])


HALO = (FIELDS, 3, ROWS, LANES)


def arrival_spots(owner_list, slot_list, own, per_dev, size, cap):
    owners = owner_list.reshape(size, per_dev)
    slots = slot_list.reshape(size, per_dev)
    mine = owners == own
    spot = jnp.arange(per_dev, dtype=jnp.int32)
    earlier = spot[None, :] < spot[:, None]
    rank = jnp.sum((mine[:, None, :] & earlier[None]).astype(jnp.int32), axis=2)
    row = jnp.arange(size, dtype=jnp.int32)[:, None] * (TILES * cap + 1) + rank
    key = jnp.where(mine, slots, -1)
    hit = key.reshape(1, -1) == spot[:, None]
    return jnp.max(jnp.where(hit, row.reshape(1, -1), 0), axis=1)


def exchanged_bits(rows, group):
    rows = list(rows)
    for bit in range(4):
        step = 1 << bit
        low = (group & step) == 0
        for index in range(16):
            if index & step:
                continue
            first, second = rows[index], rows[index | step]
            rows[index] = jnp.where(low, first, pltpu.roll(second, 8 * step, 1))
            rows[index | step] = jnp.where(low, pltpu.roll(first, LANES - 8 * step, 1), second)
    return rows


def unpack_kernel(size, cap, table, come, state, far_side, near_side, speed, scratch):
    message = TILES * cap + 1
    best = come[message - 1]
    for source in range(1, size):
        best = jnp.maximum(best, come[(source + 1) * message - 1])
    speed[...] = jnp.broadcast_to(best, speed.shape)
    group = lax.broadcasted_iota(jnp.int32, (8, LANES), 1) // BLOCK
    even = lax.broadcasted_iota(jnp.int32, (8, LANES), 0) % 2 == 0
    half = FIELDS * BZ * 8
    places = [place_of(plane) for plane in range(BLOCK)]

    def gather(couple, slot):
        p, q = divmod(slot, BZ)
        first = table[slot]
        for h in range(2):
            for f in range(FIELDS):
                row = couple * half + (f * BZ + q) * 8 + 2 * p + h
                value = come[first + ((2 * couple + h) * FIELDS + f) * cap]
                scratch[row : row + 1, :] = value

    def arrange(couple, f):
        first = couple * half + f * BZ * 8
        moved = exchanged_bits(
            [scratch[first + q * 8 : first + q * 8 + 8, :] for q in range(BZ)], group
        )
        for second in range(2):
            for j in range(4):
                lower = moved[second * BLOCK + j]
                upper = moved[second * BLOCK + j + 4]
                planes = (
                    jnp.where(even, lower, pltpu.roll(upper, 1, 0)),
                    jnp.where(even, pltpu.roll(lower, 7, 0), upper),
                )
                for h in range(2):
                    state[f, places[4 * couple + 2 * h + second], j * 8 : j * 8 + 8, :] = planes[h]

    for slot in range(BY * BZ):
        gather(0, slot)
    for f in range(FIELDS):
        for slot in range(f, BY * BZ, FIELDS):
            gather(1, slot)
        arrange(0, f)
    for f in range(FIELDS):
        arrange(1, f)
    for f in range(FIELDS):
        for place in range(3):
            far_side[f, place] = state[f, place]
            near_side[f, place] = state[f, BLOCK - 3 + place]


def unpack(table, come, size, cap):
    halo = jax.ShapeDtypeStruct(HALO, jnp.float32)
    return pl.pallas_call(
        functools.partial(unpack_kernel, size, cap),
        out_shape=(
            jax.ShapeDtypeStruct((FIELDS, BLOCK, ROWS, LANES), jnp.float32),
            halo,
            halo,
            jax.ShapeDtypeStruct((8, LANES), jnp.float32),
        ),
        in_specs=[SMEM, VMEM],
        out_specs=(VMEM,) * 4,
        scratch_shapes=[pltpu.VMEM((FIELDS * (PAIRS // 2) * BZ * 8, LANES), jnp.float32)],
        compiler_params=params(),
        cost_estimate=cost(5_000_000, 2_000_000),
        name="unpack",
    )(table, come)


def y_up(x):
    return jnp.concatenate([x[8:], pltpu.roll(x[:8], 7, 0)], axis=0)


def y_down(x):
    return jnp.concatenate([pltpu.roll(x[24:], 1, 0), x[:24]], axis=0)


def y_up_two(x):
    return jnp.concatenate([x[16:], pltpu.roll(x[:8], 7, 0), pltpu.roll(x[8:16], 7, 0)], axis=0)


def inverse(x):
    return 1.0 / x


def smoothness(before, after):
    curve = after - before
    middle = 0.5 * (after + before)
    base = curve * curve * (13.0 / 12.0) + smooth_epsilon
    plus = middle + curve
    minus = middle - curve
    left = inverse(base + plus * plus)
    centre = inverse(base + middle * middle)
    right = inverse(base + minus * minus)
    return curve, left * left, centre * centre, right * right


def upwind_term(left, centre, right, jump_before, jump_after):
    right = 3.0 * right
    top = left * (jump_before + jump_before) + right * jump_after
    return top * inverse(left + 6.0 * centre + right)


def periodic_divergence(half_flux, scaled, up, up_two, down):
    plus = half_flux + scaled
    minus = half_flux - scaled

    def side(values):
        after = up(values) - values
        curve, left, centre, right = smoothness(down(after), after)
        above = up(curve)
        return curve, above, left, centre, right, above - curve

    curve, _, left, centre, right, jump = side(plus)
    face = 6.0 * (half_flux + up(half_flux)) - curve
    face = face - upwind_term(down(left), centre, up(right), down(jump), jump)
    _, curve, left, centre, right, jump = side(minus)
    face = face + (upwind_term(up_two(right), up(centre), left, up(jump), jump) - curve)
    return face - down(face)


def ring_divergence(half_flux, scaled):
    count = len(half_flux)

    def up(values):
        return values[1:] + [pltpu.roll(values[0], 7, 0)]

    def down(values):
        return [pltpu.roll(values[-1], 1, 0)] + values[:-1]

    def side(values):
        after = [above - value for above, value in zip(up(values), values)]
        parts = [smoothness(before, step) for before, step in zip(down(after), after)]
        curve, left, centre, right = (list(part) for part in zip(*parts))
        jump = [above - value for above, value in zip(up(curve), curve)]
        return curve, left, centre, right, jump

    curve, left, centre, right, jump = side([a + b for a, b in zip(half_flux, scaled)])
    terms = zip(down(left), centre, up(right), down(jump), jump)
    face = [
        6.0 * (here + above) - bend - upwind_term(*term)
        for here, above, bend, term in zip(half_flux, up(half_flux), curve, terms)
    ]
    curve, left, centre, right, jump = side([a - b for a, b in zip(half_flux, scaled)])
    terms = zip(up(right), centre, down(left), jump, down(jump))
    other = [upwind_term(*term) - bend for bend, term in zip(curve, terms)]
    face = [one + two for one, two in zip(face, up(other))]
    return [here - below for here, below in zip(face, down(face))]


def x_divergence(half_flux, scaled, plus_at, minus_at, centre_at):
    faces = {i: 6.0 * (half_flux[i] + half_flux[i + 1]) for i in centre_at}

    def add(i, value):
        faces[i] = faces[i] + value if i in faces else value

    def side(sign):
        values = {i: half_flux[i] + sign * scaled[i] for i in half_flux}
        steps = {i: values[i + 1] - values[i] for i in values if i + 1 in values}
        return {i: smoothness(steps[i - 1], steps[i]) for i in steps if i - 1 in steps}

    parts = side(1)
    for i in plus_at:
        curve, left, centre, right = zip(parts[i - 1], parts[i], parts[i + 1])
        term = upwind_term(left[0], centre[1], right[2], curve[1] - curve[0], curve[2] - curve[1])
        add(i, -(curve[1] + term))
    parts = side(-1)
    for i in minus_at:
        curve, left, centre, right = zip(parts[i - 1], parts[i], parts[i + 1])
        term = upwind_term(right[2], centre[1], left[0], curve[2] - curve[1], curve[1] - curve[0])
        add(i - 1, term - curve[1])
    total = {}
    for i in range(BLOCK):
        if i in faces:
            total[i] = faces[i]
        if i - 1 in faces:
            total[i] = total[i] - faces[i - 1] if i in total else -faces[i - 1]
    return total


INNER = (range(2, 6), range(2, 6), range(0, 7))
FAR = ((-1, 0, 1), (0, 1), (-1,))
NEAR = ((6, 7), (6, 7, 8), (7,))
EVERY = (range(-1, 8), range(0, 9), range(-1, 8))


def ring_divergence(half_flux, scaled):
    count = len(half_flux)

    def up(values):
        return values[1:] + [pltpu.roll(values[0], 7, 0)]

    def down(values):
        return [pltpu.roll(values[-1], 1, 0)] + values[:-1]

    def side(values):
        after = [above - value for above, value in zip(up(values), values)]
        parts = [smoothness(before, step) for before, step in zip(down(after), after)]
        curve, left, centre, right = (list(part) for part in zip(*parts))
        jump = [above - value for above, value in zip(up(curve), curve)]
        return curve, left, centre, right, jump

    curve, left, centre, right, jump = side([a + b for a, b in zip(half_flux, scaled)])
    terms = zip(down(left), centre, up(right), down(jump), jump)
    face = [
        6.0 * (here + above) - bend - upwind_term(*term)
        for here, above, bend, term in zip(half_flux, up(half_flux), curve, terms)
    ]
    curve, left, centre, right, jump = side([a - b for a, b in zip(half_flux, scaled)])
    terms = zip(up(right), centre, down(left), jump, down(jump))
    other = [upwind_term(*term) - bend for bend, term in zip(curve, terms)]
    face = [one + two for one, two in zip(face, up(other))]
    return [here - below for here, below in zip(face, down(face))]


def open_divergence(half_flux, scaled):
    count = len(half_flux)
    plus = [a + b for a, b in zip(half_flux, scaled)]
    minus = [a - b for a, b in zip(half_flux, scaled)]
    faces = [None] * count

    def side(values):
        steps = [values[i + 1] - values[i] for i in range(count - 1)]
        parts = [None] + [smoothness(steps[i - 1], steps[i]) for i in range(1, count - 1)]
        return parts

    parts = side(plus)
    for i in range(2, count - 3):
        jump_before = parts[i][0] - parts[i - 1][0]
        jump_after = parts[i + 1][0] - parts[i][0]
        faces[i] = 6.0 * (half_flux[i] + half_flux[i + 1]) - parts[i][0] - upwind_term(
            parts[i - 1][1], parts[i][2], parts[i + 1][3], jump_before, jump_after
        )
    parts = side(minus)
    for i in range(3, count - 2):
        jump_before = parts[i][0] - parts[i - 1][0]
        jump_after = parts[i + 1][0] - parts[i][0]
        faces[i - 1] = faces[i - 1] + (
            upwind_term(parts[i + 1][3], parts[i][2], parts[i - 1][1], jump_after, jump_before)
            - parts[i][0]
        )
    return [faces[i] - faces[i - 1] for i in range(3, count - 3)]


def half_velocities(fields):
    density, mom_x, mom_y, mom_z, energy = fields
    over = 0.5 / density
    vel = (mom_x * over, mom_y * over, mom_z * over)
    kinetic = mom_x * vel[0] + mom_y * vel[1] + mom_z * vel[2]
    pressure = (gamma_gas - 1.0) * (energy - kinetic)
    return vel, pressure


def half_flux(fields, field, direction, speed, pressure):
    if field == 0:
        return 0.5 * fields[1 + direction]
    if field == 4:
        return (fields[4] + pressure) * speed
    flux = fields[field] * speed
    return flux + 0.5 * pressure if field == 1 + direction else flux


def plane_kernel(with_inner, *refs):
    *states, speed, out, turned = refs
    half_speed = 0.5 * speed[0:1, :]
    lane = lax.broadcasted_iota(jnp.int32, (LANES, LANES), 1)
    to_turned = (lane % 8) * 16 + lane // 8
    to_plain = (lane % 16) * 8 + lane // 16

    for part in range(2):
        state, first = (states[0], 4 * part) if len(states) == 1 else (states[part], 0)
        for f in range(FIELDS):
            plain = state[f, first : first + 4].reshape(LANES, LANES)
            turned[f] = jnp.take_along_axis(plain, to_turned, axis=1).T
        for place in range(4):
            fields = [state[f, first + place] for f in range(FIELDS)]
            vel, pressure = half_velocities(fields)
            for field in range(FIELDS):
                out[field, part * 4 + place] = periodic_divergence(
                    half_flux(fields, field, 1, vel[1], pressure),
                    half_speed * fields[field],
                    y_up,
                    y_up_two,
                    y_down,
                )
        columns = [
            [turned[f, row : row + 8] for row in range(0, LANES, 8)] for f in range(FIELDS)
        ]
        along = [half_velocities(fields) for fields in zip(*columns)]
        for field in range(FIELDS):
            fluxes = [
                half_flux(fields, field, 2, vel[2], pressure)
                for fields, (vel, pressure) in zip(zip(*columns), along)
            ]
            scaled = [half_speed * value for value in columns[field]]
            total = jnp.concatenate(ring_divergence(fluxes, scaled), axis=0)
            plain = jnp.take_along_axis(total.T, to_plain, axis=1)
            out[field, part * 4 : part * 4 + 4] += plain.reshape(4, ROWS, LANES)

    def group(j, carry):
        rows = pl.ds(pl.multiple_of(j * 8, 8), 8)

        def get(f, place):
            return states[0][f, place, rows, :]

        for field, along_x in across(get, half_speed, range(BLOCK), INNER):
            for place in range(BLOCK):
                out[field, place, rows, :] += along_x[place]
        return carry

    if with_inner:
        lax.fori_loop(0, 4, group, 0)


def along_planes(states, speed, with_inner):
    return pl.pallas_call(
        functools.partial(plane_kernel, with_inner),
        out_shape=jax.ShapeDtypeStruct((FIELDS, BLOCK, ROWS, LANES), jnp.float32),
        in_specs=[VMEM] * (len(states) + 1),
        out_specs=VMEM,
        scratch_shapes=[pltpu.VMEM((FIELDS, LANES, LANES), jnp.float32)],
        compiler_params=params(),
        cost_estimate=cost(20_000_000, 1_000_000),
        name="planes",
    )(*states, speed)


def along_one_field(field, get, speeds, pressures, half_speed, span, parts):
    sign = sign_of_x()
    fluxes, scaled = {}, {}
    for place in span:
        if field == 0:
            flux = (0.5 * sign) * get(1, place)
        elif field == 4:
            flux = (get(4, place) + pressures[place]) * speeds[place]
        else:
            flux = get(field, place) * speeds[place]
            if field == 1:
                flux = flux + (0.5 * sign) * pressures[place]
        fluxes[place] = flux
        scaled[place] = half_speed * get(field, place)
    return x_divergence(fluxes, scaled, *parts)


def across(get, half_speed, span, parts):
    sign = sign_of_x()
    speeds, pressures = {}, {}
    for place in span:
        vel, pressure = half_velocities([get(f, place) for f in range(FIELDS)])
        speeds[place] = sign * vel[0]
        pressures[place] = pressure
    for field in range(FIELDS):
        yield field, along_one_field(field, get, speeds, pressures, half_speed, span, parts)


WITH_HALOS = range(-3, BLOCK + 3)


def with_halos(far, near, inside, rows):
    def get(f, place):
        if place < 0:
            return far[f, -1 - place, rows, :]
        if place >= BLOCK:
            return near[f, BLOCK + 2 - place, rows, :]
        return inside(f, place)

    return get


def first_kernel(is_far, *refs):
    if is_far:
        state, sides, halo, speed, other, middle, side, top = refs
    else:
        state, sides, halo, speed, middle, side, top = refs
    first, parts, span = (0, FAR, range(-3, 4)) if is_far else (4, NEAR, range(4, 11))
    half_speed = 0.5 * speed[0:1, :]
    factor = (courant / 6.0) / speed[0:1, :]

    def group(j, best):
        rows = pl.ds(pl.multiple_of(j * 8, 8), 8)

        def inside(f, place):
            return state[f, place, rows, :]

        get = with_halos(halo, halo, inside, rows)
        for field, along_x in across(get, half_speed, span, parts):
            for k in range(4):
                total = sides[field, first + k, rows, :]
                if first + k in along_x:
                    total = total + along_x[first + k]
                value = get(field, first + k) - factor * total
                middle[field, k, rows, :] = value
                at = k if is_far else k - 1
                if 0 <= at < 3:
                    side[field, at, rows, :] = value
        for k in range(4):
            best = jnp.maximum(best, wave_speed([middle[f, k, rows, :] for f in range(FIELDS)]))
        return best

    start = other[...] if is_far else jnp.zeros((8, LANES), jnp.float32)
    best = lax.fori_loop(0, 4, group, start)
    top[...] = jnp.full((8, LANES), jnp.max(best), jnp.float32) if is_far else best


def first_stage(is_far, *operands):
    return pl.pallas_call(
        functools.partial(first_kernel, is_far),
        out_shape=(
            jax.ShapeDtypeStruct((FIELDS, 4, ROWS, LANES), jnp.float32),
            jax.ShapeDtypeStruct(HALO, jnp.float32),
            jax.ShapeDtypeStruct((8, LANES), jnp.float32),
        ),
        in_specs=[VMEM] * len(operands),
        out_specs=(VMEM,) * 3,
        compiler_params=params(),
        cost_estimate=cost(15_000_000, 2_000_000),
        name="first_far" if is_far else "first_near",
    )(*operands)


def second_kernel(
    state, middle_far, middle_near, sides, far, near, first_speed, speed,
    out_hbm, out, speeds, pressures, sems,
):
    half_speed = 0.5 * speed[0:1, :]
    factor = (courant / 12.0) / first_speed[0:1, :]
    planes = [place_of(place) for place in range(BLOCK)]
    sign = sign_of_x()

    def rows_and_get(j):
        rows = pl.ds(pl.multiple_of(j * 8, 8), 8)

        def inside(f, place):
            return (middle_far, middle_near)[place // 4][f, place % 4, rows, :]

        return rows, with_halos(far, near, inside, rows)

    def primitives(j, carry):
        rows, get = rows_and_get(j)
        for place in WITH_HALOS:
            vel, pressure = half_velocities([get(f, place) for f in range(FIELDS)])
            speeds[place + 3, rows, :] = sign * vel[0]
            pressures[place + 3, rows, :] = pressure
        return carry

    lax.fori_loop(0, 4, primitives, 0)

    def one_field(field, j):
        rows, get = rows_and_get(j)
        along_x = along_one_field(
            field,
            get,
            {place: speeds[place + 3, rows, :] for place in WITH_HALOS},
            {place: pressures[place + 3, rows, :] for place in WITH_HALOS},
            half_speed,
            WITH_HALOS,
            EVERY,
        )
        for place in range(BLOCK):
            total = along_x[place] + sides[field, place, rows, :]
            value = 0.5 * state[field, place, rows, :] + (
                0.5 * get(field, place) - factor * total
            )
            out[field, planes[place], pl.ds(j, 8, stride=4), :] = value

    copies = []
    for field in range(FIELDS):

        def group(j, carry, field=field):
            one_field(field, j)
            return carry

        lax.fori_loop(0, 4, group, 0)
        copies.append(pltpu.make_async_copy(out.at[field], out_hbm.at[field], sems.at[field]))
        copies[-1].start()
    for copy in copies:
        copy.wait()


def second_stage(*operands):
    whole = (FIELDS, BLOCK, ROWS, LANES)
    kept = pltpu.VMEM((BLOCK + 6, ROWS, LANES), jnp.float32)
    return pl.pallas_call(
        second_kernel,
        out_shape=jax.ShapeDtypeStruct(whole, jnp.float32),
        in_specs=[VMEM] * len(operands),
        out_specs=pl.BlockSpec(memory_space=pltpu.HBM),
        scratch_shapes=[
            pltpu.VMEM(whole, jnp.float32),
            kept,
            kept,
            pltpu.SemaphoreType.DMA((FIELDS,)),
        ],
        compiler_params=params(),
        cost_estimate=cost(30_000_000, 3_000_000),
        name="second_stage",
    )(*operands)


def everyone_max(value, axis, size):
    reach = 1
    while reach * 4 < size:
        reach *= 4
    while reach:
        copies = [value]
        for times in range(1, 4):
            turn = reach * times
            if turn < size:
                pairs = [(i, i ^ turn) for i in range(size)]
                copies.append(lax.ppermute(value, axis, pairs))
        value = functools.reduce(jnp.maximum, copies)
        reach //= 4
    return value


def per_device(blocks, owner_list, slot_list):
    size = lax.axis_size("gx")
    own = lax.axis_index("gx")
    per_dev = blocks.shape[0]
    cap = max(2, 2 * per_dev // size)

    parts = pack(tiled_rows(blocks), owner_list, size, cap, per_dev)
    parts, owner_list, slot_list = lax.optimization_barrier((parts, owner_list, slot_list))
    come = lax.all_to_all(parts, "gx", split_axis=0, concat_axis=0, tiled=True)
    table = arrival_spots(owner_list, slot_list, own, per_dev, size, cap)
    state, far_side, near_side, speed = unpack(table, come.reshape(-1, 1, LANES), size, cap)
    far = from_far(far_side, size)
    near = from_near(near_side, size)
    sides = along_planes((state,), speed, True)
    middle_near, near_side, top = first_stage(False, state, sides, near, speed)
    middle_far, far_side, top = first_stage(True, state, sides, far, speed, top)
    far = from_far(far_side, size)
    near = from_near(near_side, size)
    second = everyone_max(top, "gx", size)
    sides = along_planes((middle_far, middle_near), second, False)
    return second_stage(state, middle_far, middle_near, sides, far, near, speed, second)


def solution(mesh):
    return jax.shard_map(
        per_device,
        mesh=mesh,
        in_specs=(P(("runs", "gx"), None, None), P("runs"), P("runs")),
        out_specs=P(None, ("runs", "gx"), None, None),
        check_vma=False,
    )
```

```python
import functools

import jax
import jax.numpy as jnp
from jax import lax
from jax.experimental import pallas as pl
from jax.experimental.pallas import tpu as pltpu
from jax.sharding import PartitionSpec as P

BLOCK = 8
BY = 4
BZ = 16
FIELDS = 5
LANES = 128
ROWS = BY * BLOCK
PAIRS = BLOCK // 2
TILES = PAIRS * FIELDS

gamma_gas = 1.4
courant = 0.25
smooth_epsilon = 1e-06

VMEM = pl.BlockSpec(memory_space=pltpu.VMEM)
SMEM = pl.BlockSpec(memory_space=pltpu.SMEM)


def params(mebibytes=40):
    return pltpu.CompilerParams(vmem_limit_bytes=mebibytes * 1024 * 1024)


def cost(flops, size):
    return pl.CostEstimate(flops=flops, bytes_accessed=size, transcendentals=0)


def wave_speed(fields):
    density, mom_x, mom_y, mom_z, energy = fields
    inverse = 1.0 / density
    vel = (mom_x * inverse, mom_y * inverse, mom_z * inverse)
    kinetic = 0.5 * (mom_x * vel[0] + mom_y * vel[1] + mom_z * vel[2])
    pressure = (gamma_gas - 1.0) * (energy - kinetic)
    sound = jnp.sqrt(gamma_gas * pressure * inverse)
    fastest = jnp.maximum(jnp.maximum(jnp.abs(vel[0]), jnp.abs(vel[1])), jnp.abs(vel[2]))
    return fastest + sound


def tiled_rows(blocks):
    count = blocks.shape[0] // 8
    groups = blocks.reshape(count, 8, FIELDS, PAIRS, LANES).transpose(2, 0, 3, 1, 4)
    return groups.reshape(FIELDS * count * PAIRS * 8, 1, LANES)


def pack_kernel(
    size, cap, per_dev, owner_hbm, rows_hbm, out_hbm, owner, rows, tiled, out, top, count, member, sems
):
    own = lax.axis_index("gx")
    fetch_owner = pltpu.make_async_copy(owner_hbm, owner, sems.at[0])
    fetch_rows = pltpu.make_async_copy(rows_hbm, rows, sems.at[1])
    fetch_tiled = pltpu.make_async_copy(rows_hbm.at[:, 0], tiled, sems.at[4])
    fetch_owner.start()
    fetch_rows.start()
    fetch_tiled.start()

    def clear(dest, carry):
        count[dest] = 0
        return carry

    lax.fori_loop(0, size, clear, 0, unroll=8)
    fetch_owner.wait()

    def note(block, carry):
        dest = owner[own * per_dev + block]
        rank = count[dest]
        count[dest] = rank + 1
        member[dest * cap + rank] = lax.div(block, 8) * (PAIRS * 8) + lax.rem(block, 8)
        return carry

    lax.fori_loop(0, per_dev, note, 0, unroll=8)
    fetch_rows.wait()
    tiles = TILES * cap

    def message(dest, carry):
        @pl.when(count[dest] > 0)
        def _():
            for rank in range(cap):
                first = member[dest * cap + rank]
                for pair in range(PAIRS):
                    for f in range(FIELDS):
                        to = dest * tiles + (pair * FIELDS + f) * cap + rank
                        out[to] = rows[first + f * (per_dev * PAIRS) + pair * 8]
            part = out.at[pl.ds(dest * tiles, tiles)]
            pltpu.make_async_copy(part, out_hbm.at[dest, pl.ds(0, tiles)], sems.at[2]).start()

        return carry

    lax.fori_loop(0, size, message, 0)
    fetch_tiled.wait()
    best = jnp.zeros((8, LANES), jnp.float32)
    step = per_dev * PAIRS
    for first in range(0, step, 8):
        fields = [tiled[f * step + first : f * step + first + 8, :] for f in range(FIELDS)]
        best = jnp.maximum(best, wave_speed(fields))
    most = jnp.full((1, LANES), jnp.max(best), jnp.float32)
    for dest in range(size):
        top[dest] = most
    send_top = pltpu.make_async_copy(top, out_hbm.at[:, tiles], sems.at[3])
    send_top.start()
    half = out.at[pl.ds(0, per_dev * TILES)]
    pltpu.make_async_copy(half, half, sems.at[2]).wait()
    send_top.wait()


def pack(rows, owner_list, size, cap, per_dev):
    return pl.pallas_call(
        functools.partial(pack_kernel, size, cap, per_dev),
        out_shape=jax.ShapeDtypeStruct((size, TILES * cap + 1, 1, LANES), jnp.float32),
        in_specs=[pl.BlockSpec(memory_space=pltpu.HBM)] * 2,
        out_specs=pl.BlockSpec(memory_space=pltpu.HBM),
        scratch_shapes=[
            pltpu.SMEM(owner_list.shape, jnp.int32),
            pltpu.VMEM(rows.shape, jnp.float32),
            pltpu.VMEM((rows.shape[0], LANES), jnp.float32),
            pltpu.VMEM((size * TILES * cap, 1, LANES), jnp.float32),
            pltpu.VMEM((size, 1, LANES), jnp.float32),
            pltpu.SMEM((size,), jnp.int32),
            pltpu.SMEM((size * cap,), jnp.int32),
            pltpu.SemaphoreType.DMA((5,)),
        ],
        compiler_params=params(62),
        cost_estimate=cost(1_000_000, 3_000_000),
        name="pack",
    )(owner_list, rows)


def turned_round():
    return lax.axis_index("gx") % 2


def place_of(plane):
    return jnp.where(turned_round() == 0, plane, BLOCK - 1 - plane)


def sign_of_x():
    return jnp.where(turned_round() == 0, 1.0, -1.0).astype(jnp.float32)


def from_far(far_side, size):
    pairs = [(i, (i - 1 if i % 2 == 0 else i + 1) % size) for i in range(size)]
    return lax.ppermute(far_side, "gx", pairs)


def from_near(near_side, size):
    return lax.ppermute(near_side, "gx", [(i, i ^ 1) for i in range(size)])


HALO = (FIELDS, 3, ROWS, LANES)


def arrival_spots(owner_list, slot_list, own, per_dev, size, cap):
    owners = owner_list.reshape(size, per_dev)
    slots = slot_list.reshape(size, per_dev)
    mine = owners == own
    spot = jnp.arange(per_dev, dtype=jnp.int32)
    earlier = spot[None, :] < spot[:, None]
    rank = jnp.sum((mine[:, None, :] & earlier[None]).astype(jnp.int32), axis=2)
    row = jnp.arange(size, dtype=jnp.int32)[:, None] * (TILES * cap + 1) + rank
    key = jnp.where(mine, slots, -1)
    hit = key.reshape(1, -1) == spot[:, None]
    return jnp.max(jnp.where(hit, row.reshape(1, -1), 0), axis=1)


def exchanged_bits(rows, group):
    rows = list(rows)
    for bit in range(4):
        step = 1 << bit
        low = (group & step) == 0
        for index in range(16):
            if index & step:
                continue
            first, second = rows[index], rows[index | step]
            rows[index] = jnp.where(low, first, pltpu.roll(second, 8 * step, 1))
            rows[index | step] = jnp.where(low, pltpu.roll(first, LANES - 8 * step, 1), second)
    return rows


def unpack_kernel(size, cap, table, come, state, far_side, near_side, speed, scratch):
    message = TILES * cap + 1
    best = come[message - 1]
    for source in range(1, size):
        best = jnp.maximum(best, come[(source + 1) * message - 1])
    speed[...] = jnp.broadcast_to(best, speed.shape)
    group = lax.broadcasted_iota(jnp.int32, (8, LANES), 1) // BLOCK
    even = lax.broadcasted_iota(jnp.int32, (8, LANES), 0) % 2 == 0
    half = FIELDS * BZ * 8
    places = [place_of(plane) for plane in range(BLOCK)]

    def gather(couple, slot):
        p, q = divmod(slot, BZ)
        first = table[slot]
        for h in range(2):
            for f in range(FIELDS):
                row = couple * half + (f * BZ + q) * 8 + 2 * p + h
                value = come[first + ((2 * couple + h) * FIELDS + f) * cap]
                scratch[row : row + 1, :] = value

    def arrange(couple, f):
        first = couple * half + f * BZ * 8
        moved = exchanged_bits(
            [scratch[first + q * 8 : first + q * 8 + 8, :] for q in range(BZ)], group
        )
        for second in range(2):
            for j in range(4):
                lower = moved[second * BLOCK + j]
                upper = moved[second * BLOCK + j + 4]
                planes = (
                    jnp.where(even, lower, pltpu.roll(upper, 1, 0)),
                    jnp.where(even, pltpu.roll(lower, 7, 0), upper),
                )
                for h in range(2):
                    state[f, places[4 * couple + 2 * h + second], j * 8 : j * 8 + 8, :] = planes[h]

    for slot in range(BY * BZ):
        gather(0, slot)
    for f in range(FIELDS):
        for slot in range(f, BY * BZ, FIELDS):
            gather(1, slot)
        arrange(0, f)
    for f in range(FIELDS):
        arrange(1, f)
    for f in range(FIELDS):
        for place in range(3):
            far_side[f, place] = state[f, place]
            near_side[f, place] = state[f, BLOCK - 3 + place]


def unpack(table, come, size, cap):
    halo = jax.ShapeDtypeStruct(HALO, jnp.float32)
    return pl.pallas_call(
        functools.partial(unpack_kernel, size, cap),
        out_shape=(
            jax.ShapeDtypeStruct((FIELDS, BLOCK, ROWS, LANES), jnp.float32),
            halo,
            halo,
            jax.ShapeDtypeStruct((8, LANES), jnp.float32),
        ),
        in_specs=[SMEM, VMEM],
        out_specs=(VMEM,) * 4,
        scratch_shapes=[pltpu.VMEM((FIELDS * (PAIRS // 2) * BZ * 8, LANES), jnp.float32)],
        compiler_params=params(),
        cost_estimate=cost(5_000_000, 2_000_000),
        name="unpack",
    )(table, come)


def y_up(x):
    return jnp.concatenate([x[8:], pltpu.roll(x[:8], 7, 0)], axis=0)


def y_down(x):
    return jnp.concatenate([pltpu.roll(x[24:], 1, 0), x[:24]], axis=0)


def y_up_two(x):
    return jnp.concatenate([x[16:], pltpu.roll(x[:8], 7, 0), pltpu.roll(x[8:16], 7, 0)], axis=0)


def inverse(x):
    return 1.0 / x


def smoothness(before, after):
    curve = after - before
    middle = 0.5 * (after + before)
    base = curve * curve * (13.0 / 12.0) + smooth_epsilon
    plus = middle + curve
    minus = middle - curve
    left = inverse(base + plus * plus)
    centre = inverse(base + middle * middle)
    right = inverse(base + minus * minus)
    return curve, left * left, centre * centre, right * right


def upwind_term(left, centre, right, jump_before, jump_after):
    right = 3.0 * right
    top = left * (jump_before + jump_before) + right * jump_after
    return top * inverse(left + 6.0 * centre + right)


def periodic_divergence(half_flux, scaled, up, up_two, down):
    plus = half_flux + scaled
    minus = half_flux - scaled

    def side(values):
        after = up(values) - values
        curve, left, centre, right = smoothness(down(after), after)
        above = up(curve)
        return curve, above, left, centre, right, above - curve

    curve, _, left, centre, right, jump = side(plus)
    face = 6.0 * (half_flux + up(half_flux)) - curve
    face = face - upwind_term(down(left), centre, up(right), down(jump), jump)
    _, curve, left, centre, right, jump = side(minus)
    face = face + (upwind_term(up_two(right), up(centre), left, up(jump), jump) - curve)
    return face - down(face)


def ring_divergence(half_flux, scaled):
    count = len(half_flux)

    def up(values):
        return values[1:] + [pltpu.roll(values[0], 7, 0)]

    def down(values):
        return [pltpu.roll(values[-1], 1, 0)] + values[:-1]

    def side(values):
        after = [above - value for above, value in zip(up(values), values)]
        parts = [smoothness(before, step) for before, step in zip(down(after), after)]
        curve, left, centre, right = (list(part) for part in zip(*parts))
        jump = [above - value for above, value in zip(up(curve), curve)]
        return curve, left, centre, right, jump

    curve, left, centre, right, jump = side([a + b for a, b in zip(half_flux, scaled)])
    terms = zip(down(left), centre, up(right), down(jump), jump)
    face = [
        6.0 * (here + above) - bend - upwind_term(*term)
        for here, above, bend, term in zip(half_flux, up(half_flux), curve, terms)
    ]
    curve, left, centre, right, jump = side([a - b for a, b in zip(half_flux, scaled)])
    terms = zip(up(right), centre, down(left), jump, down(jump))
    other = [upwind_term(*term) - bend for bend, term in zip(curve, terms)]
    face = [one + two for one, two in zip(face, up(other))]
    return [here - below for here, below in zip(face, down(face))]


def x_divergence(half_flux, scaled, plus_at, minus_at, centre_at):
    faces = {i: 6.0 * (half_flux[i] + half_flux[i + 1]) for i in centre_at}

    def add(i, value):
        faces[i] = faces[i] + value if i in faces else value

    def side(sign):
        values = {i: half_flux[i] + sign * scaled[i] for i in half_flux}
        steps = {i: values[i + 1] - values[i] for i in values if i + 1 in values}
        return {i: smoothness(steps[i - 1], steps[i]) for i in steps if i - 1 in steps}

    parts = side(1)
    for i in plus_at:
        curve, left, centre, right = zip(parts[i - 1], parts[i], parts[i + 1])
        term = upwind_term(left[0], centre[1], right[2], curve[1] - curve[0], curve[2] - curve[1])
        add(i, -(curve[1] + term))
    parts = side(-1)
    for i in minus_at:
        curve, left, centre, right = zip(parts[i - 1], parts[i], parts[i + 1])
        term = upwind_term(right[2], centre[1], left[0], curve[2] - curve[1], curve[1] - curve[0])
        add(i - 1, term - curve[1])
    total = {}
    for i in range(BLOCK):
        if i in faces:
            total[i] = faces[i]
        if i - 1 in faces:
            total[i] = total[i] - faces[i - 1] if i in total else -faces[i - 1]
    return total


INNER = (range(2, 6), range(2, 6), range(0, 7))
FAR = ((-1, 0, 1), (0, 1), (-1,))
NEAR = ((6, 7), (6, 7, 8), (7,))
EVERY = (range(-1, 8), range(0, 9), range(-1, 8))


def ring_divergence(half_flux, scaled):
    count = len(half_flux)

    def up(values):
        return values[1:] + [pltpu.roll(values[0], 7, 0)]

    def down(values):
        return [pltpu.roll(values[-1], 1, 0)] + values[:-1]

    def side(values):
        after = [above - value for above, value in zip(up(values), values)]
        parts = [smoothness(before, step) for before, step in zip(down(after), after)]
        curve, left, centre, right = (list(part) for part in zip(*parts))
        jump = [above - value for above, value in zip(up(curve), curve)]
        return curve, left, centre, right, jump

    curve, left, centre, right, jump = side([a + b for a, b in zip(half_flux, scaled)])
    terms = zip(down(left), centre, up(right), down(jump), jump)
    face = [
        6.0 * (here + above) - bend - upwind_term(*term)
        for here, above, bend, term in zip(half_flux, up(half_flux), curve, terms)
    ]
    curve, left, centre, right, jump = side([a - b for a, b in zip(half_flux, scaled)])
    terms = zip(up(right), centre, down(left), jump, down(jump))
    other = [upwind_term(*term) - bend for bend, term in zip(curve, terms)]
    face = [one + two for one, two in zip(face, up(other))]
    return [here - below for here, below in zip(face, down(face))]


def open_divergence(half_flux, scaled):
    count = len(half_flux)
    plus = [a + b for a, b in zip(half_flux, scaled)]
    minus = [a - b for a, b in zip(half_flux, scaled)]
    faces = [None] * count

    def side(values):
        steps = [values[i + 1] - values[i] for i in range(count - 1)]
        parts = [None] + [smoothness(steps[i - 1], steps[i]) for i in range(1, count - 1)]
        return parts

    parts = side(plus)
    for i in range(2, count - 3):
        jump_before = parts[i][0] - parts[i - 1][0]
        jump_after = parts[i + 1][0] - parts[i][0]
        faces[i] = 6.0 * (half_flux[i] + half_flux[i + 1]) - parts[i][0] - upwind_term(
            parts[i - 1][1], parts[i][2], parts[i + 1][3], jump_before, jump_after
        )
    parts = side(minus)
    for i in range(3, count - 2):
        jump_before = parts[i][0] - parts[i - 1][0]
        jump_after = parts[i + 1][0] - parts[i][0]
        faces[i - 1] = faces[i - 1] + (
            upwind_term(parts[i + 1][3], parts[i][2], parts[i - 1][1], jump_after, jump_before)
            - parts[i][0]
        )
    return [faces[i] - faces[i - 1] for i in range(3, count - 3)]


def half_velocities(fields):
    density, mom_x, mom_y, mom_z, energy = fields
    over = 0.5 / density
    vel = (mom_x * over, mom_y * over, mom_z * over)
    kinetic = mom_x * vel[0] + mom_y * vel[1] + mom_z * vel[2]
    pressure = (gamma_gas - 1.0) * (energy - kinetic)
    return vel, pressure


def half_flux(fields, field, direction, speed, pressure):
    if field == 0:
        return 0.5 * fields[1 + direction]
    if field == 4:
        return (fields[4] + pressure) * speed
    flux = fields[field] * speed
    return flux + 0.5 * pressure if field == 1 + direction else flux


def plane_kernel(with_inner, *refs):
    *states, speed, out, turned = refs
    half_speed = 0.5 * speed[0:1, :]
    lane = lax.broadcasted_iota(jnp.int32, (LANES, LANES), 1)
    to_turned = (lane % 8) * 16 + lane // 8
    to_plain = (lane % 16) * 8 + lane // 16

    for part in range(2):
        state, first = (states[0], 4 * part) if len(states) == 1 else (states[part], 0)
        for f in range(FIELDS):
            plain = state[f, first : first + 4].reshape(LANES, LANES)
            turned[f] = jnp.take_along_axis(plain, to_turned, axis=1).T
        for place in range(4):
            fields = [state[f, first + place] for f in range(FIELDS)]
            vel, pressure = half_velocities(fields)
            for field in range(FIELDS):
                out[field, part * 4 + place] = periodic_divergence(
                    half_flux(fields, field, 1, vel[1], pressure),
                    half_speed * fields[field],
                    y_up,
                    y_up_two,
                    y_down,
                )
        columns = [
            [turned[f, row : row + 8] for row in range(0, LANES, 8)] for f in range(FIELDS)
        ]
        along = [half_velocities(fields) for fields in zip(*columns)]
        for field in range(FIELDS):
            fluxes = [
                half_flux(fields, field, 2, vel[2], pressure)
                for fields, (vel, pressure) in zip(zip(*columns), along)
            ]
            scaled = [half_speed * value for value in columns[field]]
            total = jnp.concatenate(ring_divergence(fluxes, scaled), axis=0)
            plain = jnp.take_along_axis(total.T, to_plain, axis=1)
            out[field, part * 4 : part * 4 + 4] += plain.reshape(4, ROWS, LANES)

    def group(j, carry):
        rows = pl.ds(pl.multiple_of(j * 8, 8), 8)

        def get(f, place):
            return states[0][f, place, rows, :]

        for field, along_x in across(get, half_speed, range(BLOCK), INNER):
            for place in range(BLOCK):
                out[field, place, rows, :] += along_x[place]
        return carry

    if with_inner:
        lax.fori_loop(0, 4, group, 0)


def along_planes(states, speed, with_inner):
    return pl.pallas_call(
        functools.partial(plane_kernel, with_inner),
        out_shape=jax.ShapeDtypeStruct((FIELDS, BLOCK, ROWS, LANES), jnp.float32),
        in_specs=[VMEM] * (len(states) + 1),
        out_specs=VMEM,
        scratch_shapes=[pltpu.VMEM((FIELDS, LANES, LANES), jnp.float32)],
        compiler_params=params(),
        cost_estimate=cost(20_000_000, 1_000_000),
        name="planes",
    )(*states, speed)


def across(get, half_speed, span, parts):
    sign = sign_of_x()
    speeds, pressures = {}, {}
    for place in span:
        vel, pressure = half_velocities([get(f, place) for f in range(FIELDS)])
        speeds[place] = sign * vel[0]
        pressures[place] = pressure
    for field in range(FIELDS):
        fluxes, scaled = {}, {}
        for place in span:
            if field == 0:
                flux = (0.5 * sign) * get(1, place)
            elif field == 4:
                flux = (get(4, place) + pressures[place]) * speeds[place]
            else:
                flux = get(field, place) * speeds[place]
                if field == 1:
                    flux = flux + (0.5 * sign) * pressures[place]
            fluxes[place] = flux
            scaled[place] = half_speed * get(field, place)
        yield field, x_divergence(fluxes, scaled, *parts)


WITH_HALOS = range(-3, BLOCK + 3)


def with_halos(far, near, inside, rows):
    def get(f, place):
        if place < 0:
            return far[f, -1 - place, rows, :]
        if place >= BLOCK:
            return near[f, BLOCK + 2 - place, rows, :]
        return inside(f, place)

    return get


def first_kernel(is_far, *refs):
    if is_far:
        state, sides, halo, speed, other, middle, side, top = refs
    else:
        state, sides, halo, speed, middle, side, top = refs
    first, parts, span = (0, FAR, range(-3, 4)) if is_far else (4, NEAR, range(4, 11))
    half_speed = 0.5 * speed[0:1, :]
    factor = (courant / 6.0) / speed[0:1, :]

    def group(j, best):
        rows = pl.ds(pl.multiple_of(j * 8, 8), 8)

        def inside(f, place):
            return state[f, place, rows, :]

        get = with_halos(halo, halo, inside, rows)
        for field, along_x in across(get, half_speed, span, parts):
            for k in range(4):
                total = sides[field, first + k, rows, :]
                if first + k in along_x:
                    total = total + along_x[first + k]
                value = get(field, first + k) - factor * total
                middle[field, k, rows, :] = value
                at = k if is_far else k - 1
                if 0 <= at < 3:
                    side[field, at, rows, :] = value
        for k in range(4):
            best = jnp.maximum(best, wave_speed([middle[f, k, rows, :] for f in range(FIELDS)]))
        return best

    start = other[...] if is_far else jnp.zeros((8, LANES), jnp.float32)
    best = lax.fori_loop(0, 4, group, start)
    top[...] = jnp.full((8, LANES), jnp.max(best), jnp.float32) if is_far else best


def first_stage(is_far, *operands):
    return pl.pallas_call(
        functools.partial(first_kernel, is_far),
        out_shape=(
            jax.ShapeDtypeStruct((FIELDS, 4, ROWS, LANES), jnp.float32),
            jax.ShapeDtypeStruct(HALO, jnp.float32),
            jax.ShapeDtypeStruct((8, LANES), jnp.float32),
        ),
        in_specs=[VMEM] * len(operands),
        out_specs=(VMEM,) * 3,
        compiler_params=params(),
        cost_estimate=cost(15_000_000, 2_000_000),
        name="first_far" if is_far else "first_near",
    )(*operands)


def second_kernel(state, middle_far, middle_near, sides, far, near, first_speed, speed, out):
    half_speed = 0.5 * speed[0:1, :]
    factor = (courant / 12.0) / first_speed[0:1, :]
    planes = [place_of(place) for place in range(BLOCK)]

    def group(j, carry):
        rows = pl.ds(pl.multiple_of(j * 8, 8), 8)
        spread = pl.ds(j, 8, stride=4)

        def inside(f, place):
            return (middle_far, middle_near)[place // 4][f, place % 4, rows, :]

        get = with_halos(far, near, inside, rows)
        for field, along_x in across(get, half_speed, WITH_HALOS, EVERY):
            for place in range(BLOCK):
                total = along_x[place] + sides[field, place, rows, :]
                value = 0.5 * state[field, place, rows, :] + (
                    0.5 * get(field, place) - factor * total
                )
                out[field, planes[place], spread, :] = value
        return carry

    lax.fori_loop(0, 4, group, 0)


def second_stage(*operands):
    return pl.pallas_call(
        second_kernel,
        out_shape=jax.ShapeDtypeStruct((FIELDS, BLOCK, ROWS, LANES), jnp.float32),
        in_specs=[VMEM] * len(operands),
        out_specs=VMEM,
        compiler_params=params(),
        cost_estimate=cost(30_000_000, 3_000_000),
        name="second_stage",
    )(*operands)


def everyone_max(value, axis, size):
    reach = 1
    while reach * 4 < size:
        reach *= 4
    while reach:
        copies = [value]
        for times in range(1, 4):
            turn = reach * times
            if turn < size:
                turn += 2 if times == 1 and reach > 1 else 0
                pairs = [(i, i ^ turn) for i in range(size)]
                copies.append(lax.ppermute(value, axis, pairs))
        value = functools.reduce(jnp.maximum, copies)
        reach //= 4
    return value


def per_device(blocks, owner_list, slot_list):
    size = lax.axis_size("gx")
    own = lax.axis_index("gx")
    per_dev = blocks.shape[0]
    cap = max(2, 2 * per_dev // size)

    parts = pack(tiled_rows(blocks), owner_list, size, cap, per_dev)
    parts, owner_list, slot_list = lax.optimization_barrier((parts, owner_list, slot_list))
    come = lax.all_to_all(parts, "gx", split_axis=0, concat_axis=0, tiled=True)
    table = arrival_spots(owner_list, slot_list, own, per_dev, size, cap)
    state, far_side, near_side, speed = unpack(table, come.reshape(-1, 1, LANES), size, cap)
    far = from_far(far_side, size)
    near = from_near(near_side, size)
    sides = along_planes((state,), speed, True)
    middle_near, near_side, top = first_stage(False, state, sides, near, speed)
    middle_far, far_side, top = first_stage(True, state, sides, far, speed, top)
    far = from_far(far_side, size)
    near = from_near(near_side, size)
    second = everyone_max(top, "gx", size)
    sides = along_planes((middle_far, middle_near), second, False)
    return second_stage(state, middle_far, middle_near, sides, far, near, speed, second)


def solution(mesh):
    return jax.shard_map(
        per_device,
        mesh=mesh,
        in_specs=(P(("runs", "gx"), None, None), P("runs"), P("runs")),
        out_specs=P(None, ("runs", "gx"), None, None),
        check_vma=False,
    )
```

```python
import functools

import jax
import jax.numpy as jnp
from jax import lax
from jax.experimental import pallas as pl
from jax.experimental.pallas import tpu as pltpu
from jax.sharding import PartitionSpec as P

BLOCK = 8
BY = 4
BZ = 16
FIELDS = 5
LANES = 128
ROWS = BY * BLOCK
PAIRS = BLOCK // 2
TILES = PAIRS * FIELDS

gamma_gas = 1.4
courant = 0.25
smooth_epsilon = 1e-06

VMEM = pl.BlockSpec(memory_space=pltpu.VMEM)
SMEM = pl.BlockSpec(memory_space=pltpu.SMEM)


def params(mebibytes=40):
    return pltpu.CompilerParams(vmem_limit_bytes=mebibytes * 1024 * 1024)


def cost(flops, size):
    return pl.CostEstimate(flops=flops, bytes_accessed=size, transcendentals=0)


def wave_speed(fields):
    density, mom_x, mom_y, mom_z, energy = fields
    inverse = 1.0 / density
    vel = (mom_x * inverse, mom_y * inverse, mom_z * inverse)
    kinetic = 0.5 * (mom_x * vel[0] + mom_y * vel[1] + mom_z * vel[2])
    pressure = (gamma_gas - 1.0) * (energy - kinetic)
    sound = jnp.sqrt(gamma_gas * pressure * inverse)
    fastest = jnp.maximum(jnp.maximum(jnp.abs(vel[0]), jnp.abs(vel[1])), jnp.abs(vel[2]))
    return fastest + sound


def tiled_rows(blocks):
    count = blocks.shape[0] // 8
    groups = blocks.reshape(count, 8, FIELDS, PAIRS, LANES).transpose(2, 0, 3, 1, 4)
    return groups.reshape(FIELDS * count * PAIRS * 8, 1, LANES)


def pack_kernel(
    size, cap, per_dev, owner_hbm, rows_hbm, out_hbm, owner, rows, tiled, out, top, count, member, sems
):
    own = lax.axis_index("gx")
    fetch_owner = pltpu.make_async_copy(owner_hbm, owner, sems.at[0])
    fetch_rows = pltpu.make_async_copy(rows_hbm, rows, sems.at[1])
    fetch_tiled = pltpu.make_async_copy(rows_hbm.at[:, 0], tiled, sems.at[4])
    fetch_owner.start()
    fetch_rows.start()
    fetch_tiled.start()

    def clear(dest, carry):
        count[dest] = 0
        return carry

    lax.fori_loop(0, size, clear, 0, unroll=8)
    fetch_owner.wait()

    def note(block, carry):
        dest = owner[own * per_dev + block]
        rank = count[dest]
        count[dest] = rank + 1
        member[dest * cap + rank] = lax.div(block, 8) * (PAIRS * 8) + lax.rem(block, 8)
        return carry

    lax.fori_loop(0, per_dev, note, 0, unroll=8)
    fetch_rows.wait()
    tiles = TILES * cap

    def message(dest, carry):
        @pl.when(count[dest] > 0)
        def _():
            for rank in range(cap):
                first = member[dest * cap + rank]
                for pair in range(PAIRS):
                    for f in range(FIELDS):
                        to = dest * tiles + (pair * FIELDS + f) * cap + rank
                        out[to] = rows[first + f * (per_dev * PAIRS) + pair * 8]
            part = out.at[pl.ds(dest * tiles, tiles)]
            pltpu.make_async_copy(part, out_hbm.at[dest, pl.ds(0, tiles)], sems.at[2]).start()

        return carry

    lax.fori_loop(0, size, message, 0)
    fetch_tiled.wait()
    best = jnp.zeros((8, LANES), jnp.float32)
    step = per_dev * PAIRS
    for first in range(0, step, 8):
        fields = [tiled[f * step + first : f * step + first + 8, :] for f in range(FIELDS)]
        best = jnp.maximum(best, wave_speed(fields))
    most = jnp.full((1, LANES), jnp.max(best), jnp.float32)
    for dest in range(size):
        top[dest] = most
    send_top = pltpu.make_async_copy(top, out_hbm.at[:, tiles], sems.at[3])
    send_top.start()
    half = out.at[pl.ds(0, per_dev * TILES)]
    pltpu.make_async_copy(half, half, sems.at[2]).wait()
    send_top.wait()


def pack(rows, owner_list, size, cap, per_dev):
    return pl.pallas_call(
        functools.partial(pack_kernel, size, cap, per_dev),
        out_shape=jax.ShapeDtypeStruct((size, TILES * cap + 1, 1, LANES), jnp.float32),
        in_specs=[pl.BlockSpec(memory_space=pltpu.HBM)] * 2,
        out_specs=pl.BlockSpec(memory_space=pltpu.HBM),
        scratch_shapes=[
            pltpu.SMEM(owner_list.shape, jnp.int32),
            pltpu.VMEM(rows.shape, jnp.float32),
            pltpu.VMEM((rows.shape[0], LANES), jnp.float32),
            pltpu.VMEM((size * TILES * cap, 1, LANES), jnp.float32),
            pltpu.VMEM((size, 1, LANES), jnp.float32),
            pltpu.SMEM((size,), jnp.int32),
            pltpu.SMEM((size * cap,), jnp.int32),
            pltpu.SemaphoreType.DMA((5,)),
        ],
        compiler_params=params(62),
        cost_estimate=cost(1_000_000, 3_000_000),
        name="pack",
    )(owner_list, rows)


def turned_round():
    return lax.axis_index("gx") % 2


def place_of(plane):
    return jnp.where(turned_round() == 0, plane, BLOCK - 1 - plane)


def sign_of_x():
    return jnp.where(turned_round() == 0, 1.0, -1.0).astype(jnp.float32)


def from_far(far_side, size):
    pairs = [(i, (i - 1 if i % 2 == 0 else i + 1) % size) for i in range(size)]
    return lax.ppermute(far_side, "gx", pairs)


def from_near(near_side, size):
    return lax.ppermute(near_side, "gx", [(i, i ^ 1) for i in range(size)])


HALO = (FIELDS, 3, ROWS, LANES)


def arrival_spots(owner_list, slot_list, own, per_dev, size, cap):
    owners = owner_list.reshape(size, per_dev)
    slots = slot_list.reshape(size, per_dev)
    mine = owners == own
    spot = jnp.arange(per_dev, dtype=jnp.int32)
    earlier = spot[None, :] < spot[:, None]
    rank = jnp.sum((mine[:, None, :] & earlier[None]).astype(jnp.int32), axis=2)
    row = jnp.arange(size, dtype=jnp.int32)[:, None] * (TILES * cap + 1) + rank
    key = jnp.where(mine, slots, -1)
    hit = key.reshape(1, -1) == spot[:, None]
    return jnp.max(jnp.where(hit, row.reshape(1, -1), 0), axis=1)


def exchanged_bits(rows, group):
    rows = list(rows)
    for bit in range(4):
        step = 1 << bit
        low = (group & step) == 0
        for index in range(16):
            if index & step:
                continue
            first, second = rows[index], rows[index | step]
            rows[index] = jnp.where(low, first, pltpu.roll(second, 8 * step, 1))
            rows[index | step] = jnp.where(low, pltpu.roll(first, LANES - 8 * step, 1), second)
    return rows


def unpack_kernel(size, cap, table, come, state, far_side, near_side, speed, scratch):
    message = TILES * cap + 1
    best = come[message - 1]
    for source in range(1, size):
        best = jnp.maximum(best, come[(source + 1) * message - 1])
    speed[...] = jnp.broadcast_to(best, speed.shape)
    group = lax.broadcasted_iota(jnp.int32, (8, LANES), 1) // BLOCK
    even = lax.broadcasted_iota(jnp.int32, (8, LANES), 0) % 2 == 0
    half = FIELDS * BZ * 8
    places = [place_of(plane) for plane in range(BLOCK)]

    def gather(couple, slot):
        p, q = divmod(slot, BZ)
        first = table[slot]
        for h in range(2):
            for f in range(FIELDS):
                row = couple * half + (f * BZ + q) * 8 + 2 * p + h
                value = come[first + ((2 * couple + h) * FIELDS + f) * cap]
                scratch[row : row + 1, :] = value

    def arrange(couple, f):
        first = couple * half + f * BZ * 8
        moved = exchanged_bits(
            [scratch[first + q * 8 : first + q * 8 + 8, :] for q in range(BZ)], group
        )
        for second in range(2):
            for j in range(4):
                lower = moved[second * BLOCK + j]
                upper = moved[second * BLOCK + j + 4]
                planes = (
                    jnp.where(even, lower, pltpu.roll(upper, 1, 0)),
                    jnp.where(even, pltpu.roll(lower, 7, 0), upper),
                )
                for h in range(2):
                    state[f, places[4 * couple + 2 * h + second], j * 8 : j * 8 + 8, :] = planes[h]

    for slot in range(BY * BZ):
        gather(0, slot)
    for f in range(FIELDS):
        for slot in range(f, BY * BZ, FIELDS):
            gather(1, slot)
        arrange(0, f)
    for f in range(FIELDS):
        arrange(1, f)
    for f in range(FIELDS):
        for place in range(3):
            far_side[f, place] = state[f, place]
            near_side[f, place] = state[f, BLOCK - 3 + place]


def unpack(table, come, size, cap):
    halo = jax.ShapeDtypeStruct(HALO, jnp.float32)
    return pl.pallas_call(
        functools.partial(unpack_kernel, size, cap),
        out_shape=(
            jax.ShapeDtypeStruct((FIELDS, BLOCK, ROWS, LANES), jnp.float32),
            halo,
            halo,
            jax.ShapeDtypeStruct((8, LANES), jnp.float32),
        ),
        in_specs=[SMEM, VMEM],
        out_specs=(VMEM,) * 4,
        scratch_shapes=[pltpu.VMEM((FIELDS * (PAIRS // 2) * BZ * 8, LANES), jnp.float32)],
        compiler_params=params(),
        cost_estimate=cost(5_000_000, 2_000_000),
        name="unpack",
    )(table, come)


def y_up(x):
    return jnp.concatenate([x[8:], pltpu.roll(x[:8], 7, 0)], axis=0)


def y_down(x):
    return jnp.concatenate([pltpu.roll(x[24:], 1, 0), x[:24]], axis=0)


def y_up_two(x):
    return jnp.concatenate([x[16:], pltpu.roll(x[:8], 7, 0), pltpu.roll(x[8:16], 7, 0)], axis=0)


def inverse(x):
    return 1.0 / x


def smoothness(before, after):
    curve = after - before
    middle = 0.5 * (after + before)
    base = curve * curve * (13.0 / 12.0) + smooth_epsilon
    plus = middle + curve
    minus = middle - curve
    left = inverse(base + plus * plus)
    centre = inverse(base + middle * middle)
    right = inverse(base + minus * minus)
    return curve, left * left, centre * centre, right * right


def upwind_term(left, centre, right, jump_before, jump_after):
    right = 3.0 * right
    top = left * (jump_before + jump_before) + right * jump_after
    return top * inverse(left + 6.0 * centre + right)


def periodic_divergence(half_flux, scaled, up, up_two, down):
    plus = half_flux + scaled
    minus = half_flux - scaled

    def side(values):
        after = up(values) - values
        curve, left, centre, right = smoothness(down(after), after)
        above = up(curve)
        return curve, above, left, centre, right, above - curve

    curve, _, left, centre, right, jump = side(plus)
    face = 6.0 * (half_flux + up(half_flux)) - curve
    face = face - upwind_term(down(left), centre, up(right), down(jump), jump)
    _, curve, left, centre, right, jump = side(minus)
    face = face + (upwind_term(up_two(right), up(centre), left, up(jump), jump) - curve)
    return face - down(face)


def ring_divergence(half_flux, scaled):
    count = len(half_flux)

    def up(values):
        return values[1:] + [pltpu.roll(values[0], 7, 0)]

    def down(values):
        return [pltpu.roll(values[-1], 1, 0)] + values[:-1]

    def side(values):
        after = [above - value for above, value in zip(up(values), values)]
        parts = [smoothness(before, step) for before, step in zip(down(after), after)]
        curve, left, centre, right = (list(part) for part in zip(*parts))
        jump = [above - value for above, value in zip(up(curve), curve)]
        return curve, left, centre, right, jump

    curve, left, centre, right, jump = side([a + b for a, b in zip(half_flux, scaled)])
    terms = zip(down(left), centre, up(right), down(jump), jump)
    face = [
        6.0 * (here + above) - bend - upwind_term(*term)
        for here, above, bend, term in zip(half_flux, up(half_flux), curve, terms)
    ]
    curve, left, centre, right, jump = side([a - b for a, b in zip(half_flux, scaled)])
    terms = zip(up(right), centre, down(left), jump, down(jump))
    other = [upwind_term(*term) - bend for bend, term in zip(curve, terms)]
    face = [one + two for one, two in zip(face, up(other))]
    return [here - below for here, below in zip(face, down(face))]


def x_divergence(half_flux, scaled, plus_at, minus_at, centre_at):
    faces = {i: 6.0 * (half_flux[i] + half_flux[i + 1]) for i in centre_at}

    def add(i, value):
        faces[i] = faces[i] + value if i in faces else value

    def side(sign):
        values = {i: half_flux[i] + sign * scaled[i] for i in half_flux}
        steps = {i: values[i + 1] - values[i] for i in values if i + 1 in values}
        return {i: smoothness(steps[i - 1], steps[i]) for i in steps if i - 1 in steps}

    parts = side(1)
    for i in plus_at:
        curve, left, centre, right = zip(parts[i - 1], parts[i], parts[i + 1])
        term = upwind_term(left[0], centre[1], right[2], curve[1] - curve[0], curve[2] - curve[1])
        add(i, -(curve[1] + term))
    parts = side(-1)
    for i in minus_at:
        curve, left, centre, right = zip(parts[i - 1], parts[i], parts[i + 1])
        term = upwind_term(right[2], centre[1], left[0], curve[2] - curve[1], curve[1] - curve[0])
        add(i - 1, term - curve[1])
    total = {}
    for i in range(BLOCK):
        if i in faces:
            total[i] = faces[i]
        if i - 1 in faces:
            total[i] = total[i] - faces[i - 1] if i in total else -faces[i - 1]
    return total


INNER = (range(2, 6), range(2, 6), range(0, 7))
FAR = ((-1, 0, 1), (0, 1), (-1,))
NEAR = ((6, 7), (6, 7, 8), (7,))
EVERY = (range(-1, 8), range(0, 9), range(-1, 8))


def ring_divergence(half_flux, scaled):
    count = len(half_flux)

    def up(values):
        return values[1:] + [pltpu.roll(values[0], 7, 0)]

    def down(values):
        return [pltpu.roll(values[-1], 1, 0)] + values[:-1]

    def side(values):
        after = [above - value for above, value in zip(up(values), values)]
        parts = [smoothness(before, step) for before, step in zip(down(after), after)]
        curve, left, centre, right = (list(part) for part in zip(*parts))
        jump = [above - value for above, value in zip(up(curve), curve)]
        return curve, left, centre, right, jump

    curve, left, centre, right, jump = side([a + b for a, b in zip(half_flux, scaled)])
    terms = zip(down(left), centre, up(right), down(jump), jump)
    face = [
        6.0 * (here + above) - bend - upwind_term(*term)
        for here, above, bend, term in zip(half_flux, up(half_flux), curve, terms)
    ]
    curve, left, centre, right, jump = side([a - b for a, b in zip(half_flux, scaled)])
    terms = zip(up(right), centre, down(left), jump, down(jump))
    other = [upwind_term(*term) - bend for bend, term in zip(curve, terms)]
    face = [one + two for one, two in zip(face, up(other))]
    return [here - below for here, below in zip(face, down(face))]


def open_divergence(half_flux, scaled):
    count = len(half_flux)
    plus = [a + b for a, b in zip(half_flux, scaled)]
    minus = [a - b for a, b in zip(half_flux, scaled)]
    faces = [None] * count

    def side(values):
        steps = [values[i + 1] - values[i] for i in range(count - 1)]
        parts = [None] + [smoothness(steps[i - 1], steps[i]) for i in range(1, count - 1)]
        return parts

    parts = side(plus)
    for i in range(2, count - 3):
        jump_before = parts[i][0] - parts[i - 1][0]
        jump_after = parts[i + 1][0] - parts[i][0]
        faces[i] = 6.0 * (half_flux[i] + half_flux[i + 1]) - parts[i][0] - upwind_term(
            parts[i - 1][1], parts[i][2], parts[i + 1][3], jump_before, jump_after
        )
    parts = side(minus)
    for i in range(3, count - 2):
        jump_before = parts[i][0] - parts[i - 1][0]
        jump_after = parts[i + 1][0] - parts[i][0]
        faces[i - 1] = faces[i - 1] + (
            upwind_term(parts[i + 1][3], parts[i][2], parts[i - 1][1], jump_after, jump_before)
            - parts[i][0]
        )
    return [faces[i] - faces[i - 1] for i in range(3, count - 3)]


def half_velocities(fields):
    density, mom_x, mom_y, mom_z, energy = fields
    over = 0.5 / density
    vel = (mom_x * over, mom_y * over, mom_z * over)
    kinetic = mom_x * vel[0] + mom_y * vel[1] + mom_z * vel[2]
    pressure = (gamma_gas - 1.0) * (energy - kinetic)
    return vel, pressure


def half_flux(fields, field, direction, speed, pressure):
    if field == 0:
        return 0.5 * fields[1 + direction]
    if field == 4:
        return (fields[4] + pressure) * speed
    flux = fields[field] * speed
    return flux + 0.5 * pressure if field == 1 + direction else flux


def plane_kernel(with_inner, *refs):
    *states, speed, out, turned = refs
    half_speed = 0.5 * speed[0:1, :]
    lane = lax.broadcasted_iota(jnp.int32, (LANES, LANES), 1)
    to_turned = (lane % 8) * 16 + lane // 8
    to_plain = (lane % 16) * 8 + lane // 16

    for part in range(2):
        state, first = (states[0], 4 * part) if len(states) == 1 else (states[part], 0)
        for f in range(FIELDS):
            plain = state[f, first : first + 4].reshape(LANES, LANES)
            turned[f] = jnp.take_along_axis(plain, to_turned, axis=1).T
        for place in range(4):
            fields = [state[f, first + place] for f in range(FIELDS)]
            vel, pressure = half_velocities(fields)
            for field in range(FIELDS):
                out[field, part * 4 + place] = periodic_divergence(
                    half_flux(fields, field, 1, vel[1], pressure),
                    half_speed * fields[field],
                    y_up,
                    y_up_two,
                    y_down,
                )
        columns = [
            [turned[f, row : row + 8] for row in range(0, LANES, 8)] for f in range(FIELDS)
        ]
        along = [half_velocities(fields) for fields in zip(*columns)]
        for field in range(FIELDS):
            fluxes = [
                half_flux(fields, field, 2, vel[2], pressure)
                for fields, (vel, pressure) in zip(zip(*columns), along)
            ]
            scaled = [half_speed * value for value in columns[field]]
            total = jnp.concatenate(ring_divergence(fluxes, scaled), axis=0)
            plain = jnp.take_along_axis(total.T, to_plain, axis=1)
            out[field, part * 4 : part * 4 + 4] += plain.reshape(4, ROWS, LANES)

    def group(j, carry):
        rows = pl.ds(pl.multiple_of(j * 8, 8), 8)

        def get(f, place):
            return states[0][f, place, rows, :]

        for field, along_x in across(get, half_speed, range(BLOCK), INNER):
            for place in range(BLOCK):
                out[field, place, rows, :] += along_x[place]
        return carry

    if with_inner:
        lax.fori_loop(0, 4, group, 0)


def along_planes(states, speed, with_inner):
    return pl.pallas_call(
        functools.partial(plane_kernel, with_inner),
        out_shape=jax.ShapeDtypeStruct((FIELDS, BLOCK, ROWS, LANES), jnp.float32),
        in_specs=[VMEM] * (len(states) + 1),
        out_specs=VMEM,
        scratch_shapes=[pltpu.VMEM((FIELDS, LANES, LANES), jnp.float32)],
        compiler_params=params(),
        cost_estimate=cost(20_000_000, 1_000_000),
        name="planes",
    )(*states, speed)


def across(get, half_speed, span, parts):
    sign = sign_of_x()
    speeds, pressures = {}, {}
    for place in span:
        vel, pressure = half_velocities([get(f, place) for f in range(FIELDS)])
        speeds[place] = sign * vel[0]
        pressures[place] = pressure
    for field in range(FIELDS):
        fluxes, scaled = {}, {}
        for place in span:
            if field == 0:
                flux = (0.5 * sign) * get(1, place)
            elif field == 4:
                flux = (get(4, place) + pressures[place]) * speeds[place]
            else:
                flux = get(field, place) * speeds[place]
                if field == 1:
                    flux = flux + (0.5 * sign) * pressures[place]
            fluxes[place] = flux
            scaled[place] = half_speed * get(field, place)
        yield field, x_divergence(fluxes, scaled, *parts)


WITH_HALOS = range(-3, BLOCK + 3)


def with_halos(far, near, inside, rows):
    def get(f, place):
        if place < 0:
            return far[f, -1 - place, rows, :]
        if place >= BLOCK:
            return near[f, BLOCK + 2 - place, rows, :]
        return inside(f, place)

    return get


def first_kernel(is_far, *refs):
    if is_far:
        state, sides, halo, speed, other, middle, side, top = refs
    else:
        state, sides, halo, speed, middle, side, top = refs
    first, parts, span = (0, FAR, range(-3, 4)) if is_far else (4, NEAR, range(4, 11))
    half_speed = 0.5 * speed[0:1, :]
    factor = (courant / 6.0) / speed[0:1, :]

    def group(j, best):
        rows = pl.ds(pl.multiple_of(j * 8, 8), 8)

        def inside(f, place):
            return state[f, place, rows, :]

        get = with_halos(halo, halo, inside, rows)
        for field, along_x in across(get, half_speed, span, parts):
            for k in range(4):
                total = sides[field, first + k, rows, :]
                if first + k in along_x:
                    total = total + along_x[first + k]
                value = get(field, first + k) - factor * total
                middle[field, k, rows, :] = value
                at = k if is_far else k - 1
                if 0 <= at < 3:
                    side[field, at, rows, :] = value
        for k in range(4):
            best = jnp.maximum(best, wave_speed([middle[f, k, rows, :] for f in range(FIELDS)]))
        return best

    start = other[...] if is_far else jnp.zeros((8, LANES), jnp.float32)
    best = lax.fori_loop(0, 4, group, start)
    top[...] = jnp.full((8, LANES), jnp.max(best), jnp.float32) if is_far else best


def first_stage(is_far, *operands):
    return pl.pallas_call(
        functools.partial(first_kernel, is_far),
        out_shape=(
            jax.ShapeDtypeStruct((FIELDS, 4, ROWS, LANES), jnp.float32),
            jax.ShapeDtypeStruct(HALO, jnp.float32),
            jax.ShapeDtypeStruct((8, LANES), jnp.float32),
        ),
        in_specs=[VMEM] * len(operands),
        out_specs=(VMEM,) * 3,
        compiler_params=params(),
        cost_estimate=cost(15_000_000, 2_000_000),
        name="first_far" if is_far else "first_near",
    )(*operands)


def second_kernel(state, middle_far, middle_near, sides, far, near, first_speed, speed, out):
    half_speed = 0.5 * speed[0:1, :]
    factor = (courant / 12.0) / first_speed[0:1, :]
    planes = [place_of(place) for place in range(BLOCK)]

    def group(j, carry):
        rows = pl.ds(pl.multiple_of(j * 8, 8), 8)
        spread = pl.ds(j, 8, stride=4)

        def inside(f, place):
            return (middle_far, middle_near)[place // 4][f, place % 4, rows, :]

        get = with_halos(far, near, inside, rows)
        for field, along_x in across(get, half_speed, WITH_HALOS, EVERY):
            for place in range(BLOCK):
                total = along_x[place] + sides[field, place, rows, :]
                value = 0.5 * state[field, place, rows, :] + (
                    0.5 * get(field, place) - factor * total
                )
                out[field, planes[place], spread, :] = value
        return carry

    lax.fori_loop(0, 4, group, 0)


def second_stage(*operands):
    return pl.pallas_call(
        second_kernel,
        out_shape=jax.ShapeDtypeStruct((FIELDS, BLOCK, ROWS, LANES), jnp.float32),
        in_specs=[VMEM] * len(operands),
        out_specs=VMEM,
        compiler_params=params(),
        cost_estimate=cost(30_000_000, 3_000_000),
        name="second_stage",
    )(*operands)


def everyone_max(value, axis, size):
    reach = 1
    while reach * 4 < size:
        reach *= 4
    while reach:
        copies = [value]
        for times in range(1, 4):
            turn = reach * times
            if turn < size:
                pairs = [(i, i ^ turn) for i in range(size)]
                copies.append(lax.ppermute(value, axis, pairs))
        value = functools.reduce(jnp.maximum, copies)
        reach //= 4
    return value


def per_device(blocks, owner_list, slot_list):
    size = lax.axis_size("gx")
    own = lax.axis_index("gx")
    per_dev = blocks.shape[0]
    cap = max(2, 2 * per_dev // size)

    parts = pack(tiled_rows(blocks), owner_list, size, cap, per_dev)
    parts, owner_list, slot_list = lax.optimization_barrier((parts, owner_list, slot_list))
    come = lax.all_to_all(parts, "gx", split_axis=0, concat_axis=0, tiled=True)
    table = arrival_spots(owner_list, slot_list, own, per_dev, size, cap)
    state, far_side, near_side, speed = unpack(table, come.reshape(-1, 1, LANES), size, cap)
    far = from_far(far_side, size)
    near = from_near(near_side, size)
    sides = along_planes((state,), speed, True)
    middle_near, near_side, top = first_stage(False, state, sides, near, speed)
    middle_far, far_side, top = first_stage(True, state, sides, far, speed, top)
    far = from_far(far_side, size)
    near = from_near(near_side, size)
    second = everyone_max(top, "gx", size)
    sides = along_planes((middle_far, middle_near), second, False)
    return second_stage(state, middle_far, middle_near, sides, far, near, speed, second)


def solution(mesh):
    return jax.shard_map(
        per_device,
        mesh=mesh,
        in_specs=(P(("runs", "gx"), None, None), P("runs"), P("runs")),
        out_specs=P(None, ("runs", "gx"), None, None),
        check_vma=False,
    )
```

```python
import functools

import jax
import jax.numpy as jnp
from jax import lax
from jax.experimental import pallas as pl
from jax.experimental.pallas import tpu as pltpu
from jax.sharding import PartitionSpec as P

BLOCK = 8
BY = 4
BZ = 16
FIELDS = 5
LANES = 128
ROWS = BY * BLOCK
PAIRS = BLOCK // 2
TILES = PAIRS * FIELDS

gamma_gas = 1.4
courant = 0.25
smooth_epsilon = 1e-06

VMEM = pl.BlockSpec(memory_space=pltpu.VMEM)
SMEM = pl.BlockSpec(memory_space=pltpu.SMEM)


def params(mebibytes=40):
    return pltpu.CompilerParams(vmem_limit_bytes=mebibytes * 1024 * 1024)


def cost(flops, size):
    return pl.CostEstimate(flops=flops, bytes_accessed=size, transcendentals=0)


def wave_speed(fields):
    density, mom_x, mom_y, mom_z, energy = fields
    inverse = 1.0 / density
    vel = (mom_x * inverse, mom_y * inverse, mom_z * inverse)
    kinetic = 0.5 * (mom_x * vel[0] + mom_y * vel[1] + mom_z * vel[2])
    pressure = (gamma_gas - 1.0) * (energy - kinetic)
    sound = jnp.sqrt(gamma_gas * pressure * inverse)
    fastest = jnp.maximum(jnp.maximum(jnp.abs(vel[0]), jnp.abs(vel[1])), jnp.abs(vel[2]))
    return fastest + sound


def tiled_rows(blocks):
    count = blocks.shape[0] // 8
    groups = blocks.reshape(count, 8, FIELDS, PAIRS, LANES).transpose(2, 0, 3, 1, 4)
    return groups.reshape(FIELDS * count * PAIRS * 8, 1, LANES)


def pack_kernel(
    size, cap, per_dev, owner_hbm, rows_hbm, out_hbm, owner, rows, tiled, out, top, count, member, sems
):
    own = lax.axis_index("gx")
    fetch_owner = pltpu.make_async_copy(owner_hbm, owner, sems.at[0])
    fetch_rows = pltpu.make_async_copy(rows_hbm, rows, sems.at[1])
    fetch_tiled = pltpu.make_async_copy(rows_hbm.at[:, 0], tiled, sems.at[4])
    fetch_owner.start()
    fetch_rows.start()
    fetch_tiled.start()

    def clear(dest, carry):
        count[dest] = 0
        return carry

    lax.fori_loop(0, size, clear, 0, unroll=8)
    fetch_owner.wait()

    def note(block, carry):
        dest = owner[own * per_dev + block]
        rank = count[dest]
        count[dest] = rank + 1
        member[dest * cap + rank] = lax.div(block, 8) * (PAIRS * 8) + lax.rem(block, 8)
        return carry

    lax.fori_loop(0, per_dev, note, 0, unroll=8)
    fetch_rows.wait()
    tiles = TILES * cap

    def message(dest, carry):
        @pl.when(count[dest] > 0)
        def _():
            for rank in range(cap):
                first = member[dest * cap + rank]
                for pair in range(PAIRS):
                    for f in range(FIELDS):
                        to = dest * tiles + (pair * FIELDS + f) * cap + rank
                        out[to] = rows[first + f * (per_dev * PAIRS) + pair * 8]
            part = out.at[pl.ds(dest * tiles, tiles)]
            pltpu.make_async_copy(part, out_hbm.at[dest, pl.ds(0, tiles)], sems.at[2]).start()

        return carry

    lax.fori_loop(0, size, message, 0)
    fetch_tiled.wait()
    best = jnp.zeros((8, LANES), jnp.float32)
    step = per_dev * PAIRS
    for first in range(0, step, 8):
        fields = [tiled[f * step + first : f * step + first + 8, :] for f in range(FIELDS)]
        best = jnp.maximum(best, wave_speed(fields))
    most = jnp.full((1, LANES), jnp.max(best), jnp.float32)
    for dest in range(size):
        top[dest] = most
    send_top = pltpu.make_async_copy(top, out_hbm.at[:, tiles], sems.at[3])
    send_top.start()
    half = out.at[pl.ds(0, per_dev * TILES)]
    pltpu.make_async_copy(half, half, sems.at[2]).wait()
    send_top.wait()


def pack(rows, owner_list, size, cap, per_dev):
    return pl.pallas_call(
        functools.partial(pack_kernel, size, cap, per_dev),
        out_shape=jax.ShapeDtypeStruct((size, TILES * cap + 1, 1, LANES), jnp.float32),
        in_specs=[pl.BlockSpec(memory_space=pltpu.HBM)] * 2,
        out_specs=pl.BlockSpec(memory_space=pltpu.HBM),
        scratch_shapes=[
            pltpu.SMEM(owner_list.shape, jnp.int32),
            pltpu.VMEM(rows.shape, jnp.float32),
            pltpu.VMEM((rows.shape[0], LANES), jnp.float32),
            pltpu.VMEM((size * TILES * cap, 1, LANES), jnp.float32),
            pltpu.VMEM((size, 1, LANES), jnp.float32),
            pltpu.SMEM((size,), jnp.int32),
            pltpu.SMEM((size * cap,), jnp.int32),
            pltpu.SemaphoreType.DMA((5,)),
        ],
        compiler_params=params(62),
        cost_estimate=cost(1_000_000, 3_000_000),
        name="pack",
    )(owner_list, rows)


def turned_round():
    return lax.axis_index("gx") % 2


def place_of(plane):
    return jnp.where(turned_round() == 0, plane, BLOCK - 1 - plane)


def sign_of_x():
    return jnp.where(turned_round() == 0, 1.0, -1.0).astype(jnp.float32)


def from_far(far_side, size):
    pairs = [(i, (i - 1 if i % 2 == 0 else i + 1) % size) for i in range(size)]
    return lax.ppermute(far_side, "gx", pairs)


def from_near(near_side, size):
    return lax.ppermute(near_side, "gx", [(i, i ^ 1) for i in range(size)])


HALO = (FIELDS, 3, ROWS, LANES)


def arrival_spots(owner_list, slot_list, own, per_dev, size, cap):
    owners = owner_list.reshape(size, per_dev)
    slots = slot_list.reshape(size, per_dev)
    mine = owners == own
    spot = jnp.arange(per_dev, dtype=jnp.int32)
    earlier = spot[None, :] < spot[:, None]
    rank = jnp.sum((mine[:, None, :] & earlier[None]).astype(jnp.int32), axis=2)
    row = jnp.arange(size, dtype=jnp.int32)[:, None] * (TILES * cap + 1) + rank
    key = jnp.where(mine, slots, -1)
    hit = key.reshape(1, -1) == spot[:, None]
    return jnp.max(jnp.where(hit, row.reshape(1, -1), 0), axis=1)


def exchanged_bits(rows, group):
    rows = list(rows)
    for bit in range(4):
        step = 1 << bit
        low = (group & step) == 0
        for index in range(16):
            if index & step:
                continue
            first, second = rows[index], rows[index | step]
            rows[index] = jnp.where(low, first, pltpu.roll(second, 8 * step, 1))
            rows[index | step] = jnp.where(low, pltpu.roll(first, LANES - 8 * step, 1), second)
    return rows


def unpack_kernel(size, cap, table, come, state, far_side, near_side, speed, scratch):
    message = TILES * cap + 1
    best = come[message - 1]
    for source in range(1, size):
        best = jnp.maximum(best, come[(source + 1) * message - 1])
    speed[...] = jnp.broadcast_to(best, speed.shape)
    group = lax.broadcasted_iota(jnp.int32, (8, LANES), 1) // BLOCK
    even = lax.broadcasted_iota(jnp.int32, (8, LANES), 0) % 2 == 0
    half = FIELDS * BZ * 8
    places = [place_of(plane) for plane in range(BLOCK)]

    def gather(couple, slot):
        p, q = divmod(slot, BZ)
        first = table[slot]
        for h in range(2):
            for f in range(FIELDS):
                row = couple * half + (f * BZ + q) * 8 + 2 * p + h
                value = come[first + ((2 * couple + h) * FIELDS + f) * cap]
                scratch[row : row + 1, :] = value

    def arrange(couple, f):
        first = couple * half + f * BZ * 8
        moved = exchanged_bits(
            [scratch[first + q * 8 : first + q * 8 + 8, :] for q in range(BZ)], group
        )
        for second in range(2):
            for j in range(4):
                lower = moved[second * BLOCK + j]
                upper = moved[second * BLOCK + j + 4]
                planes = (
                    jnp.where(even, lower, pltpu.roll(upper, 1, 0)),
                    jnp.where(even, pltpu.roll(lower, 7, 0), upper),
                )
                for h in range(2):
                    state[f, places[4 * couple + 2 * h + second], j * 8 : j * 8 + 8, :] = planes[h]

    for slot in range(BY * BZ):
        gather(0, slot)
    for f in range(FIELDS):
        for slot in range(f, BY * BZ, FIELDS):
            gather(1, slot)
        arrange(0, f)
    for f in range(FIELDS):
        arrange(1, f)
    for f in range(FIELDS):
        for place in range(3):
            far_side[f, place] = state[f, place]
            near_side[f, place] = state[f, BLOCK - 3 + place]


def unpack(table, come, size, cap):
    halo = jax.ShapeDtypeStruct(HALO, jnp.float32)
    return pl.pallas_call(
        functools.partial(unpack_kernel, size, cap),
        out_shape=(
            jax.ShapeDtypeStruct((FIELDS, BLOCK, ROWS, LANES), jnp.float32),
            halo,
            halo,
            jax.ShapeDtypeStruct((8, LANES), jnp.float32),
        ),
        in_specs=[SMEM, VMEM],
        out_specs=(VMEM,) * 4,
        scratch_shapes=[pltpu.VMEM((FIELDS * (PAIRS // 2) * BZ * 8, LANES), jnp.float32)],
        compiler_params=params(),
        cost_estimate=cost(5_000_000, 2_000_000),
        name="unpack",
    )(table, come)


def y_up(x):
    return jnp.concatenate([x[8:], pltpu.roll(x[:8], 7, 0)], axis=0)


def y_down(x):
    return jnp.concatenate([pltpu.roll(x[24:], 1, 0), x[:24]], axis=0)


def y_up_two(x):
    return jnp.concatenate([x[16:], pltpu.roll(x[:8], 7, 0), pltpu.roll(x[8:16], 7, 0)], axis=0)


def inverse(x):
    return 1.0 / x


def smoothness(before, after):
    curve = after - before
    middle = 0.5 * (after + before)
    base = curve * curve * (13.0 / 12.0) + smooth_epsilon
    plus = middle + curve
    minus = middle - curve
    left = inverse(base + plus * plus)
    centre = inverse(base + middle * middle)
    right = inverse(base + minus * minus)
    return curve, left * left, centre * centre, right * right


def upwind_term(left, centre, right, jump_before, jump_after):
    right = 3.0 * right
    top = left * (jump_before + jump_before) + right * jump_after
    return top * inverse(left + 6.0 * centre + right)


def periodic_divergence(half_flux, scaled, up, up_two, down):
    plus = half_flux + scaled
    minus = half_flux - scaled

    def side(values):
        after = up(values) - values
        curve, left, centre, right = smoothness(down(after), after)
        above = up(curve)
        return curve, above, left, centre, right, above - curve

    curve, _, left, centre, right, jump = side(plus)
    face = 6.0 * (half_flux + up(half_flux)) - curve
    face = face - upwind_term(down(left), centre, up(right), down(jump), jump)
    _, curve, left, centre, right, jump = side(minus)
    face = face + (upwind_term(up_two(right), up(centre), left, up(jump), jump) - curve)
    return face - down(face)


def ring_divergence(half_flux, scaled):
    count = len(half_flux)

    def up(values):
        return values[1:] + [pltpu.roll(values[0], 7, 0)]

    def down(values):
        return [pltpu.roll(values[-1], 1, 0)] + values[:-1]

    def side(values):
        after = [above - value for above, value in zip(up(values), values)]
        parts = [smoothness(before, step) for before, step in zip(down(after), after)]
        curve, left, centre, right = (list(part) for part in zip(*parts))
        jump = [above - value for above, value in zip(up(curve), curve)]
        return curve, left, centre, right, jump

    curve, left, centre, right, jump = side([a + b for a, b in zip(half_flux, scaled)])
    terms = zip(down(left), centre, up(right), down(jump), jump)
    face = [
        6.0 * (here + above) - bend - upwind_term(*term)
        for here, above, bend, term in zip(half_flux, up(half_flux), curve, terms)
    ]
    curve, left, centre, right, jump = side([a - b for a, b in zip(half_flux, scaled)])
    terms = zip(up(right), centre, down(left), jump, down(jump))
    other = [upwind_term(*term) - bend for bend, term in zip(curve, terms)]
    face = [one + two for one, two in zip(face, up(other))]
    return [here - below for here, below in zip(face, down(face))]


def x_divergence(half_flux, scaled, plus_at, minus_at, centre_at):
    faces = {i: 6.0 * (half_flux[i] + half_flux[i + 1]) for i in centre_at}

    def add(i, value):
        faces[i] = faces[i] + value if i in faces else value

    def side(sign):
        values = {i: half_flux[i] + sign * scaled[i] for i in half_flux}
        steps = {i: values[i + 1] - values[i] for i in values if i + 1 in values}
        return {i: smoothness(steps[i - 1], steps[i]) for i in steps if i - 1 in steps}

    parts = side(1)
    for i in plus_at:
        curve, left, centre, right = zip(parts[i - 1], parts[i], parts[i + 1])
        term = upwind_term(left[0], centre[1], right[2], curve[1] - curve[0], curve[2] - curve[1])
        add(i, -(curve[1] + term))
    parts = side(-1)
    for i in minus_at:
        curve, left, centre, right = zip(parts[i - 1], parts[i], parts[i + 1])
        term = upwind_term(right[2], centre[1], left[0], curve[2] - curve[1], curve[1] - curve[0])
        add(i - 1, term - curve[1])
    total = {}
    for i in range(BLOCK):
        if i in faces:
            total[i] = faces[i]
        if i - 1 in faces:
            total[i] = total[i] - faces[i - 1] if i in total else -faces[i - 1]
    return total


INNER = (range(2, 6), range(2, 6), range(0, 7))
FAR = ((-1, 0, 1), (0, 1), (-1,))
NEAR = ((6, 7), (6, 7, 8), (7,))
EVERY = (range(-1, 8), range(0, 9), range(-1, 8))


def ring_divergence(half_flux, scaled):
    count = len(half_flux)

    def up(values):
        return values[1:] + [pltpu.roll(values[0], 7, 0)]

    def down(values):
        return [pltpu.roll(values[-1], 1, 0)] + values[:-1]

    def side(values):
        after = [above - value for above, value in zip(up(values), values)]
        parts = [smoothness(before, step) for before, step in zip(down(after), after)]
        curve, left, centre, right = (list(part) for part in zip(*parts))
        jump = [above - value for above, value in zip(up(curve), curve)]
        return curve, left, centre, right, jump

    curve, left, centre, right, jump = side([a + b for a, b in zip(half_flux, scaled)])
    terms = zip(down(left), centre, up(right), down(jump), jump)
    face = [
        6.0 * (here + above) - bend - upwind_term(*term)
        for here, above, bend, term in zip(half_flux, up(half_flux), curve, terms)
    ]
    curve, left, centre, right, jump = side([a - b for a, b in zip(half_flux, scaled)])
    terms = zip(up(right), centre, down(left), jump, down(jump))
    other = [upwind_term(*term) - bend for bend, term in zip(curve, terms)]
    face = [one + two for one, two in zip(face, up(other))]
    return [here - below for here, below in zip(face, down(face))]


def open_divergence(half_flux, scaled):
    count = len(half_flux)
    plus = [a + b for a, b in zip(half_flux, scaled)]
    minus = [a - b for a, b in zip(half_flux, scaled)]
    faces = [None] * count

    def side(values):
        steps = [values[i + 1] - values[i] for i in range(count - 1)]
        parts = [None] + [smoothness(steps[i - 1], steps[i]) for i in range(1, count - 1)]
        return parts

    parts = side(plus)
    for i in range(2, count - 3):
        jump_before = parts[i][0] - parts[i - 1][0]
        jump_after = parts[i + 1][0] - parts[i][0]
        faces[i] = 6.0 * (half_flux[i] + half_flux[i + 1]) - parts[i][0] - upwind_term(
            parts[i - 1][1], parts[i][2], parts[i + 1][3], jump_before, jump_after
        )
    parts = side(minus)
    for i in range(3, count - 2):
        jump_before = parts[i][0] - parts[i - 1][0]
        jump_after = parts[i + 1][0] - parts[i][0]
        faces[i - 1] = faces[i - 1] + (
            upwind_term(parts[i + 1][3], parts[i][2], parts[i - 1][1], jump_after, jump_before)
            - parts[i][0]
        )
    return [faces[i] - faces[i - 1] for i in range(3, count - 3)]


def half_velocities(fields):
    density, mom_x, mom_y, mom_z, energy = fields
    over = 0.5 / density
    vel = (mom_x * over, mom_y * over, mom_z * over)
    kinetic = mom_x * vel[0] + mom_y * vel[1] + mom_z * vel[2]
    pressure = (gamma_gas - 1.0) * (energy - kinetic)
    return vel, pressure


def half_flux(fields, field, direction, speed, pressure):
    if field == 0:
        return 0.5 * fields[1 + direction]
    if field == 4:
        return (fields[4] + pressure) * speed
    flux = fields[field] * speed
    return flux + 0.5 * pressure if field == 1 + direction else flux


def plane_kernel(with_inner, *refs):
    *states, speed, out, turned = refs
    half_speed = 0.5 * speed[0:1, :]
    lane = lax.broadcasted_iota(jnp.int32, (LANES, LANES), 1)
    to_turned = (lane % 8) * 16 + lane // 8
    to_plain = (lane % 16) * 8 + lane // 16

    for part in range(2):
        state, first = (states[0], 4 * part) if len(states) == 1 else (states[part], 0)
        for f in range(FIELDS):
            plain = state[f, first : first + 4].reshape(LANES, LANES)
            turned[f] = jnp.take_along_axis(plain, to_turned, axis=1).T
        for place in range(4):
            fields = [state[f, first + place] for f in range(FIELDS)]
            vel, pressure = half_velocities(fields)
            for field in range(FIELDS):
                out[field, part * 4 + place] = periodic_divergence(
                    half_flux(fields, field, 1, vel[1], pressure),
                    half_speed * fields[field],
                    y_up,
                    y_up_two,
                    y_down,
                )
        columns = [
            [turned[f, row : row + 8] for row in range(0, LANES, 8)] for f in range(FIELDS)
        ]
        along = [half_velocities(fields) for fields in zip(*columns)]
        for field in range(FIELDS):
            fluxes = [
                half_flux(fields, field, 2, vel[2], pressure)
                for fields, (vel, pressure) in zip(zip(*columns), along)
            ]
            scaled = [half_speed * value for value in columns[field]]
            total = jnp.concatenate(ring_divergence(fluxes, scaled), axis=0)
            plain = jnp.take_along_axis(total.T, to_plain, axis=1)
            out[field, part * 4 : part * 4 + 4] += plain.reshape(4, ROWS, LANES)

    def group(j, carry):
        rows = pl.ds(pl.multiple_of(j * 8, 8), 8)

        def get(f, place):
            return states[0][f, place, rows, :]

        for field, along_x in across(get, half_speed, range(BLOCK), INNER):
            for place in range(BLOCK):
                out[field, place, rows, :] += along_x[place]
        return carry

    if with_inner:
        lax.fori_loop(0, 4, group, 0)


def along_planes(states, speed, with_inner):
    return pl.pallas_call(
        functools.partial(plane_kernel, with_inner),
        out_shape=jax.ShapeDtypeStruct((FIELDS, BLOCK, ROWS, LANES), jnp.float32),
        in_specs=[VMEM] * (len(states) + 1),
        out_specs=VMEM,
        scratch_shapes=[pltpu.VMEM((FIELDS, LANES, LANES), jnp.float32)],
        compiler_params=params(),
        cost_estimate=cost(20_000_000, 1_000_000),
        name="planes",
    )(*states, speed)


def across(get, half_speed, span, parts):
    sign = sign_of_x()
    speeds, pressures = {}, {}
    for place in span:
        vel, pressure = half_velocities([get(f, place) for f in range(FIELDS)])
        speeds[place] = sign * vel[0]
        pressures[place] = pressure
    for field in range(FIELDS):
        fluxes, scaled = {}, {}
        for place in span:
            if field == 0:
                flux = (0.5 * sign) * get(1, place)
            elif field == 4:
                flux = (get(4, place) + pressures[place]) * speeds[place]
            else:
                flux = get(field, place) * speeds[place]
                if field == 1:
                    flux = flux + (0.5 * sign) * pressures[place]
            fluxes[place] = flux
            scaled[place] = half_speed * get(field, place)
        yield field, x_divergence(fluxes, scaled, *parts)


WITH_HALOS = range(-3, BLOCK + 3)


def with_halos(far, near, inside, rows):
    def get(f, place):
        if place < 0:
            return far[f, -1 - place, rows, :]
        if place >= BLOCK:
            return near[f, BLOCK + 2 - place, rows, :]
        return inside(f, place)

    return get


def first_kernel(is_far, *refs):
    if is_far:
        state, sides, halo, speed, other, middle, side, top = refs
    else:
        state, sides, halo, speed, middle, side, top = refs
    first, parts, span = (0, FAR, range(-3, 4)) if is_far else (4, NEAR, range(4, 11))
    half_speed = 0.5 * speed[0:1, :]
    factor = (courant / 6.0) / speed[0:1, :]

    def group(j, best):
        rows = pl.ds(pl.multiple_of(j * 8, 8), 8)

        def inside(f, place):
            return state[f, place, rows, :]

        get = with_halos(halo, halo, inside, rows)
        for field, along_x in across(get, half_speed, span, parts):
            for k in range(4):
                total = sides[field, first + k, rows, :]
                if first + k in along_x:
                    total = total + along_x[first + k]
                value = get(field, first + k) - factor * total
                middle[field, k, rows, :] = value
                at = k if is_far else k - 1
                if 0 <= at < 3:
                    side[field, at, rows, :] = value
        for k in range(4):
            best = jnp.maximum(best, wave_speed([middle[f, k, rows, :] for f in range(FIELDS)]))
        return best

    start = other[...] if is_far else jnp.zeros((8, LANES), jnp.float32)
    best = lax.fori_loop(0, 4, group, start)
    top[...] = jnp.full((8, LANES), jnp.max(best), jnp.float32) if is_far else best


def first_stage(is_far, *operands):
    return pl.pallas_call(
        functools.partial(first_kernel, is_far),
        out_shape=(
            jax.ShapeDtypeStruct((FIELDS, 4, ROWS, LANES), jnp.float32),
            jax.ShapeDtypeStruct(HALO, jnp.float32),
            jax.ShapeDtypeStruct((8, LANES), jnp.float32),
        ),
        in_specs=[VMEM] * len(operands),
        out_specs=(VMEM,) * 3,
        compiler_params=params(),
        cost_estimate=cost(15_000_000, 2_000_000),
        name="first_far" if is_far else "first_near",
    )(*operands)


def second_kernel(state, middle_far, middle_near, sides, far, near, first_speed, speed, out):
    half_speed = 0.5 * speed[0:1, :]
    factor = (courant / 12.0) / first_speed[0:1, :]
    planes = [place_of(place) for place in range(BLOCK)]

    def group(j, carry):
        rows = pl.ds(pl.multiple_of(j * 8, 8), 8)
        spread = pl.ds(j, 8, stride=4)

        def inside(f, place):
            return (middle_far, middle_near)[place // 4][f, place % 4, rows, :]

        get = with_halos(far, near, inside, rows)
        for field, along_x in across(get, half_speed, WITH_HALOS, EVERY):
            for place in range(BLOCK):
                total = along_x[place] + sides[field, place, rows, :]
                value = 0.5 * state[field, place, rows, :] + (
                    0.5 * get(field, place) - factor * total
                )
                out[field, planes[place], spread, :] = value
        return carry

    lax.fori_loop(0, 4, group, 0)


def second_stage(*operands):
    return pl.pallas_call(
        second_kernel,
        out_shape=jax.ShapeDtypeStruct((FIELDS, BLOCK, ROWS, LANES), jnp.float32),
        in_specs=[VMEM] * len(operands),
        out_specs=VMEM,
        compiler_params=params(),
        cost_estimate=cost(30_000_000, 3_000_000),
        name="second_stage",
    )(*operands)


def max_rounds(size):
    rounds = [[1]] if size > 1 else []
    low = 2
    for width in (8, 4, 4, 4):
        width = min(width, max(size // low, 1))
        if width > 1:
            rounds.insert(0, [low * times for times in range(1, width)])
        low *= width
    return rounds


def everyone_max(value, axis, size):
    for turns in max_rounds(size):
        copies = [value]
        for turn in turns:
            pairs = [(i, i ^ turn) for i in range(size)]
            copies.append(lax.ppermute(value, axis, pairs))
        value = functools.reduce(jnp.maximum, copies)
    return value


def per_device(blocks, owner_list, slot_list):
    size = lax.axis_size("gx")
    own = lax.axis_index("gx")
    per_dev = blocks.shape[0]
    cap = max(2, 2 * per_dev // size)

    parts = pack(tiled_rows(blocks), owner_list, size, cap, per_dev)
    parts, owner_list, slot_list = lax.optimization_barrier((parts, owner_list, slot_list))
    come = lax.all_to_all(parts, "gx", split_axis=0, concat_axis=0, tiled=True)
    table = arrival_spots(owner_list, slot_list, own, per_dev, size, cap)
    state, far_side, near_side, speed = unpack(table, come.reshape(-1, 1, LANES), size, cap)
    far = from_far(far_side, size)
    near = from_near(near_side, size)
    sides = along_planes((state,), speed, True)
    middle_near, near_side, top = first_stage(False, state, sides, near, speed)
    middle_far, far_side, top = first_stage(True, state, sides, far, speed, top)
    far = from_far(far_side, size)
    near = from_near(near_side, size)
    second = everyone_max(top, "gx", size)
    sides = along_planes((middle_far, middle_near), second, False)
    return second_stage(state, middle_far, middle_near, sides, far, near, speed, second)


def solution(mesh):
    return jax.shard_map(
        per_device,
        mesh=mesh,
        in_specs=(P(("runs", "gx"), None, None), P("runs"), P("runs")),
        out_specs=P(None, ("runs", "gx"), None, None),
        check_vma=False,
    )
```

```python
import functools

import jax
import jax.numpy as jnp
from jax import lax
from jax.experimental import pallas as pl
from jax.experimental.pallas import tpu as pltpu
from jax.sharding import PartitionSpec as P

BLOCK = 8
BY = 4
BZ = 16
FIELDS = 5
LANES = 128
ROWS = BY * BLOCK
PAIRS = BLOCK // 2
TILES = PAIRS * FIELDS

gamma_gas = 1.4
courant = 0.25
smooth_epsilon = 1e-06

VMEM = pl.BlockSpec(memory_space=pltpu.VMEM)
SMEM = pl.BlockSpec(memory_space=pltpu.SMEM)


def params(mebibytes=40):
    return pltpu.CompilerParams(vmem_limit_bytes=mebibytes * 1024 * 1024)


def cost(flops, size):
    return pl.CostEstimate(flops=flops, bytes_accessed=size, transcendentals=0)


def wave_speed(fields):
    density, mom_x, mom_y, mom_z, energy = fields
    inverse = 1.0 / density
    vel = (mom_x * inverse, mom_y * inverse, mom_z * inverse)
    kinetic = 0.5 * (mom_x * vel[0] + mom_y * vel[1] + mom_z * vel[2])
    pressure = (gamma_gas - 1.0) * (energy - kinetic)
    sound = jnp.sqrt(gamma_gas * pressure * inverse)
    fastest = jnp.maximum(jnp.maximum(jnp.abs(vel[0]), jnp.abs(vel[1])), jnp.abs(vel[2]))
    return fastest + sound


def tiled_rows(blocks):
    count = blocks.shape[0] // 8
    groups = blocks.reshape(count, 8, FIELDS, PAIRS, LANES).transpose(2, 0, 3, 1, 4)
    return groups.reshape(FIELDS * count * PAIRS * 8, 1, LANES)


def pack_kernel(
    size, cap, per_dev, owner_hbm, rows_hbm, out_hbm, owner, rows, tiled, out, top, count, member, sems
):
    own = lax.axis_index("gx")
    fetch_owner = pltpu.make_async_copy(owner_hbm, owner, sems.at[0])
    fetch_rows = pltpu.make_async_copy(rows_hbm, rows, sems.at[1])
    fetch_tiled = pltpu.make_async_copy(rows_hbm.at[:, 0], tiled, sems.at[4])
    fetch_owner.start()
    fetch_rows.start()
    fetch_tiled.start()

    def clear(dest, carry):
        count[dest] = 0
        return carry

    lax.fori_loop(0, size, clear, 0, unroll=8)
    fetch_owner.wait()

    def note(block, carry):
        dest = owner[own * per_dev + block]
        rank = count[dest]
        count[dest] = rank + 1
        member[dest * cap + rank] = lax.div(block, 8) * (PAIRS * 8) + lax.rem(block, 8)
        return carry

    lax.fori_loop(0, per_dev, note, 0, unroll=8)
    fetch_rows.wait()
    tiles = TILES * cap

    def message(dest, carry):
        @pl.when(count[dest] > 0)
        def _():
            for rank in range(cap):
                first = member[dest * cap + rank]
                for pair in range(PAIRS):
                    for f in range(FIELDS):
                        to = dest * tiles + (pair * FIELDS + f) * cap + rank
                        out[to] = rows[first + f * (per_dev * PAIRS) + pair * 8]
            part = out.at[pl.ds(dest * tiles, tiles)]
            pltpu.make_async_copy(part, out_hbm.at[dest, pl.ds(0, tiles)], sems.at[2]).start()

        return carry

    lax.fori_loop(0, size, message, 0)
    fetch_tiled.wait()
    best = jnp.zeros((8, LANES), jnp.float32)
    step = per_dev * PAIRS
    for first in range(0, step, 8):
        fields = [tiled[f * step + first : f * step + first + 8, :] for f in range(FIELDS)]
        best = jnp.maximum(best, wave_speed(fields))
    most = jnp.full((1, LANES), jnp.max(best), jnp.float32)
    for dest in range(size):
        top[dest] = most
    send_top = pltpu.make_async_copy(top, out_hbm.at[:, tiles], sems.at[3])
    send_top.start()
    half = out.at[pl.ds(0, per_dev * TILES)]
    pltpu.make_async_copy(half, half, sems.at[2]).wait()
    send_top.wait()


def pack(rows, owner_list, size, cap, per_dev):
    return pl.pallas_call(
        functools.partial(pack_kernel, size, cap, per_dev),
        out_shape=jax.ShapeDtypeStruct((size, TILES * cap + 1, 1, LANES), jnp.float32),
        in_specs=[pl.BlockSpec(memory_space=pltpu.HBM)] * 2,
        out_specs=pl.BlockSpec(memory_space=pltpu.HBM),
        scratch_shapes=[
            pltpu.SMEM(owner_list.shape, jnp.int32),
            pltpu.VMEM(rows.shape, jnp.float32),
            pltpu.VMEM((rows.shape[0], LANES), jnp.float32),
            pltpu.VMEM((size * TILES * cap, 1, LANES), jnp.float32),
            pltpu.VMEM((size, 1, LANES), jnp.float32),
            pltpu.SMEM((size,), jnp.int32),
            pltpu.SMEM((size * cap,), jnp.int32),
            pltpu.SemaphoreType.DMA((5,)),
        ],
        compiler_params=params(62),
        cost_estimate=cost(1_000_000, 3_000_000),
        name="pack",
    )(owner_list, rows)


def turned_round():
    return lax.axis_index("gx") % 2


def place_of(plane):
    return jnp.where(turned_round() == 0, plane, BLOCK - 1 - plane)


def sign_of_x():
    return jnp.where(turned_round() == 0, 1.0, -1.0).astype(jnp.float32)


def from_far(far_side, size):
    pairs = [(i, (i - 1 if i % 2 == 0 else i + 1) % size) for i in range(size)]
    return lax.ppermute(far_side, "gx", pairs)


def from_near(near_side, size):
    return lax.ppermute(near_side, "gx", [(i, i ^ 1) for i in range(size)])


HALO = (FIELDS, 3, ROWS, LANES)


def arrival_spots(owner_list, slot_list, own, per_dev, size, cap):
    owners = owner_list.reshape(size, per_dev)
    slots = slot_list.reshape(size, per_dev)
    mine = owners == own
    spot = jnp.arange(per_dev, dtype=jnp.int32)
    earlier = spot[None, :] < spot[:, None]
    rank = jnp.sum((mine[:, None, :] & earlier[None]).astype(jnp.int32), axis=2)
    row = jnp.arange(size, dtype=jnp.int32)[:, None] * (TILES * cap + 1) + rank
    key = jnp.where(mine, slots, -1)
    hit = key.reshape(1, -1) == spot[:, None]
    return jnp.max(jnp.where(hit, row.reshape(1, -1), 0), axis=1)


def exchanged_bits(rows, group):
    rows = list(rows)
    for bit in range(4):
        step = 1 << bit
        low = (group & step) == 0
        for index in range(16):
            if index & step:
                continue
            first, second = rows[index], rows[index | step]
            rows[index] = jnp.where(low, first, pltpu.roll(second, 8 * step, 1))
            rows[index | step] = jnp.where(low, pltpu.roll(first, LANES - 8 * step, 1), second)
    return rows


def unpack_kernel(size, cap, table, come, state, far_side, near_side, speed, scratch):
    message = TILES * cap + 1
    best = come[message - 1]
    for source in range(1, size):
        best = jnp.maximum(best, come[(source + 1) * message - 1])
    speed[...] = jnp.broadcast_to(best, speed.shape)
    group = lax.broadcasted_iota(jnp.int32, (8, LANES), 1) // BLOCK
    even = lax.broadcasted_iota(jnp.int32, (8, LANES), 0) % 2 == 0
    half = FIELDS * BZ * 8
    places = [place_of(plane) for plane in range(BLOCK)]

    def gather(couple, slot):
        p, q = divmod(slot, BZ)
        first = table[slot]
        for h in range(2):
            for f in range(FIELDS):
                row = couple * half + (f * BZ + q) * 8 + 2 * p + h
                value = come[first + ((2 * couple + h) * FIELDS + f) * cap]
                scratch[row : row + 1, :] = value

    def arrange(couple, f):
        first = couple * half + f * BZ * 8
        moved = exchanged_bits(
            [scratch[first + q * 8 : first + q * 8 + 8, :] for q in range(BZ)], group
        )
        for second in range(2):
            for j in range(4):
                lower = moved[second * BLOCK + j]
                upper = moved[second * BLOCK + j + 4]
                planes = (
                    jnp.where(even, lower, pltpu.roll(upper, 1, 0)),
                    jnp.where(even, pltpu.roll(lower, 7, 0), upper),
                )
                for h in range(2):
                    state[f, places[4 * couple + 2 * h + second], j * 8 : j * 8 + 8, :] = planes[h]

    for slot in range(BY * BZ):
        gather(0, slot)
    for f in range(FIELDS):
        for slot in range(f, BY * BZ, FIELDS):
            gather(1, slot)
        arrange(0, f)
    for f in range(FIELDS):
        arrange(1, f)
    for f in range(FIELDS):
        for place in range(3):
            far_side[f, place] = state[f, place]
            near_side[f, place] = state[f, BLOCK - 3 + place]


def unpack(table, come, size, cap):
    halo = jax.ShapeDtypeStruct(HALO, jnp.float32)
    return pl.pallas_call(
        functools.partial(unpack_kernel, size, cap),
        out_shape=(
            jax.ShapeDtypeStruct((FIELDS, BLOCK, ROWS, LANES), jnp.float32),
            halo,
            halo,
            jax.ShapeDtypeStruct((8, LANES), jnp.float32),
        ),
        in_specs=[SMEM, VMEM],
        out_specs=(VMEM,) * 4,
        scratch_shapes=[pltpu.VMEM((FIELDS * (PAIRS // 2) * BZ * 8, LANES), jnp.float32)],
        compiler_params=params(),
        cost_estimate=cost(5_000_000, 2_000_000),
        name="unpack",
    )(table, come)


def y_up(x):
    return jnp.concatenate([x[8:], pltpu.roll(x[:8], 7, 0)], axis=0)


def y_down(x):
    return jnp.concatenate([pltpu.roll(x[24:], 1, 0), x[:24]], axis=0)


def y_up_two(x):
    return jnp.concatenate([x[16:], pltpu.roll(x[:8], 7, 0), pltpu.roll(x[8:16], 7, 0)], axis=0)


def inverse(x):
    return 1.0 / x


def smoothness(before, after):
    curve = after - before
    middle = 0.5 * (after + before)
    base = curve * curve * (13.0 / 12.0) + smooth_epsilon
    plus = middle + curve
    minus = middle - curve
    left = inverse(base + plus * plus)
    centre = inverse(base + middle * middle)
    right = inverse(base + minus * minus)
    return curve, left * left, centre * centre, right * right


def upwind_term(left, centre, right, jump_before, jump_after):
    right = 3.0 * right
    top = left * (jump_before + jump_before) + right * jump_after
    return top * inverse(left + 6.0 * centre + right)


def periodic_divergence(half_flux, scaled, up, up_two, down):
    plus = half_flux + scaled
    minus = half_flux - scaled

    def side(values):
        after = up(values) - values
        curve, left, centre, right = smoothness(down(after), after)
        above = up(curve)
        return curve, above, left, centre, right, above - curve

    curve, _, left, centre, right, jump = side(plus)
    face = 6.0 * (half_flux + up(half_flux)) - curve
    face = face - upwind_term(down(left), centre, up(right), down(jump), jump)
    _, curve, left, centre, right, jump = side(minus)
    face = face + (upwind_term(up_two(right), up(centre), left, up(jump), jump) - curve)
    return face - down(face)


def ring_divergence(half_flux, scaled):
    count = len(half_flux)

    def up(values):
        return values[1:] + [pltpu.roll(values[0], 7, 0)]

    def down(values):
        return [pltpu.roll(values[-1], 1, 0)] + values[:-1]

    def side(values):
        after = [above - value for above, value in zip(up(values), values)]
        parts = [smoothness(before, step) for before, step in zip(down(after), after)]
        curve, left, centre, right = (list(part) for part in zip(*parts))
        jump = [above - value for above, value in zip(up(curve), curve)]
        return curve, left, centre, right, jump

    curve, left, centre, right, jump = side([a + b for a, b in zip(half_flux, scaled)])
    terms = zip(down(left), centre, up(right), down(jump), jump)
    face = [
        6.0 * (here + above) - bend - upwind_term(*term)
        for here, above, bend, term in zip(half_flux, up(half_flux), curve, terms)
    ]
    curve, left, centre, right, jump = side([a - b for a, b in zip(half_flux, scaled)])
    terms = zip(up(right), centre, down(left), jump, down(jump))
    other = [upwind_term(*term) - bend for bend, term in zip(curve, terms)]
    face = [one + two for one, two in zip(face, up(other))]
    return [here - below for here, below in zip(face, down(face))]


def x_divergence(half_flux, scaled, plus_at, minus_at, centre_at):
    faces = {i: 6.0 * (half_flux[i] + half_flux[i + 1]) for i in centre_at}

    def add(i, value):
        faces[i] = faces[i] + value if i in faces else value

    def side(sign):
        values = {i: half_flux[i] + sign * scaled[i] for i in half_flux}
        steps = {i: values[i + 1] - values[i] for i in values if i + 1 in values}
        return {i: smoothness(steps[i - 1], steps[i]) for i in steps if i - 1 in steps}

    parts = side(1)
    for i in plus_at:
        curve, left, centre, right = zip(parts[i - 1], parts[i], parts[i + 1])
        term = upwind_term(left[0], centre[1], right[2], curve[1] - curve[0], curve[2] - curve[1])
        add(i, -(curve[1] + term))
    parts = side(-1)
    for i in minus_at:
        curve, left, centre, right = zip(parts[i - 1], parts[i], parts[i + 1])
        term = upwind_term(right[2], centre[1], left[0], curve[2] - curve[1], curve[1] - curve[0])
        add(i - 1, term - curve[1])
    total = {}
    for i in range(BLOCK):
        if i in faces:
            total[i] = faces[i]
        if i - 1 in faces:
            total[i] = total[i] - faces[i - 1] if i in total else -faces[i - 1]
    return total


INNER = (range(2, 6), range(2, 6), range(0, 7))
FAR = ((-1, 0, 1), (0, 1), (-1,))
NEAR = ((6, 7), (6, 7, 8), (7,))
EVERY = (range(-1, 8), range(0, 9), range(-1, 8))


def ring_divergence(half_flux, scaled):
    count = len(half_flux)

    def up(values):
        return values[1:] + [pltpu.roll(values[0], 7, 0)]

    def down(values):
        return [pltpu.roll(values[-1], 1, 0)] + values[:-1]

    def side(values):
        after = [above - value for above, value in zip(up(values), values)]
        parts = [smoothness(before, step) for before, step in zip(down(after), after)]
        curve, left, centre, right = (list(part) for part in zip(*parts))
        jump = [above - value for above, value in zip(up(curve), curve)]
        return curve, left, centre, right, jump

    curve, left, centre, right, jump = side([a + b for a, b in zip(half_flux, scaled)])
    terms = zip(down(left), centre, up(right), down(jump), jump)
    face = [
        6.0 * (here + above) - bend - upwind_term(*term)
        for here, above, bend, term in zip(half_flux, up(half_flux), curve, terms)
    ]
    curve, left, centre, right, jump = side([a - b for a, b in zip(half_flux, scaled)])
    terms = zip(up(right), centre, down(left), jump, down(jump))
    other = [upwind_term(*term) - bend for bend, term in zip(curve, terms)]
    face = [one + two for one, two in zip(face, up(other))]
    return [here - below for here, below in zip(face, down(face))]


def open_divergence(half_flux, scaled):
    count = len(half_flux)
    plus = [a + b for a, b in zip(half_flux, scaled)]
    minus = [a - b for a, b in zip(half_flux, scaled)]
    faces = [None] * count

    def side(values):
        steps = [values[i + 1] - values[i] for i in range(count - 1)]
        parts = [None] + [smoothness(steps[i - 1], steps[i]) for i in range(1, count - 1)]
        return parts

    parts = side(plus)
    for i in range(2, count - 3):
        jump_before = parts[i][0] - parts[i - 1][0]
        jump_after = parts[i + 1][0] - parts[i][0]
        faces[i] = 6.0 * (half_flux[i] + half_flux[i + 1]) - parts[i][0] - upwind_term(
            parts[i - 1][1], parts[i][2], parts[i + 1][3], jump_before, jump_after
        )
    parts = side(minus)
    for i in range(3, count - 2):
        jump_before = parts[i][0] - parts[i - 1][0]
        jump_after = parts[i + 1][0] - parts[i][0]
        faces[i - 1] = faces[i - 1] + (
            upwind_term(parts[i + 1][3], parts[i][2], parts[i - 1][1], jump_after, jump_before)
            - parts[i][0]
        )
    return [faces[i] - faces[i - 1] for i in range(3, count - 3)]


def half_velocities(fields):
    density, mom_x, mom_y, mom_z, energy = fields
    over = 0.5 / density
    vel = (mom_x * over, mom_y * over, mom_z * over)
    kinetic = mom_x * vel[0] + mom_y * vel[1] + mom_z * vel[2]
    pressure = (gamma_gas - 1.0) * (energy - kinetic)
    return vel, pressure


def half_flux(fields, field, direction, speed, pressure):
    if field == 0:
        return 0.5 * fields[1 + direction]
    if field == 4:
        return (fields[4] + pressure) * speed
    flux = fields[field] * speed
    return flux + 0.5 * pressure if field == 1 + direction else flux


def plane_kernel(with_inner, *refs):
    *states, speed, out, turned = refs
    half_speed = 0.5 * speed[0:1, :]
    lane = lax.broadcasted_iota(jnp.int32, (LANES, LANES), 1)
    to_turned = (lane % 8) * 16 + lane // 8
    to_plain = (lane % 16) * 8 + lane // 16

    for part in range(2):
        state, first = (states[0], 4 * part) if len(states) == 1 else (states[part], 0)
        for f in range(FIELDS):
            plain = state[f, first : first + 4].reshape(LANES, LANES)
            turned[f] = jnp.take_along_axis(plain, to_turned, axis=1).T
        for place in range(4):
            fields = [state[f, first + place] for f in range(FIELDS)]
            vel, pressure = half_velocities(fields)
            for field in range(FIELDS):
                out[field, part * 4 + place] = periodic_divergence(
                    half_flux(fields, field, 1, vel[1], pressure),
                    half_speed * fields[field],
                    y_up,
                    y_up_two,
                    y_down,
                )
        columns = [
            [turned[f, row : row + 8] for row in range(0, LANES, 8)] for f in range(FIELDS)
        ]
        along = [half_velocities(fields) for fields in zip(*columns)]
        for field in range(FIELDS):
            fluxes = [
                half_flux(fields, field, 2, vel[2], pressure)
                for fields, (vel, pressure) in zip(zip(*columns), along)
            ]
            scaled = [half_speed * value for value in columns[field]]
            total = jnp.concatenate(ring_divergence(fluxes, scaled), axis=0)
            plain = jnp.take_along_axis(total.T, to_plain, axis=1)
            out[field, part * 4 : part * 4 + 4] += plain.reshape(4, ROWS, LANES)

    def group(j, carry):
        rows = pl.ds(pl.multiple_of(j * 8, 8), 8)

        def get(f, place):
            return states[0][f, place, rows, :]

        for field, along_x in across(get, half_speed, range(BLOCK), INNER):
            for place in range(BLOCK):
                out[field, place, rows, :] += along_x[place]
        return carry

    if with_inner:
        lax.fori_loop(0, 4, group, 0)


def along_planes(states, speed, with_inner):
    return pl.pallas_call(
        functools.partial(plane_kernel, with_inner),
        out_shape=jax.ShapeDtypeStruct((FIELDS, BLOCK, ROWS, LANES), jnp.float32),
        in_specs=[VMEM] * (len(states) + 1),
        out_specs=VMEM,
        scratch_shapes=[pltpu.VMEM((FIELDS, LANES, LANES), jnp.float32)],
        compiler_params=params(),
        cost_estimate=cost(20_000_000, 1_000_000),
        name="planes",
    )(*states, speed)


def across(get, half_speed, span, parts):
    sign = sign_of_x()
    speeds, pressures = {}, {}
    for place in span:
        vel, pressure = half_velocities([get(f, place) for f in range(FIELDS)])
        speeds[place] = sign * vel[0]
        pressures[place] = pressure
    for field in range(FIELDS):
        fluxes, scaled = {}, {}
        for place in span:
            if field == 0:
                flux = (0.5 * sign) * get(1, place)
            elif field == 4:
                flux = (get(4, place) + pressures[place]) * speeds[place]
            else:
                flux = get(field, place) * speeds[place]
                if field == 1:
                    flux = flux + (0.5 * sign) * pressures[place]
            fluxes[place] = flux
            scaled[place] = half_speed * get(field, place)
        yield field, x_divergence(fluxes, scaled, *parts)


WITH_HALOS = range(-3, BLOCK + 3)


def with_halos(far, near, inside, rows):
    def get(f, place):
        if place < 0:
            return far[f, -1 - place, rows, :]
        if place >= BLOCK:
            return near[f, BLOCK + 2 - place, rows, :]
        return inside(f, place)

    return get


def first_kernel(is_far, *refs):
    if is_far:
        state, sides, halo, speed, other, middle, side, top = refs
    else:
        state, sides, halo, speed, middle, side, top = refs
    first, parts, span = (0, FAR, range(-3, 4)) if is_far else (4, NEAR, range(4, 11))
    half_speed = 0.5 * speed[0:1, :]
    factor = (courant / 6.0) / speed[0:1, :]

    def group(j, best):
        rows = pl.ds(pl.multiple_of(j * 8, 8), 8)

        def inside(f, place):
            return state[f, place, rows, :]

        get = with_halos(halo, halo, inside, rows)
        for field, along_x in across(get, half_speed, span, parts):
            for k in range(4):
                total = sides[field, first + k, rows, :]
                if first + k in along_x:
                    total = total + along_x[first + k]
                value = get(field, first + k) - factor * total
                middle[field, k, rows, :] = value
                at = k if is_far else k - 1
                if 0 <= at < 3:
                    side[field, at, rows, :] = value
        for k in range(4):
            best = jnp.maximum(best, wave_speed([middle[f, k, rows, :] for f in range(FIELDS)]))
        return best

    start = other[...] if is_far else jnp.zeros((8, LANES), jnp.float32)
    best = lax.fori_loop(0, 4, group, start)
    top[...] = jnp.full((8, LANES), jnp.max(best), jnp.float32) if is_far else best


def first_stage(is_far, *operands):
    return pl.pallas_call(
        functools.partial(first_kernel, is_far),
        out_shape=(
            jax.ShapeDtypeStruct((FIELDS, 4, ROWS, LANES), jnp.float32),
            jax.ShapeDtypeStruct(HALO, jnp.float32),
            jax.ShapeDtypeStruct((8, LANES), jnp.float32),
        ),
        in_specs=[VMEM] * len(operands),
        out_specs=(VMEM,) * 3,
        compiler_params=params(),
        cost_estimate=cost(15_000_000, 2_000_000),
        name="first_far" if is_far else "first_near",
    )(*operands)


def second_kernel(state, middle_far, middle_near, sides, far, near, first_speed, speed, out):
    half_speed = 0.5 * speed[0:1, :]
    factor = (courant / 12.0) / first_speed[0:1, :]
    planes = [place_of(place) for place in range(BLOCK)]

    def group(j, carry):
        rows = pl.ds(pl.multiple_of(j * 8, 8), 8)
        spread = pl.ds(j, 8, stride=4)

        def inside(f, place):
            return (middle_far, middle_near)[place // 4][f, place % 4, rows, :]

        get = with_halos(far, near, inside, rows)
        for field, along_x in across(get, half_speed, WITH_HALOS, EVERY):
            for place in range(BLOCK):
                total = along_x[place] + sides[field, place, rows, :]
                value = 0.5 * state[field, place, rows, :] + (
                    0.5 * get(field, place) - factor * total
                )
                out[field, planes[place], spread, :] = value
        return carry

    lax.fori_loop(0, 4, group, 0)


def second_stage(*operands):
    return pl.pallas_call(
        second_kernel,
        out_shape=jax.ShapeDtypeStruct((FIELDS, BLOCK, ROWS, LANES), jnp.float32),
        in_specs=[VMEM] * len(operands),
        out_specs=VMEM,
        compiler_params=params(),
        cost_estimate=cost(30_000_000, 3_000_000),
        name="second_stage",
    )(*operands)


def everyone_max(value, axis, size):
    reach = 1
    while reach * 4 < size:
        reach *= 4
    while reach:
        copies = [value]
        for times in (3, 2, 1) if reach > 1 else (1, 2, 3):
            turn = reach * times
            if turn < size:
                pairs = [(i, i ^ turn) for i in range(size)]
                copies.append(lax.ppermute(value, axis, pairs))
        value = functools.reduce(jnp.maximum, copies)
        reach //= 4
    return value


def per_device(blocks, owner_list, slot_list):
    size = lax.axis_size("gx")
    own = lax.axis_index("gx")
    per_dev = blocks.shape[0]
    cap = max(2, 2 * per_dev // size)

    parts = pack(tiled_rows(blocks), owner_list, size, cap, per_dev)
    parts, owner_list, slot_list = lax.optimization_barrier((parts, owner_list, slot_list))
    come = lax.all_to_all(parts, "gx", split_axis=0, concat_axis=0, tiled=True)
    table = arrival_spots(owner_list, slot_list, own, per_dev, size, cap)
    state, far_side, near_side, speed = unpack(table, come.reshape(-1, 1, LANES), size, cap)
    far = from_far(far_side, size)
    near = from_near(near_side, size)
    sides = along_planes((state,), speed, True)
    middle_near, near_side, top = first_stage(False, state, sides, near, speed)
    middle_far, far_side, top = first_stage(True, state, sides, far, speed, top)
    far = from_far(far_side, size)
    near = from_near(near_side, size)
    second = everyone_max(top, "gx", size)
    sides = along_planes((middle_far, middle_near), second, False)
    return second_stage(state, middle_far, middle_near, sides, far, near, speed, second)


def solution(mesh):
    return jax.shard_map(
        per_device,
        mesh=mesh,
        in_specs=(P(("runs", "gx"), None, None), P("runs"), P("runs")),
        out_specs=P(None, ("runs", "gx"), None, None),
        check_vma=False,
    )
```

```python
import functools

import jax
import jax.numpy as jnp
from jax import lax
from jax.experimental import pallas as pl
from jax.experimental.pallas import tpu as pltpu
from jax.sharding import PartitionSpec as P

BLOCK = 8
BY = 4
BZ = 16
FIELDS = 5
LANES = 128
ROWS = BY * BLOCK
PAIRS = BLOCK // 2
TILES = PAIRS * FIELDS

gamma_gas = 1.4
courant = 0.25
smooth_epsilon = 1e-06

VMEM = pl.BlockSpec(memory_space=pltpu.VMEM)
SMEM = pl.BlockSpec(memory_space=pltpu.SMEM)


def params(mebibytes=40):
    return pltpu.CompilerParams(vmem_limit_bytes=mebibytes * 1024 * 1024)


def cost(flops, size):
    return pl.CostEstimate(flops=flops, bytes_accessed=size, transcendentals=0)


def wave_speed(fields):
    density, mom_x, mom_y, mom_z, energy = fields
    inverse = 1.0 / density
    vel = (mom_x * inverse, mom_y * inverse, mom_z * inverse)
    kinetic = 0.5 * (mom_x * vel[0] + mom_y * vel[1] + mom_z * vel[2])
    pressure = (gamma_gas - 1.0) * (energy - kinetic)
    sound = jnp.sqrt(gamma_gas * pressure * inverse)
    fastest = jnp.maximum(jnp.maximum(jnp.abs(vel[0]), jnp.abs(vel[1])), jnp.abs(vel[2]))
    return fastest + sound


def tiled_rows(blocks):
    count = blocks.shape[0] // 8
    groups = blocks.reshape(count, 8, FIELDS, PAIRS, LANES).transpose(2, 0, 3, 1, 4)
    return groups.reshape(FIELDS * count * PAIRS * 8, 1, LANES)


def pack_kernel(
    size, cap, per_dev, owner_hbm, rows_hbm, out_hbm, owner, rows, tiled, out, top, count, member, sems
):
    own = lax.axis_index("gx")
    fetch_owner = pltpu.make_async_copy(owner_hbm, owner, sems.at[0])
    fetch_rows = pltpu.make_async_copy(rows_hbm, rows, sems.at[1])
    fetch_tiled = pltpu.make_async_copy(rows_hbm.at[:, 0], tiled, sems.at[4])
    fetch_owner.start()
    fetch_rows.start()
    fetch_tiled.start()

    def clear(dest, carry):
        count[dest] = 0
        return carry

    lax.fori_loop(0, size, clear, 0, unroll=8)
    fetch_owner.wait()

    def note(block, carry):
        dest = owner[own * per_dev + block]
        rank = count[dest]
        count[dest] = rank + 1
        member[dest * cap + rank] = lax.div(block, 8) * (PAIRS * 8) + lax.rem(block, 8)
        return carry

    lax.fori_loop(0, per_dev, note, 0, unroll=8)
    fetch_rows.wait()
    tiles = TILES * cap

    def message(dest, carry):
        @pl.when(count[dest] > 0)
        def _():
            for rank in range(cap):
                first = member[dest * cap + rank]
                for pair in range(PAIRS):
                    for f in range(FIELDS):
                        to = dest * tiles + (pair * FIELDS + f) * cap + rank
                        out[to] = rows[first + f * (per_dev * PAIRS) + pair * 8]
            part = out.at[pl.ds(dest * tiles, tiles)]
            pltpu.make_async_copy(part, out_hbm.at[dest, pl.ds(0, tiles)], sems.at[2]).start()

        return carry

    lax.fori_loop(0, size, message, 0)
    fetch_tiled.wait()
    best = jnp.zeros((8, LANES), jnp.float32)
    step = per_dev * PAIRS
    for first in range(0, step, 8):
        fields = [tiled[f * step + first : f * step + first + 8, :] for f in range(FIELDS)]
        best = jnp.maximum(best, wave_speed(fields))
    most = jnp.full((1, LANES), jnp.max(best), jnp.float32)
    for dest in range(size):
        top[dest] = most
    send_top = pltpu.make_async_copy(top, out_hbm.at[:, tiles], sems.at[3])
    send_top.start()
    half = out.at[pl.ds(0, per_dev * TILES)]
    pltpu.make_async_copy(half, half, sems.at[2]).wait()
    send_top.wait()


def pack(rows, owner_list, size, cap, per_dev):
    return pl.pallas_call(
        functools.partial(pack_kernel, size, cap, per_dev),
        out_shape=jax.ShapeDtypeStruct((size, TILES * cap + 1, 1, LANES), jnp.float32),
        in_specs=[pl.BlockSpec(memory_space=pltpu.HBM)] * 2,
        out_specs=pl.BlockSpec(memory_space=pltpu.HBM),
        scratch_shapes=[
            pltpu.SMEM(owner_list.shape, jnp.int32),
            pltpu.VMEM(rows.shape, jnp.float32),
            pltpu.VMEM((rows.shape[0], LANES), jnp.float32),
            pltpu.VMEM((size * TILES * cap, 1, LANES), jnp.float32),
            pltpu.VMEM((size, 1, LANES), jnp.float32),
            pltpu.SMEM((size,), jnp.int32),
            pltpu.SMEM((size * cap,), jnp.int32),
            pltpu.SemaphoreType.DMA((5,)),
        ],
        compiler_params=params(62),
        cost_estimate=cost(1_000_000, 3_000_000),
        name="pack",
    )(owner_list, rows)


def turned_round():
    return lax.axis_index("gx") % 2


def place_of(plane):
    return jnp.where(turned_round() == 0, plane, BLOCK - 1 - plane)


def sign_of_x():
    return jnp.where(turned_round() == 0, 1.0, -1.0).astype(jnp.float32)


def from_far(far_side, size):
    pairs = [(i, (i - 1 if i % 2 == 0 else i + 1) % size) for i in range(size)]
    return lax.ppermute(far_side, "gx", pairs)


def from_near(near_side, size):
    return lax.ppermute(near_side, "gx", [(i, i ^ 1) for i in range(size)])


HALO = (FIELDS, 3, ROWS, LANES)


def arrival_spots(owner_list, slot_list, own, per_dev, size, cap):
    owners = owner_list.reshape(size, per_dev)
    slots = slot_list.reshape(size, per_dev)
    mine = owners == own
    spot = jnp.arange(per_dev, dtype=jnp.int32)
    earlier = spot[None, :] < spot[:, None]
    rank = jnp.sum((mine[:, None, :] & earlier[None]).astype(jnp.int32), axis=2)
    row = jnp.arange(size, dtype=jnp.int32)[:, None] * (TILES * cap + 1) + rank
    key = jnp.where(mine, slots, -1)
    hit = key.reshape(1, -1) == spot[:, None]
    return jnp.max(jnp.where(hit, row.reshape(1, -1), 0), axis=1)


def exchanged_bits(rows, group):
    rows = list(rows)
    for bit in range(4):
        step = 1 << bit
        low = (group & step) == 0
        for index in range(16):
            if index & step:
                continue
            first, second = rows[index], rows[index | step]
            rows[index] = jnp.where(low, first, pltpu.roll(second, 8 * step, 1))
            rows[index | step] = jnp.where(low, pltpu.roll(first, LANES - 8 * step, 1), second)
    return rows


def unpack_kernel(size, cap, table, come, state, far_side, near_side, speed, scratch):
    message = TILES * cap + 1
    best = come[message - 1]
    for source in range(1, size):
        best = jnp.maximum(best, come[(source + 1) * message - 1])
    speed[...] = jnp.broadcast_to(best, speed.shape)
    group = lax.broadcasted_iota(jnp.int32, (8, LANES), 1) // BLOCK
    even = lax.broadcasted_iota(jnp.int32, (8, LANES), 0) % 2 == 0
    half = FIELDS * BZ * 8
    places = [place_of(plane) for plane in range(BLOCK)]

    def gather(couple, slot):
        p, q = divmod(slot, BZ)
        first = table[slot]
        for h in range(2):
            for f in range(FIELDS):
                row = couple * half + (f * BZ + q) * 8 + 2 * p + h
                value = come[first + ((2 * couple + h) * FIELDS + f) * cap]
                scratch[row : row + 1, :] = value

    def arrange(couple, f):
        first = couple * half + f * BZ * 8
        moved = exchanged_bits(
            [scratch[first + q * 8 : first + q * 8 + 8, :] for q in range(BZ)], group
        )
        for second in range(2):
            for j in range(4):
                lower = moved[second * BLOCK + j]
                upper = moved[second * BLOCK + j + 4]
                planes = (
                    jnp.where(even, lower, pltpu.roll(upper, 1, 0)),
                    jnp.where(even, pltpu.roll(lower, 7, 0), upper),
                )
                for h in range(2):
                    state[f, places[4 * couple + 2 * h + second], j * 8 : j * 8 + 8, :] = planes[h]

    for slot in range(BY * BZ):
        gather(0, slot)
    for f in range(FIELDS):
        for slot in range(f, BY * BZ, FIELDS):
            gather(1, slot)
        arrange(0, f)
    for f in range(FIELDS):
        arrange(1, f)
    for f in range(FIELDS):
        for place in range(3):
            far_side[f, place] = state[f, place]
            near_side[f, place] = state[f, BLOCK - 3 + place]


def unpack(table, come, size, cap):
    halo = jax.ShapeDtypeStruct(HALO, jnp.float32)
    return pl.pallas_call(
        functools.partial(unpack_kernel, size, cap),
        out_shape=(
            jax.ShapeDtypeStruct((FIELDS, BLOCK, ROWS, LANES), jnp.float32),
            halo,
            halo,
            jax.ShapeDtypeStruct((8, LANES), jnp.float32),
        ),
        in_specs=[SMEM, VMEM],
        out_specs=(VMEM,) * 4,
        scratch_shapes=[pltpu.VMEM((FIELDS * (PAIRS // 2) * BZ * 8, LANES), jnp.float32)],
        compiler_params=params(),
        cost_estimate=cost(5_000_000, 2_000_000),
        name="unpack",
    )(table, come)


def y_up(x):
    return jnp.concatenate([x[8:], pltpu.roll(x[:8], 7, 0)], axis=0)


def y_down(x):
    return jnp.concatenate([pltpu.roll(x[24:], 1, 0), x[:24]], axis=0)


def y_up_two(x):
    return jnp.concatenate([x[16:], pltpu.roll(x[:8], 7, 0), pltpu.roll(x[8:16], 7, 0)], axis=0)


def inverse(x):
    return 1.0 / x


def smoothness(before, after):
    curve = after - before
    middle = 0.5 * (after + before)
    base = curve * curve * (13.0 / 12.0) + smooth_epsilon
    plus = middle + curve
    minus = middle - curve
    left = inverse(base + plus * plus)
    centre = inverse(base + middle * middle)
    right = inverse(base + minus * minus)
    return curve, left * left, centre * centre, right * right


def upwind_term(left, centre, right, jump_before, jump_after):
    right = 3.0 * right
    top = left * (jump_before + jump_before) + right * jump_after
    return top * inverse(left + 6.0 * centre + right)


def periodic_divergence(half_flux, scaled, up, up_two, down):
    plus = half_flux + scaled
    minus = half_flux - scaled

    def side(values):
        after = up(values) - values
        curve, left, centre, right = smoothness(down(after), after)
        above = up(curve)
        return curve, above, left, centre, right, above - curve

    curve, _, left, centre, right, jump = side(plus)
    face = 6.0 * (half_flux + up(half_flux)) - curve
    face = face - upwind_term(down(left), centre, up(right), down(jump), jump)
    _, curve, left, centre, right, jump = side(minus)
    face = face + (upwind_term(up_two(right), up(centre), left, up(jump), jump) - curve)
    return face - down(face)


def ring_divergence(half_flux, scaled):
    count = len(half_flux)

    def up(values):
        return values[1:] + [pltpu.roll(values[0], 7, 0)]

    def down(values):
        return [pltpu.roll(values[-1], 1, 0)] + values[:-1]

    def side(values):
        after = [above - value for above, value in zip(up(values), values)]
        parts = [smoothness(before, step) for before, step in zip(down(after), after)]
        curve, left, centre, right = (list(part) for part in zip(*parts))
        jump = [above - value for above, value in zip(up(curve), curve)]
        return curve, left, centre, right, jump

    curve, left, centre, right, jump = side([a + b for a, b in zip(half_flux, scaled)])
    terms = zip(down(left), centre, up(right), down(jump), jump)
    face = [
        6.0 * (here + above) - bend - upwind_term(*term)
        for here, above, bend, term in zip(half_flux, up(half_flux), curve, terms)
    ]
    curve, left, centre, right, jump = side([a - b for a, b in zip(half_flux, scaled)])
    terms = zip(up(right), centre, down(left), jump, down(jump))
    other = [upwind_term(*term) - bend for bend, term in zip(curve, terms)]
    face = [one + two for one, two in zip(face, up(other))]
    return [here - below for here, below in zip(face, down(face))]


def x_divergence(half_flux, scaled, plus_at, minus_at, centre_at):
    faces = {i: 6.0 * (half_flux[i] + half_flux[i + 1]) for i in centre_at}

    def add(i, value):
        faces[i] = faces[i] + value if i in faces else value

    def side(sign):
        values = {i: half_flux[i] + sign * scaled[i] for i in half_flux}
        steps = {i: values[i + 1] - values[i] for i in values if i + 1 in values}
        return {i: smoothness(steps[i - 1], steps[i]) for i in steps if i - 1 in steps}

    parts = side(1)
    for i in plus_at:
        curve, left, centre, right = zip(parts[i - 1], parts[i], parts[i + 1])
        term = upwind_term(left[0], centre[1], right[2], curve[1] - curve[0], curve[2] - curve[1])
        add(i, -(curve[1] + term))
    parts = side(-1)
    for i in minus_at:
        curve, left, centre, right = zip(parts[i - 1], parts[i], parts[i + 1])
        term = upwind_term(right[2], centre[1], left[0], curve[2] - curve[1], curve[1] - curve[0])
        add(i - 1, term - curve[1])
    total = {}
    for i in range(BLOCK):
        if i in faces:
            total[i] = faces[i]
        if i - 1 in faces:
            total[i] = total[i] - faces[i - 1] if i in total else -faces[i - 1]
    return total


INNER = (range(2, 6), range(2, 6), range(0, 7))
FAR = ((-1, 0, 1), (0, 1), (-1,))
NEAR = ((6, 7), (6, 7, 8), (7,))
EVERY = (range(-1, 8), range(0, 9), range(-1, 8))


def ring_divergence(half_flux, scaled):
    count = len(half_flux)

    def up(values):
        return values[1:] + [pltpu.roll(values[0], 7, 0)]

    def down(values):
        return [pltpu.roll(values[-1], 1, 0)] + values[:-1]

    def side(values):
        after = [above - value for above, value in zip(up(values), values)]
        parts = [smoothness(before, step) for before, step in zip(down(after), after)]
        curve, left, centre, right = (list(part) for part in zip(*parts))
        jump = [above - value for above, value in zip(up(curve), curve)]
        return curve, left, centre, right, jump

    curve, left, centre, right, jump = side([a + b for a, b in zip(half_flux, scaled)])
    terms = zip(down(left), centre, up(right), down(jump), jump)
    face = [
        6.0 * (here + above) - bend - upwind_term(*term)
        for here, above, bend, term in zip(half_flux, up(half_flux), curve, terms)
    ]
    curve, left, centre, right, jump = side([a - b for a, b in zip(half_flux, scaled)])
    terms = zip(up(right), centre, down(left), jump, down(jump))
    other = [upwind_term(*term) - bend for bend, term in zip(curve, terms)]
    face = [one + two for one, two in zip(face, up(other))]
    return [here - below for here, below in zip(face, down(face))]


def open_divergence(half_flux, scaled):
    count = len(half_flux)
    plus = [a + b for a, b in zip(half_flux, scaled)]
    minus = [a - b for a, b in zip(half_flux, scaled)]
    faces = [None] * count

    def side(values):
        steps = [values[i + 1] - values[i] for i in range(count - 1)]
        parts = [None] + [smoothness(steps[i - 1], steps[i]) for i in range(1, count - 1)]
        return parts

    parts = side(plus)
    for i in range(2, count - 3):
        jump_before = parts[i][0] - parts[i - 1][0]
        jump_after = parts[i + 1][0] - parts[i][0]
        faces[i] = 6.0 * (half_flux[i] + half_flux[i + 1]) - parts[i][0] - upwind_term(
            parts[i - 1][1], parts[i][2], parts[i + 1][3], jump_before, jump_after
        )
    parts = side(minus)
    for i in range(3, count - 2):
        jump_before = parts[i][0] - parts[i - 1][0]
        jump_after = parts[i + 1][0] - parts[i][0]
        faces[i - 1] = faces[i - 1] + (
            upwind_term(parts[i + 1][3], parts[i][2], parts[i - 1][1], jump_after, jump_before)
            - parts[i][0]
        )
    return [faces[i] - faces[i - 1] for i in range(3, count - 3)]


def half_velocities(fields):
    density, mom_x, mom_y, mom_z, energy = fields
    over = 0.5 / density
    vel = (mom_x * over, mom_y * over, mom_z * over)
    kinetic = mom_x * vel[0] + mom_y * vel[1] + mom_z * vel[2]
    pressure = (gamma_gas - 1.0) * (energy - kinetic)
    return vel, pressure


def half_flux(fields, field, direction, speed, pressure):
    if field == 0:
        return 0.5 * fields[1 + direction]
    if field == 4:
        return (fields[4] + pressure) * speed
    flux = fields[field] * speed
    return flux + 0.5 * pressure if field == 1 + direction else flux


def plane_kernel(with_inner, *refs):
    *states, speed, out, turned = refs
    half_speed = 0.5 * speed[0:1, :]
    lane = lax.broadcasted_iota(jnp.int32, (LANES, LANES), 1)
    to_turned = (lane % 8) * 16 + lane // 8
    to_plain = (lane % 16) * 8 + lane // 16

    for part in range(2):
        state, first = (states[0], 4 * part) if len(states) == 1 else (states[part], 0)
        for f in range(FIELDS):
            plain = state[f, first : first + 4].reshape(LANES, LANES)
            turned[f] = jnp.take_along_axis(plain, to_turned, axis=1).T
        for place in range(4):
            fields = [state[f, first + place] for f in range(FIELDS)]
            vel, pressure = half_velocities(fields)
            for field in range(FIELDS):
                out[field, part * 4 + place] = periodic_divergence(
                    half_flux(fields, field, 1, vel[1], pressure),
                    half_speed * fields[field],
                    y_up,
                    y_up_two,
                    y_down,
                )
        columns = [
            [turned[f, row : row + 8] for row in range(0, LANES, 8)] for f in range(FIELDS)
        ]
        along = [half_velocities(fields) for fields in zip(*columns)]
        for field in range(FIELDS):
            fluxes = [
                half_flux(fields, field, 2, vel[2], pressure)
                for fields, (vel, pressure) in zip(zip(*columns), along)
            ]
            scaled = [half_speed * value for value in columns[field]]
            total = jnp.concatenate(ring_divergence(fluxes, scaled), axis=0)
            plain = jnp.take_along_axis(total.T, to_plain, axis=1)
            out[field, part * 4 : part * 4 + 4] += plain.reshape(4, ROWS, LANES)

    def group(j, carry):
        rows = pl.ds(pl.multiple_of(j * 8, 8), 8)

        def get(f, place):
            return states[0][f, place, rows, :]

        for field, along_x in across(get, half_speed, range(BLOCK), INNER):
            for place in range(BLOCK):
                out[field, place, rows, :] += along_x[place]
        return carry

    if with_inner:
        lax.fori_loop(0, 4, group, 0)


def along_planes(states, speed, with_inner):
    return pl.pallas_call(
        functools.partial(plane_kernel, with_inner),
        out_shape=jax.ShapeDtypeStruct((FIELDS, BLOCK, ROWS, LANES), jnp.float32),
        in_specs=[VMEM] * (len(states) + 1),
        out_specs=VMEM,
        scratch_shapes=[pltpu.VMEM((FIELDS, LANES, LANES), jnp.float32)],
        compiler_params=params(),
        cost_estimate=cost(20_000_000, 1_000_000),
        name="planes",
    )(*states, speed)


def across(get, half_speed, span, parts):
    sign = sign_of_x()
    speeds, pressures = {}, {}
    for place in span:
        vel, pressure = half_velocities([get(f, place) for f in range(FIELDS)])
        speeds[place] = sign * vel[0]
        pressures[place] = pressure
    for field in range(FIELDS):
        fluxes, scaled = {}, {}
        for place in span:
            if field == 0:
                flux = (0.5 * sign) * get(1, place)
            elif field == 4:
                flux = (get(4, place) + pressures[place]) * speeds[place]
            else:
                flux = get(field, place) * speeds[place]
                if field == 1:
                    flux = flux + (0.5 * sign) * pressures[place]
            fluxes[place] = flux
            scaled[place] = half_speed * get(field, place)
        yield field, x_divergence(fluxes, scaled, *parts)


WITH_HALOS = range(-3, BLOCK + 3)


def with_halos(far, near, inside, rows):
    def get(f, place):
        if place < 0:
            return far[f, -1 - place, rows, :]
        if place >= BLOCK:
            return near[f, BLOCK + 2 - place, rows, :]
        return inside(f, place)

    return get


def first_kernel(is_far, *refs):
    if is_far:
        state, sides, halo, speed, other, middle, side, top = refs
    else:
        state, sides, halo, speed, middle, side, top = refs
    first, parts, span = (0, FAR, range(-3, 4)) if is_far else (4, NEAR, range(4, 11))
    half_speed = 0.5 * speed[0:1, :]
    factor = (courant / 6.0) / speed[0:1, :]

    def group(j, best):
        rows = pl.ds(pl.multiple_of(j * 8, 8), 8)

        def inside(f, place):
            return state[f, place, rows, :]

        get = with_halos(halo, halo, inside, rows)
        for field, along_x in across(get, half_speed, span, parts):
            for k in range(4):
                total = sides[field, first + k, rows, :]
                if first + k in along_x:
                    total = total + along_x[first + k]
                value = get(field, first + k) - factor * total
                middle[field, k, rows, :] = value
                at = k if is_far else k - 1
                if 0 <= at < 3:
                    side[field, at, rows, :] = value
        for k in range(4):
            best = jnp.maximum(best, wave_speed([middle[f, k, rows, :] for f in range(FIELDS)]))
        return best

    start = other[...] if is_far else jnp.zeros((8, LANES), jnp.float32)
    best = lax.fori_loop(0, 4, group, start)
    top[...] = jnp.full((8, LANES), jnp.max(best), jnp.float32) if is_far else best


def first_stage(is_far, *operands):
    return pl.pallas_call(
        functools.partial(first_kernel, is_far),
        out_shape=(
            jax.ShapeDtypeStruct((FIELDS, 4, ROWS, LANES), jnp.float32),
            jax.ShapeDtypeStruct(HALO, jnp.float32),
            jax.ShapeDtypeStruct((8, LANES), jnp.float32),
        ),
        in_specs=[VMEM] * len(operands),
        out_specs=(VMEM,) * 3,
        compiler_params=params(),
        cost_estimate=cost(15_000_000, 2_000_000),
        name="first_far" if is_far else "first_near",
    )(*operands)


def second_kernel(state, middle_far, middle_near, sides, far, near, first_speed, speed, out):
    half_speed = 0.5 * speed[0:1, :]
    factor = (courant / 12.0) / first_speed[0:1, :]
    planes = [place_of(place) for place in range(BLOCK)]

    def group(j, carry):
        rows = pl.ds(pl.multiple_of(j * 8, 8), 8)
        spread = pl.ds(j, 8, stride=4)

        def inside(f, place):
            return (middle_far, middle_near)[place // 4][f, place % 4, rows, :]

        get = with_halos(far, near, inside, rows)
        for field, along_x in across(get, half_speed, WITH_HALOS, EVERY):
            for place in range(BLOCK):
                total = along_x[place] + sides[field, place, rows, :]
                value = 0.5 * state[field, place, rows, :] + (
                    0.5 * get(field, place) - factor * total
                )
                out[field, planes[place], spread, :] = value
        return carry

    lax.fori_loop(0, 4, group, 0)


def second_stage(*operands):
    return pl.pallas_call(
        second_kernel,
        out_shape=jax.ShapeDtypeStruct((FIELDS, BLOCK, ROWS, LANES), jnp.float32),
        in_specs=[VMEM] * len(operands),
        out_specs=VMEM,
        compiler_params=params(),
        cost_estimate=cost(30_000_000, 3_000_000),
        name="second_stage",
    )(*operands)


def everyone_max(value, axis, size):
    reach = 1
    while reach * 4 < size:
        reach *= 4
    while reach:
        copies = [value]
        for times in (1, 2, 3) if reach > 1 else (3, 2, 1):
            turn = reach * times
            if turn < size:
                pairs = [(i, i ^ turn) for i in range(size)]
                copies.append(lax.ppermute(value, axis, pairs))
        value = functools.reduce(jnp.maximum, copies)
        reach //= 4
    return value


def per_device(blocks, owner_list, slot_list):
    size = lax.axis_size("gx")
    own = lax.axis_index("gx")
    per_dev = blocks.shape[0]
    cap = max(2, 2 * per_dev // size)

    parts = pack(tiled_rows(blocks), owner_list, size, cap, per_dev)
    parts, owner_list, slot_list = lax.optimization_barrier((parts, owner_list, slot_list))
    come = lax.all_to_all(parts, "gx", split_axis=0, concat_axis=0, tiled=True)
    table = arrival_spots(owner_list, slot_list, own, per_dev, size, cap)
    state, far_side, near_side, speed = unpack(table, come.reshape(-1, 1, LANES), size, cap)
    far = from_far(far_side, size)
    near = from_near(near_side, size)
    sides = along_planes((state,), speed, True)
    middle_near, near_side, top = first_stage(False, state, sides, near, speed)
    middle_far, far_side, top = first_stage(True, state, sides, far, speed, top)
    far = from_far(far_side, size)
    near = from_near(near_side, size)
    second = everyone_max(top, "gx", size)
    sides = along_planes((middle_far, middle_near), second, False)
    return second_stage(state, middle_far, middle_near, sides, far, near, speed, second)


def solution(mesh):
    return jax.shard_map(
        per_device,
        mesh=mesh,
        in_specs=(P(("runs", "gx"), None, None), P("runs"), P("runs")),
        out_specs=P(None, ("runs", "gx"), None, None),
        check_vma=False,
    )
```
